32 devices in a mesh: seq: 8 (over z, y), head: 4 (over x, core).
Axes of the slice: x: 2, y: 2, z: 4, core: 2. Of those that a mesh axis runs over, the one named last changes fastest.
Arguments:
- block_input: bfloat16 [8, 512, 4096], P(None, 'seq'), may hold values from -6 to 6
- lengths: int32 [8], replicated, may hold values from 1 to 4096, as said below
- cache_keys: bfloat16 [8, 4096, 4096], P(None, 'seq', 'head'), may hold values from -6 to 6
- cache_values: bfloat16 [8, 4096, 4096], P(None, 'seq', 'head'), may hold values from -6 to 6
- w_query: bfloat16 [4096, 4096], P('seq', 'head'), may hold values from -1 to 1
- w_key: bfloat16 [4096, 4096], P('seq', 'head'), may hold values from -1 to 1
- w_value: bfloat16 [4096, 4096], P('seq', 'head'), may hold values from -0.09375 to 0.09375
- w_attn_out: bfloat16 [4096, 2048], P('head'), may hold values from -0.09375 to 0.09375
- norm_gain: float32 [2048], replicated, may hold values from 0.25 to 1.75
- w_in: bfloat16 [2048, 2, 4096], P(None, None, 'head'), may hold values from -0.125 to 0.125
- w_bc: bfloat16 [2048, 128], replicated, may hold values from -0.125 to 0.125
- w_dt: bfloat16 [2048, 64], P(None, 'head'), may hold values from -0.125 to 0.125
- dt_bias: float32 [64], P('head'), may hold values from -5 to 0
- a_log: float32 [64], P('head'), may hold values from -4 to 1
- d_skip: float32 [64], P('head'), may hold values from 0.5 to 1.5
- gated_gain: float32 [4096], P('head'), may hold values from 0.1 to 1.9
- w_out: bfloat16 [4096, 2048], P('head'), may hold values from -0.09375 to 0.09375
- ssm_init: float32 [8, 64, 4096], P(None, 'head'), may hold values from -6 to 6
Outputs:
- mixed: bfloat16 [8, 512, 2048], P(None, 'seq', 'head')
- new_keys: bfloat16 [8, 512, 4096], P(None, 'seq', 'head')
- new_values: bfloat16 [8, 512, 4096], P(None, 'seq', 'head')
- chain_states: float32 [8, 8, 64, 4096], P(None, 'seq', 'head')
- greatest_logit: float32 [8, 512, 32], P(None, 'seq', 'head')
The draws below stay inside these ranges and needn't reach their ends.
Inputs may be any that keep to these rules, and one draw needn't show every extreme that they name: `lengths`: every request has at least one cached token, and one request's cache holds exactly 4096 tokens.
All inputs are finite; a program needn't handle non-finite values.
Results may differ from the reference program's by a relative error of at most 0.019.
Values may be sent and summed in bfloat16 or wider, within the bound.
No kernel may reach another device: no remote copies, remote signals or barrier semaphores. Data moves between devices by JAX's collectives and lax.ppermute only.
A program may use at most 256 MiB of HBM per device.

```python
import math
import jax
import jax.numpy as jnp
from jax import lax

D = 2048
DCAT = 4096
HEADS = 32
HEAD_DIM = 128
ATT = 4096
MHEADS = 64
MHEAD_DIM = 64
STATE = 64
D_INNER = 4096
REQS = 8
GROUP = 512
TOK_REQ = 64
CACHE_MAX = 4096
N_SEQ = 8


def draw_lengths(key, part):
    key_lengths, key_pick = jax.random.split(key)
    drawn = jax.random.randint(key_lengths, (REQS,), 1, CACHE_MAX + 1)
    chosen = jax.random.randint(key_pick, (), 0, REQS)
    return jnp.where(jnp.arange(REQS) == chosen, CACHE_MAX, drawn).astype(jnp.int32)


def projection_draw(key, salt):
    base = jax.random.truncated_normal(jax.random.fold_in(key, salt), -5.0, 5.0, (DCAT, ATT), jnp.float32) * (1.0 / math.sqrt(DCAT))
    return base.astype(jnp.bfloat16)


def draw_w_query(key, part):
    return projection_draw(key, 5201)


def draw_w_key(key, part):
    return projection_draw(key, 5202)


def draw_block_input(key, part):
    noise = jax.random.truncated_normal(jax.random.fold_in(key, 5301), -6.0, 6.0, (REQS, GROUP, DCAT), jnp.float32)
    return noise.astype(jnp.bfloat16)


def level_of(own_key, extent, cuts, low, largest):
    factor_of = 1.0
    for axis_at, shards_of in cuts:
        steps = jax.random.uniform(jax.random.fold_in(jax.random.fold_in(own_key, 6), axis_at), (shards_of,), jnp.float32, low / len(cuts), largest / len(cuts))
        factor_of = factor_of * jnp.repeat(jnp.exp(steps), extent[axis_at] // shards_of).reshape((-1,) + (1,) * (len(extent) - 1 - axis_at))
    return factor_of


def centred(stream_key, shape, scale, bound, pieces=(), kind=jnp.bfloat16):
    values = jax.random.normal(stream_key, shape, jnp.float32) * scale
    if len(pieces) > 0:
        values = level_of(stream_key, shape, pieces, -0.22, 0.18) * values
    return jnp.clip(values, min=-bound, max=bound).astype(kind)


def setup_inputs(seed: int = 0) -> dict:
    seeds = jax.random.split(jax.random.key(seed), 19)
    block_input = draw_block_input(jax.random.fold_in(seeds[18], 71), 0)
    lengths = draw_lengths(jax.random.fold_in(seeds[18], 71), 0)
    cache_keys = centred(seeds[2], (REQS, CACHE_MAX, ATT), 1.0, 6.0, ((1, 8), (2, 4)))
    cache_values = centred(seeds[3], (REQS, CACHE_MAX, ATT), 1.0, 6.0, ((1, 8), (2, 4)))
    w_query = draw_w_query(jax.random.fold_in(seeds[18], 71), 0)
    w_key = draw_w_key(jax.random.fold_in(seeds[18], 71), 0)
    w_value = centred(seeds[6], (DCAT, ATT), DCAT ** -0.5, 0.09375, ((0, 8), (1, 4)))
    w_attn_out = centred(seeds[7], (ATT, D), ATT ** -0.5, 0.09375, ((0, 4),))
    norm_gain = jnp.clip(1.0 + 0.15 * jax.random.normal(seeds[8], (D,), jnp.float32), 0.25, 1.75)
    w_in = centred(seeds[9], (D, 2, D_INNER), D ** -0.5, 0.125, ((2, 4),))
    w_bc = centred(seeds[10], (D, 2 * STATE), D ** -0.5, 0.125)
    w_dt = centred(seeds[11], (D, MHEADS), D ** -0.5, 0.125, ((1, 4),))
    dt_bias = jnp.clip(-5.0 + 5.0 * jax.random.uniform(seeds[12], (MHEADS,), jnp.float32) ** level_of(seeds[12], (MHEADS,), ((0, 4),), -0.2, 0.2), -5.0, 0.0)
    a_log = jnp.clip(-4.0 + 5.0 * jax.random.uniform(seeds[13], (MHEADS,), jnp.float32) ** level_of(seeds[13], (MHEADS,), ((0, 4),), -0.2, 0.2), -4.0, 1.0)
    d_skip = jnp.clip(0.5 + 1.0 * jax.random.uniform(seeds[14], (MHEADS,), jnp.float32) ** level_of(seeds[14], (MHEADS,), ((0, 4),), -0.2, 0.2), 0.5, 1.5)
    gated_gain = jnp.clip(1.0 + 0.18 * jax.random.normal(seeds[15], (D_INNER,), jnp.float32), 0.1, 1.9)
    w_out = centred(seeds[16], (D_INNER, D), D_INNER ** -0.5, 0.09375, ((0, 4),))
    ssm_init = centred(seeds[17], (REQS, MHEADS, MHEAD_DIM * STATE), 1.0, 6.0, ((1, 4),), jnp.float32)
    return dict(block_input=block_input, lengths=lengths, cache_keys=cache_keys, cache_values=cache_values, w_query=w_query, w_key=w_key, w_value=w_value, w_attn_out=w_attn_out, norm_gain=norm_gain, w_in=w_in, w_bc=w_bc, w_dt=w_dt, dt_bias=dt_bias, a_log=a_log, d_skip=d_skip, gated_gain=gated_gain, w_out=w_out, ssm_init=ssm_init)


def rotate(values, positions):
    half_dim = values.shape[-1] // 2
    frequency = jnp.exp(jnp.arange(half_dim, dtype=jnp.float32) * (-2.0 * math.log(10000.0) / values.shape[-1]))
    angles = positions.astype(jnp.float32)[:, :, None, None] * frequency
    cosine = jnp.cos(angles)
    sine_part = jnp.sin(angles)
    front_half = values[..., :half_dim]
    back_half = values[..., half_dim:]
    return jnp.concatenate([front_half * cosine - back_half * sine_part, back_half * cosine + front_half * sine_part], axis=-1)

def reference(block_input, lengths, cache_keys, cache_values, w_query, w_key, w_value, w_attn_out, norm_gain, w_in, w_bc, w_dt, dt_bias, a_log, d_skip, gated_gain, w_out, ssm_init):
    flat_input = block_input.reshape(REQS * GROUP, DCAT)
    positions = lengths[:, None] + jnp.arange(GROUP, dtype=jnp.int32)[None, :]

    def project(weight_matrix):
        return jnp.dot(flat_input, weight_matrix, preferred_element_type=jnp.float32).reshape(REQS, GROUP, HEADS, HEAD_DIM)
    queries = rotate(project(w_query), positions).astype(jnp.bfloat16)
    new_keys = rotate(project(w_key), positions).astype(jnp.bfloat16)
    new_values = project(w_value).astype(jnp.bfloat16)
    all_keys = jnp.concatenate([cache_keys.reshape(REQS, CACHE_MAX, HEADS, HEAD_DIM), new_keys], axis=1)
    all_values = jnp.concatenate([cache_values.reshape(REQS, CACHE_MAX, HEADS, HEAD_DIM), new_values], axis=1)
    group_mask = jnp.arange(GROUP, dtype=jnp.int32)[None, :] <= jnp.arange(GROUP, dtype=jnp.int32)[:, None]
    score_scale = 1.0 / math.sqrt(HEAD_DIM)

    def attend(request_items):
        query_one, keys_one, values_one, length_one = request_items
        cache_mask = jnp.broadcast_to((jnp.arange(CACHE_MAX, dtype=jnp.int32) < length_one)[None, :], (GROUP, CACHE_MAX))
        live_mask = jnp.concatenate([cache_mask, group_mask], axis=1)

        def per_head(head_items):
            query_head, keys_head, values_head = head_items
            scores = jnp.dot(query_head.astype(jnp.float32), keys_head.astype(jnp.float32).T) * score_scale
            masked = jnp.where(live_mask, scores, -1e+30)
            peaks = lax.optimization_barrier(jnp.max(masked, axis=1))
            weights = jnp.where(live_mask, jnp.exp(masked - peaks[:, None]), 0.0)
            totals = lax.optimization_barrier(jnp.sum(weights, axis=1))
            output = jnp.dot(weights.astype(jnp.bfloat16), values_head, preferred_element_type=jnp.float32) / totals[:, None]
            return (output, peaks)
        outputs, peak_rows = lax.map(per_head, (jnp.transpose(query_one, (1, 0, 2)), jnp.transpose(keys_one, (1, 0, 2)), jnp.transpose(values_one, (1, 0, 2))))
        return (jnp.transpose(outputs, (1, 0, 2)), peak_rows.T)
    attended, greatest_logit = lax.map(attend, (queries, all_keys, all_values, lengths))
    attended = attended.reshape(REQS * GROUP, ATT).astype(jnp.bfloat16)
    attn_proj = jnp.dot(attended, w_attn_out, preferred_element_type=jnp.float32).reshape(REQS, GROUP, D)
    hidden = block_input[:, :, :D].astype(jnp.float32)
    normed = (hidden * lax.rsqrt(lax.optimization_barrier(jnp.mean(hidden * hidden, axis=-1, keepdims=True)) + 1e-05) * norm_gain).astype(jnp.bfloat16)
    flat_normed = normed.reshape(REQS * GROUP, D)
    gate_inner = jnp.dot(flat_normed, w_in.reshape(D, 2 * D_INNER), preferred_element_type=jnp.float32).reshape(REQS, GROUP, 2, D_INNER)
    gate_part = gate_inner[:, :, 0]
    inner_act = jax.nn.silu(gate_inner[:, :, 1])
    bc_part = jnp.dot(flat_normed, w_bc, preferred_element_type=jnp.float32).reshape(REQS, GROUP, 2 * STATE)
    input_map = bc_part[..., :STATE]
    output_map = bc_part[..., STATE:]
    step_size = jax.nn.softplus(jnp.dot(flat_normed, w_dt, preferred_element_type=jnp.float32).reshape(REQS, GROUP, MHEADS) + dt_bias)
    log_decay = -step_size * jnp.exp(a_log)
    inner_heads = inner_act.reshape(REQS, GROUP, MHEADS, MHEAD_DIM)

    def to_blocks(series):
        moved = jnp.moveaxis(series, 1, 0)
        return moved.reshape((N_SEQ, TOK_REQ) + moved.shape[1:])

    def token_step(carry_state, token_items):
        decay_one, size_one, inner_one, input_one, output_one = token_items
        carry_state = jnp.exp(decay_one)[:, :, None, None] * carry_state + (size_one[:, :, None] * inner_one)[:, :, :, None] * input_one[:, None, None, :]
        reading = jnp.einsum('rhpn,rn->rhp', carry_state, output_one, precision=lax.Precision.HIGHEST)
        return (carry_state, reading)

    def block_step(carry_state, block_items):
        carry_state, readings = lax.scan(token_step, carry_state, block_items)
        return (carry_state, (carry_state, readings))
    initial = ssm_init.reshape(REQS, MHEADS, MHEAD_DIM, STATE)
    final_state, (block_states, readings) = lax.scan(block_step, initial, (to_blocks(log_decay), to_blocks(step_size), to_blocks(inner_heads), to_blocks(input_map), to_blocks(output_map)))
    readings = jnp.moveaxis(readings.reshape(GROUP, REQS, MHEADS, MHEAD_DIM), 0, 1)
    read_out = readings + d_skip[:, None] * inner_heads
    chain_states = jnp.transpose(block_states, (1, 0, 2, 3, 4)).reshape(REQS, N_SEQ, MHEADS, MHEAD_DIM * STATE)
    mixed_inner = read_out.reshape(REQS, GROUP, D_INNER) * jax.nn.silu(gate_part)
    mean_square = lax.optimization_barrier(jnp.mean(mixed_inner * mixed_inner, axis=-1, keepdims=True))
    gated = (mixed_inner * gated_gain).astype(jnp.bfloat16)
    mamba_proj = jnp.dot(gated.reshape(REQS * GROUP, D_INNER), w_out, preferred_element_type=jnp.float32).reshape(REQS, GROUP, D) * lax.rsqrt(mean_square + 1e-05)
    mixed = (hidden + attn_proj + mamba_proj).astype(jnp.bfloat16)
    return (mixed, new_keys.reshape(REQS, GROUP, ATT), new_values.reshape(REQS, GROUP, ATT), chain_states, greatest_logit)
```

```python
import functools
import math

import jax
import jax.numpy as jnp
from jax import lax
from jax.experimental import pallas as pl
from jax.experimental.pallas import tpu as pltpu
from jax.sharding import PartitionSpec as P

D = 2048
HEAD_DIM = 128
MHEAD_DIM = 64
STATE = 64
D_INNER = 4096
SCALE = 1.0 / math.sqrt(HEAD_DIM)
EXP2_SCALE = SCALE * math.log2(math.e)
DEAD = -1e30
GROUPS = 2


def ring_order(count):
    y_count = max(1, count // 4)
    z_count = count // y_count
    order = []
    for y in range(y_count):
        turn = range(z_count) if y % 2 == 0 else range(z_count - 1, -1, -1)
        order += [z * y_count + y for z in turn]
    return order


def ring_step(block, order, distance):
    count = len(order)
    route = [(order[i], order[(i + distance) % count]) for i in range(count)]
    return lax.ppermute(block, "seq", route)


def ring_gather(block, order):
    count = len(order)
    half = block.shape[0] // 2
    pieces = [(0, 0, block)]
    ahead = back = block
    for step in range(1, count // 2):
        ahead = ring_step(ahead, order, 1)
        back = ring_step(back, order, -1)
        pieces += [(step, 0, ahead), (-step, 0, back)]
    pieces.append((count // 2, 0, ring_step(ahead[:half], order, 1)))
    pieces.append((count // 2, half, ring_step(back[half:], order, -1)))
    return pieces


def ring_sum(parts, order):
    count = len(order)
    far = count // 2
    half = parts[0].shape[0] // 2
    add = lambda a, b: (a.astype(jnp.float32) + b.astype(jnp.float32)).astype(jnp.bfloat16)
    ahead = ring_step(parts[far][:half], order, 1)
    back = ring_step(parts[far][half:], order, -1)
    top, bottom = parts[far - 1], parts[-(far - 1)]
    ahead = jnp.concatenate([add(ahead, top[:half]), top[half:]], axis=0)
    back = jnp.concatenate([bottom[:half], add(back, bottom[half:])], axis=0)
    for step in range(far - 1, 0, -1):
        ahead = ring_step(ahead, order, 1)
        back = ring_step(back, order, -1)
        if step > 1:
            ahead = add(ahead, parts[step - 1])
            back = add(back, parts[-(step - 1)])
    return (
        ahead.astype(jnp.float32) + back.astype(jnp.float32) + parts[0].astype(jnp.float32)
    )


def after(value, *earlier):
    return lax.optimization_barrier((value,) + earlier)[0]


def rope_kernel(value_ref, cosine_ref, sine_ref, out_ref):
    cosine = cosine_ref[...]
    sine = sine_ref[...]
    for head in range(value_ref.shape[1] // HEAD_DIM):
        at = slice(head * HEAD_DIM, (head + 1) * HEAD_DIM)
        part = value_ref[:, at]
        turned = part * cosine + pltpu.roll(part, HEAD_DIM // 2, 1) * sine
        out_ref[:, at] = turned.astype(out_ref.dtype)


def rope(value, cosine, sine):
    rows, width = value.shape
    block = min(rows, 128)
    return pl.pallas_call(
        rope_kernel,
        grid=(rows // block,),
        in_specs=[
            pl.BlockSpec((block, width), lambda i: (i, 0)),
            pl.BlockSpec((block, HEAD_DIM), lambda i: (i, 0)),
            pl.BlockSpec((block, HEAD_DIM), lambda i: (i, 0)),
        ],
        out_specs=pl.BlockSpec((block, width), lambda i: (i, 0)),
        out_shape=jax.ShapeDtypeStruct((rows, width), jnp.bfloat16),
        cost_estimate=pl.CostEstimate(
            flops=4 * rows * width, bytes_accessed=6 * rows * width, transcendentals=0
        ),
        name="rope",
    )(value, cosine, sine)


def dot_nt(a, b):
    return lax.dot_general(a, b, (((1,), (1,)), ((), ())), preferred_element_type=jnp.float32)


def dot_tn(a, b):
    return lax.dot_general(a, b, (((0,), (0,)), ((), ())), preferred_element_type=jnp.float32)


def cache_kernel(slots, place_ref, live_ref, *refs):
    query_refs = refs[:slots]
    key_ref, value_ref, joined_ref, out_ref, peak_ref, total_ref = refs[slots:]
    tok_block = query_refs[0].shape[1]
    keys, width = key_ref.shape[1:]
    tokens = tok_block * slots
    for slot in range(slots):
        start = pl.multiple_of(place_ref[slot] * tok_block, tok_block)
        joined_ref[0, pl.ds(start, tok_block), :] = query_refs[slot][0]
    live = live_ref[pl.program_id(0)]
    bias = jnp.where(
        lax.broadcasted_iota(jnp.int32, (keys, 128), 0) < live, 0.0, DEAD
    ).astype(jnp.float32)
    bias = jnp.concatenate([bias] * (tokens // 128), axis=1)
    for head in range(width // HEAD_DIM):
        at = slice(head * HEAD_DIM, (head + 1) * HEAD_DIM)
        scores = dot_nt(key_ref[0, :, at], joined_ref[0, :, at]) + bias
        peak = jnp.max(scores, axis=0, keepdims=True)
        weights = jnp.exp2((scores - peak) * EXP2_SCALE)
        total_ref[0, head : head + 1, :] = jnp.sum(weights, axis=0, keepdims=True)
        peak_ref[0, head : head + 1, :] = peak
        out_ref[0, at, :] = dot_tn(value_ref[0, :, at], weights.astype(jnp.bfloat16)).astype(
            out_ref.dtype
        )


def cache_part(places, live, query_slots, keys, values):
    slots = len(query_slots)
    requests, tok_block, width = query_slots[0].shape
    tokens = tok_block * slots
    cache_block = keys.shape[1]
    heads = width // HEAD_DIM
    one = lambda rows: pl.BlockSpec((1, rows, width), lambda r, *_: (r, 0, 0))
    stat = pl.BlockSpec((1, heads, tokens), lambda r, *_: (r, 0, 0))
    return pl.pallas_call(
        functools.partial(cache_kernel, slots),
        grid_spec=pltpu.PrefetchScalarGridSpec(
            num_scalar_prefetch=2,
            grid=(requests,),
            in_specs=[one(tok_block)] * slots + [one(cache_block), one(cache_block)],
            out_specs=[
                one(tokens),
                pl.BlockSpec((1, width, tokens), lambda r, *_: (r, 0, 0)),
                stat,
                stat,
            ],
        ),
        out_shape=[
            jax.ShapeDtypeStruct((requests, tokens, width), jnp.bfloat16),
            jax.ShapeDtypeStruct((requests, width, tokens), jnp.bfloat16),
            jax.ShapeDtypeStruct((requests, heads, tokens), jnp.float32),
            jax.ShapeDtypeStruct((requests, heads, tokens), jnp.float32),
        ],
        compiler_params=pltpu.CompilerParams(vmem_limit_bytes=48 * 1024 * 1024),
        cost_estimate=pl.CostEstimate(
            flops=4 * requests * tokens * cache_block * width,
            bytes_accessed=2 * requests * width * (3 * tokens + 2 * cache_block),
            transcendentals=requests * tokens * cache_block * heads,
        ),
        name="cache_part",
    )(places, live, *query_slots, keys, values)


def group_scores(first, key, query):
    scores = dot_nt(key, query)
    shape = scores.shape
    live = first + lax.broadcasted_iota(jnp.int32, shape, 0) <= lax.broadcasted_iota(
        jnp.int32, shape, 1
    )
    return jnp.where(live, scores, DEAD)


def peak_kernel(first_ref, query_ref, key_ref, peak_ref, out_ref):
    for head in range(query_ref.shape[2] // HEAD_DIM):
        at = slice(head * HEAD_DIM, (head + 1) * HEAD_DIM)
        scores = group_scores(first_ref[0], key_ref[0, :, at], query_ref[0, :, at])
        out_ref[0, head : head + 1, :] = jnp.maximum(
            peak_ref[0, head : head + 1, :], jnp.max(scores, axis=0, keepdims=True)
        )


def group_peaks(first, queries, new_keys, peaks):
    requests, tokens, width = queries.shape
    tok_block = new_keys.shape[1]
    heads = width // HEAD_DIM
    one = lambda rows: pl.BlockSpec((1, rows, width), lambda r, *_: (r, 0, 0))
    stat = pl.BlockSpec((1, heads, tokens), lambda r, *_: (r, 0, 0))
    return pl.pallas_call(
        peak_kernel,
        grid_spec=pltpu.PrefetchScalarGridSpec(
            num_scalar_prefetch=1,
            grid=(requests,),
            in_specs=[one(tokens), one(tok_block), stat],
            out_specs=stat,
        ),
        out_shape=jax.ShapeDtypeStruct(peaks.shape, jnp.float32),
        compiler_params=pltpu.CompilerParams(vmem_limit_bytes=32 * 1024 * 1024),
        cost_estimate=pl.CostEstimate(
            flops=2 * requests * tokens * tok_block * width,
            bytes_accessed=2 * requests * width * tokens,
            transcendentals=0,
        ),
        name="group_peaks",
    )(first, queries, new_keys, peaks)


def finish_kernel(slots, first_ref, place_ref, *refs):
    query_ref, key_ref, value_ref, cache_ref, peak_ref, total_ref, best_ref = refs[:7]
    sum_ref, *part_refs = refs[7:-1]
    joined_ref = refs[-1]
    tok_block = key_ref.shape[1]
    for head in range(query_ref.shape[2] // HEAD_DIM):
        at = slice(head * HEAD_DIM, (head + 1) * HEAD_DIM)
        row = slice(head, head + 1)
        scores = group_scores(first_ref[0], key_ref[0, :, at], query_ref[0, :, at])
        best = best_ref[0, row, :]
        weights = jnp.exp2((scores - best) * EXP2_SCALE)
        rescale = jnp.exp2((peak_ref[0, row, :] - best) * EXP2_SCALE)
        sum_ref[0, row, :] = total_ref[0, row, :] * rescale + jnp.sum(
            weights, axis=0, keepdims=True
        )
        joined = cache_ref[0, at, :].astype(jnp.float32) * rescale + dot_tn(
            value_ref[0, :, at], weights.astype(jnp.bfloat16)
        )
        joined_ref[:, at] = joined.T.astype(jnp.bfloat16)
    for slot in range(slots):
        start = pl.multiple_of(place_ref[slot] * tok_block, tok_block)
        part_refs[slot][0] = joined_ref[pl.ds(start, tok_block), :]


def finish_part(begin, requests, first, places, queries, new_keys, new_values, cached, peaks, totals, best):
    tokens, width = queries.shape[1:]
    tok_block = new_keys.shape[1]
    slots = tokens // tok_block
    heads = width // HEAD_DIM
    one = lambda rows: pl.BlockSpec((1, rows, width), lambda r, *_: (r + begin, 0, 0))
    stat = pl.BlockSpec((1, heads, tokens), lambda r, *_: (r + begin, 0, 0))
    return pl.pallas_call(
        functools.partial(finish_kernel, slots),
        grid_spec=pltpu.PrefetchScalarGridSpec(
            num_scalar_prefetch=2,
            grid=(requests,),
            in_specs=[
                one(tokens),
                one(tok_block),
                one(tok_block),
                pl.BlockSpec((1, width, tokens), lambda r, *_: (r + begin, 0, 0)),
                stat,
                stat,
                stat,
            ],
            out_specs=[pl.BlockSpec((1, heads, tokens), lambda r, *_: (r, 0, 0))]
            + [pl.BlockSpec((1, tok_block, width), lambda r, *_: (r, 0, 0))] * slots,
            scratch_shapes=[pltpu.VMEM((tokens, width), jnp.bfloat16)],
        ),
        out_shape=[jax.ShapeDtypeStruct((requests, heads, tokens), jnp.float32)]
        + [jax.ShapeDtypeStruct((requests, tok_block, width), jnp.bfloat16)] * slots,
        compiler_params=pltpu.CompilerParams(vmem_limit_bytes=48 * 1024 * 1024),
        cost_estimate=pl.CostEstimate(
            flops=4 * requests * tokens * tok_block * width,
            bytes_accessed=6 * requests * width * tokens,
            transcendentals=requests * tokens * tok_block * heads,
        ),
        name="finish_part",
    )(first, places, queries, new_keys, new_values, cached, peaks, totals, best)


def head_sum(terms, head_count, head_index):
    if head_count != 4:
        return lax.psum_scatter(
            terms.astype(jnp.bfloat16), "head", scatter_dimension=1, tiled=True
        ).astype(jnp.float32)
    width = terms.shape[1] // 4
    chunk = lambda index: lax.dynamic_slice_in_dim(terms, index * width, width, 1)
    core, column = head_index % 2, head_index // 2
    near, far = 2 * column, 2 * (1 - column)
    got = lax.ppermute(
        jnp.concatenate([chunk(near + 1 - core), chunk(far + 1 - core)], axis=1).astype(
            jnp.bfloat16
        ),
        "head",
        [(h, h ^ 1) for h in range(4)],
    ).astype(jnp.float32)
    keep = chunk(near + core) + got[:, :width]
    give = chunk(far + core) + got[:, width:]
    return keep + lax.ppermute(
        give.astype(jnp.bfloat16), "head", [(h, h ^ 2) for h in range(4)]
    ).astype(jnp.float32)


def entry_states(through, local_state, base, seq_index, seq_count):
    factor = through[:, :, None]
    if seq_count != 8:
        entry = base
        for turn in range(seq_count - 1):
            leaving = (factor * entry + local_state).astype(jnp.bfloat16)
            entry = entry + lax.ppermute(leaving, "seq", [(turn, turn + 1)]).astype(jnp.float32)
        return entry
    swap = [(i, i ^ 1) for i in range(8)]
    other_state = lax.ppermute(local_state.astype(jnp.bfloat16), "seq", swap).astype(jnp.float32)
    other_factor = lax.ppermute(through, "seq", swap)[:, :, None]
    is_first = seq_index % 2 == 0
    first_state = jnp.where(is_first, local_state, other_state)
    second_state = jnp.where(is_first, other_state, local_state)
    first_factor = jnp.where(is_first, factor, other_factor)
    second_factor = jnp.where(is_first, other_factor, factor)
    pair_state = second_factor * first_state + second_state
    pair_factor = first_factor * second_factor
    entry = base
    for turn in range(3):
        leaving = (pair_factor * entry + pair_state).astype(jnp.bfloat16)
        route = [(2 * turn + y, 2 * turn + 2 + y) for y in range(2)]
        entry = entry + lax.ppermute(leaving, "seq", route).astype(jnp.float32)
    return jnp.where(is_first, entry, first_factor * entry + first_state)


def shards(
    block_input,
    lengths,
    cache_keys,
    cache_values,
    w_query,
    w_key,
    w_value,
    w_attn_out,
    norm_gain,
    w_in,
    w_bc,
    w_dt,
    dt_bias,
    a_log,
    d_skip,
    gated_gain,
    w_out,
    ssm_init,
):
    requests, tok_block, _ = block_input.shape
    seq_count = lax.axis_size("seq")
    seq_index = lax.axis_index("seq")
    head_count = lax.axis_size("head")
    head_index = lax.axis_index("head")
    local_att = w_query.shape[1]
    local_heads = local_att // HEAD_DIM
    cache_block = cache_keys.shape[1]
    rows = w_query.shape[0]
    tokens = requests * tok_block
    flat_input = block_input.reshape(tokens, block_input.shape[2])

    order = ring_order(seq_count)
    place = [order.index(i) for i in range(seq_count)]
    order_table = jnp.asarray(order, jnp.int32)
    ring_index = jnp.asarray(place, jnp.int32)[seq_index]
    origin = lambda offset: order_table[(ring_index - offset + seq_count) % seq_count]

    def project(pieces):
        total = None
        for offset, row, piece in pieces:
            start = origin(offset) * rows + row
            part = lax.dynamic_slice_in_dim(flat_input, start, piece.shape[0], 1)
            term = jnp.dot(part, piece, preferred_element_type=jnp.float32)
            total = term if total is None else total + term
        return total

    positions = (
        lengths[:, None] + seq_index * tok_block + jnp.arange(tok_block, dtype=jnp.int32)[None, :]
    ).reshape(tokens)
    half_dim = HEAD_DIM // 2
    frequency = jnp.exp(
        jnp.arange(half_dim, dtype=jnp.float32) * (-2.0 * math.log(10000.0) / HEAD_DIM)
    )
    angles = positions.astype(jnp.float32)[:, None] * frequency
    cosine = jnp.cos(angles)
    sine = jnp.sin(angles)
    cosine = jnp.concatenate([cosine, cosine], axis=1)
    sine = jnp.concatenate([-sine, sine], axis=1)

    query_pieces = ring_gather(w_query, order)
    key_pieces = ring_gather(after(w_key, query_pieces[-1][2]), order)
    value_pieces = ring_gather(after(w_value, key_pieces[-1][2]), order)
    queries = rope(project(query_pieces), cosine, sine).reshape(requests, tok_block, local_att)
    new_keys = rope(project(key_pieces), cosine, sine).reshape(requests, tok_block, local_att)
    new_values = project(value_pieces).astype(jnp.bfloat16).reshape(requests, tok_block, local_att)

    half = seq_count // 2
    query_ring = ring_gather(queries, order)
    offsets = [0] + [sign * step for step in range(1, half) for sign in (1, -1)] + [half]
    query_slots = [piece for _, _, piece in query_ring[:-2]]
    query_slots.append(jnp.concatenate([query_ring[-2][2], query_ring[-1][2]], axis=0))
    places = jnp.stack([origin(offset) for offset in offsets]).astype(jnp.int32)
    live = jnp.clip(lengths - seq_index * cache_block, 0, cache_block).astype(jnp.int32)
    first = (seq_index * tok_block).astype(jnp.int32).reshape(1)
    all_queries, cached, peaks, totals = cache_part(
        places, live, query_slots, cache_keys, cache_values
    )
    best = lax.pmax(group_peaks(first, all_queries, new_keys, peaks), "seq")

    own = lambda stat: lax.dynamic_slice_in_dim(stat, seq_index * tok_block, tok_block, 2)
    greatest_logit = jnp.transpose(own(best), (0, 2, 1)) * SCALE
    group = requests // GROUPS
    attended = []
    for begin in range(0, requests, group):
        sums, *parts = finish_part(
            begin, group, first, places, all_queries, new_keys, new_values, cached, peaks, totals, best
        )
        denominator = jnp.transpose(own(lax.psum(sums, "seq")), (0, 2, 1))
        terms = {-offset: part for offset, part in zip(offsets, parts)}
        terms[half] = terms[-half]
        numerator = ring_sum(terms, order).reshape(group, tok_block, local_heads, HEAD_DIM)
        attended.append((numerator / denominator[..., None]).astype(jnp.bfloat16))
    attended = jnp.concatenate(attended, axis=0).reshape(tokens, local_att)
    attn_terms = jnp.dot(attended, w_attn_out, preferred_element_type=jnp.float32)

    hidden = block_input[:, :, :D].astype(jnp.float32)
    normed = (
        hidden * lax.rsqrt(jnp.mean(hidden * hidden, axis=-1, keepdims=True) + 1e-05) * norm_gain
    ).astype(jnp.bfloat16)
    flat_normed = normed.reshape(tokens, D)
    local_inner = w_in.shape[2]
    local_mheads = local_inner // MHEAD_DIM
    gate_inner = jnp.dot(
        flat_normed, w_in.reshape(D, 2 * local_inner), preferred_element_type=jnp.float32
    ).reshape(requests, tok_block, 2, local_inner)
    gate_part = gate_inner[:, :, 0]
    inner_heads = jax.nn.silu(gate_inner[:, :, 1]).reshape(
        requests, tok_block, local_mheads, MHEAD_DIM
    )
    bc_part = jnp.dot(flat_normed, w_bc, preferred_element_type=jnp.float32).reshape(
        requests, tok_block, 2 * STATE
    )
    input_map = bc_part[..., :STATE]
    output_map = bc_part[..., STATE:]
    step_size = jax.nn.softplus(
        jnp.dot(flat_normed, w_dt, preferred_element_type=jnp.float32).reshape(
            requests, tok_block, local_mheads
        )
        + dt_bias
    )
    log_decay = -step_size * jnp.exp(a_log)
    cumulative = jnp.cumsum(log_decay, axis=1)
    causal = jnp.arange(tok_block)[None, :] <= jnp.arange(tok_block)[:, None]
    head_major = jnp.transpose(cumulative, (0, 2, 1))
    differences = head_major[:, :, :, None] - head_major[:, :, None, :]
    decays = jnp.where(causal, jnp.exp(jnp.where(causal, differences, 0.0)), 0.0)
    contact = jnp.einsum("rtn,run->rtu", output_map, input_map, precision=lax.Precision.HIGHEST)
    mixing = decays * contact[:, None] * jnp.transpose(step_size, (0, 2, 1))[:, :, None, :]
    intra_part = jnp.einsum("rhtu,ruhp->rthp", mixing, inner_heads, precision=lax.Precision.HIGHEST)
    tail_decay = jnp.exp(cumulative[:, -1:, :] - cumulative) * step_size
    local_state = jnp.einsum(
        "ruhp,run->rhpn",
        inner_heads * tail_decay[..., None],
        input_map,
        precision=lax.Precision.HIGHEST,
    ).reshape(requests, local_mheads, MHEAD_DIM * STATE)
    through = jnp.exp(cumulative[:, -1, :])
    base = jnp.where(seq_index == 0, ssm_init, 0.0)
    if seq_count == 8:
        base = jnp.where(seq_index < 2, ssm_init, 0.0)
    incoming = entry_states(through, local_state, base, seq_index, seq_count)
    entry_state = incoming.reshape(requests, local_mheads, MHEAD_DIM, STATE)
    inter_part = (
        jnp.einsum("rhpn,rtn->rthp", entry_state, output_map, precision=lax.Precision.HIGHEST)
        * jnp.exp(cumulative)[..., None]
    )
    read_out = intra_part + inter_part + d_skip[:, None] * inner_heads
    chain_states = (through[:, :, None] * incoming + local_state)[:, None]
    mixed_inner = read_out.reshape(requests, tok_block, local_inner) * jax.nn.silu(gate_part)
    squares = lax.psum(jnp.sum(mixed_inner * mixed_inner, axis=-1).reshape(1, tokens), "head")
    gated = (mixed_inner * gated_gain).astype(jnp.bfloat16)
    mamba_terms = jnp.dot(
        gated.reshape(tokens, local_inner), w_out, preferred_element_type=jnp.float32
    ) * lax.rsqrt(squares.reshape(tokens, 1) / D_INNER + 1e-05)

    summed = head_sum(attn_terms + mamba_terms, head_count, head_index)
    local_width = D // head_count
    residual = lax.dynamic_slice_in_dim(
        hidden.reshape(tokens, D), head_index * local_width, local_width, 1
    )
    mixed = (residual + summed).astype(jnp.bfloat16).reshape(requests, tok_block, local_width)
    return (mixed, new_keys, new_values, chain_states, greatest_logit)


def solution(mesh):
    placed = (
        P(None, "seq", None),
        P(),
        P(None, "seq", "head"),
        P(None, "seq", "head"),
        P("seq", "head"),
        P("seq", "head"),
        P("seq", "head"),
        P("head", None),
        P(),
        P(None, None, "head"),
        P(),
        P(None, "head"),
        P("head"),
        P("head"),
        P("head"),
        P("head"),
        P("head", None),
        P(None, "head", None),
    )
    return jax.shard_map(
        shards,
        mesh=mesh,
        in_specs=placed,
        out_specs=(
            P(None, "seq", "head"),
            P(None, "seq", "head"),
            P(None, "seq", "head"),
            P(None, "seq", "head", None),
            P(None, "seq", "head"),
        ),
        check_vma=False,
    )
```

```python
import functools
import math

import jax
import jax.numpy as jnp
from jax import lax
from jax.experimental import pallas as pl
from jax.experimental.pallas import tpu as pltpu
from jax.sharding import PartitionSpec as P

D = 2048
HEAD_DIM = 128
MHEAD_DIM = 64
STATE = 64
D_INNER = 4096
SCALE = 1.0 / math.sqrt(HEAD_DIM)
EXP2_SCALE = SCALE * math.log2(math.e)
DEAD = -1e30
GROUPS = 2


def ring_order(count):
    y_count = max(1, count // 4)
    z_count = count // y_count
    order = []
    for y in range(y_count):
        turn = range(z_count) if y % 2 == 0 else range(z_count - 1, -1, -1)
        order += [z * y_count + y for z in turn]
    return order


def ring_step(block, order, distance):
    count = len(order)
    route = [(order[i], order[(i + distance) % count]) for i in range(count)]
    return lax.ppermute(block, "seq", route)


class Ring:
    def __init__(self, block, order):
        self.order = order
        self.steps = len(order) // 2
        self.done = 0
        self.block = self.ahead = self.back = block
        self.pieces = [(0, 0, block)]
        self.landed = 1
        self.used = 0
        self.total = None

    def step(self, clock):
        self.landed = len(self.pieces)
        if self.done == self.steps:
            return []
        self.done += 1
        half = self.block.shape[0] // 2
        last = self.done == self.steps
        ahead = self.ahead[:half] if last else self.ahead
        back = self.back[half:] if last else self.back
        ahead, back = clock.hold(ahead, back)
        self.ahead = ring_step(ahead, self.order, 1)
        self.back = ring_step(back, self.order, -1)
        if last:
            self.pieces += [(self.steps, 0, self.ahead), (self.steps, half, self.back)]
        else:
            self.pieces += [(self.done, 0, self.ahead), (-self.done, 0, self.back)]
        return [self.ahead, self.back]


class Clock:
    def __init__(self):
        self.fence = ()

    def hold(self, *values):
        held = lax.optimization_barrier(tuple(values) + self.fence)[: len(values)]
        return held[0] if len(values) == 1 else held

    def turn(self, rings, work=None):
        moved = [array for ring in rings for array in ring.step(self)]
        done = work() if work is not None else ()
        self.fence = tuple(moved) + tuple(done)


def butterfly(value, axis, count, combine):
    bit = 1
    while bit < count:
        value = combine(value, lax.ppermute(value, axis, [(i, i ^ bit) for i in range(count)]))
        bit *= 2
    return value


def ring_sum(parts, order):
    count = len(order)
    far = count // 2
    half = parts[0].shape[0] // 2
    add = lambda a, b: (a.astype(jnp.float32) + b.astype(jnp.float32)).astype(jnp.bfloat16)
    ahead = ring_step(parts[far][:half], order, 1)
    back = ring_step(parts[far][half:], order, -1)
    top, bottom = parts[far - 1], parts[-(far - 1)]
    ahead = jnp.concatenate([add(ahead, top[:half]), top[half:]], axis=0)
    back = jnp.concatenate([bottom[:half], add(back, bottom[half:])], axis=0)
    for step in range(far - 1, 0, -1):
        ahead = ring_step(ahead, order, 1)
        back = ring_step(back, order, -1)
        if step > 1:
            ahead = add(ahead, parts[step - 1])
            back = add(back, parts[-(step - 1)])
    return (
        ahead.astype(jnp.float32) + back.astype(jnp.float32) + parts[0].astype(jnp.float32)
    )


def rope_kernel(value_ref, cosine_ref, sine_ref, out_ref):
    cosine = cosine_ref[...]
    sine = sine_ref[...]
    for head in range(value_ref.shape[1] // HEAD_DIM):
        at = slice(head * HEAD_DIM, (head + 1) * HEAD_DIM)
        part = value_ref[:, at]
        turned = part * cosine + pltpu.roll(part, HEAD_DIM // 2, 1) * sine
        out_ref[:, at] = turned.astype(out_ref.dtype)


def rope(value, cosine, sine):
    rows, width = value.shape
    block = min(rows, 128)
    return pl.pallas_call(
        rope_kernel,
        grid=(rows // block,),
        in_specs=[
            pl.BlockSpec((block, width), lambda i: (i, 0)),
            pl.BlockSpec((block, HEAD_DIM), lambda i: (i, 0)),
            pl.BlockSpec((block, HEAD_DIM), lambda i: (i, 0)),
        ],
        out_specs=pl.BlockSpec((block, width), lambda i: (i, 0)),
        out_shape=jax.ShapeDtypeStruct((rows, width), jnp.bfloat16),
        cost_estimate=pl.CostEstimate(
            flops=4 * rows * width, bytes_accessed=6 * rows * width, transcendentals=0
        ),
        name="rope",
    )(value, cosine, sine)


def dot_nt(a, b):
    return lax.dot_general(a, b, (((1,), (1,)), ((), ())), preferred_element_type=jnp.float32)


def dot_tn(a, b):
    return lax.dot_general(a, b, (((0,), (0,)), ((), ())), preferred_element_type=jnp.float32)


def cache_kernel(slots, place_ref, live_ref, *refs):
    query_refs = refs[:slots]
    key_ref, value_ref, joined_ref, out_ref, peak_ref, total_ref = refs[slots:]
    tok_block = query_refs[0].shape[1]
    keys, width = key_ref.shape[1:]
    tokens = tok_block * slots
    for slot in range(slots):
        start = pl.multiple_of(place_ref[slot] * tok_block, tok_block)
        joined_ref[0, pl.ds(start, tok_block), :] = query_refs[slot][0]
    live = live_ref[pl.program_id(0)]
    bias = jnp.where(
        lax.broadcasted_iota(jnp.int32, (keys, 128), 0) < live, 0.0, DEAD
    ).astype(jnp.float32)
    bias = jnp.concatenate([bias] * (tokens // 128), axis=1)
    for head in range(width // HEAD_DIM):
        at = slice(head * HEAD_DIM, (head + 1) * HEAD_DIM)
        scores = dot_nt(key_ref[0, :, at], joined_ref[0, :, at]) + bias
        peak = jnp.max(scores, axis=0, keepdims=True)
        weights = jnp.exp2((scores - peak) * EXP2_SCALE)
        total_ref[0, head : head + 1, :] = jnp.sum(weights, axis=0, keepdims=True)
        peak_ref[0, head : head + 1, :] = peak
        out_ref[0, at, :] = dot_tn(value_ref[0, :, at], weights.astype(jnp.bfloat16)).astype(
            out_ref.dtype
        )


def cache_part(begin, requests, places, live, query_slots, keys, values):
    slots = len(query_slots)
    tok_block, width = query_slots[0].shape[1:]
    tokens = tok_block * slots
    cache_block = keys.shape[1]
    heads = width // HEAD_DIM
    one = lambda rows, start: pl.BlockSpec((1, rows, width), lambda r, *_: (r + start, 0, 0))
    stat = pl.BlockSpec((1, heads, tokens), lambda r, *_: (r, 0, 0))
    return pl.pallas_call(
        functools.partial(cache_kernel, slots),
        grid_spec=pltpu.PrefetchScalarGridSpec(
            num_scalar_prefetch=2,
            grid=(requests,),
            in_specs=[
                one(tok_block, 0 if slot.shape[0] == requests else begin) for slot in query_slots
            ]
            + [one(cache_block, begin), one(cache_block, begin)],
            out_specs=[
                one(tokens, 0),
                pl.BlockSpec((1, width, tokens), lambda r, *_: (r, 0, 0)),
                stat,
                stat,
            ],
        ),
        out_shape=[
            jax.ShapeDtypeStruct((requests, tokens, width), jnp.bfloat16),
            jax.ShapeDtypeStruct((requests, width, tokens), jnp.bfloat16),
            jax.ShapeDtypeStruct((requests, heads, tokens), jnp.float32),
            jax.ShapeDtypeStruct((requests, heads, tokens), jnp.float32),
        ],
        compiler_params=pltpu.CompilerParams(vmem_limit_bytes=48 * 1024 * 1024),
        cost_estimate=pl.CostEstimate(
            flops=4 * requests * tokens * cache_block * width,
            bytes_accessed=2 * requests * width * (3 * tokens + 2 * cache_block),
            transcendentals=requests * tokens * cache_block * heads,
        ),
        name="cache_part",
    )(places, live, *query_slots, keys, values)


def group_scores(first, key, query):
    scores = dot_nt(key, query)
    shape = scores.shape
    live = first + lax.broadcasted_iota(jnp.int32, shape, 0) <= lax.broadcasted_iota(
        jnp.int32, shape, 1
    )
    return jnp.where(live, scores, DEAD)


def peak_kernel(first_ref, query_ref, key_ref, peak_ref, out_ref):
    for head in range(query_ref.shape[2] // HEAD_DIM):
        at = slice(head * HEAD_DIM, (head + 1) * HEAD_DIM)
        scores = group_scores(first_ref[0], key_ref[0, :, at], query_ref[0, :, at])
        out_ref[0, head : head + 1, :] = jnp.maximum(
            peak_ref[0, head : head + 1, :], jnp.max(scores, axis=0, keepdims=True)
        )


def group_peaks(begin, first, queries, new_keys, peaks):
    requests, tokens, width = queries.shape
    tok_block = new_keys.shape[1]
    heads = width // HEAD_DIM
    one = lambda rows, start: pl.BlockSpec((1, rows, width), lambda r, *_: (r + start, 0, 0))
    stat = pl.BlockSpec((1, heads, tokens), lambda r, *_: (r, 0, 0))
    return pl.pallas_call(
        peak_kernel,
        grid_spec=pltpu.PrefetchScalarGridSpec(
            num_scalar_prefetch=1,
            grid=(requests,),
            in_specs=[one(tokens, 0), one(tok_block, begin), stat],
            out_specs=stat,
        ),
        out_shape=jax.ShapeDtypeStruct(peaks.shape, jnp.float32),
        compiler_params=pltpu.CompilerParams(vmem_limit_bytes=32 * 1024 * 1024),
        cost_estimate=pl.CostEstimate(
            flops=2 * requests * tokens * tok_block * width,
            bytes_accessed=2 * requests * width * tokens,
            transcendentals=0,
        ),
        name="group_peaks",
    )(first, queries, new_keys, peaks)


def finish_kernel(slots, first_ref, place_ref, *refs):
    query_ref, key_ref, value_ref, cache_ref, peak_ref, total_ref, best_ref = refs[:7]
    sum_ref, *part_refs = refs[7:-1]
    joined_ref = refs[-1]
    tok_block = key_ref.shape[1]
    for head in range(query_ref.shape[2] // HEAD_DIM):
        at = slice(head * HEAD_DIM, (head + 1) * HEAD_DIM)
        row = slice(head, head + 1)
        scores = group_scores(first_ref[0], key_ref[0, :, at], query_ref[0, :, at])
        best = best_ref[0, row, :]
        weights = jnp.exp2((scores - best) * EXP2_SCALE)
        rescale = jnp.exp2((peak_ref[0, row, :] - best) * EXP2_SCALE)
        sum_ref[0, row, :] = total_ref[0, row, :] * rescale + jnp.sum(
            weights, axis=0, keepdims=True
        )
        joined = cache_ref[0, at, :].astype(jnp.float32) * rescale + dot_tn(
            value_ref[0, :, at], weights.astype(jnp.bfloat16)
        )
        joined_ref[:, at] = joined.T.astype(jnp.bfloat16)
    for slot in range(slots):
        start = pl.multiple_of(place_ref[slot] * tok_block, tok_block)
        part_refs[slot][0] = joined_ref[pl.ds(start, tok_block), :]


def finish_part(begin, first, places, queries, new_keys, new_values, cached, peaks, totals, best):
    requests, tokens, width = queries.shape
    tok_block = new_keys.shape[1]
    slots = tokens // tok_block
    heads = width // HEAD_DIM
    one = lambda rows, start: pl.BlockSpec((1, rows, width), lambda r, *_: (r + start, 0, 0))
    stat = lambda start: pl.BlockSpec((1, heads, tokens), lambda r, *_: (r + start, 0, 0))
    return pl.pallas_call(
        functools.partial(finish_kernel, slots),
        grid_spec=pltpu.PrefetchScalarGridSpec(
            num_scalar_prefetch=2,
            grid=(requests,),
            in_specs=[
                one(tokens, 0),
                one(tok_block, begin),
                one(tok_block, begin),
                pl.BlockSpec((1, width, tokens), lambda r, *_: (r, 0, 0)),
                stat(0),
                stat(0),
                stat(begin),
            ],
            out_specs=[stat(0)] + [one(tok_block, 0)] * slots,
            scratch_shapes=[pltpu.VMEM((tokens, width), jnp.bfloat16)],
        ),
        out_shape=[jax.ShapeDtypeStruct((requests, heads, tokens), jnp.float32)]
        + [jax.ShapeDtypeStruct((requests, tok_block, width), jnp.bfloat16)] * slots,
        compiler_params=pltpu.CompilerParams(vmem_limit_bytes=48 * 1024 * 1024),
        cost_estimate=pl.CostEstimate(
            flops=4 * requests * tokens * tok_block * width,
            bytes_accessed=6 * requests * width * tokens,
            transcendentals=requests * tokens * tok_block * heads,
        ),
        name="finish_part",
    )(first, places, queries, new_keys, new_values, cached, peaks, totals, best)


def head_sum(terms, head_count, head_index):
    if head_count != 4:
        return lax.psum_scatter(
            terms.astype(jnp.bfloat16), "head", scatter_dimension=1, tiled=True
        ).astype(jnp.float32)
    width = terms.shape[1] // 4
    chunk = lambda index: lax.dynamic_slice_in_dim(terms, index * width, width, 1)
    core, column = head_index % 2, head_index // 2
    near, far = 2 * column, 2 * (1 - column)
    got = lax.ppermute(
        jnp.concatenate([chunk(near + 1 - core), chunk(far + 1 - core)], axis=1).astype(
            jnp.bfloat16
        ),
        "head",
        [(h, h ^ 1) for h in range(4)],
    ).astype(jnp.float32)
    keep = chunk(near + core) + got[:, :width]
    give = chunk(far + core) + got[:, width:]
    return keep + lax.ppermute(
        give.astype(jnp.bfloat16), "head", [(h, h ^ 2) for h in range(4)]
    ).astype(jnp.float32)


class Relay:
    def __init__(self, through, local_state, initial, seq_index, seq_count):
        self.factor = through[:, :, None]
        self.local = local_state
        self.seq_count = seq_count
        self.paired = seq_count == 8
        self.hops = seq_count - 1
        if not self.paired:
            self.entry = jnp.where(seq_index == 0, initial, 0.0)
            self.hop = 0
            return
        self.hops = 3
        self.hop = 0
        self.swap = [(i, i ^ 1) for i in range(8)]
        self.is_first = is_first = seq_index % 2 == 0
        self.half = half = local_state.shape[1] // 2
        mine = jnp.where(is_first, local_state[:, :half], local_state[:, half:])
        other = jnp.where(is_first, local_state[:, half:], local_state[:, :half])
        got = self.exchange(other)
        other_factor = lax.ppermute(through, "seq", self.swap)[:, :, None]
        first_state = jnp.where(is_first, mine, got)
        second_state = jnp.where(is_first, got, mine)
        side = lambda value: jnp.where(is_first, value[:, :half], value[:, half:])
        first_factor = side(jnp.where(is_first, self.factor, other_factor))
        second_factor = side(jnp.where(is_first, other_factor, self.factor))
        self.first_state, self.first_factor = first_state, first_factor
        self.pair_state = second_factor * first_state + second_state
        self.pair_factor = first_factor * second_factor
        self.entry = jnp.where(seq_index < 2, side(initial), 0.0)

    def exchange(self, value):
        return lax.ppermute(value.astype(jnp.bfloat16), "seq", self.swap).astype(jnp.float32)

    def advance(self, clock):
        factor, state = (
            (self.pair_factor, self.pair_state) if self.paired else (self.factor, self.local)
        )
        entry = clock.hold(self.entry)
        leaving = (factor * entry + state).astype(jnp.bfloat16)
        if self.paired:
            route = [(2 * self.hop + y, 2 * self.hop + 2 + y) for y in range(2)]
        else:
            route = [(self.hop, self.hop + 1)]
        self.hop += 1
        self.entry = entry + lax.ppermute(leaving, "seq", route).astype(jnp.float32)
        return (self.entry,)

    def result(self, clock):
        while self.hop < self.hops:
            self.advance(clock)
        entry = clock.hold(self.entry)
        if not self.paired:
            return entry
        second = self.first_factor * entry + self.first_state
        got = self.exchange(jnp.where(self.is_first, second, entry))
        mine = jnp.where(self.is_first, entry, second)
        return jnp.concatenate(
            [jnp.where(self.is_first, mine, got), jnp.where(self.is_first, got, mine)], axis=1
        )


def shards(
    block_input,
    lengths,
    cache_keys,
    cache_values,
    w_query,
    w_key,
    w_value,
    w_attn_out,
    norm_gain,
    w_in,
    w_bc,
    w_dt,
    dt_bias,
    a_log,
    d_skip,
    gated_gain,
    w_out,
    ssm_init,
):
    requests, tok_block, _ = block_input.shape
    seq_count = lax.axis_size("seq")
    seq_index = lax.axis_index("seq")
    head_count = lax.axis_size("head")
    head_index = lax.axis_index("head")
    local_att = w_query.shape[1]
    local_heads = local_att // HEAD_DIM
    cache_block = cache_keys.shape[1]
    rows = w_query.shape[0]
    tokens = requests * tok_block
    flat_input = block_input.reshape(tokens, block_input.shape[2])

    order = ring_order(seq_count)
    place = [order.index(i) for i in range(seq_count)]
    order_table = jnp.asarray(order, jnp.int32)
    ring_index = jnp.asarray(place, jnp.int32)[seq_index]
    origin = lambda offset: order_table[(ring_index - offset + seq_count) % seq_count]

    def project(ring, whole=False):
        landed = len(ring.pieces) if whole else ring.landed
        for offset, row, piece in ring.pieces[ring.used : landed]:
            start = origin(offset) * rows + row
            part = lax.dynamic_slice_in_dim(flat_input, start, piece.shape[0], 1)
            term = jnp.dot(part, piece, preferred_element_type=jnp.float32)
            ring.total = term if ring.total is None else ring.total + term
        ring.used = landed
        return ring.total

    positions = (
        lengths[:, None] + seq_index * tok_block + jnp.arange(tok_block, dtype=jnp.int32)[None, :]
    ).reshape(tokens)
    half_dim = HEAD_DIM // 2
    frequency = jnp.exp(
        jnp.arange(half_dim, dtype=jnp.float32) * (-2.0 * math.log(10000.0) / HEAD_DIM)
    )
    angles = positions.astype(jnp.float32)[:, None] * frequency
    cosine = jnp.cos(angles)
    sine = jnp.sin(angles)
    cosine = jnp.concatenate([cosine, cosine], axis=1)
    sine = jnp.concatenate([-sine, sine], axis=1)

    clock = Clock()
    half = seq_count // 2
    group = requests // GROUPS
    local_inner = w_in.shape[2]
    local_mheads = local_inner // MHEAD_DIM
    local_width = D // head_count
    exact = functools.partial(jnp.einsum, precision=lax.Precision.HIGHEST)
    mix = {}

    def mix_steps():
        hidden = clock.hold(flat_input)[:, :D].astype(jnp.float32)
        scale = lax.rsqrt(jnp.mean(hidden * hidden, axis=-1, keepdims=True) + 1e-05)
        normed = (hidden * scale * norm_gain).astype(jnp.bfloat16)
        mix["normed"] = normed
        bc_part = jnp.dot(normed, w_bc, preferred_element_type=jnp.float32).reshape(
            requests, tok_block, 2 * STATE
        )
        mix["input_map"] = bc_part[..., :STATE]
        mix["output_map"] = bc_part[..., STATE:]
        step_size = jax.nn.softplus(
            jnp.dot(normed, w_dt, preferred_element_type=jnp.float32).reshape(
                requests, tok_block, local_mheads
            )
            + dt_bias
        )
        log_decay = -step_size * jnp.exp(a_log)
        causal = jnp.arange(tok_block)[None, :] <= jnp.arange(tok_block)[:, None]
        mix["causal"] = causal
        mix["step_size"] = step_size
        mix["cumulative"] = exact("tu,ruh->rth", causal.astype(jnp.float32), log_decay)
        return (mix["normed"], bc_part, step_size, mix["cumulative"])

    def mix_inner():
        normed = clock.hold(mix["normed"])
        gate_inner = jnp.dot(
            normed, w_in.reshape(D, 2 * local_inner), preferred_element_type=jnp.float32
        ).reshape(tokens, 2, local_inner)
        mix["gate"] = jax.nn.silu(gate_inner[:, 0])
        mix["inner"] = jax.nn.silu(gate_inner[:, 1]).reshape(
            requests, tok_block, local_mheads, MHEAD_DIM
        )
        return (mix["gate"], mix["inner"])

    def mix_local():
        cumulative = clock.hold(mix["cumulative"])
        tail_decay = jnp.exp(cumulative[:, -1:, :] - cumulative) * mix["step_size"]
        mix["local"] = exact(
            "ruhp,run->rhpn", mix["inner"] * tail_decay[..., None], mix["input_map"]
        ).reshape(requests, local_mheads, MHEAD_DIM * STATE)
        mix["through"] = jnp.exp(cumulative[:, -1, :])
        return (mix["local"],)

    def mix_intra():
        cumulative, causal = clock.hold(mix["cumulative"]), mix["causal"]
        head_major = jnp.transpose(cumulative, (0, 2, 1))
        differences = head_major[:, :, :, None] - head_major[:, :, None, :]
        decays = jnp.where(causal, jnp.exp(jnp.where(causal, differences, 0.0)), 0.0)
        contact = exact("rtn,run->rtu", mix["output_map"], mix["input_map"])
        mixing = (
            decays * contact[:, None] * jnp.transpose(mix["step_size"], (0, 2, 1))[:, :, None, :]
        )
        mix["read"] = (
            exact("rhtu,ruhp->rthp", mixing, mix["inner"]) + d_skip[:, None] * mix["inner"]
        )
        return (mix["read"],)

    def mix_out():
        incoming = clock.hold(mix["entry"])
        entry_state = incoming.reshape(requests, local_mheads, MHEAD_DIM, STATE)
        inter_part = (
            exact("rhpn,rtn->rthp", entry_state, mix["output_map"])
            * jnp.exp(mix["cumulative"])[..., None]
        )
        mix["chain"] = (mix["through"][:, :, None] * incoming + mix["local"])[:, None]
        inner = (mix["read"] + inter_part).reshape(tokens, local_inner) * mix["gate"]
        squares = butterfly(
            jnp.sum(inner * inner, axis=-1, keepdims=True).reshape(1, tokens),
            "head",
            head_count,
            jnp.add,
        )
        gated = (inner * gated_gain).astype(jnp.bfloat16)
        mix["terms"] = jnp.dot(gated, w_out, preferred_element_type=jnp.float32) * lax.rsqrt(
            squares.reshape(tokens, 1) / D_INNER + 1e-05
        )
        return (mix["terms"], mix["chain"])

    query_ring = Ring(w_query, order)
    relay = None
    works = [mix_steps, mix_inner, mix_local]
    while query_ring.done < query_ring.steps - 1:
        clock.turn([query_ring], works.pop(0) if works else None)
    while works:
        clock.turn([], works.pop(0))

    def start_relay():
        nonlocal relay
        query_total = project(query_ring)
        relay = Relay(mix["through"], clock.hold(mix["local"]), ssm_init, seq_index, seq_count)
        return (relay.pair_state, query_total) if relay.paired else (query_total,)

    clock.turn([query_ring], start_relay)

    key_ring = Ring(w_key, order)

    def make_queries():
        moved = relay.advance(clock)
        total = project(query_ring, whole=True)
        queries = rope(total, cosine, sine).reshape(requests, tok_block, local_att)
        return (queries,) + tuple(moved)

    clock.turn([key_ring], make_queries)
    queries = clock.fence[2]

    slot_ring = Ring(queries, order)

    def relay_turn():
        moved = relay.advance(clock)
        clock_moved = mix_intra()
        return tuple(moved) + tuple(clock_moved)

    def relay_end():
        mix["entry"] = relay.result(clock)
        return (mix["entry"],)

    def key_terms():
        return (project(key_ring),)

    works = [relay_turn, relay_end, mix_out, key_terms]
    while slot_ring.done < slot_ring.steps:
        clock.turn([slot_ring, key_ring], works.pop(0) if works else None)
    while works:
        clock.turn([key_ring], works.pop(0))

    offsets = [0] + [sign * step for step in range(1, half) for sign in (1, -1)] + [half]
    places = jnp.stack([origin(offset) for offset in offsets]).astype(jnp.int32)
    live = jnp.clip(lengths - seq_index * cache_block, 0, cache_block).astype(jnp.int32)
    first = (seq_index * tok_block).astype(jnp.int32).reshape(1)
    value_ring = Ring(w_value, order)
    cached = []
    state = {}

    def meet_cache(index):
        full = [piece for _, _, piece in slot_ring.pieces[:-2]]
        slots = full + [slot_ring.pieces[-2 + index][2]]
        slots[0] = clock.hold(slots[0])
        begin = index * group
        cached.append(
            cache_part(
                begin,
                group,
                places,
                live[begin : begin + group],
                slots,
                cache_keys,
                cache_values,
            )
        )
        return tuple(cached[-1])

    def cache_first():
        total = project(key_ring, whole=True)
        state["keys"] = rope(total, cosine, sine).reshape(requests, tok_block, local_att)
        return meet_cache(0) + (state["keys"],)

    def cache_second():
        done = meet_cache(1)
        state["peaks"] = jnp.concatenate(
            [
                group_peaks(index * group, first, part[0], state["keys"], part[2])
                for index, part in enumerate(cached)
            ],
            axis=0,
        )
        return done + (state["peaks"],)

    def join_peaks():
        state["best"] = butterfly(clock.hold(state["peaks"]), "seq", seq_count, jnp.maximum)
        return (state["best"], project(value_ring))

    works = [cache_first, cache_second, join_peaks]
    while value_ring.done < value_ring.steps:
        clock.turn([value_ring], works.pop(0) if works else None)
    while works:
        clock.turn([], works.pop(0))
    new_keys = state["keys"]
    best = clock.hold(state["best"])
    new_values = (
        project(value_ring, whole=True)
        .astype(jnp.bfloat16)
        .reshape(requests, tok_block, local_att)
    )

    own = lambda stat: lax.dynamic_slice_in_dim(stat, seq_index * tok_block, tok_block, 2)
    greatest_logit = jnp.transpose(own(best), (0, 2, 1)) * SCALE
    residual = lax.dynamic_slice_in_dim(
        flat_input, head_index * local_width, local_width, 1
    ).astype(jnp.float32)
    mixed = []
    for index, (joined, out, peaks, totals) in enumerate(cached):
        begin = index * group
        sums, *parts = finish_part(
            begin, first, places, joined, new_keys, new_values, out, peaks, totals, best
        )
        sums = butterfly(sums, "seq", seq_count, jnp.add)
        denominator = jnp.transpose(own(sums), (0, 2, 1))
        terms = {-offset: part for offset, part in zip(offsets, parts)}
        terms[half] = terms[-half]
        numerator = ring_sum(terms, order).reshape(group, tok_block, local_heads, HEAD_DIM)
        attended = (
            (numerator / denominator[..., None])
            .astype(jnp.bfloat16)
            .reshape(group * tok_block, local_att)
        )
        at = slice(begin * tok_block, (begin + group) * tok_block)
        attn_terms = jnp.dot(attended, w_attn_out, preferred_element_type=jnp.float32)
        summed = head_sum(attn_terms + mix["terms"][at], head_count, head_index)
        mixed.append(
            (residual[at] + summed)
            .astype(jnp.bfloat16)
            .reshape(group, tok_block, local_width)
        )
    return (
        jnp.concatenate(mixed, axis=0),
        new_keys,
        new_values,
        mix["chain"],
        greatest_logit,
    )


def solution(mesh):
    placed = (
        P(None, "seq", None),
        P(),
        P(None, "seq", "head"),
        P(None, "seq", "head"),
        P("seq", "head"),
        P("seq", "head"),
        P("seq", "head"),
        P("head", None),
        P(),
        P(None, None, "head"),
        P(),
        P(None, "head"),
        P("head"),
        P("head"),
        P("head"),
        P("head"),
        P("head", None),
        P(None, "head", None),
    )
    return jax.shard_map(
        shards,
        mesh=mesh,
        in_specs=placed,
        out_specs=(
            P(None, "seq", "head"),
            P(None, "seq", "head"),
            P(None, "seq", "head"),
            P(None, "seq", "head", None),
            P(None, "seq", "head"),
        ),
        check_vma=False,
    )
```

```python
import functools
import math

import jax
import jax.numpy as jnp
from jax import lax
from jax.experimental import pallas as pl
from jax.experimental.pallas import tpu as pltpu
from jax.sharding import PartitionSpec as P

D = 2048
HEAD_DIM = 128
MHEAD_DIM = 64
STATE = 64
D_INNER = 4096
SCALE = 1.0 / math.sqrt(HEAD_DIM)
EXP2_SCALE = SCALE * math.log2(math.e)
DEAD = -1e30
GROUPS = 2


def ring_order(count):
    y_count = max(1, count // 4)
    z_count = count // y_count
    order = []
    for y in range(y_count):
        turn = range(z_count) if y % 2 == 0 else range(z_count - 1, -1, -1)
        order += [z * y_count + y for z in turn]
    return order


def ring_step(block, order, distance):
    count = len(order)
    route = [(order[i], order[(i + distance) % count]) for i in range(count)]
    return lax.ppermute(block, "seq", route)


class Ring:
    def __init__(self, block, order, first_row=0):
        self.order = order
        self.steps = len(order) // 2
        self.done = 0
        self.first_row = first_row
        self.block = self.ahead = self.back = block
        self.pieces = [(0, first_row, block)]

    def step(self, clock):
        self.done += 1
        half = self.block.shape[0] // 2
        last = self.done == self.steps
        ahead = self.ahead[:half] if last else self.ahead
        back = self.back[half:] if last else self.back
        ahead, back = clock.hold(ahead, back)
        self.ahead = ring_step(ahead, self.order, 1)
        self.back = ring_step(back, self.order, -1)
        at = self.first_row
        if last:
            self.pieces += [(self.steps, at, self.ahead), (self.steps, at + half, self.back)]
        else:
            self.pieces += [(self.done, at, self.ahead), (-self.done, at, self.back)]
        return [self.ahead, self.back]


class Clock:
    def __init__(self):
        self.fence = ()
        self.late = ()

    def hold(self, *values):
        held = lax.optimization_barrier(tuple(values) + self.fence)[: len(values)]
        return held[0] if len(values) == 1 else held

    def turn(self, ring=None, work=None):
        moved = tuple(ring.step(self)) if ring is not None else ()
        done, deferred = work() if work is not None else ((), ())
        self.fence = self.late + tuple(done)
        self.late = moved + tuple(deferred)


def butterfly(value, axis, count, combine):
    bit = 1
    while bit < count:
        value = combine(value, lax.ppermute(value, axis, [(i, i ^ bit) for i in range(count)]))
        bit *= 2
    return value


def ring_sum(parts, order):
    far = len(order) // 2
    add = lambda a, b: (a.astype(jnp.float32) + b.astype(jnp.float32)).astype(jnp.bfloat16)
    ahead = ring_step(parts[far][0], order, 1)
    back = ring_step(parts[far][1], order, -1)
    ahead = jnp.concatenate([add(ahead, parts[far - 1][0]), parts[far - 1][1]], axis=0)
    back = jnp.concatenate([parts[1 - far][0], add(back, parts[1 - far][1])], axis=0)
    whole = lambda offset: jnp.concatenate(parts[offset], axis=0)
    for step in range(far - 1, 0, -1):
        ahead = ring_step(ahead, order, 1)
        back = ring_step(back, order, -1)
        if step > 1:
            ahead = add(ahead, whole(step - 1))
            back = add(back, whole(1 - step))
    return ahead.astype(jnp.float32) + back.astype(jnp.float32) + whole(0).astype(jnp.float32)


def project_kernel(count, turned, places_ref, *refs):
    input_refs, weight_refs = refs[:count], refs[count : 2 * count]
    cosine_ref, sine_ref, out_ref = refs[2 * count :]
    total = None
    for input_ref, weight_ref in zip(input_refs, weight_refs):
        term = jnp.dot(input_ref[...], weight_ref[...], preferred_element_type=jnp.float32)
        total = term if total is None else total + term
    if not turned:
        out_ref[...] = total.astype(out_ref.dtype)
        return
    cosine = cosine_ref[...]
    sine = sine_ref[...]
    for head in range(out_ref.shape[1] // HEAD_DIM):
        at = slice(head * HEAD_DIM, (head + 1) * HEAD_DIM)
        part = total[:, at]
        rolled = pltpu.roll(part, HEAD_DIM // 2, 1)
        out_ref[:, at] = (part * cosine + rolled * sine).astype(out_ref.dtype)


def project(places, offsets, rows, value, pieces, cosine, sine, turned):
    tokens = value.shape[0]
    width = pieces[0][2].shape[1]
    block = min(width, 256)
    input_specs, weight_specs = [], []
    for offset, row, piece in pieces:
        depth = piece.shape[0]

        def place(j, places_ref, slot=offsets.index(offset), scale=rows // depth, at=row // depth):
            return (0, places_ref[slot] * scale + at)

        input_specs.append(pl.BlockSpec((tokens, depth), place))
        weight_specs.append(pl.BlockSpec((depth, block), lambda j, *_: (0, j)))
    angle = pl.BlockSpec((tokens, HEAD_DIM), lambda j, *_: (0, 0))
    return pl.pallas_call(
        functools.partial(project_kernel, len(pieces), turned),
        grid_spec=pltpu.PrefetchScalarGridSpec(
            num_scalar_prefetch=1,
            grid=(width // block,),
            in_specs=input_specs + weight_specs + [angle, angle],
            out_specs=pl.BlockSpec((tokens, block), lambda j, *_: (0, j)),
        ),
        out_shape=jax.ShapeDtypeStruct((tokens, width), jnp.bfloat16),
        compiler_params=pltpu.CompilerParams(vmem_limit_bytes=40 * 1024 * 1024),
        cost_estimate=pl.CostEstimate(
            flops=2 * tokens * value.shape[1] * width,
            bytes_accessed=2 * (tokens + width) * value.shape[1],
            transcendentals=0,
        ),
        name="project",
    )(places, *[value] * len(pieces), *[piece for _, _, piece in pieces], cosine, sine)


def silu(value):
    return value / (1.0 + jnp.exp(-value))


def exact_dot(a, b):
    return jnp.dot(a, b, precision=lax.Precision.HIGHEST, preferred_element_type=jnp.float32)


def spread(heads, block):
    shape = (heads, heads * block)
    column = lax.broadcasted_iota(jnp.int32, shape, 1) // block
    return (column == lax.broadcasted_iota(jnp.int32, shape, 0)).astype(jnp.float32)


def enter_kernel(input_ref, gain_ref, bc_ref, dt_ref, bias_ref, weight_ref, act_ref, map_ref, size_ref, normed_ref):
    @pl.when(pl.program_id(0) == 0)
    def _():
        rows = input_ref.shape[0]
        chunk = min(rows, 64)
        for start in range(0, rows, chunk):
            at = slice(start, start + chunk)
            hidden = input_ref[at, :].astype(jnp.float32)
            scale = lax.rsqrt(jnp.mean(hidden * hidden, axis=-1, keepdims=True) + 1e-05)
            normed_ref[at, :] = (hidden * scale * gain_ref[...]).astype(jnp.bfloat16)
        normed = normed_ref[...]
        map_ref[...] = jnp.dot(normed, bc_ref[...], preferred_element_type=jnp.float32)
        size = jnp.dot(normed, dt_ref[...], preferred_element_type=jnp.float32) + bias_ref[...]
        size_ref[...] = jnp.maximum(size, 0.0) + jnp.log1p(jnp.exp(-jnp.abs(size)))

    act_ref[...] = silu(
        jnp.dot(normed_ref[...], weight_ref[...], preferred_element_type=jnp.float32)
    )


def enter_mixer(flat_input, norm_gain, w_bc, w_dt, dt_bias, weight):
    tokens = flat_input.shape[0]
    width = weight.shape[1]
    block = min(width, 512)
    heads = w_dt.shape[1]
    whole = lambda *shape: pl.BlockSpec(shape, lambda j: (0, 0))
    return pl.pallas_call(
        enter_kernel,
        grid=(width // block,),
        in_specs=[
            whole(tokens, D),
            whole(1, D),
            whole(D, 2 * STATE),
            whole(D, heads),
            whole(1, heads),
            pl.BlockSpec((D, block), lambda j: (0, j)),
        ],
        out_specs=[
            pl.BlockSpec((tokens, block), lambda j: (0, j)),
            whole(tokens, 2 * STATE),
            whole(tokens, heads),
        ],
        out_shape=[
            jax.ShapeDtypeStruct((tokens, width), jnp.float32),
            jax.ShapeDtypeStruct((tokens, 2 * STATE), jnp.float32),
            jax.ShapeDtypeStruct((tokens, heads), jnp.float32),
        ],
        scratch_shapes=[pltpu.VMEM((tokens, D), jnp.bfloat16)],
        compiler_params=pltpu.CompilerParams(vmem_limit_bytes=40 * 1024 * 1024),
        cost_estimate=pl.CostEstimate(
            flops=2 * tokens * D * width,
            bytes_accessed=2 * D * (width + tokens) + 4 * tokens * width,
            transcendentals=tokens * width,
        ),
        name="enter_mixer",
    )(flat_input, norm_gain.reshape(1, D), w_bc, w_dt, dt_bias.reshape(1, heads), weight)


def inside_kernel(inner_ref, map_ref, decay_ref, size_ref, decay_row_ref, size_row_ref, skip_ref, read_ref, local_ref, through_ref):
    tokens, heads = decay_ref.shape[1:]
    inner = inner_ref[...]
    input_map = map_ref[:, :STATE]
    output_map = map_ref[:, STATE:]
    decay = decay_ref[0]
    by_head = spread(heads, MHEAD_DIM)
    wide = (tokens, heads * tokens)
    contact = dot_nt(
        output_map.astype(jnp.bfloat16),
        jnp.concatenate([input_map.astype(jnp.bfloat16)] * heads, axis=0),
    )
    source = lax.rem(lax.broadcasted_iota(jnp.int32, wide, 1), tokens)
    causal = source <= lax.broadcasted_iota(jnp.int32, wide, 0)
    difference = exact_dot(decay, spread(heads, tokens)) - decay_row_ref[0]
    mixing = jnp.exp(jnp.where(causal, difference, DEAD)) * contact * size_row_ref[0]
    mixing = mixing.astype(jnp.bfloat16)
    inner_low = inner.astype(jnp.bfloat16)
    together = min(heads, 256 // MHEAD_DIM)
    shape = (together * tokens, together * MHEAD_DIM)
    own = (
        lax.broadcasted_iota(jnp.int32, shape, 0) // tokens
        == lax.broadcasted_iota(jnp.int32, shape, 1) // MHEAD_DIM
    )
    for begin in range(0, heads, together):
        at = slice(begin * MHEAD_DIM, (begin + together) * MHEAD_DIM)
        stacked = jnp.concatenate([inner_low[:, at]] * together, axis=0)
        stacked = jnp.where(own, stacked, jnp.zeros_like(stacked))
        read_ref[:, at] = (
            jnp.dot(
                mixing[:, begin * tokens : (begin + together) * tokens],
                stacked,
                preferred_element_type=jnp.float32,
            )
            + skip_ref[:, at] * inner[:, at]
        )
    last = decay[tokens - 1 :, :]
    tail = exact_dot(jnp.exp(last - decay) * size_ref[0], by_head)
    local_ref[0] = dot_tn(input_map.astype(jnp.bfloat16), (inner * tail).astype(jnp.bfloat16))
    through_ref[0] = exact_dot(jnp.exp(jnp.broadcast_to(last, (8, heads))), by_head)[:1]


def inside_block(requests, act, maps, decay, size, decay_row, size_row, skip):
    tokens, heads = decay.shape[1:]
    inner = act.shape[1] // 2
    one = lambda *shape: pl.BlockSpec((1,) + shape, lambda r: (r, 0, 0))
    return pl.pallas_call(
        inside_kernel,
        grid=(requests,),
        in_specs=[
            pl.BlockSpec((tokens, inner), lambda r: (r, 1)),
            pl.BlockSpec((tokens, 2 * STATE), lambda r: (r, 0)),
            one(tokens, heads),
            one(tokens, heads),
            one(1, heads * tokens),
            one(1, heads * tokens),
            pl.BlockSpec((1, inner), lambda r: (0, 0)),
        ],
        out_specs=[
            pl.BlockSpec((tokens, inner), lambda r: (r, 0)),
            one(STATE, inner),
            one(1, inner),
        ],
        out_shape=[
            jax.ShapeDtypeStruct((requests * tokens, inner), jnp.float32),
            jax.ShapeDtypeStruct((requests, STATE, inner), jnp.float32),
            jax.ShapeDtypeStruct((requests, 1, inner), jnp.float32),
        ],
        compiler_params=pltpu.CompilerParams(vmem_limit_bytes=40 * 1024 * 1024),
        cost_estimate=pl.CostEstimate(
            flops=12 * requests * tokens * tokens * inner,
            bytes_accessed=16 * requests * tokens * inner,
            transcendentals=requests * tokens * tokens * heads,
        ),
        name="inside_block",
    )(act, maps, decay, size, decay_row, size_row, skip)


def leave_kernel(entry_ref, map_ref, decay_ref, read_ref, gate_ref, gain_ref, local_ref, through_ref, gated_ref, square_ref, chain_ref):
    heads = decay_ref.shape[2]
    entry = entry_ref[0]
    grown = exact_dot(jnp.exp(decay_ref[0]), spread(heads, MHEAD_DIM))
    inter = jnp.dot(
        map_ref[:, STATE:].astype(jnp.bfloat16),
        entry.astype(jnp.bfloat16),
        preferred_element_type=jnp.float32,
    )
    mixed = (read_ref[...] + inter * grown) * gate_ref[...]
    squares = jnp.sum(mixed * mixed, axis=1, keepdims=True)
    square_ref[...] = jnp.broadcast_to(squares, square_ref.shape)
    gated_ref[...] = (mixed * gain_ref[...]).astype(jnp.bfloat16)
    chain_ref[0] = through_ref[0] * entry + local_ref[0]


def leave_mixer(entry, maps, decay, read, act, gain, local, through):
    requests, tokens, heads = decay.shape
    inner = read.shape[1]
    one = lambda *shape: pl.BlockSpec((1,) + shape, lambda r: (r, 0, 0))
    flat = lambda width: pl.BlockSpec((tokens, width), lambda r: (r, 0))
    return pl.pallas_call(
        leave_kernel,
        grid=(requests,),
        in_specs=[
            one(STATE, inner),
            flat(2 * STATE),
            one(tokens, heads),
            flat(inner),
            flat(inner),
            pl.BlockSpec((1, inner), lambda r: (0, 0)),
            one(STATE, inner),
            one(1, inner),
        ],
        out_specs=[flat(inner), flat(128), one(STATE, inner)],
        out_shape=[
            jax.ShapeDtypeStruct((requests * tokens, inner), jnp.bfloat16),
            jax.ShapeDtypeStruct((requests * tokens, 128), jnp.float32),
            jax.ShapeDtypeStruct((requests, STATE, inner), jnp.float32),
        ],
        compiler_params=pltpu.CompilerParams(vmem_limit_bytes=40 * 1024 * 1024),
        cost_estimate=pl.CostEstimate(
            flops=2 * requests * tokens * STATE * inner,
            bytes_accessed=24 * requests * tokens * inner,
            transcendentals=requests * tokens * heads,
        ),
        name="leave_mixer",
    )(entry, maps, decay, read, act, gain, local, through)


def dot_nt(a, b):
    return lax.dot_general(a, b, (((1,), (1,)), ((), ())), preferred_element_type=jnp.float32)


def dot_tn(a, b):
    return lax.dot_general(a, b, (((0,), (0,)), ((), ())), preferred_element_type=jnp.float32)


def cache_kernel(slots, place_ref, live_ref, *refs):
    query_refs = refs[:slots]
    key_ref, value_ref, joined_ref, out_ref, peak_ref, total_ref = refs[slots:]
    tok_block = query_refs[0].shape[1]
    keys, width = key_ref.shape[1:]
    tokens = tok_block * slots
    for slot in range(slots):
        start = pl.multiple_of(place_ref[slot] * tok_block, tok_block)
        joined_ref[0, pl.ds(start, tok_block), :] = query_refs[slot][0]
    live = live_ref[pl.program_id(0)]
    bias = jnp.where(
        lax.broadcasted_iota(jnp.int32, (keys, 128), 0) < live, 0.0, DEAD
    ).astype(jnp.float32)
    bias = jnp.concatenate([bias] * (tokens // 128), axis=1)
    for head in range(width // HEAD_DIM):
        at = slice(head * HEAD_DIM, (head + 1) * HEAD_DIM)
        scores = dot_nt(key_ref[0, :, at], joined_ref[0, :, at]) + bias
        peak = jnp.max(scores, axis=0, keepdims=True)
        weights = jnp.exp2((scores - peak) * EXP2_SCALE)
        total_ref[0, head : head + 1, :] = jnp.sum(weights, axis=0, keepdims=True)
        peak_ref[0, head : head + 1, :] = peak
        out_ref[0, at, :] = dot_tn(value_ref[0, :, at], weights.astype(jnp.bfloat16)).astype(
            out_ref.dtype
        )


def cache_part(begin, at, requests, places, live, query_slots, keys, values):
    slots = len(query_slots)
    tok_block, width = query_slots[0].shape[1:]
    tokens = tok_block * slots
    cache_block = keys.shape[1]
    heads = width // HEAD_DIM
    one = lambda rows, start: pl.BlockSpec((1, rows, width), lambda r, *_: (r + start, 0, 0))
    stat = pl.BlockSpec((1, heads, tokens), lambda r, *_: (r, 0, 0))
    return pl.pallas_call(
        functools.partial(cache_kernel, slots),
        grid_spec=pltpu.PrefetchScalarGridSpec(
            num_scalar_prefetch=2,
            grid=(requests,),
            in_specs=[
                one(tok_block, 0 if slot.shape[0] == requests else at) for slot in query_slots
            ]
            + [one(cache_block, begin), one(cache_block, begin)],
            out_specs=[
                one(tokens, 0),
                pl.BlockSpec((1, width, tokens), lambda r, *_: (r, 0, 0)),
                stat,
                stat,
            ],
        ),
        out_shape=[
            jax.ShapeDtypeStruct((requests, tokens, width), jnp.bfloat16),
            jax.ShapeDtypeStruct((requests, width, tokens), jnp.bfloat16),
            jax.ShapeDtypeStruct((requests, heads, tokens), jnp.float32),
            jax.ShapeDtypeStruct((requests, heads, tokens), jnp.float32),
        ],
        compiler_params=pltpu.CompilerParams(vmem_limit_bytes=48 * 1024 * 1024),
        cost_estimate=pl.CostEstimate(
            flops=4 * requests * tokens * cache_block * width,
            bytes_accessed=2 * requests * width * (3 * tokens + 2 * cache_block),
            transcendentals=requests * tokens * cache_block * heads,
        ),
        name="cache_part",
    )(places, live, *query_slots, keys, values)


def group_scores(first, key, query):
    scores = dot_nt(key, query)
    shape = scores.shape
    live = first + lax.broadcasted_iota(jnp.int32, shape, 0) <= lax.broadcasted_iota(
        jnp.int32, shape, 1
    )
    return jnp.where(live, scores, DEAD)


def peak_kernel(first_ref, query_ref, key_ref, peak_ref, out_ref):
    for head in range(query_ref.shape[2] // HEAD_DIM):
        at = slice(head * HEAD_DIM, (head + 1) * HEAD_DIM)
        scores = group_scores(first_ref[0], key_ref[0, :, at], query_ref[0, :, at])
        out_ref[0, head : head + 1, :] = jnp.maximum(
            peak_ref[0, head : head + 1, :], jnp.max(scores, axis=0, keepdims=True)
        )


def group_peaks(begin, first, queries, new_keys, peaks):
    requests, tokens, width = queries.shape
    tok_block = new_keys.shape[1]
    heads = width // HEAD_DIM
    one = lambda rows, start: pl.BlockSpec((1, rows, width), lambda r, *_: (r + start, 0, 0))
    stat = pl.BlockSpec((1, heads, tokens), lambda r, *_: (r, 0, 0))
    return pl.pallas_call(
        peak_kernel,
        grid_spec=pltpu.PrefetchScalarGridSpec(
            num_scalar_prefetch=1,
            grid=(requests,),
            in_specs=[one(tokens, 0), one(tok_block, begin), stat],
            out_specs=stat,
        ),
        out_shape=jax.ShapeDtypeStruct(peaks.shape, jnp.float32),
        compiler_params=pltpu.CompilerParams(vmem_limit_bytes=32 * 1024 * 1024),
        cost_estimate=pl.CostEstimate(
            flops=2 * requests * tokens * tok_block * width,
            bytes_accessed=2 * requests * width * tokens,
            transcendentals=0,
        ),
        name="group_peaks",
    )(first, queries, new_keys, peaks)


def finish_kernel(slots, first_ref, place_ref, *refs):
    query_ref, key_ref, value_ref, cache_ref, peak_ref, total_ref, best_ref = refs[:7]
    sum_ref, *part_refs = refs[7:-1]
    joined_ref = refs[-1]
    tok_block = key_ref.shape[1]
    for head in range(query_ref.shape[2] // HEAD_DIM):
        at = slice(head * HEAD_DIM, (head + 1) * HEAD_DIM)
        row = slice(head, head + 1)
        scores = group_scores(first_ref[0], key_ref[0, :, at], query_ref[0, :, at])
        best = best_ref[0, row, :]
        weights = jnp.exp2((scores - best) * EXP2_SCALE)
        rescale = jnp.exp2((peak_ref[0, row, :] - best) * EXP2_SCALE)
        sum_ref[0, row, :] = total_ref[0, row, :] * rescale + jnp.sum(
            weights, axis=0, keepdims=True
        )
        joined = cache_ref[0, at, :].astype(jnp.float32) * rescale + dot_tn(
            value_ref[0, :, at], weights.astype(jnp.bfloat16)
        )
        joined_ref[:, at] = joined.T.astype(jnp.bfloat16)
    for slot in range(slots):
        start = pl.multiple_of(place_ref[slot] * tok_block, tok_block)
        part_refs[slot][0] = joined_ref[pl.ds(start, tok_block), :]


def finish_part(begin, first, places, queries, new_keys, new_values, cached, peaks, totals, best):
    requests, tokens, width = queries.shape
    tok_block = new_keys.shape[1]
    slots = tokens // tok_block
    heads = width // HEAD_DIM
    one = lambda rows, start: pl.BlockSpec((1, rows, width), lambda r, *_: (r + start, 0, 0))
    stat = lambda start: pl.BlockSpec((1, heads, tokens), lambda r, *_: (r + start, 0, 0))
    return pl.pallas_call(
        functools.partial(finish_kernel, slots),
        grid_spec=pltpu.PrefetchScalarGridSpec(
            num_scalar_prefetch=2,
            grid=(requests,),
            in_specs=[
                one(tokens, 0),
                one(tok_block, begin),
                one(tok_block, begin),
                pl.BlockSpec((1, width, tokens), lambda r, *_: (r, 0, 0)),
                stat(0),
                stat(0),
                stat(begin),
            ],
            out_specs=[stat(0)] + [one(tok_block, 0)] * slots,
            scratch_shapes=[pltpu.VMEM((tokens, width), jnp.bfloat16)],
        ),
        out_shape=[jax.ShapeDtypeStruct((requests, heads, tokens), jnp.float32)]
        + [jax.ShapeDtypeStruct((requests, tok_block, width), jnp.bfloat16)] * slots,
        compiler_params=pltpu.CompilerParams(vmem_limit_bytes=48 * 1024 * 1024),
        cost_estimate=pl.CostEstimate(
            flops=4 * requests * tokens * tok_block * width,
            bytes_accessed=6 * requests * width * tokens,
            transcendentals=requests * tokens * tok_block * heads,
        ),
        name="finish_part",
    )(first, places, queries, new_keys, new_values, cached, peaks, totals, best)


def head_sum(terms, head_count, head_index):
    if head_count != 4:
        return lax.psum_scatter(
            terms.astype(jnp.bfloat16), "head", scatter_dimension=1, tiled=True
        ).astype(jnp.float32)
    width = terms.shape[1] // 4
    chunk = lambda index: lax.dynamic_slice_in_dim(terms, index * width, width, 1)
    core, column = head_index % 2, head_index // 2
    near, far = 2 * column, 2 * (1 - column)
    got = lax.ppermute(
        jnp.concatenate([chunk(near + 1 - core), chunk(far + 1 - core)], axis=1).astype(
            jnp.bfloat16
        ),
        "head",
        [(h, h ^ 1) for h in range(4)],
    ).astype(jnp.float32)
    keep = chunk(near + core) + got[:, :width]
    give = chunk(far + core) + got[:, width:]
    return keep + lax.ppermute(
        give.astype(jnp.bfloat16), "head", [(h, h ^ 2) for h in range(4)]
    ).astype(jnp.float32)


class Relay:
    def __init__(self, through, local, initial, seq_index, seq_count):
        self.factor, self.local = through, local
        self.paired = seq_count == 8
        self.hop = 0
        if not self.paired:
            self.hops = seq_count - 1
            self.entry = jnp.where(seq_index == 0, initial, 0.0)
            return
        self.hops = 3
        self.swap = [(i, i ^ 1) for i in range(8)]
        self.is_first = is_first = seq_index % 2 == 0
        half = local.shape[2] // 2
        side = lambda value: jnp.where(is_first, value[..., :half], value[..., half:])
        mine = side(local)
        got = self.exchange(jnp.where(is_first, local[..., half:], local[..., :half]))
        other_factor = side(lax.ppermute(through, "seq", self.swap))
        factor = side(through)
        self.first_state = jnp.where(is_first, mine, got)
        second_state = jnp.where(is_first, got, mine)
        self.first_factor = jnp.where(is_first, factor, other_factor)
        second_factor = jnp.where(is_first, other_factor, factor)
        self.pair_state = second_factor * self.first_state + second_state
        self.pair_factor = self.first_factor * second_factor
        self.entry = jnp.where(seq_index < 2, side(initial), 0.0)

    def exchange(self, value):
        return lax.ppermute(value.astype(jnp.bfloat16), "seq", self.swap).astype(jnp.float32)

    def advance(self, clock):
        if self.hop == self.hops:
            return
        factor, state = (
            (self.pair_factor, self.pair_state) if self.paired else (self.factor, self.local)
        )
        entry = clock.hold(self.entry)
        leaving = (factor * entry + state).astype(jnp.bfloat16)
        if self.paired:
            route = [(2 * self.hop + y, 2 * self.hop + 2 + y) for y in range(2)]
        else:
            route = [(self.hop, self.hop + 1)]
        self.hop += 1
        self.entry = entry + lax.ppermute(leaving, "seq", route).astype(jnp.float32)

    def result(self, clock):
        while self.hop < self.hops:
            self.advance(clock)
        entry = clock.hold(self.entry)
        if not self.paired:
            return entry
        second = self.first_factor * entry + self.first_state
        got = self.exchange(jnp.where(self.is_first, second, entry))
        mine = jnp.where(self.is_first, entry, second)
        return jnp.concatenate(
            [jnp.where(self.is_first, mine, got), jnp.where(self.is_first, got, mine)], axis=2
        )


def shards(
    block_input,
    lengths,
    cache_keys,
    cache_values,
    w_query,
    w_key,
    w_value,
    w_attn_out,
    norm_gain,
    w_in,
    w_bc,
    w_dt,
    dt_bias,
    a_log,
    d_skip,
    gated_gain,
    w_out,
    ssm_init,
):
    requests, tok_block, _ = block_input.shape
    seq_count = lax.axis_size("seq")
    seq_index = lax.axis_index("seq")
    head_count = lax.axis_size("head")
    head_index = lax.axis_index("head")
    local_att = w_query.shape[1]
    local_heads = local_att // HEAD_DIM
    cache_block = cache_keys.shape[1]
    rows = w_query.shape[0]
    tokens = requests * tok_block
    flat_input = block_input.reshape(tokens, block_input.shape[2])

    order = ring_order(seq_count)
    half = seq_count // 2
    offsets = [0] + [sign * step for step in range(1, half) for sign in (1, -1)] + [half]
    places = jnp.asarray(
        [
            [order[(order.index(i) - offset) % seq_count] for offset in offsets]
            for i in range(seq_count)
        ],
        jnp.int32,
    )[seq_index]

    positions = (
        lengths[:, None] + seq_index * tok_block + jnp.arange(tok_block, dtype=jnp.int32)[None, :]
    ).reshape(tokens)
    half_dim = HEAD_DIM // 2
    frequency = jnp.exp(
        jnp.arange(half_dim, dtype=jnp.float32) * (-2.0 * math.log(10000.0) / HEAD_DIM)
    )
    angles = positions.astype(jnp.float32)[:, None] * frequency
    cosine = jnp.cos(angles)
    sine = jnp.sin(angles)
    cosine = jnp.concatenate([cosine, cosine], axis=1)
    sine = jnp.concatenate([-sine, sine], axis=1)

    clock = Clock()
    group = requests // GROUPS
    part_size = group // 2
    local_inner = w_in.shape[2]
    local_mheads = local_inner // MHEAD_DIM
    local_width = D // head_count
    made = {}

    def weight_rings(weight):
        top = weight.shape[0] // 2
        return [Ring(weight[:top], order), Ring(weight[top:], order, top)]

    def product(rings, turned):
        pieces = []
        for ring in rings:
            pieces += ring.pieces
            if pieces[-1][2].shape[0] < 128:
                (offset, row, upper), (_, _, lower) = pieces[-2:]
                pieces[-2:] = [(offset, row, jnp.concatenate([upper, lower], axis=0))]
        return project(
            places, offsets, rows, flat_input, pieces, cosine, sine, turned
        ).reshape(requests, tok_block, local_att)

    def order_weight():
        made["w_in"] = w_in.reshape(D, 2 * local_inner)
        return (made["w_in"],), ()

    def enter():
        made["act"], made["maps"], size = enter_mixer(
            clock.hold(flat_input), norm_gain, w_bc, w_dt, dt_bias, made["w_in"]
        )
        size = size.reshape(requests, tok_block, local_mheads)
        log_decay = -size * jnp.exp(a_log)
        causal = jnp.arange(tok_block)[None, :] <= jnp.arange(tok_block)[:, None]
        decay = jnp.einsum(
            "tu,ruh->rth", causal.astype(jnp.float32), log_decay, precision=lax.Precision.HIGHEST
        )
        by_row = lambda value: jnp.transpose(value, (0, 2, 1)).reshape(
            requests, 1, local_mheads * tok_block
        )
        made["size"], made["decay"] = size, decay
        made["size_row"], made["decay_row"] = by_row(size), by_row(decay)
        return (made["act"], made["size_row"], made["decay_row"]), ()

    def inside():
        made["read"], made["local"], made["through"] = inside_block(
            requests,
            clock.hold(made["act"]),
            made["maps"],
            made["decay"],
            made["size"],
            made["decay_row"],
            made["size_row"],
            jnp.repeat(d_skip, MHEAD_DIM).reshape(1, local_inner),
        )
        return (made["read"], made["local"]), ()

    def initial_state():
        first_state = clock.hold(ssm_init).reshape(requests, local_mheads, MHEAD_DIM, STATE)
        made["initial"] = jnp.transpose(first_state, (0, 3, 1, 2)).reshape(
            requests, STATE, local_inner
        )
        return (made["initial"],), ()

    def start_relay():
        made["relay"] = relay = Relay(
            made["through"], clock.hold(made["local"]), made["initial"], seq_index, seq_count
        )
        return (), ((relay.pair_state,) if relay.paired else ())

    def hop():
        made["relay"].advance(clock)
        return (), (made["relay"].entry,)

    def end_relay():
        made["entry"] = made["relay"].result(clock)
        return (), (made["entry"],)

    def leave():
        gated, squares, chain = leave_mixer(
            clock.hold(made["entry"]),
            made["maps"],
            made["decay"],
            made["read"],
            made["act"],
            gated_gain.reshape(1, local_inner),
            made["local"],
            made["through"],
        )
        made["gated"] = gated
        made["squares"] = butterfly(
            squares[:, :1].reshape(1, tokens), "head", head_count, jnp.add
        )
        made["chain"] = chain
        return (gated,), (made["squares"],)

    def leave_terms():
        made["terms"] = jnp.dot(
            clock.hold(made["gated"]), w_out, preferred_element_type=jnp.float32
        ) * lax.rsqrt(made["squares"].reshape(tokens, 1) / D_INNER + 1e-05)
        return (made["terms"],), ()

    def leave_chain():
        chain = clock.hold(made["chain"]).reshape(requests, STATE, local_mheads, MHEAD_DIM)
        made["chain"] = jnp.transpose(chain, (0, 2, 3, 1)).reshape(
            requests, 1, local_mheads, MHEAD_DIM * STATE
        )
        return (made["chain"],), ()

    query_rings = weight_rings(w_query)
    key_rings = weight_rings(w_key)
    value_rings = weight_rings(w_value)
    slot_rings = []
    live = jnp.clip(lengths - seq_index * cache_block, 0, cache_block).astype(jnp.int32)
    first = (seq_index * tok_block).astype(jnp.int32).reshape(1)
    cached = []

    def make_queries():
        queries = product(query_rings, True)
        slot_rings.extend(
            Ring(queries[begin : begin + group], order) for begin in range(0, requests, group)
        )
        return (queries,), ()

    def make_keys():
        made["keys"] = product(key_rings, True)
        return (made["keys"],), ()

    def meet_cache(index):
        def work():
            ring = slot_rings[index // 2]
            at = (index % 2) * part_size
            begin = index * part_size
            slots = [piece for _, _, piece in ring.pieces[:-2]]
            slots.append(ring.pieces[-2 + index % 2][2])
            slots[0] = clock.hold(slots[0])
            cached.append(
                cache_part(
                    begin,
                    at,
                    part_size,
                    places,
                    live[begin : begin + part_size],
                    slots,
                    cache_keys,
                    cache_values,
                )
            )
            return tuple(cached[-1]), ()

        return work

    def make_peaks():
        keys = clock.hold(made["keys"])
        made["peaks"] = jnp.concatenate(
            [
                group_peaks(index * part_size, first, part[0], keys, part[2])
                for index, part in enumerate(cached)
            ],
            axis=0,
        )
        return (made["peaks"],), ()

    def join_peaks():
        made["best"] = butterfly(clock.hold(made["peaks"]), "seq", seq_count, jnp.maximum)
        return (), ()

    def steps(rings, begin, end):
        return [ring for _ in range(begin, end) for ring in rings]

    def run(sends, works):
        for index in range(max(len(sends), len(works))):
            clock.turn(
                sends[index] if index < len(sends) else None,
                works[index] if index < len(works) else None,
            )

    run(
        steps(query_rings, 0, half),
        [order_weight, None, enter, inside, initial_state, start_relay, None, hop],
    )
    run(steps(key_rings, 0, 1), [make_queries])
    run(
        steps(slot_rings, 0, half),
        [None, hop, None, None, hop, None, None, end_relay],
    )
    run(
        steps(key_rings, 1, half) + steps(value_rings, 0, half),
        [meet_cache(0), meet_cache(1), meet_cache(2), meet_cache(3), leave, leave_terms]
        + [make_keys, make_peaks, join_peaks, None, None, leave_chain],
    )

    new_keys = made["keys"]
    best = made["best"]
    new_values = product(value_rings, False)

    own = lambda stat: lax.dynamic_slice_in_dim(stat, seq_index * tok_block, tok_block, 2)
    greatest_logit = jnp.transpose(own(best), (0, 2, 1)) * SCALE
    residual = lax.dynamic_slice_in_dim(
        flat_input, head_index * local_width, local_width, 1
    ).astype(jnp.float32)
    mixed = []
    for index in range(GROUPS):
        begin = index * group
        sums, parts = [], []
        for inner_index in range(2):
            joined, out, peaks, totals = cached[2 * index + inner_index]
            some_sums, *some_parts = finish_part(
                begin + inner_index * part_size,
                first,
                places,
                joined,
                new_keys,
                new_values,
                out,
                peaks,
                totals,
                best,
            )
            sums.append(some_sums)
            parts.append(some_parts)
        sums = butterfly(jnp.concatenate(sums, axis=0), "seq", seq_count, jnp.add)
        denominator = jnp.transpose(own(sums), (0, 2, 1))
        terms = {-offset: pair for offset, pair in zip(offsets, zip(*parts))}
        terms[half] = terms[-half]
        numerator = ring_sum(terms, order).reshape(group, tok_block, local_heads, HEAD_DIM)
        attended = (
            (numerator / denominator[..., None])
            .astype(jnp.bfloat16)
            .reshape(group * tok_block, local_att)
        )
        at = slice(begin * tok_block, (begin + group) * tok_block)
        attn_terms = jnp.dot(attended, w_attn_out, preferred_element_type=jnp.float32)
        summed = head_sum(attn_terms + made["terms"][at], head_count, head_index)
        mixed.append(
            (residual[at] + summed)
            .astype(jnp.bfloat16)
            .reshape(group, tok_block, local_width)
        )
    return (
        jnp.concatenate(mixed, axis=0),
        new_keys,
        new_values,
        made["chain"],
        greatest_logit,
    )


def solution(mesh):
    placed = (
        P(None, "seq", None),
        P(),
        P(None, "seq", "head"),
        P(None, "seq", "head"),
        P("seq", "head"),
        P("seq", "head"),
        P("seq", "head"),
        P("head", None),
        P(),
        P(None, None, "head"),
        P(),
        P(None, "head"),
        P("head"),
        P("head"),
        P("head"),
        P("head"),
        P("head", None),
        P(None, "head", None),
    )
    return jax.shard_map(
        shards,
        mesh=mesh,
        in_specs=placed,
        out_specs=(
            P(None, "seq", "head"),
            P(None, "seq", "head"),
            P(None, "seq", "head"),
            P(None, "seq", "head", None),
            P(None, "seq", "head"),
        ),
        check_vma=False,
    )
```

```python
import functools
import math

import jax
import jax.numpy as jnp
from jax import lax
from jax.experimental import pallas as pl
from jax.experimental.pallas import tpu as pltpu
from jax.sharding import PartitionSpec as P

D = 2048
HEAD_DIM = 128
MHEAD_DIM = 64
STATE = 64
D_INNER = 4096
SCALE = 1.0 / math.sqrt(HEAD_DIM)
EXP2_SCALE = SCALE * math.log2(math.e)
DEAD = -1e30
GROUPS = 2
VMEM_BYTES = 56 * 1024 * 1024


def ring_order(count):
    y_count = max(1, count // 4)
    z_count = count // y_count
    order = []
    for y in range(y_count):
        turn = range(z_count) if y % 2 == 0 else range(z_count - 1, -1, -1)
        order += [z * y_count + y for z in turn]
    return order


def ring_step(block, order, distance):
    count = len(order)
    route = [(order[i], order[(i + distance) % count]) for i in range(count)]
    return lax.ppermute(block, "seq", route)


class Ring:
    def __init__(self, block, order, first_row=0):
        self.order = order
        self.steps = len(order) // 2
        self.done = 0
        self.first_row = first_row
        self.block = self.ahead = self.back = block
        self.pieces = [(0, first_row, block)]

    def step(self, clock):
        self.done += 1
        half = self.block.shape[0] // 2
        last = self.done == self.steps
        ahead = self.ahead[:half] if last else self.ahead
        back = self.back[half:] if last else self.back
        ahead, back = clock.hold(ahead, back)
        self.ahead = ring_step(ahead, self.order, 1)
        self.back = ring_step(back, self.order, -1)
        at = self.first_row
        if last:
            self.pieces += [(self.steps, at, self.ahead), (self.steps, at + half, self.back)]
        else:
            self.pieces += [(self.done, at, self.ahead), (-self.done, at, self.back)]
        return [self.ahead, self.back]


class Clock:
    def __init__(self):
        self.fence = ()
        self.late = ()

    def hold(self, *values):
        held = lax.optimization_barrier(tuple(values) + self.fence)[: len(values)]
        return held[0] if len(values) == 1 else held

    def turn(self, ring=None, work=None):
        moved = tuple(ring.step(self)) if ring is not None else ()
        done, deferred = work() if work is not None else ((), ())
        self.fence = self.late + tuple(done)
        self.late = moved + tuple(deferred)


def butterfly(value, axis, count, combine):
    bit = 1
    while bit < count:
        value = combine(value, lax.ppermute(value, axis, [(i, i ^ bit) for i in range(count)]))
        bit *= 2
    return value


def ring_sum(parts, order):
    far = len(order) // 2
    half = parts[0].shape[0] // 2
    add = lambda a, b: (a.astype(jnp.float32) + b.astype(jnp.float32)).astype(jnp.bfloat16)
    ahead = ring_step(parts[far][:half], order, 1)
    back = ring_step(parts[far][half:], order, -1)
    top, bottom = parts[far - 1], parts[1 - far]
    ahead = jnp.concatenate([add(ahead, top[:half]), top[half:]], axis=0)
    back = jnp.concatenate([bottom[:half], add(back, bottom[half:])], axis=0)
    for step in range(far - 1, 0, -1):
        ahead = ring_step(ahead, order, 1)
        back = ring_step(back, order, -1)
        if step > 1:
            ahead = add(ahead, parts[step - 1])
            back = add(back, parts[1 - step])
    return (
        ahead.astype(jnp.float32) + back.astype(jnp.float32) + parts[0].astype(jnp.float32)
    )


def project_kernel(count, turned, places_ref, *refs):
    input_refs, weight_refs = refs[:count], refs[count : 2 * count]
    cosine_ref, sine_ref, out_ref = refs[2 * count :]
    total = None
    for input_ref, weight_ref in zip(input_refs, weight_refs):
        term = jnp.dot(input_ref[...], weight_ref[...], preferred_element_type=jnp.float32)
        total = term if total is None else total + term
    if not turned:
        out_ref[...] = total.astype(out_ref.dtype)
        return
    cosine = cosine_ref[...]
    sine = sine_ref[...]
    for head in range(out_ref.shape[1] // HEAD_DIM):
        at = slice(head * HEAD_DIM, (head + 1) * HEAD_DIM)
        part = total[:, at]
        rolled = pltpu.roll(part, HEAD_DIM // 2, 1)
        out_ref[:, at] = (part * cosine + rolled * sine).astype(out_ref.dtype)


def project(places, offsets, rows, value, pieces, cosine, sine, turned):
    tokens = value.shape[0]
    width = pieces[0][2].shape[1]
    block = min(width, 256)
    input_specs, weight_specs = [], []
    for offset, row, piece in pieces:
        depth = piece.shape[0]

        def place(j, places_ref, slot=offsets.index(offset), scale=rows // depth, at=row // depth):
            return (0, places_ref[slot] * scale + at)

        input_specs.append(pl.BlockSpec((tokens, depth), place))
        weight_specs.append(pl.BlockSpec((depth, block), lambda j, *_: (0, j)))
    angle = pl.BlockSpec((tokens, HEAD_DIM), lambda j, *_: (0, 0))
    return pl.pallas_call(
        functools.partial(project_kernel, len(pieces), turned),
        grid_spec=pltpu.PrefetchScalarGridSpec(
            num_scalar_prefetch=1,
            grid=(width // block,),
            in_specs=input_specs + weight_specs + [angle, angle],
            out_specs=pl.BlockSpec((tokens, block), lambda j, *_: (0, j)),
        ),
        out_shape=jax.ShapeDtypeStruct((tokens, width), jnp.bfloat16),
        compiler_params=pltpu.CompilerParams(vmem_limit_bytes=VMEM_BYTES),
        cost_estimate=pl.CostEstimate(
            flops=2 * tokens * value.shape[1] * width,
            bytes_accessed=2 * (tokens + width) * value.shape[1],
            transcendentals=0,
        ),
        name="project",
    )(places, *[value] * len(pieces), *[piece for _, _, piece in pieces], cosine, sine)


def silu(value):
    return value / (1.0 + jnp.exp(-value))


def exact_dot(a, b):
    return jnp.dot(a, b, precision=lax.Precision.HIGHEST, preferred_element_type=jnp.float32)


def spread(heads, block):
    shape = (heads, heads * block)
    column = lax.broadcasted_iota(jnp.int32, shape, 1) // block
    return (column == lax.broadcasted_iota(jnp.int32, shape, 0)).astype(jnp.float32)


def enter_kernel(input_ref, gain_ref, bc_ref, dt_ref, bias_ref, weight_ref, act_ref, map_ref, size_ref, normed_ref):
    @pl.when(pl.program_id(0) == 0)
    def _():
        rows = input_ref.shape[0]
        chunk = min(rows, 64)
        for start in range(0, rows, chunk):
            at = slice(start, start + chunk)
            hidden = input_ref[at, :].astype(jnp.float32)
            scale = lax.rsqrt(jnp.mean(hidden * hidden, axis=-1, keepdims=True) + 1e-05)
            normed_ref[at, :] = (hidden * scale * gain_ref[...]).astype(jnp.bfloat16)
        normed = normed_ref[...]
        map_ref[...] = jnp.dot(normed, bc_ref[...], preferred_element_type=jnp.float32)
        size = jnp.dot(normed, dt_ref[...], preferred_element_type=jnp.float32) + bias_ref[...]
        size_ref[...] = jnp.maximum(size, 0.0) + jnp.log1p(jnp.exp(-jnp.abs(size)))

    act_ref[...] = silu(
        jnp.dot(normed_ref[...], weight_ref[...], preferred_element_type=jnp.float32)
    )


def enter_mixer(flat_input, norm_gain, w_bc, w_dt, dt_bias, weight):
    tokens = flat_input.shape[0]
    width = weight.shape[1]
    block = min(width, 512)
    heads = w_dt.shape[1]
    whole = lambda *shape: pl.BlockSpec(shape, lambda j: (0, 0))
    return pl.pallas_call(
        enter_kernel,
        grid=(width // block,),
        in_specs=[
            whole(tokens, D),
            whole(1, D),
            whole(D, 2 * STATE),
            whole(D, heads),
            whole(1, heads),
            pl.BlockSpec((D, block), lambda j: (0, j)),
        ],
        out_specs=[
            pl.BlockSpec((tokens, block), lambda j: (0, j)),
            whole(tokens, 2 * STATE),
            whole(tokens, heads),
        ],
        out_shape=[
            jax.ShapeDtypeStruct((tokens, width), jnp.float32),
            jax.ShapeDtypeStruct((tokens, 2 * STATE), jnp.float32),
            jax.ShapeDtypeStruct((tokens, heads), jnp.float32),
        ],
        scratch_shapes=[pltpu.VMEM((tokens, D), jnp.bfloat16)],
        compiler_params=pltpu.CompilerParams(vmem_limit_bytes=VMEM_BYTES),
        cost_estimate=pl.CostEstimate(
            flops=2 * tokens * D * width,
            bytes_accessed=2 * D * (width + tokens) + 4 * tokens * width,
            transcendentals=tokens * width,
        ),
        name="enter_mixer",
    )(flat_input, norm_gain.reshape(1, D), w_bc, w_dt, dt_bias.reshape(1, heads), weight)


def inside_kernel(inner_ref, map_ref, decay_ref, size_ref, decay_row_ref, size_row_ref, skip_ref, read_ref, local_ref, through_ref):
    tokens, heads = decay_ref.shape[1:]
    inner = inner_ref[...]
    input_map = map_ref[:, :STATE]
    output_map = map_ref[:, STATE:]
    decay = decay_ref[0]
    by_head = spread(heads, MHEAD_DIM)
    wide = (tokens, heads * tokens)
    contact = dot_nt(
        output_map.astype(jnp.bfloat16),
        jnp.concatenate([input_map.astype(jnp.bfloat16)] * heads, axis=0),
    )
    source = lax.rem(lax.broadcasted_iota(jnp.int32, wide, 1), tokens)
    causal = source <= lax.broadcasted_iota(jnp.int32, wide, 0)
    difference = exact_dot(decay, spread(heads, tokens)) - decay_row_ref[0]
    mixing = jnp.exp(jnp.where(causal, difference, DEAD)) * contact * size_row_ref[0]
    mixing = mixing.astype(jnp.bfloat16)
    inner_low = inner.astype(jnp.bfloat16)
    together = min(heads, 256 // MHEAD_DIM)
    shape = (together * tokens, together * MHEAD_DIM)
    own = (
        lax.broadcasted_iota(jnp.int32, shape, 0) // tokens
        == lax.broadcasted_iota(jnp.int32, shape, 1) // MHEAD_DIM
    )
    for begin in range(0, heads, together):
        at = slice(begin * MHEAD_DIM, (begin + together) * MHEAD_DIM)
        stacked = jnp.concatenate([inner_low[:, at]] * together, axis=0)
        stacked = jnp.where(own, stacked, jnp.zeros_like(stacked))
        read_ref[:, at] = (
            jnp.dot(
                mixing[:, begin * tokens : (begin + together) * tokens],
                stacked,
                preferred_element_type=jnp.float32,
            )
            + skip_ref[:, at] * inner[:, at]
        )
    last = decay[tokens - 1 :, :]
    tail = exact_dot(jnp.exp(last - decay) * size_ref[0], by_head)
    local_ref[0] = dot_tn(input_map.astype(jnp.bfloat16), (inner * tail).astype(jnp.bfloat16))
    through_ref[0] = exact_dot(jnp.exp(jnp.broadcast_to(last, (8, heads))), by_head)[:1]


def inside_block(requests, act, maps, decay, size, decay_row, size_row, skip):
    tokens, heads = decay.shape[1:]
    inner = act.shape[1] // 2
    one = lambda *shape: pl.BlockSpec((1,) + shape, lambda r: (r, 0, 0))
    return pl.pallas_call(
        inside_kernel,
        grid=(requests,),
        in_specs=[
            pl.BlockSpec((tokens, inner), lambda r: (r, 1)),
            pl.BlockSpec((tokens, 2 * STATE), lambda r: (r, 0)),
            one(tokens, heads),
            one(tokens, heads),
            one(1, heads * tokens),
            one(1, heads * tokens),
            pl.BlockSpec((1, inner), lambda r: (0, 0)),
        ],
        out_specs=[
            pl.BlockSpec((tokens, inner), lambda r: (r, 0)),
            one(STATE, inner),
            one(1, inner),
        ],
        out_shape=[
            jax.ShapeDtypeStruct((requests * tokens, inner), jnp.float32),
            jax.ShapeDtypeStruct((requests, STATE, inner), jnp.float32),
            jax.ShapeDtypeStruct((requests, 1, inner), jnp.float32),
        ],
        compiler_params=pltpu.CompilerParams(vmem_limit_bytes=VMEM_BYTES),
        cost_estimate=pl.CostEstimate(
            flops=12 * requests * tokens * tokens * inner,
            bytes_accessed=16 * requests * tokens * inner,
            transcendentals=requests * tokens * tokens * heads,
        ),
        name="inside_block",
    )(act, maps, decay, size, decay_row, size_row, skip)


def leave_kernel(entry_ref, map_ref, decay_ref, read_ref, gate_ref, gain_ref, local_ref, through_ref, gated_ref, square_ref, chain_ref):
    heads = decay_ref.shape[2]
    entry = entry_ref[0]
    grown = exact_dot(jnp.exp(decay_ref[0]), spread(heads, MHEAD_DIM))
    inter = jnp.dot(
        map_ref[:, STATE:].astype(jnp.bfloat16),
        entry.astype(jnp.bfloat16),
        preferred_element_type=jnp.float32,
    )
    mixed = (read_ref[...] + inter * grown) * gate_ref[...]
    squares = jnp.sum(mixed * mixed, axis=1, keepdims=True)
    square_ref[...] = jnp.broadcast_to(squares, square_ref.shape)
    gated_ref[...] = (mixed * gain_ref[...]).astype(jnp.bfloat16)
    chain_ref[0] = through_ref[0] * entry + local_ref[0]


def leave_mixer(entry, maps, decay, read, act, gain, local, through):
    requests, tokens, heads = decay.shape
    inner = read.shape[1]
    one = lambda *shape: pl.BlockSpec((1,) + shape, lambda r: (r, 0, 0))
    flat = lambda width: pl.BlockSpec((tokens, width), lambda r: (r, 0))
    return pl.pallas_call(
        leave_kernel,
        grid=(requests,),
        in_specs=[
            one(STATE, inner),
            flat(2 * STATE),
            one(tokens, heads),
            flat(inner),
            flat(inner),
            pl.BlockSpec((1, inner), lambda r: (0, 0)),
            one(STATE, inner),
            one(1, inner),
        ],
        out_specs=[flat(inner), flat(128), one(STATE, inner)],
        out_shape=[
            jax.ShapeDtypeStruct((requests * tokens, inner), jnp.bfloat16),
            jax.ShapeDtypeStruct((requests * tokens, 128), jnp.float32),
            jax.ShapeDtypeStruct((requests, STATE, inner), jnp.float32),
        ],
        compiler_params=pltpu.CompilerParams(vmem_limit_bytes=VMEM_BYTES),
        cost_estimate=pl.CostEstimate(
            flops=2 * requests * tokens * STATE * inner,
            bytes_accessed=24 * requests * tokens * inner,
            transcendentals=requests * tokens * heads,
        ),
        name="leave_mixer",
    )(entry, maps, decay, read, act, gain, local, through)


def dot_nt(a, b):
    return lax.dot_general(a, b, (((1,), (1,)), ((), ())), preferred_element_type=jnp.float32)


def dot_tn(a, b):
    return lax.dot_general(a, b, (((0,), (0,)), ((), ())), preferred_element_type=jnp.float32)


def cache_kernel(slots, place_ref, live_ref, *refs):
    query_refs = refs[:slots]
    key_ref, value_ref, joined_ref, out_ref, peak_ref, total_ref = refs[slots:]
    tok_block = query_refs[0].shape[1]
    keys, width = key_ref.shape[1:]
    tokens = tok_block * slots
    for slot in range(slots):
        start = pl.multiple_of(place_ref[slot] * tok_block, tok_block)
        joined_ref[0, pl.ds(start, tok_block), :] = query_refs[slot][0]
    live = live_ref[pl.program_id(0)]
    bias = jnp.where(
        lax.broadcasted_iota(jnp.int32, (keys, 128), 0) < live, 0.0, DEAD
    ).astype(jnp.float32)
    bias = jnp.concatenate([bias] * (tokens // 128), axis=1)
    for head in range(width // HEAD_DIM):
        at = slice(head * HEAD_DIM, (head + 1) * HEAD_DIM)
        scores = dot_nt(key_ref[0, :, at], joined_ref[0, :, at]) + bias
        peak = jnp.max(scores, axis=0, keepdims=True)
        weights = jnp.exp2((scores - peak) * EXP2_SCALE)
        total_ref[0, head : head + 1, :] = jnp.sum(weights, axis=0, keepdims=True)
        peak_ref[0, head : head + 1, :] = peak
        out_ref[0, at, :] = dot_tn(value_ref[0, :, at], weights.astype(jnp.bfloat16)).astype(
            out_ref.dtype
        )


def cache_part(begin, places, live, query_slots, keys, values):
    slots = len(query_slots)
    requests, tok_block, width = query_slots[0].shape
    tokens = tok_block * slots
    cache_block = keys.shape[1]
    heads = width // HEAD_DIM
    one = lambda rows, start: pl.BlockSpec((1, rows, width), lambda r, *_: (r + start, 0, 0))
    stat = pl.BlockSpec((1, heads, tokens), lambda r, *_: (r, 0, 0))
    return pl.pallas_call(
        functools.partial(cache_kernel, slots),
        grid_spec=pltpu.PrefetchScalarGridSpec(
            num_scalar_prefetch=2,
            grid=(requests,),
            in_specs=[one(tok_block, 0)] * slots + [one(cache_block, begin)] * 2,
            out_specs=[
                one(tokens, 0),
                pl.BlockSpec((1, width, tokens), lambda r, *_: (r, 0, 0)),
                stat,
                stat,
            ],
        ),
        out_shape=[
            jax.ShapeDtypeStruct((requests, tokens, width), jnp.bfloat16),
            jax.ShapeDtypeStruct((requests, width, tokens), jnp.bfloat16),
            jax.ShapeDtypeStruct((requests, heads, tokens), jnp.float32),
            jax.ShapeDtypeStruct((requests, heads, tokens), jnp.float32),
        ],
        compiler_params=pltpu.CompilerParams(vmem_limit_bytes=VMEM_BYTES),
        cost_estimate=pl.CostEstimate(
            flops=4 * requests * tokens * cache_block * width,
            bytes_accessed=2 * requests * width * (3 * tokens + 2 * cache_block),
            transcendentals=requests * tokens * cache_block * heads,
        ),
        name="cache_part",
    )(places, live, *query_slots, keys, values)


def group_scores(first, key, query):
    scores = dot_nt(key, query)
    shape = scores.shape
    live = first + lax.broadcasted_iota(jnp.int32, shape, 0) <= lax.broadcasted_iota(
        jnp.int32, shape, 1
    )
    return jnp.where(live, scores, DEAD)


def peak_kernel(first_ref, query_ref, key_ref, peak_ref, out_ref):
    for head in range(query_ref.shape[2] // HEAD_DIM):
        at = slice(head * HEAD_DIM, (head + 1) * HEAD_DIM)
        scores = group_scores(first_ref[0], key_ref[0, :, at], query_ref[0, :, at])
        out_ref[0, head : head + 1, :] = jnp.maximum(
            peak_ref[0, head : head + 1, :], jnp.max(scores, axis=0, keepdims=True)
        )


def group_peaks(begin, first, queries, new_keys, peaks):
    requests, tokens, width = queries.shape
    tok_block = new_keys.shape[1]
    heads = width // HEAD_DIM
    one = lambda rows, start: pl.BlockSpec((1, rows, width), lambda r, *_: (r + start, 0, 0))
    stat = pl.BlockSpec((1, heads, tokens), lambda r, *_: (r, 0, 0))
    return pl.pallas_call(
        peak_kernel,
        grid_spec=pltpu.PrefetchScalarGridSpec(
            num_scalar_prefetch=1,
            grid=(requests,),
            in_specs=[one(tokens, 0), one(tok_block, begin), stat],
            out_specs=stat,
        ),
        out_shape=jax.ShapeDtypeStruct(peaks.shape, jnp.float32),
        compiler_params=pltpu.CompilerParams(vmem_limit_bytes=VMEM_BYTES),
        cost_estimate=pl.CostEstimate(
            flops=2 * requests * tokens * tok_block * width,
            bytes_accessed=2 * requests * width * tokens,
            transcendentals=0,
        ),
        name="group_peaks",
    )(first, queries, new_keys, peaks)


def finish_kernel(slots, first_ref, place_ref, *refs):
    query_ref, key_ref, value_ref, cache_ref, peak_ref, total_ref, best_ref = refs[:7]
    sum_ref, *part_refs = refs[7:-1]
    joined_ref = refs[-1]
    tok_block = key_ref.shape[1]
    for head in range(query_ref.shape[2] // HEAD_DIM):
        at = slice(head * HEAD_DIM, (head + 1) * HEAD_DIM)
        row = slice(head, head + 1)
        scores = group_scores(first_ref[0], key_ref[0, :, at], query_ref[0, :, at])
        best = best_ref[0, row, :]
        weights = jnp.exp2((scores - best) * EXP2_SCALE)
        rescale = jnp.exp2((peak_ref[0, row, :] - best) * EXP2_SCALE)
        sum_ref[0, row, :] = total_ref[0, row, :] * rescale + jnp.sum(
            weights, axis=0, keepdims=True
        )
        joined = cache_ref[0, at, :].astype(jnp.float32) * rescale + dot_tn(
            value_ref[0, :, at], weights.astype(jnp.bfloat16)
        )
        joined_ref[:, at] = joined.T.astype(jnp.bfloat16)
    for slot in range(slots):
        start = pl.multiple_of(place_ref[slot] * tok_block, tok_block)
        part_refs[slot][0] = joined_ref[pl.ds(start, tok_block), :]


def finish_part(begin, first, places, queries, new_keys, new_values, cached, peaks, totals, best):
    requests, tokens, width = queries.shape
    tok_block = new_keys.shape[1]
    slots = tokens // tok_block
    heads = width // HEAD_DIM
    one = lambda rows, start: pl.BlockSpec((1, rows, width), lambda r, *_: (r + start, 0, 0))
    stat = lambda start: pl.BlockSpec((1, heads, tokens), lambda r, *_: (r + start, 0, 0))
    return pl.pallas_call(
        functools.partial(finish_kernel, slots),
        grid_spec=pltpu.PrefetchScalarGridSpec(
            num_scalar_prefetch=2,
            grid=(requests,),
            in_specs=[
                one(tokens, 0),
                one(tok_block, begin),
                one(tok_block, begin),
                pl.BlockSpec((1, width, tokens), lambda r, *_: (r, 0, 0)),
                stat(0),
                stat(0),
                stat(begin),
            ],
            out_specs=[stat(0)] + [one(tok_block, 0)] * slots,
            scratch_shapes=[pltpu.VMEM((tokens, width), jnp.bfloat16)],
        ),
        out_shape=[jax.ShapeDtypeStruct((requests, heads, tokens), jnp.float32)]
        + [jax.ShapeDtypeStruct((requests, tok_block, width), jnp.bfloat16)] * slots,
        compiler_params=pltpu.CompilerParams(vmem_limit_bytes=VMEM_BYTES),
        cost_estimate=pl.CostEstimate(
            flops=4 * requests * tokens * tok_block * width,
            bytes_accessed=6 * requests * width * tokens,
            transcendentals=requests * tokens * tok_block * heads,
        ),
        name="finish_part",
    )(first, places, queries, new_keys, new_values, cached, peaks, totals, best)


def head_sum(terms, head_count, head_index):
    if head_count != 4:
        return lax.psum_scatter(
            terms.astype(jnp.bfloat16), "head", scatter_dimension=1, tiled=True
        ).astype(jnp.float32)
    width = terms.shape[1] // 4
    chunk = lambda index: lax.dynamic_slice_in_dim(terms, index * width, width, 1)
    core, column = head_index % 2, head_index // 2
    near, far = 2 * column, 2 * (1 - column)
    got = lax.ppermute(
        jnp.concatenate([chunk(near + 1 - core), chunk(far + 1 - core)], axis=1).astype(
            jnp.bfloat16
        ),
        "head",
        [(h, h ^ 1) for h in range(4)],
    ).astype(jnp.float32)
    keep = chunk(near + core) + got[:, :width]
    give = chunk(far + core) + got[:, width:]
    return keep + lax.ppermute(
        give.astype(jnp.bfloat16), "head", [(h, h ^ 2) for h in range(4)]
    ).astype(jnp.float32)


class Relay:
    def __init__(self, through, local, initial, seq_index, seq_count):
        self.factor, self.local = through, local
        self.paired = seq_count == 8
        self.hop = 0
        if not self.paired:
            self.hops = seq_count - 1
            self.entry = jnp.where(seq_index == 0, initial, 0.0)
            return
        self.hops = 3
        self.swap = [(i, i ^ 1) for i in range(8)]
        self.is_first = is_first = seq_index % 2 == 0
        half = local.shape[2] // 2
        side = lambda value: jnp.where(is_first, value[..., :half], value[..., half:])
        mine = side(local)
        got = self.exchange(jnp.where(is_first, local[..., half:], local[..., :half]))
        other_factor = side(lax.ppermute(through, "seq", self.swap))
        factor = side(through)
        self.first_state = jnp.where(is_first, mine, got)
        second_state = jnp.where(is_first, got, mine)
        self.first_factor = jnp.where(is_first, factor, other_factor)
        second_factor = jnp.where(is_first, other_factor, factor)
        self.pair_state = second_factor * self.first_state + second_state
        self.pair_factor = self.first_factor * second_factor
        self.entry = jnp.where(seq_index < 2, side(initial), 0.0)

    def exchange(self, value):
        return lax.ppermute(value.astype(jnp.bfloat16), "seq", self.swap).astype(jnp.float32)

    def advance(self, clock):
        if self.hop == self.hops:
            return
        factor, state = (
            (self.pair_factor, self.pair_state) if self.paired else (self.factor, self.local)
        )
        entry = clock.hold(self.entry)
        leaving = (factor * entry + state).astype(jnp.bfloat16)
        if self.paired:
            route = [(2 * self.hop + y, 2 * self.hop + 2 + y) for y in range(2)]
        else:
            route = [(self.hop, self.hop + 1)]
        self.hop += 1
        self.entry = entry + lax.ppermute(leaving, "seq", route).astype(jnp.float32)

    def result(self, clock):
        while self.hop < self.hops:
            self.advance(clock)
        entry = clock.hold(self.entry)
        if not self.paired:
            return entry
        second = self.first_factor * entry + self.first_state
        got = self.exchange(jnp.where(self.is_first, second, entry))
        mine = jnp.where(self.is_first, entry, second)
        return jnp.concatenate(
            [jnp.where(self.is_first, mine, got), jnp.where(self.is_first, got, mine)], axis=2
        )


def shards(
    block_input,
    lengths,
    cache_keys,
    cache_values,
    w_query,
    w_key,
    w_value,
    w_attn_out,
    norm_gain,
    w_in,
    w_bc,
    w_dt,
    dt_bias,
    a_log,
    d_skip,
    gated_gain,
    w_out,
    ssm_init,
):
    requests, tok_block, _ = block_input.shape
    seq_count = lax.axis_size("seq")
    seq_index = lax.axis_index("seq")
    head_count = lax.axis_size("head")
    head_index = lax.axis_index("head")
    local_att = w_query.shape[1]
    local_heads = local_att // HEAD_DIM
    cache_block = cache_keys.shape[1]
    rows = w_query.shape[0]
    tokens = requests * tok_block
    flat_input = block_input.reshape(tokens, block_input.shape[2])

    order = ring_order(seq_count)
    half = seq_count // 2
    offsets = [0] + [sign * step for step in range(1, half) for sign in (1, -1)] + [half]
    places = jnp.asarray(
        [
            [order[(order.index(i) - offset) % seq_count] for offset in offsets]
            for i in range(seq_count)
        ],
        jnp.int32,
    )[seq_index]

    positions = (
        lengths[:, None] + seq_index * tok_block + jnp.arange(tok_block, dtype=jnp.int32)[None, :]
    ).reshape(tokens)
    half_dim = HEAD_DIM // 2
    frequency = jnp.exp(
        jnp.arange(half_dim, dtype=jnp.float32) * (-2.0 * math.log(10000.0) / HEAD_DIM)
    )
    angles = positions.astype(jnp.float32)[:, None] * frequency
    cosine = jnp.cos(angles)
    sine = jnp.sin(angles)
    cosine = jnp.concatenate([cosine, cosine], axis=1)
    sine = jnp.concatenate([-sine, sine], axis=1)

    clock = Clock()
    group = requests // GROUPS
    local_inner = w_in.shape[2]
    local_mheads = local_inner // MHEAD_DIM
    local_width = D // head_count
    made = {}

    def product(ring, turned):
        pieces = list(ring.pieces)
        if pieces[-1][2].shape[0] < 128:
            (offset, row, upper), (_, _, lower) = pieces[-2:]
            pieces[-2:] = [(offset, row, jnp.concatenate([upper, lower], axis=0))]
        return project(
            places, offsets, rows, flat_input, pieces, cosine, sine, turned
        ).reshape(requests, tok_block, local_att)

    def order_weight():
        made["w_in"] = w_in.reshape(D, 2 * local_inner)
        return (made["w_in"],), ()

    def enter():
        made["act"], made["maps"], size = enter_mixer(
            clock.hold(flat_input), norm_gain, w_bc, w_dt, dt_bias, made["w_in"]
        )
        size = size.reshape(requests, tok_block, local_mheads)
        log_decay = -size * jnp.exp(a_log)
        causal = jnp.arange(tok_block)[None, :] <= jnp.arange(tok_block)[:, None]
        decay = jnp.einsum(
            "tu,ruh->rth", causal.astype(jnp.float32), log_decay, precision=lax.Precision.HIGHEST
        )
        by_row = lambda value: jnp.transpose(value, (0, 2, 1)).reshape(
            requests, 1, local_mheads * tok_block
        )
        made["size"], made["decay"] = size, decay
        made["size_row"], made["decay_row"] = by_row(size), by_row(decay)
        return (made["act"], made["size_row"], made["decay_row"]), ()

    def inside():
        made["read"], made["local"], made["through"] = inside_block(
            requests,
            clock.hold(made["act"]),
            made["maps"],
            made["decay"],
            made["size"],
            made["decay_row"],
            made["size_row"],
            jnp.repeat(d_skip, MHEAD_DIM).reshape(1, local_inner),
        )
        return (made["read"], made["local"]), ()

    def initial_state():
        first_state = clock.hold(ssm_init).reshape(requests, local_mheads, MHEAD_DIM, STATE)
        made["initial"] = jnp.transpose(first_state, (0, 3, 1, 2)).reshape(
            requests, STATE, local_inner
        )
        return (made["initial"],), ()

    def start_relay():
        made["relay"] = relay = Relay(
            made["through"], clock.hold(made["local"]), made["initial"], seq_index, seq_count
        )
        return (), ((relay.pair_state,) if relay.paired else ())

    def hop():
        made["relay"].advance(clock)
        return (), (made["relay"].entry,)

    def end_relay():
        made["entry"] = made["relay"].result(clock)
        return (), (made["entry"],)

    def leave():
        gated, squares, chain = leave_mixer(
            clock.hold(made["entry"]),
            made["maps"],
            made["decay"],
            made["read"],
            made["act"],
            gated_gain.reshape(1, local_inner),
            made["local"],
            made["through"],
        )
        made["gated"] = gated
        made["squares"] = butterfly(
            squares[:, :1].reshape(1, tokens), "head", head_count, jnp.add
        )
        made["chain"] = chain
        return (gated,), (made["squares"],)

    def leave_terms():
        made["terms"] = jnp.dot(
            clock.hold(made["gated"]), w_out, preferred_element_type=jnp.float32
        ) * lax.rsqrt(made["squares"].reshape(tokens, 1) / D_INNER + 1e-05)
        return (made["terms"],), ()

    def leave_chain():
        chain = clock.hold(made["chain"]).reshape(requests, STATE, local_mheads, MHEAD_DIM)
        made["chain"] = jnp.transpose(chain, (0, 2, 3, 1)).reshape(
            requests, 1, local_mheads, MHEAD_DIM * STATE
        )
        return (made["chain"],), ()

    query_ring, key_ring, value_ring = (Ring(w, order) for w in (w_query, w_key, w_value))
    slot_rings = []
    live = jnp.clip(lengths - seq_index * cache_block, 0, cache_block).astype(jnp.int32)
    first = (seq_index * tok_block).astype(jnp.int32).reshape(1)
    cached = []

    def make_queries():
        queries = product(query_ring, True)
        slot_rings.extend(
            Ring(queries[begin : begin + group], order) for begin in range(0, requests, group)
        )
        return (queries,), ()

    def make_keys():
        made["keys"] = product(key_ring, True)
        return (made["keys"],), ()

    def meet_cache(index):
        def work():
            ring = slot_rings[index]
            begin = index * group
            slots = [piece for _, _, piece in ring.pieces[:-2]]
            slots.append(jnp.concatenate([ring.pieces[-2][2], ring.pieces[-1][2]], axis=0))
            slots[0] = clock.hold(slots[0])
            cached.append(
                cache_part(
                    begin, places, live[begin : begin + group], slots, cache_keys, cache_values
                )
            )
            return tuple(cached[-1]), ()

        return work

    def make_peaks():
        keys = clock.hold(made["keys"])
        made["peaks"] = jnp.concatenate(
            [
                group_peaks(index * group, first, part[0], keys, part[2])
                for index, part in enumerate(cached)
            ],
            axis=0,
        )
        return (made["peaks"],), ()

    def join_peaks():
        made["best"] = butterfly(clock.hold(made["peaks"]), "seq", seq_count, jnp.maximum)
        return (), ()

    def steps(rings, begin, end):
        return [ring for _ in range(begin, end) for ring in rings]

    def run(sends, works):
        for index in range(max(len(sends), len(works))):
            clock.turn(
                sends[index] if index < len(sends) else None,
                works[index] if index < len(works) else None,
            )

    run(
        steps([query_ring, key_ring], 0, half),
        [order_weight, enter, inside, initial_state, start_relay, hop, hop, hop],
    )
    run(steps([value_ring], 0, 1), [make_queries])
    run(
        steps(slot_rings, 0, half),
        [end_relay, make_keys, leave, leave_terms, leave_chain],
    )
    run(
        steps([value_ring], 1, half),
        [meet_cache(0), meet_cache(1), make_peaks, join_peaks],
    )

    new_keys = made["keys"]
    best = made["best"]
    new_values = product(value_ring, False)

    own = lambda stat: lax.dynamic_slice_in_dim(stat, seq_index * tok_block, tok_block, 2)
    greatest_logit = jnp.transpose(own(best), (0, 2, 1)) * SCALE
    residual = lax.dynamic_slice_in_dim(
        flat_input, head_index * local_width, local_width, 1
    ).astype(jnp.float32)
    mixed = []
    for index in range(GROUPS):
        begin = index * group
        joined, out, peaks, totals = cached[index]
        sums, *parts = finish_part(
            begin, first, places, joined, new_keys, new_values, out, peaks, totals, best
        )
        sums = butterfly(sums, "seq", seq_count, jnp.add)
        denominator = jnp.transpose(own(sums), (0, 2, 1))
        terms = {-offset: part for offset, part in zip(offsets, parts)}
        terms[half] = terms[-half]
        numerator = ring_sum(terms, order).reshape(group, tok_block, local_heads, HEAD_DIM)
        attended = (
            (numerator / denominator[..., None])
            .astype(jnp.bfloat16)
            .reshape(group * tok_block, local_att)
        )
        at = slice(begin * tok_block, (begin + group) * tok_block)
        attn_terms = jnp.dot(attended, w_attn_out, preferred_element_type=jnp.float32)
        summed = head_sum(attn_terms + made["terms"][at], head_count, head_index)
        mixed.append(
            (residual[at] + summed)
            .astype(jnp.bfloat16)
            .reshape(group, tok_block, local_width)
        )
    return (
        jnp.concatenate(mixed, axis=0),
        new_keys,
        new_values,
        made["chain"],
        greatest_logit,
    )


def solution(mesh):
    placed = (
        P(None, "seq", None),
        P(),
        P(None, "seq", "head"),
        P(None, "seq", "head"),
        P("seq", "head"),
        P("seq", "head"),
        P("seq", "head"),
        P("head", None),
        P(),
        P(None, None, "head"),
        P(),
        P(None, "head"),
        P("head"),
        P("head"),
        P("head"),
        P("head"),
        P("head", None),
        P(None, "head", None),
    )
    return jax.shard_map(
        shards,
        mesh=mesh,
        in_specs=placed,
        out_specs=(
            P(None, "seq", "head"),
            P(None, "seq", "head"),
            P(None, "seq", "head"),
            P(None, "seq", "head", None),
            P(None, "seq", "head"),
        ),
        check_vma=False,
    )
```

```python
import functools
import math

import jax
import jax.numpy as jnp
from jax import lax
from jax.experimental import pallas as pl
from jax.experimental.pallas import tpu as pltpu
from jax.sharding import PartitionSpec as P

D = 2048
HEAD_DIM = 128
MHEAD_DIM = 64
STATE = 64
D_INNER = 4096
SCALE = 1.0 / math.sqrt(HEAD_DIM)
EXP2_SCALE = SCALE * math.log2(math.e)
DEAD = -1e30
GROUPS = 2
VMEM_BYTES = 56 * 1024 * 1024


def ring_order(count):
    y_count = max(1, count // 4)
    z_count = count // y_count
    order = []
    for y in range(y_count):
        turn = range(z_count) if y % 2 == 0 else range(z_count - 1, -1, -1)
        order += [z * y_count + y for z in turn]
    return order


def ring_step(block, order, distance):
    count = len(order)
    route = [(order[i], order[(i + distance) % count]) for i in range(count)]
    return lax.ppermute(block, "seq", route)


class Ring:
    def __init__(self, block, order, first_row=0):
        self.order = order
        self.steps = len(order) // 2
        self.done = 0
        self.first_row = first_row
        self.block = self.ahead = self.back = block
        self.pieces = [(0, first_row, block)]

    def step(self, clock):
        self.done += 1
        half = self.block.shape[0] // 2
        last = self.done == self.steps
        ahead = self.ahead[:half] if last else self.ahead
        back = self.back[half:] if last else self.back
        ahead, back = clock.hold(ahead, back)
        self.ahead = ring_step(ahead, self.order, 1)
        self.back = ring_step(back, self.order, -1)
        at = self.first_row
        if last:
            self.pieces += [(self.steps, at, self.ahead), (self.steps, at + half, self.back)]
        else:
            self.pieces += [(self.done, at, self.ahead), (-self.done, at, self.back)]
        return [self.ahead, self.back]


class Clock:
    def __init__(self):
        self.fence = ()
        self.late = ()

    def hold(self, *values):
        held = lax.optimization_barrier(tuple(values) + self.fence)[: len(values)]
        return held[0] if len(values) == 1 else held

    def turn(self, ring=None, work=None):
        moved = tuple(ring.step(self)) if ring is not None else ()
        done, deferred = work() if work is not None else ((), ())
        self.fence = self.late + tuple(done)
        self.late = moved + tuple(deferred)


def butterfly(value, axis, count, combine):
    bit = 1
    while bit < count:
        value = combine(value, lax.ppermute(value, axis, [(i, i ^ bit) for i in range(count)]))
        bit *= 2
    return value


def ring_sum(parts, order):
    far = len(order) // 2
    half = parts[0].shape[0] // 2
    add = lambda a, b: (a.astype(jnp.float32) + b.astype(jnp.float32)).astype(jnp.bfloat16)
    ahead = ring_step(parts[far][:half], order, 1)
    back = ring_step(parts[far][half:], order, -1)
    top, bottom = parts[far - 1], parts[1 - far]
    ahead = jnp.concatenate([add(ahead, top[:half]), top[half:]], axis=0)
    back = jnp.concatenate([bottom[:half], add(back, bottom[half:])], axis=0)
    for step in range(far - 1, 0, -1):
        ahead = ring_step(ahead, order, 1)
        back = ring_step(back, order, -1)
        if step > 1:
            ahead = add(ahead, parts[step - 1])
            back = add(back, parts[1 - step])
    return (
        ahead.astype(jnp.float32) + back.astype(jnp.float32) + parts[0].astype(jnp.float32)
    )


def project_kernel(count, turned, places_ref, *refs):
    input_refs, weight_refs = refs[:count], refs[count : 2 * count]
    cosine_ref, sine_ref, *base_ref, out_ref = refs[2 * count :]
    total = base_ref[0][...] if base_ref else None
    for input_ref, weight_ref in zip(input_refs, weight_refs):
        term = jnp.dot(input_ref[...], weight_ref[...], preferred_element_type=jnp.float32)
        total = term if total is None else total + term
    if not turned:
        out_ref[...] = total.astype(out_ref.dtype)
        return
    cosine = cosine_ref[...]
    sine = sine_ref[...]
    for head in range(out_ref.shape[1] // HEAD_DIM):
        at = slice(head * HEAD_DIM, (head + 1) * HEAD_DIM)
        part = total[:, at]
        rolled = pltpu.roll(part, HEAD_DIM // 2, 1)
        out_ref[:, at] = (part * cosine + rolled * sine).astype(out_ref.dtype)


def project(places, offsets, rows, value, pieces, cosine, sine, turned, base=(), kind=jnp.bfloat16):
    tokens = value.shape[0]
    width = pieces[0][2].shape[1]
    block = min(width, 256)
    input_specs, weight_specs = [], []
    for offset, row, piece in pieces:
        depth = piece.shape[0]

        def place(j, places_ref, slot=offsets.index(offset), scale=rows // depth, at=row // depth):
            return (0, places_ref[slot] * scale + at)

        input_specs.append(pl.BlockSpec((tokens, depth), place))
        weight_specs.append(pl.BlockSpec((depth, block), lambda j, *_: (0, j)))
    angle = pl.BlockSpec((tokens, HEAD_DIM), lambda j, *_: (0, 0))
    return pl.pallas_call(
        functools.partial(project_kernel, len(pieces), turned),
        grid_spec=pltpu.PrefetchScalarGridSpec(
            num_scalar_prefetch=1,
            grid=(width // block,),
            in_specs=input_specs
            + weight_specs
            + [angle, angle]
            + [pl.BlockSpec((tokens, block), lambda j, *_: (0, j))] * len(base),
            out_specs=pl.BlockSpec((tokens, block), lambda j, *_: (0, j)),
        ),
        out_shape=jax.ShapeDtypeStruct((tokens, width), kind),
        compiler_params=pltpu.CompilerParams(vmem_limit_bytes=VMEM_BYTES),
        cost_estimate=pl.CostEstimate(
            flops=2 * tokens * sum(piece.shape[0] for _, _, piece in pieces) * width,
            bytes_accessed=2 * (tokens + width) * value.shape[1],
            transcendentals=0,
        ),
        name="project",
    )(places, *[value] * len(pieces), *[piece for _, _, piece in pieces], cosine, sine, *base)


def silu(value):
    return value / (1.0 + jnp.exp(-value))


def exact_dot(a, b):
    return jnp.dot(a, b, precision=lax.Precision.HIGHEST, preferred_element_type=jnp.float32)


def spread(heads, block):
    shape = (heads, heads * block)
    column = lax.broadcasted_iota(jnp.int32, shape, 1) // block
    return (column == lax.broadcasted_iota(jnp.int32, shape, 0)).astype(jnp.float32)


def enter_kernel(input_ref, gain_ref, bc_ref, dt_ref, bias_ref, weight_ref, act_ref, map_ref, size_ref, normed_ref):
    @pl.when(pl.program_id(0) == 0)
    def _():
        rows = input_ref.shape[0]
        chunk = min(rows, 64)
        for start in range(0, rows, chunk):
            at = slice(start, start + chunk)
            hidden = input_ref[at, :].astype(jnp.float32)
            scale = lax.rsqrt(jnp.mean(hidden * hidden, axis=-1, keepdims=True) + 1e-05)
            normed_ref[at, :] = (hidden * scale * gain_ref[...]).astype(jnp.bfloat16)
        normed = normed_ref[...]
        map_ref[...] = jnp.dot(normed, bc_ref[...], preferred_element_type=jnp.float32)
        size = jnp.dot(normed, dt_ref[...], preferred_element_type=jnp.float32) + bias_ref[...]
        size_ref[...] = jnp.maximum(size, 0.0) + jnp.log1p(jnp.exp(-jnp.abs(size)))

    act_ref[...] = silu(
        jnp.dot(normed_ref[...], weight_ref[...], preferred_element_type=jnp.float32)
    )


def enter_mixer(flat_input, norm_gain, w_bc, w_dt, dt_bias, weight):
    tokens = flat_input.shape[0]
    width = weight.shape[1]
    block = min(width, 512)
    heads = w_dt.shape[1]
    whole = lambda *shape: pl.BlockSpec(shape, lambda j: (0, 0))
    return pl.pallas_call(
        enter_kernel,
        grid=(width // block,),
        in_specs=[
            whole(tokens, D),
            whole(1, D),
            whole(D, 2 * STATE),
            whole(D, heads),
            whole(1, heads),
            pl.BlockSpec((D, block), lambda j: (0, j)),
        ],
        out_specs=[
            pl.BlockSpec((tokens, block), lambda j: (0, j)),
            whole(tokens, 2 * STATE),
            whole(tokens, heads),
        ],
        out_shape=[
            jax.ShapeDtypeStruct((tokens, width), jnp.float32),
            jax.ShapeDtypeStruct((tokens, 2 * STATE), jnp.float32),
            jax.ShapeDtypeStruct((tokens, heads), jnp.float32),
        ],
        scratch_shapes=[pltpu.VMEM((tokens, D), jnp.bfloat16)],
        compiler_params=pltpu.CompilerParams(vmem_limit_bytes=VMEM_BYTES),
        cost_estimate=pl.CostEstimate(
            flops=2 * tokens * D * width,
            bytes_accessed=2 * D * (width + tokens) + 4 * tokens * width,
            transcendentals=tokens * width,
        ),
        name="enter_mixer",
    )(flat_input, norm_gain.reshape(1, D), w_bc, w_dt, dt_bias.reshape(1, heads), weight)


def inside_kernel(inner_ref, map_ref, decay_ref, size_ref, decay_row_ref, size_row_ref, skip_ref, read_ref, local_ref, through_ref):
    tokens, heads = decay_ref.shape[1:]
    inner = inner_ref[...]
    input_map = map_ref[:, :STATE]
    output_map = map_ref[:, STATE:]
    decay = decay_ref[0]
    by_head = spread(heads, MHEAD_DIM)
    wide = (tokens, heads * tokens)
    contact = dot_nt(
        output_map.astype(jnp.bfloat16),
        jnp.concatenate([input_map.astype(jnp.bfloat16)] * heads, axis=0),
    )
    source = lax.rem(lax.broadcasted_iota(jnp.int32, wide, 1), tokens)
    causal = source <= lax.broadcasted_iota(jnp.int32, wide, 0)
    difference = exact_dot(decay, spread(heads, tokens)) - decay_row_ref[0]
    mixing = jnp.exp(jnp.where(causal, difference, DEAD)) * contact * size_row_ref[0]
    mixing = mixing.astype(jnp.bfloat16)
    inner_low = inner.astype(jnp.bfloat16)
    together = min(heads, 256 // MHEAD_DIM)
    shape = (together * tokens, together * MHEAD_DIM)
    own = (
        lax.broadcasted_iota(jnp.int32, shape, 0) // tokens
        == lax.broadcasted_iota(jnp.int32, shape, 1) // MHEAD_DIM
    )
    for begin in range(0, heads, together):
        at = slice(begin * MHEAD_DIM, (begin + together) * MHEAD_DIM)
        stacked = jnp.concatenate([inner_low[:, at]] * together, axis=0)
        stacked = jnp.where(own, stacked, jnp.zeros_like(stacked))
        read_ref[:, at] = (
            jnp.dot(
                mixing[:, begin * tokens : (begin + together) * tokens],
                stacked,
                preferred_element_type=jnp.float32,
            )
            + skip_ref[:, at] * inner[:, at]
        )
    last = decay[tokens - 1 :, :]
    tail = exact_dot(jnp.exp(last - decay) * size_ref[0], by_head)
    local_ref[0] = dot_tn(input_map.astype(jnp.bfloat16), (inner * tail).astype(jnp.bfloat16))
    through_ref[0] = exact_dot(jnp.exp(jnp.broadcast_to(last, (8, heads))), by_head)[:1]


def inside_block(requests, act, maps, decay, size, decay_row, size_row, skip):
    tokens, heads = decay.shape[1:]
    inner = act.shape[1] // 2
    one = lambda *shape: pl.BlockSpec((1,) + shape, lambda r: (r, 0, 0))
    return pl.pallas_call(
        inside_kernel,
        grid=(requests,),
        in_specs=[
            pl.BlockSpec((tokens, inner), lambda r: (r, 1)),
            pl.BlockSpec((tokens, 2 * STATE), lambda r: (r, 0)),
            one(tokens, heads),
            one(tokens, heads),
            one(1, heads * tokens),
            one(1, heads * tokens),
            pl.BlockSpec((1, inner), lambda r: (0, 0)),
        ],
        out_specs=[
            pl.BlockSpec((tokens, inner), lambda r: (r, 0)),
            one(STATE, inner),
            one(1, inner),
        ],
        out_shape=[
            jax.ShapeDtypeStruct((requests * tokens, inner), jnp.float32),
            jax.ShapeDtypeStruct((requests, STATE, inner), jnp.float32),
            jax.ShapeDtypeStruct((requests, 1, inner), jnp.float32),
        ],
        compiler_params=pltpu.CompilerParams(vmem_limit_bytes=VMEM_BYTES),
        cost_estimate=pl.CostEstimate(
            flops=12 * requests * tokens * tokens * inner,
            bytes_accessed=16 * requests * tokens * inner,
            transcendentals=requests * tokens * tokens * heads,
        ),
        name="inside_block",
    )(act, maps, decay, size, decay_row, size_row, skip)


def leave_kernel(entry_ref, map_ref, decay_ref, read_ref, gate_ref, gain_ref, local_ref, through_ref, gated_ref, square_ref, chain_ref):
    heads = decay_ref.shape[2]
    entry = entry_ref[0]
    grown = exact_dot(jnp.exp(decay_ref[0]), spread(heads, MHEAD_DIM))
    inter = jnp.dot(
        map_ref[:, STATE:].astype(jnp.bfloat16),
        entry.astype(jnp.bfloat16),
        preferred_element_type=jnp.float32,
    )
    mixed = (read_ref[...] + inter * grown) * gate_ref[...]
    squares = jnp.sum(mixed * mixed, axis=1, keepdims=True)
    square_ref[...] = jnp.broadcast_to(squares, square_ref.shape)
    gated_ref[...] = (mixed * gain_ref[...]).astype(jnp.bfloat16)
    chain_ref[0] = through_ref[0] * entry + local_ref[0]


def leave_mixer(entry, maps, decay, read, act, gain, local, through):
    requests, tokens, heads = decay.shape
    inner = read.shape[1]
    one = lambda *shape: pl.BlockSpec((1,) + shape, lambda r: (r, 0, 0))
    flat = lambda width: pl.BlockSpec((tokens, width), lambda r: (r, 0))
    return pl.pallas_call(
        leave_kernel,
        grid=(requests,),
        in_specs=[
            one(STATE, inner),
            flat(2 * STATE),
            one(tokens, heads),
            flat(inner),
            flat(inner),
            pl.BlockSpec((1, inner), lambda r: (0, 0)),
            one(STATE, inner),
            one(1, inner),
        ],
        out_specs=[flat(inner), flat(128), one(STATE, inner)],
        out_shape=[
            jax.ShapeDtypeStruct((requests * tokens, inner), jnp.bfloat16),
            jax.ShapeDtypeStruct((requests * tokens, 128), jnp.float32),
            jax.ShapeDtypeStruct((requests, STATE, inner), jnp.float32),
        ],
        compiler_params=pltpu.CompilerParams(vmem_limit_bytes=VMEM_BYTES),
        cost_estimate=pl.CostEstimate(
            flops=2 * requests * tokens * STATE * inner,
            bytes_accessed=24 * requests * tokens * inner,
            transcendentals=requests * tokens * heads,
        ),
        name="leave_mixer",
    )(entry, maps, decay, read, act, gain, local, through)


def dot_nt(a, b):
    return lax.dot_general(a, b, (((1,), (1,)), ((), ())), preferred_element_type=jnp.float32)


def dot_tn(a, b):
    return lax.dot_general(a, b, (((0,), (0,)), ((), ())), preferred_element_type=jnp.float32)


def group_scores(first, key, query):
    scores = dot_nt(key, query)
    shape = scores.shape
    live = first + lax.broadcasted_iota(jnp.int32, shape, 0) <= lax.broadcasted_iota(
        jnp.int32, shape, 1
    )
    return jnp.where(live, scores, DEAD)


def cache_kernel(slots, first_ref, place_ref, live_ref, *refs):
    query_refs = refs[:slots]
    key_ref, value_ref, group_ref, joined_ref, out_ref, peak_ref, total_ref = refs[slots:]
    tok_block = query_refs[0].shape[1]
    keys, width = key_ref.shape[1:]
    tokens = tok_block * slots
    for slot in range(slots):
        start = pl.multiple_of(place_ref[slot] * tok_block, tok_block)
        joined_ref[0, pl.ds(start, tok_block), :] = query_refs[slot][0]
    live = live_ref[pl.program_id(0)]
    bias = jnp.where(
        lax.broadcasted_iota(jnp.int32, (keys, 128), 0) < live, 0.0, DEAD
    ).astype(jnp.float32)
    bias = jnp.concatenate([bias] * (tokens // 128), axis=1)
    for head in range(width // HEAD_DIM):
        at = slice(head * HEAD_DIM, (head + 1) * HEAD_DIM)
        query = joined_ref[0, :, at]
        scores = dot_nt(key_ref[0, :, at], query) + bias
        peak = jnp.maximum(
            jnp.max(scores, axis=0, keepdims=True),
            jnp.max(
                group_scores(first_ref[0], group_ref[0, :, at], query), axis=0, keepdims=True
            ),
        )
        weights = jnp.exp2((scores - peak) * EXP2_SCALE)
        total_ref[0, head : head + 1, :] = jnp.sum(weights, axis=0, keepdims=True)
        peak_ref[0, head : head + 1, :] = peak
        out_ref[0, at, :] = dot_tn(value_ref[0, :, at], weights.astype(jnp.bfloat16)).astype(
            out_ref.dtype
        )


def cache_part(begin, first, places, live, query_slots, keys, values, new_keys):
    slots = len(query_slots)
    requests, tok_block, width = query_slots[0].shape
    tokens = tok_block * slots
    cache_block = keys.shape[1]
    heads = width // HEAD_DIM
    one = lambda rows, start: pl.BlockSpec((1, rows, width), lambda r, *_: (r + start, 0, 0))
    stat = pl.BlockSpec((1, heads, tokens), lambda r, *_: (r, 0, 0))
    return pl.pallas_call(
        functools.partial(cache_kernel, slots),
        grid_spec=pltpu.PrefetchScalarGridSpec(
            num_scalar_prefetch=3,
            grid=(requests,),
            in_specs=[one(tok_block, 0)] * slots
            + [one(cache_block, begin)] * 2
            + [one(tok_block, begin)],
            out_specs=[
                one(tokens, 0),
                pl.BlockSpec((1, width, tokens), lambda r, *_: (r, 0, 0)),
                stat,
                stat,
            ],
        ),
        out_shape=[
            jax.ShapeDtypeStruct((requests, tokens, width), jnp.bfloat16),
            jax.ShapeDtypeStruct((requests, width, tokens), jnp.bfloat16),
            jax.ShapeDtypeStruct((requests, heads, tokens), jnp.float32),
            jax.ShapeDtypeStruct((requests, heads, tokens), jnp.float32),
        ],
        compiler_params=pltpu.CompilerParams(vmem_limit_bytes=VMEM_BYTES),
        cost_estimate=pl.CostEstimate(
            flops=4 * requests * tokens * cache_block * width,
            bytes_accessed=2 * requests * width * (3 * tokens + 2 * cache_block),
            transcendentals=requests * tokens * cache_block * heads,
        ),
        name="cache_part",
    )(first, places, live, *query_slots, keys, values, new_keys)


def finish_kernel(slots, first_ref, place_ref, *refs):
    query_ref, key_ref, value_ref, cache_ref, peak_ref, total_ref, best_ref = refs[:7]
    sum_ref, *part_refs = refs[7:-1]
    joined_ref = refs[-1]
    tok_block = key_ref.shape[1]
    for head in range(query_ref.shape[2] // HEAD_DIM):
        at = slice(head * HEAD_DIM, (head + 1) * HEAD_DIM)
        row = slice(head, head + 1)
        scores = group_scores(first_ref[0], key_ref[0, :, at], query_ref[0, :, at])
        best = best_ref[0, row, :]
        weights = jnp.exp2((scores - best) * EXP2_SCALE)
        rescale = jnp.exp2((peak_ref[0, row, :] - best) * EXP2_SCALE)
        sum_ref[0, row, :] = total_ref[0, row, :] * rescale + jnp.sum(
            weights, axis=0, keepdims=True
        )
        joined = cache_ref[0, at, :].astype(jnp.float32) * rescale + dot_tn(
            value_ref[0, :, at], weights.astype(jnp.bfloat16)
        )
        joined_ref[:, at] = joined.astype(jnp.bfloat16).T
    for slot in range(slots):
        start = pl.multiple_of(place_ref[slot] * tok_block, tok_block)
        part_refs[slot][0] = joined_ref[pl.ds(start, tok_block), :]


def finish_part(begin, first, places, queries, new_keys, new_values, cached, peaks, totals, best):
    requests, tokens, width = queries.shape
    tok_block = new_keys.shape[1]
    slots = tokens // tok_block
    heads = width // HEAD_DIM
    one = lambda rows, start: pl.BlockSpec((1, rows, width), lambda r, *_: (r + start, 0, 0))
    stat = lambda start: pl.BlockSpec((1, heads, tokens), lambda r, *_: (r + start, 0, 0))
    return pl.pallas_call(
        functools.partial(finish_kernel, slots),
        grid_spec=pltpu.PrefetchScalarGridSpec(
            num_scalar_prefetch=2,
            grid=(requests,),
            in_specs=[
                one(tokens, 0),
                one(tok_block, begin),
                one(tok_block, begin),
                pl.BlockSpec((1, width, tokens), lambda r, *_: (r, 0, 0)),
                stat(0),
                stat(0),
                stat(begin),
            ],
            out_specs=[stat(0)] + [one(tok_block, 0)] * slots,
            scratch_shapes=[pltpu.VMEM((tokens, width), jnp.bfloat16)],
        ),
        out_shape=[jax.ShapeDtypeStruct((requests, heads, tokens), jnp.float32)]
        + [jax.ShapeDtypeStruct((requests, tok_block, width), jnp.bfloat16)] * slots,
        compiler_params=pltpu.CompilerParams(vmem_limit_bytes=VMEM_BYTES),
        cost_estimate=pl.CostEstimate(
            flops=4 * requests * tokens * tok_block * width,
            bytes_accessed=6 * requests * width * tokens,
            transcendentals=requests * tokens * tok_block * heads,
        ),
        name="finish_part",
    )(first, places, queries, new_keys, new_values, cached, peaks, totals, best)


def head_sum(terms, head_count, head_index):
    if head_count != 4:
        return lax.psum_scatter(
            terms.astype(jnp.bfloat16), "head", scatter_dimension=1, tiled=True
        ).astype(jnp.float32)
    width = terms.shape[1] // 4
    chunk = lambda index: lax.dynamic_slice_in_dim(terms, index * width, width, 1)
    core, column = head_index % 2, head_index // 2
    near, far = 2 * column, 2 * (1 - column)
    got = lax.ppermute(
        jnp.concatenate([chunk(near + 1 - core), chunk(far + 1 - core)], axis=1).astype(
            jnp.bfloat16
        ),
        "head",
        [(h, h ^ 1) for h in range(4)],
    ).astype(jnp.float32)
    keep = chunk(near + core) + got[:, :width]
    give = chunk(far + core) + got[:, width:]
    return keep + lax.ppermute(
        give.astype(jnp.bfloat16), "head", [(h, h ^ 2) for h in range(4)]
    ).astype(jnp.float32)


class Relay:
    def __init__(self, through, local, initial, seq_index, seq_count):
        self.factor, self.local = through, local
        self.paired = seq_count == 8
        self.hop = 0
        if not self.paired:
            self.hops = seq_count - 1
            self.entry = jnp.where(seq_index == 0, initial, 0.0)
            return
        self.hops = 3
        self.swap = [(i, i ^ 1) for i in range(8)]
        self.is_first = is_first = seq_index % 2 == 0
        half = local.shape[2] // 2
        side = lambda value: jnp.where(is_first, value[..., :half], value[..., half:])
        mine = side(local)
        got = self.exchange(jnp.where(is_first, local[..., half:], local[..., :half]))
        other_factor = side(lax.ppermute(through, "seq", self.swap))
        factor = side(through)
        self.first_state = jnp.where(is_first, mine, got)
        second_state = jnp.where(is_first, got, mine)
        self.first_factor = jnp.where(is_first, factor, other_factor)
        second_factor = jnp.where(is_first, other_factor, factor)
        self.pair_state = second_factor * self.first_state + second_state
        self.pair_factor = self.first_factor * second_factor
        self.entry = jnp.where(seq_index < 2, side(initial), 0.0)

    def exchange(self, value):
        return lax.ppermute(value.astype(jnp.bfloat16), "seq", self.swap).astype(jnp.float32)

    def advance(self, clock):
        if self.hop == self.hops:
            return
        factor, state = (
            (self.pair_factor, self.pair_state) if self.paired else (self.factor, self.local)
        )
        entry = clock.hold(self.entry)
        leaving = (factor * entry + state).astype(jnp.bfloat16)
        if self.paired:
            route = [(2 * self.hop + y, 2 * self.hop + 2 + y) for y in range(2)]
        else:
            route = [(self.hop, self.hop + 1)]
        self.hop += 1
        self.entry = entry + lax.ppermute(leaving, "seq", route).astype(jnp.float32)

    def result(self, clock):
        while self.hop < self.hops:
            self.advance(clock)
        entry = clock.hold(self.entry)
        if not self.paired:
            return entry
        second = self.first_factor * entry + self.first_state
        got = self.exchange(jnp.where(self.is_first, second, entry))
        mine = jnp.where(self.is_first, entry, second)
        return jnp.concatenate(
            [jnp.where(self.is_first, mine, got), jnp.where(self.is_first, got, mine)], axis=2
        )


def shards(
    block_input,
    lengths,
    cache_keys,
    cache_values,
    w_query,
    w_key,
    w_value,
    w_attn_out,
    norm_gain,
    w_in,
    w_bc,
    w_dt,
    dt_bias,
    a_log,
    d_skip,
    gated_gain,
    w_out,
    ssm_init,
):
    requests, tok_block, _ = block_input.shape
    seq_count = lax.axis_size("seq")
    seq_index = lax.axis_index("seq")
    head_count = lax.axis_size("head")
    head_index = lax.axis_index("head")
    local_att = w_query.shape[1]
    local_heads = local_att // HEAD_DIM
    cache_block = cache_keys.shape[1]
    rows = w_query.shape[0]
    tokens = requests * tok_block
    flat_input = block_input.reshape(tokens, block_input.shape[2])

    order = ring_order(seq_count)
    half = seq_count // 2
    offsets = [0] + [sign * step for step in range(1, half) for sign in (1, -1)] + [half]
    places = jnp.asarray(
        [
            [order[(order.index(i) - offset) % seq_count] for offset in offsets]
            for i in range(seq_count)
        ],
        jnp.int32,
    )[seq_index]

    positions = (
        lengths[:, None] + seq_index * tok_block + jnp.arange(tok_block, dtype=jnp.int32)[None, :]
    ).reshape(tokens)
    half_dim = HEAD_DIM // 2
    frequency = jnp.exp(
        jnp.arange(half_dim, dtype=jnp.float32) * (-2.0 * math.log(10000.0) / HEAD_DIM)
    )
    angles = positions.astype(jnp.float32)[:, None] * frequency
    cosine = jnp.cos(angles)
    sine = jnp.sin(angles)
    cosine = jnp.concatenate([cosine, cosine], axis=1)
    sine = jnp.concatenate([-sine, sine], axis=1)

    clock = Clock()
    group = requests // GROUPS
    local_inner = w_in.shape[2]
    local_mheads = local_inner // MHEAD_DIM
    local_width = D // head_count
    made = {}

    def product(pieces, turned, base=(), kind=jnp.bfloat16):
        pieces = list(pieces)
        if pieces[-1][2].shape[0] < 128:
            (offset, row, upper), (_, _, lower) = pieces[-2:]
            pieces[-2:] = [(offset, row, jnp.concatenate([upper, lower], axis=0))]
        return project(
            places, offsets, rows, flat_input, pieces, cosine, sine, turned, base, kind
        )

    by_request = lambda value: value.reshape(requests, tok_block, local_att)

    def order_weight():
        made["w_in"] = w_in.reshape(D, 2 * local_inner)
        return (made["w_in"],), ()

    def enter():
        made["act"], made["maps"], size = enter_mixer(
            clock.hold(flat_input), norm_gain, w_bc, w_dt, dt_bias, made["w_in"]
        )
        size = size.reshape(requests, tok_block, local_mheads)
        log_decay = -size * jnp.exp(a_log)
        causal = jnp.arange(tok_block)[None, :] <= jnp.arange(tok_block)[:, None]
        decay = jnp.einsum(
            "tu,ruh->rth", causal.astype(jnp.float32), log_decay, precision=lax.Precision.HIGHEST
        )
        by_row = lambda value: jnp.transpose(value, (0, 2, 1)).reshape(
            requests, 1, local_mheads * tok_block
        )
        made["size"], made["decay"] = size, decay
        made["size_row"], made["decay_row"] = by_row(size), by_row(decay)
        return (made["act"], made["size_row"], made["decay_row"]), ()

    def inside():
        made["read"], made["local"], made["through"] = inside_block(
            requests,
            clock.hold(made["act"]),
            made["maps"],
            made["decay"],
            made["size"],
            made["decay_row"],
            made["size_row"],
            jnp.repeat(d_skip, MHEAD_DIM).reshape(1, local_inner),
        )
        return (made["read"], made["local"]), ()

    def initial_state():
        first_state = clock.hold(ssm_init).reshape(requests, local_mheads, MHEAD_DIM, STATE)
        made["initial"] = jnp.transpose(first_state, (0, 3, 1, 2)).reshape(
            requests, STATE, local_inner
        )
        return (made["initial"],), ()

    def start_relay():
        made["relay"] = relay = Relay(
            made["through"], clock.hold(made["local"]), made["initial"], seq_index, seq_count
        )
        return (), ((relay.pair_state,) if relay.paired else ())

    def hop():
        made["relay"].advance(clock)
        return (), (made["relay"].entry,)

    def end_relay():
        made["entry"] = made["relay"].result(clock)
        return (), (made["entry"],)

    def leave():
        gated, squares, chain = leave_mixer(
            clock.hold(made["entry"]),
            made["maps"],
            made["decay"],
            made["read"],
            made["act"],
            gated_gain.reshape(1, local_inner),
            made["local"],
            made["through"],
        )
        made["gated"] = gated
        made["squares"] = butterfly(
            squares[:, :1].reshape(1, tokens), "head", head_count, jnp.add
        )
        made["chain"] = chain
        return (gated,), (made["squares"],)

    def leave_terms():
        made["terms"] = jnp.dot(
            clock.hold(made["gated"]), w_out, preferred_element_type=jnp.float32
        ) * lax.rsqrt(made["squares"].reshape(tokens, 1) / D_INNER + 1e-05)
        return (made["terms"],), ()

    def leave_chain():
        chain = clock.hold(made["chain"]).reshape(requests, STATE, local_mheads, MHEAD_DIM)
        made["chain"] = jnp.transpose(chain, (0, 2, 3, 1)).reshape(
            requests, 1, local_mheads, MHEAD_DIM * STATE
        )
        return (made["chain"],), ()

    query_ring, key_ring, value_ring = (Ring(w, order) for w in (w_query, w_key, w_value))
    slot_rings = []
    live = jnp.clip(lengths - seq_index * cache_block, 0, cache_block).astype(jnp.int32)
    first = (seq_index * tok_block).astype(jnp.int32).reshape(1)
    cached = []

    def make_queries():
        queries = by_request(product(query_ring.pieces, True))
        slot_rings.extend(
            Ring(queries[begin : begin + group], order) for begin in range(0, requests, group)
        )
        return (queries,), ()

    def make_keys():
        made["keys"] = by_request(product(key_ring.pieces, True))
        return (made["keys"],), ()

    def meet_cache(index):
        def work():
            ring = slot_rings[index]
            begin = index * group
            slots = [piece for _, _, piece in ring.pieces[:-2]]
            slots.append(jnp.concatenate([ring.pieces[-2][2], ring.pieces[-1][2]], axis=0))
            slots[0] = clock.hold(slots[0])
            cached.append(
                cache_part(
                    begin,
                    first,
                    places,
                    live[begin : begin + group],
                    slots,
                    cache_keys,
                    cache_values,
                    made["keys"],
                )
            )
            return tuple(cached[-1]), ()

        return work

    def join_peaks():
        peaks = jnp.concatenate([clock.hold(part[2]) for part in cached], axis=0)
        made["best"] = butterfly(peaks, "seq", seq_count, jnp.maximum)
        return leave_chain()[0], (made["best"],)

    def make_values():
        made["values"] = product(
            [(0, 0, clock.hold(value_ring.block))] + value_ring.pieces[1:-2],
            False,
            kind=jnp.float32,
        )
        return (made["values"],), ()

    def steps(rings, begin, end):
        return [ring for _ in range(begin, end) for ring in rings]

    def run(sends, works):
        for index in range(max(len(sends), len(works))):
            clock.turn(
                sends[index] if index < len(sends) else None,
                works[index] if index < len(works) else None,
            )

    both = steps([query_ring, key_ring], 0, half - 2) + [query_ring] * 2 + [key_ring] * 2
    works = [order_weight, enter, inside, initial_state, start_relay, hop, hop]
    run(both, works + [None] * (len(both) - 1 - len(works)) + [make_queries])
    run(
        steps(slot_rings, 0, half),
        [hop, make_keys, end_relay, None, leave, None, leave_terms],
    )
    run(
        steps([value_ring], 0, half),
        [meet_cache(0), meet_cache(1)] + [None] * (half - 4) + [join_peaks, make_values],
    )

    new_keys = made["keys"]
    best = made["best"]
    new_values = by_request(product(value_ring.pieces[-2:], False, base=(made["values"],)))

    own = lambda stat: lax.dynamic_slice_in_dim(stat, seq_index * tok_block, tok_block, 2)
    greatest_logit = jnp.transpose(own(best), (0, 2, 1)) * SCALE
    residual = lax.dynamic_slice_in_dim(
        flat_input, head_index * local_width, local_width, 1
    ).astype(jnp.float32)
    mixed = []
    for index in range(GROUPS):
        begin = index * group
        joined, out, peaks, totals = cached[index]
        sums, *parts = finish_part(
            begin, first, places, joined, new_keys, new_values, out, peaks, totals, best
        )
        sums = butterfly(sums, "seq", seq_count, jnp.add)
        denominator = jnp.transpose(own(sums), (0, 2, 1))
        terms = {-offset: part for offset, part in zip(offsets, parts)}
        terms[half] = terms[-half]
        numerator = ring_sum(terms, order).reshape(group, tok_block, local_heads, HEAD_DIM)
        attended = (
            (numerator / denominator[..., None])
            .astype(jnp.bfloat16)
            .reshape(group * tok_block, local_att)
        )
        at = slice(begin * tok_block, (begin + group) * tok_block)
        attn_terms = jnp.dot(attended, w_attn_out, preferred_element_type=jnp.float32)
        summed = head_sum(attn_terms + made["terms"][at], head_count, head_index)
        mixed.append(
            (residual[at] + summed)
            .astype(jnp.bfloat16)
            .reshape(group, tok_block, local_width)
        )
    return (
        jnp.concatenate(mixed, axis=0),
        new_keys,
        new_values,
        made["chain"],
        greatest_logit,
    )


def solution(mesh):
    placed = (
        P(None, "seq", None),
        P(),
        P(None, "seq", "head"),
        P(None, "seq", "head"),
        P("seq", "head"),
        P("seq", "head"),
        P("seq", "head"),
        P("head", None),
        P(),
        P(None, None, "head"),
        P(),
        P(None, "head"),
        P("head"),
        P("head"),
        P("head"),
        P("head"),
        P("head", None),
        P(None, "head", None),
    )
    return jax.shard_map(
        shards,
        mesh=mesh,
        in_specs=placed,
        out_specs=(
            P(None, "seq", "head"),
            P(None, "seq", "head"),
            P(None, "seq", "head"),
            P(None, "seq", "head", None),
            P(None, "seq", "head"),
        ),
        check_vma=False,
    )
```

```python
import functools
import math

import jax
import jax.numpy as jnp
from jax import lax
from jax.experimental import pallas as pl
from jax.experimental.pallas import tpu as pltpu
from jax.sharding import PartitionSpec as P

D = 2048
HEAD_DIM = 128
MHEAD_DIM = 64
STATE = 64
D_INNER = 4096
SCALE = 1.0 / math.sqrt(HEAD_DIM)
EXP2_SCALE = SCALE * math.log2(math.e)
DEAD = -1e30
GROUPS = 2
VMEM_BYTES = 56 * 1024 * 1024


def ring_order(count):
    y_count = max(1, count // 4)
    z_count = count // y_count
    order = []
    for y in range(y_count):
        turn = range(z_count) if y % 2 == 0 else range(z_count - 1, -1, -1)
        order += [z * y_count + y for z in turn]
    return order


def ring_step(block, order, distance):
    count = len(order)
    route = [(order[i], order[(i + distance) % count]) for i in range(count)]
    return lax.ppermute(block, "seq", route)


class Ring:
    def __init__(self, block, order, first_row=0):
        self.order = order
        self.steps = len(order) // 2
        self.done = 0
        self.first_row = first_row
        self.block = self.ahead = self.back = block
        self.pieces = [(0, first_row, block)]

    def step(self, clock):
        self.done += 1
        half = self.block.shape[0] // 2
        last = self.done == self.steps
        ahead = self.ahead[:half] if last else self.ahead
        back = self.back[half:] if last else self.back
        ahead, back = clock.hold(ahead, back)
        self.ahead = ring_step(ahead, self.order, 1)
        self.back = ring_step(back, self.order, -1)
        at = self.first_row
        if last:
            self.pieces += [(self.steps, at, self.ahead), (self.steps, at + half, self.back)]
        else:
            self.pieces += [(self.done, at, self.ahead), (-self.done, at, self.back)]
        return [self.ahead, self.back]


class Clock:
    def __init__(self):
        self.fence = ()
        self.late = ()

    def hold(self, *values):
        held = lax.optimization_barrier(tuple(values) + self.fence)[: len(values)]
        return held[0] if len(values) == 1 else held

    def turn(self, ring=None, work=None):
        moved = tuple(ring.step(self)) if ring is not None else ()
        done, deferred = work() if work is not None else ((), ())
        self.fence = self.late + tuple(done)
        self.late = moved + tuple(deferred)


class Exchange:
    def __init__(self, value, axis, count, combine):
        self.value, self.axis, self.count, self.combine = value, axis, count, combine
        self.bit = 1

    def step(self):
        if self.bit < self.count:
            route = [(i, i ^ self.bit) for i in range(self.count)]
            got = lax.ppermute(self.value, self.axis, route)
            self.value = self.combine(self.value, got)
            self.bit *= 2
        return (self.value,)

    def result(self):
        while self.bit < self.count:
            self.step()
        return self.value


class RingSum:
    def __init__(self, parts, order):
        self.parts, self.order = parts, order
        self.left = len(order) // 2
        self.half = parts[0].shape[0] // 2
        self.ahead = self.back = None

    def add(self, a, b):
        return (a.astype(jnp.float32) + b.astype(jnp.float32)).astype(jnp.bfloat16)

    def step(self, clock):
        half, left, far = self.half, self.left, len(self.order) // 2
        top, bottom = self.parts[left], self.parts[-left]
        if left == far:
            ahead, back = top[:half], bottom[half:]
        elif left == far - 1:
            ahead = jnp.concatenate([self.add(self.ahead, top[:half]), top[half:]], axis=0)
            back = jnp.concatenate([bottom[:half], self.add(self.back, bottom[half:])], axis=0)
        else:
            ahead, back = self.add(self.ahead, top), self.add(self.back, bottom)
        ahead, back = clock.hold(ahead, back)
        self.ahead = ring_step(ahead, self.order, 1)
        self.back = ring_step(back, self.order, -1)
        self.left -= 1
        return [self.ahead, self.back]

    def total(self):
        return sum(value.astype(jnp.float32) for value in (self.ahead, self.back, self.parts[0]))


def project_kernel(count, turned, places_ref, *refs):
    input_refs, weight_refs = refs[:count], refs[count : 2 * count]
    cosine_ref, sine_ref, *base_ref, out_ref = refs[2 * count :]
    total = base_ref[0][...] if base_ref else None
    for input_ref, weight_ref in zip(input_refs, weight_refs):
        term = jnp.dot(input_ref[...], weight_ref[...], preferred_element_type=jnp.float32)
        total = term if total is None else total + term
    if not turned:
        out_ref[...] = total.astype(out_ref.dtype)
        return
    cosine = cosine_ref[...]
    sine = sine_ref[...]
    for head in range(out_ref.shape[1] // HEAD_DIM):
        at = slice(head * HEAD_DIM, (head + 1) * HEAD_DIM)
        part = total[:, at]
        rolled = pltpu.roll(part, HEAD_DIM // 2, 1)
        out_ref[:, at] = (part * cosine + rolled * sine).astype(out_ref.dtype)


def project(places, offsets, rows, value, pieces, cosine, sine, turned, base=(), kind=jnp.bfloat16):
    tokens = value.shape[0]
    width = pieces[0][2].shape[1]
    block = min(width, 256)
    input_specs, weight_specs = [], []
    for offset, row, piece in pieces:
        depth = piece.shape[0]

        def place(j, places_ref, slot=offsets.index(offset), scale=rows // depth, at=row // depth):
            return (0, places_ref[slot] * scale + at)

        input_specs.append(pl.BlockSpec((tokens, depth), place))
        weight_specs.append(pl.BlockSpec((depth, block), lambda j, *_: (0, j)))
    angle = pl.BlockSpec((tokens, HEAD_DIM), lambda j, *_: (0, 0))
    return pl.pallas_call(
        functools.partial(project_kernel, len(pieces), turned),
        grid_spec=pltpu.PrefetchScalarGridSpec(
            num_scalar_prefetch=1,
            grid=(width // block,),
            in_specs=input_specs
            + weight_specs
            + [angle, angle]
            + [pl.BlockSpec((tokens, block), lambda j, *_: (0, j))] * len(base),
            out_specs=pl.BlockSpec((tokens, block), lambda j, *_: (0, j)),
        ),
        out_shape=jax.ShapeDtypeStruct((tokens, width), kind),
        compiler_params=pltpu.CompilerParams(vmem_limit_bytes=VMEM_BYTES),
        cost_estimate=pl.CostEstimate(
            flops=2 * tokens * sum(piece.shape[0] for _, _, piece in pieces) * width,
            bytes_accessed=2 * (tokens + width) * value.shape[1],
            transcendentals=0,
        ),
        name="project",
    )(places, *[value] * len(pieces), *[piece for _, _, piece in pieces], cosine, sine, *base)


def silu(value):
    return value / (1.0 + jnp.exp(-value))


def exact_dot(a, b):
    return jnp.dot(a, b, precision=lax.Precision.HIGHEST, preferred_element_type=jnp.float32)


def spread(heads, block):
    shape = (heads, heads * block)
    column = lax.broadcasted_iota(jnp.int32, shape, 1) // block
    return (column == lax.broadcasted_iota(jnp.int32, shape, 0)).astype(jnp.float32)


def enter_kernel(input_ref, gain_ref, bc_ref, dt_ref, bias_ref, weight_ref, act_ref, map_ref, size_ref, normed_ref):
    @pl.when(pl.program_id(0) == 0)
    def _():
        rows = input_ref.shape[0]
        chunk = min(rows, 64)
        for start in range(0, rows, chunk):
            at = slice(start, start + chunk)
            hidden = input_ref[at, :].astype(jnp.float32)
            scale = lax.rsqrt(jnp.mean(hidden * hidden, axis=-1, keepdims=True) + 1e-05)
            normed_ref[at, :] = (hidden * scale * gain_ref[...]).astype(jnp.bfloat16)
        normed = normed_ref[...]
        map_ref[...] = jnp.dot(normed, bc_ref[...], preferred_element_type=jnp.float32)
        size = jnp.dot(normed, dt_ref[...], preferred_element_type=jnp.float32) + bias_ref[...]
        size_ref[...] = jnp.maximum(size, 0.0) + jnp.log1p(jnp.exp(-jnp.abs(size)))

    act_ref[...] = silu(
        jnp.dot(normed_ref[...], weight_ref[...], preferred_element_type=jnp.float32)
    )


def enter_mixer(flat_input, norm_gain, w_bc, w_dt, dt_bias, weight):
    tokens = flat_input.shape[0]
    width = weight.shape[1]
    block = min(width, 512)
    heads = w_dt.shape[1]
    whole = lambda *shape: pl.BlockSpec(shape, lambda j: (0, 0))
    return pl.pallas_call(
        enter_kernel,
        grid=(width // block,),
        in_specs=[
            whole(tokens, D),
            whole(1, D),
            whole(D, 2 * STATE),
            whole(D, heads),
            whole(1, heads),
            pl.BlockSpec((D, block), lambda j: (0, j)),
        ],
        out_specs=[
            pl.BlockSpec((tokens, block), lambda j: (0, j)),
            whole(tokens, 2 * STATE),
            whole(tokens, heads),
        ],
        out_shape=[
            jax.ShapeDtypeStruct((tokens, width), jnp.float32),
            jax.ShapeDtypeStruct((tokens, 2 * STATE), jnp.float32),
            jax.ShapeDtypeStruct((tokens, heads), jnp.float32),
        ],
        scratch_shapes=[pltpu.VMEM((tokens, D), jnp.bfloat16)],
        compiler_params=pltpu.CompilerParams(vmem_limit_bytes=VMEM_BYTES),
        cost_estimate=pl.CostEstimate(
            flops=2 * tokens * D * width,
            bytes_accessed=2 * D * (width + tokens) + 4 * tokens * width,
            transcendentals=tokens * width,
        ),
        name="enter_mixer",
    )(flat_input, norm_gain.reshape(1, D), w_bc, w_dt, dt_bias.reshape(1, heads), weight)


def inside_kernel(inner_ref, map_ref, decay_ref, size_ref, decay_row_ref, size_row_ref, skip_ref, read_ref, local_ref, through_ref):
    tokens, heads = decay_ref.shape[1:]
    inner = inner_ref[...]
    input_map = map_ref[:, :STATE]
    output_map = map_ref[:, STATE:]
    decay = decay_ref[0]
    by_head = spread(heads, MHEAD_DIM)
    wide = (tokens, heads * tokens)
    contact = dot_nt(
        output_map.astype(jnp.bfloat16),
        jnp.concatenate([input_map.astype(jnp.bfloat16)] * heads, axis=0),
    )
    source = lax.rem(lax.broadcasted_iota(jnp.int32, wide, 1), tokens)
    causal = source <= lax.broadcasted_iota(jnp.int32, wide, 0)
    difference = exact_dot(decay, spread(heads, tokens)) - decay_row_ref[0]
    mixing = jnp.exp(jnp.where(causal, difference, DEAD)) * contact * size_row_ref[0]
    mixing = mixing.astype(jnp.bfloat16)
    inner_low = inner.astype(jnp.bfloat16)
    together = min(heads, 256 // MHEAD_DIM)
    shape = (together * tokens, together * MHEAD_DIM)
    own = (
        lax.broadcasted_iota(jnp.int32, shape, 0) // tokens
        == lax.broadcasted_iota(jnp.int32, shape, 1) // MHEAD_DIM
    )
    for begin in range(0, heads, together):
        at = slice(begin * MHEAD_DIM, (begin + together) * MHEAD_DIM)
        stacked = jnp.concatenate([inner_low[:, at]] * together, axis=0)
        stacked = jnp.where(own, stacked, jnp.zeros_like(stacked))
        read_ref[:, at] = (
            jnp.dot(
                mixing[:, begin * tokens : (begin + together) * tokens],
                stacked,
                preferred_element_type=jnp.float32,
            )
            + skip_ref[:, at] * inner[:, at]
        )
    last = decay[tokens - 1 :, :]
    tail = exact_dot(jnp.exp(last - decay) * size_ref[0], by_head)
    local_ref[0] = dot_tn(input_map.astype(jnp.bfloat16), (inner * tail).astype(jnp.bfloat16))
    through_ref[0] = exact_dot(jnp.exp(jnp.broadcast_to(last, (8, heads))), by_head)[:1]


def inside_block(requests, act, maps, decay, size, decay_row, size_row, skip):
    tokens, heads = decay.shape[1:]
    inner = act.shape[1] // 2
    one = lambda *shape: pl.BlockSpec((1,) + shape, lambda r: (r, 0, 0))
    return pl.pallas_call(
        inside_kernel,
        grid=(requests,),
        in_specs=[
            pl.BlockSpec((tokens, inner), lambda r: (r, 1)),
            pl.BlockSpec((tokens, 2 * STATE), lambda r: (r, 0)),
            one(tokens, heads),
            one(tokens, heads),
            one(1, heads * tokens),
            one(1, heads * tokens),
            pl.BlockSpec((1, inner), lambda r: (0, 0)),
        ],
        out_specs=[
            pl.BlockSpec((tokens, inner), lambda r: (r, 0)),
            one(STATE, inner),
            one(1, inner),
        ],
        out_shape=[
            jax.ShapeDtypeStruct((requests * tokens, inner), jnp.float32),
            jax.ShapeDtypeStruct((requests, STATE, inner), jnp.float32),
            jax.ShapeDtypeStruct((requests, 1, inner), jnp.float32),
        ],
        compiler_params=pltpu.CompilerParams(vmem_limit_bytes=VMEM_BYTES),
        cost_estimate=pl.CostEstimate(
            flops=12 * requests * tokens * tokens * inner,
            bytes_accessed=16 * requests * tokens * inner,
            transcendentals=requests * tokens * tokens * heads,
        ),
        name="inside_block",
    )(act, maps, decay, size, decay_row, size_row, skip)


def leave_kernel(entry_ref, map_ref, decay_ref, read_ref, gate_ref, gain_ref, local_ref, through_ref, gated_ref, square_ref, chain_ref):
    heads = decay_ref.shape[2]
    entry = entry_ref[0]
    grown = exact_dot(jnp.exp(decay_ref[0]), spread(heads, MHEAD_DIM))
    inter = jnp.dot(
        map_ref[:, STATE:].astype(jnp.bfloat16),
        entry.astype(jnp.bfloat16),
        preferred_element_type=jnp.float32,
    )
    mixed = (read_ref[...] + inter * grown) * gate_ref[...]
    squares = jnp.sum(mixed * mixed, axis=1, keepdims=True)
    square_ref[...] = jnp.broadcast_to(squares, square_ref.shape)
    gated_ref[...] = (mixed * gain_ref[...]).astype(jnp.bfloat16)
    chain_ref[0] = through_ref[0] * entry + local_ref[0]


def leave_mixer(entry, maps, decay, read, act, gain, local, through):
    requests, tokens, heads = decay.shape
    inner = read.shape[1]
    one = lambda *shape: pl.BlockSpec((1,) + shape, lambda r: (r, 0, 0))
    flat = lambda width: pl.BlockSpec((tokens, width), lambda r: (r, 0))
    return pl.pallas_call(
        leave_kernel,
        grid=(requests,),
        in_specs=[
            one(STATE, inner),
            flat(2 * STATE),
            one(tokens, heads),
            flat(inner),
            flat(inner),
            pl.BlockSpec((1, inner), lambda r: (0, 0)),
            one(STATE, inner),
            one(1, inner),
        ],
        out_specs=[flat(inner), flat(128), one(STATE, inner)],
        out_shape=[
            jax.ShapeDtypeStruct((requests * tokens, inner), jnp.bfloat16),
            jax.ShapeDtypeStruct((requests * tokens, 128), jnp.float32),
            jax.ShapeDtypeStruct((requests, STATE, inner), jnp.float32),
        ],
        compiler_params=pltpu.CompilerParams(vmem_limit_bytes=VMEM_BYTES),
        cost_estimate=pl.CostEstimate(
            flops=2 * requests * tokens * STATE * inner,
            bytes_accessed=24 * requests * tokens * inner,
            transcendentals=requests * tokens * heads,
        ),
        name="leave_mixer",
    )(entry, maps, decay, read, act, gain, local, through)


def dot_nt(a, b):
    return lax.dot_general(a, b, (((1,), (1,)), ((), ())), preferred_element_type=jnp.float32)


def dot_tn(a, b):
    return lax.dot_general(a, b, (((0,), (0,)), ((), ())), preferred_element_type=jnp.float32)


def group_scores(first, key, query):
    scores = dot_nt(key, query)
    shape = scores.shape
    live = first + lax.broadcasted_iota(jnp.int32, shape, 0) <= lax.broadcasted_iota(
        jnp.int32, shape, 1
    )
    return jnp.where(live, scores, DEAD)


def cache_kernel(slots, first_ref, place_ref, live_ref, *refs):
    query_refs = refs[:slots]
    key_ref, value_ref, group_ref, joined_ref, out_ref, peak_ref, total_ref = refs[slots:]
    tok_block = query_refs[0].shape[1]
    keys, width = key_ref.shape[1:]
    tokens = tok_block * slots
    for slot in range(slots):
        start = pl.multiple_of(place_ref[slot] * tok_block, tok_block)
        joined_ref[0, pl.ds(start, tok_block), :] = query_refs[slot][0]
    live = live_ref[pl.program_id(0)]
    bias = jnp.where(
        lax.broadcasted_iota(jnp.int32, (keys, 128), 0) < live, 0.0, DEAD
    ).astype(jnp.float32)
    bias = jnp.concatenate([bias] * (tokens // 128), axis=1)
    for head in range(width // HEAD_DIM):
        at = slice(head * HEAD_DIM, (head + 1) * HEAD_DIM)
        query = joined_ref[0, :, at]
        scores = dot_nt(key_ref[0, :, at], query) + bias
        peak = jnp.maximum(
            jnp.max(scores, axis=0, keepdims=True),
            jnp.max(
                group_scores(first_ref[0], group_ref[0, :, at], query), axis=0, keepdims=True
            ),
        )
        weights = jnp.exp2((scores - peak) * EXP2_SCALE)
        total_ref[0, head : head + 1, :] = jnp.sum(weights, axis=0, keepdims=True)
        peak_ref[0, head : head + 1, :] = peak
        out_ref[0, at, :] = dot_tn(value_ref[0, :, at], weights.astype(jnp.bfloat16)).astype(
            out_ref.dtype
        )


def cache_part(begin, first, places, live, query_slots, keys, values, new_keys):
    slots = len(query_slots)
    requests, tok_block, width = query_slots[0].shape
    tokens = tok_block * slots
    cache_block = keys.shape[1]
    heads = width // HEAD_DIM
    one = lambda rows, start: pl.BlockSpec((1, rows, width), lambda r, *_: (r + start, 0, 0))
    stat = pl.BlockSpec((1, heads, tokens), lambda r, *_: (r, 0, 0))
    return pl.pallas_call(
        functools.partial(cache_kernel, slots),
        grid_spec=pltpu.PrefetchScalarGridSpec(
            num_scalar_prefetch=3,
            grid=(requests,),
            in_specs=[one(tok_block, 0)] * slots
            + [one(cache_block, begin)] * 2
            + [one(tok_block, begin)],
            out_specs=[
                one(tokens, 0),
                pl.BlockSpec((1, width, tokens), lambda r, *_: (r, 0, 0)),
                stat,
                stat,
            ],
        ),
        out_shape=[
            jax.ShapeDtypeStruct((requests, tokens, width), jnp.bfloat16),
            jax.ShapeDtypeStruct((requests, width, tokens), jnp.bfloat16),
            jax.ShapeDtypeStruct((requests, heads, tokens), jnp.float32),
            jax.ShapeDtypeStruct((requests, heads, tokens), jnp.float32),
        ],
        compiler_params=pltpu.CompilerParams(vmem_limit_bytes=VMEM_BYTES),
        cost_estimate=pl.CostEstimate(
            flops=4 * requests * tokens * cache_block * width,
            bytes_accessed=2 * requests * width * (3 * tokens + 2 * cache_block),
            transcendentals=requests * tokens * cache_block * heads,
        ),
        name="cache_part",
    )(first, places, live, *query_slots, keys, values, new_keys)


def finish_kernel(slots, first_ref, place_ref, *refs):
    query_ref, key_ref, value_ref, cache_ref, peak_ref, total_ref, best_ref = refs[:7]
    sum_ref, *part_refs = refs[7:-1]
    joined_ref = refs[-1]
    tok_block = key_ref.shape[1]
    for head in range(query_ref.shape[2] // HEAD_DIM):
        at = slice(head * HEAD_DIM, (head + 1) * HEAD_DIM)
        row = slice(head, head + 1)
        scores = group_scores(first_ref[0], key_ref[0, :, at], query_ref[0, :, at])
        best = best_ref[0, row, :]
        weights = jnp.exp2((scores - best) * EXP2_SCALE)
        rescale = jnp.exp2((peak_ref[0, row, :] - best) * EXP2_SCALE)
        sum_ref[0, row, :] = total_ref[0, row, :] * rescale + jnp.sum(
            weights, axis=0, keepdims=True
        )
        joined = cache_ref[0, at, :].astype(jnp.float32) * rescale + dot_tn(
            value_ref[0, :, at], weights.astype(jnp.bfloat16)
        )
        joined_ref[:, at] = joined.astype(jnp.bfloat16).T
    for slot in range(slots):
        start = pl.multiple_of(place_ref[slot] * tok_block, tok_block)
        part_refs[slot][0] = joined_ref[pl.ds(start, tok_block), :]


def finish_part(begin, first, places, queries, new_keys, new_values, cached, peaks, totals, best):
    requests, tokens, width = queries.shape
    tok_block = new_keys.shape[1]
    slots = tokens // tok_block
    heads = width // HEAD_DIM
    one = lambda rows, start: pl.BlockSpec((1, rows, width), lambda r, *_: (r + start, 0, 0))
    stat = lambda start: pl.BlockSpec((1, heads, tokens), lambda r, *_: (r + start, 0, 0))
    return pl.pallas_call(
        functools.partial(finish_kernel, slots),
        grid_spec=pltpu.PrefetchScalarGridSpec(
            num_scalar_prefetch=2,
            grid=(requests,),
            in_specs=[
                one(tokens, 0),
                one(tok_block, begin),
                one(tok_block, begin),
                pl.BlockSpec((1, width, tokens), lambda r, *_: (r, 0, 0)),
                stat(0),
                stat(0),
                stat(begin),
            ],
            out_specs=[stat(0)] + [one(tok_block, 0)] * slots,
            scratch_shapes=[pltpu.VMEM((tokens, width), jnp.bfloat16)],
        ),
        out_shape=[jax.ShapeDtypeStruct((requests, heads, tokens), jnp.float32)]
        + [jax.ShapeDtypeStruct((requests, tok_block, width), jnp.bfloat16)] * slots,
        compiler_params=pltpu.CompilerParams(vmem_limit_bytes=VMEM_BYTES),
        cost_estimate=pl.CostEstimate(
            flops=4 * requests * tokens * tok_block * width,
            bytes_accessed=6 * requests * width * tokens,
            transcendentals=requests * tokens * tok_block * heads,
        ),
        name="finish_part",
    )(first, places, queries, new_keys, new_values, cached, peaks, totals, best)


def head_sum(terms, head_count, head_index):
    if head_count != 4:
        return lax.psum_scatter(
            terms.astype(jnp.bfloat16), "head", scatter_dimension=1, tiled=True
        ).astype(jnp.float32)
    width = terms.shape[1] // 4
    chunk = lambda index: lax.dynamic_slice_in_dim(terms, index * width, width, 1)
    core, column = head_index % 2, head_index // 2
    near, far = 2 * column, 2 * (1 - column)
    got = lax.ppermute(
        jnp.concatenate([chunk(near + 1 - core), chunk(far + 1 - core)], axis=1).astype(
            jnp.bfloat16
        ),
        "head",
        [(h, h ^ 1) for h in range(4)],
    ).astype(jnp.float32)
    keep = chunk(near + core) + got[:, :width]
    give = chunk(far + core) + got[:, width:]
    return keep + lax.ppermute(
        give.astype(jnp.bfloat16), "head", [(h, h ^ 2) for h in range(4)]
    ).astype(jnp.float32)


class Relay:
    def __init__(self, through, local, initial, seq_index, seq_count):
        self.factor, self.local = through, local
        self.paired = seq_count == 8
        self.hop = 0
        if not self.paired:
            self.hops = seq_count - 1
            self.entry = jnp.where(seq_index == 0, initial, 0.0)
            return
        self.hops = 3
        self.swap = [(i, i ^ 1) for i in range(8)]
        self.is_first = is_first = seq_index % 2 == 0
        half = local.shape[2] // 2
        side = lambda value: jnp.where(is_first, value[..., :half], value[..., half:])
        mine = side(local)
        got = self.exchange(jnp.where(is_first, local[..., half:], local[..., :half]))
        other_factor = side(lax.ppermute(through, "seq", self.swap))
        factor = side(through)
        self.first_state = jnp.where(is_first, mine, got)
        second_state = jnp.where(is_first, got, mine)
        self.first_factor = jnp.where(is_first, factor, other_factor)
        second_factor = jnp.where(is_first, other_factor, factor)
        self.pair_state = second_factor * self.first_state + second_state
        self.pair_factor = self.first_factor * second_factor
        self.entry = jnp.where(seq_index < 2, side(initial), 0.0)

    def exchange(self, value):
        return lax.ppermute(value.astype(jnp.bfloat16), "seq", self.swap).astype(jnp.float32)

    def advance(self, clock):
        if self.hop == self.hops:
            return
        factor, state = (
            (self.pair_factor, self.pair_state) if self.paired else (self.factor, self.local)
        )
        entry = clock.hold(self.entry)
        leaving = (factor * entry + state).astype(jnp.bfloat16)
        if self.paired:
            route = [(2 * self.hop + y, 2 * self.hop + 2 + y) for y in range(2)]
        else:
            route = [(self.hop, self.hop + 1)]
        self.hop += 1
        self.entry = entry + lax.ppermute(leaving, "seq", route).astype(jnp.float32)

    def result(self, clock):
        while self.hop < self.hops:
            self.advance(clock)
        entry = clock.hold(self.entry)
        if not self.paired:
            return entry
        second = self.first_factor * entry + self.first_state
        got = self.exchange(jnp.where(self.is_first, second, entry))
        mine = jnp.where(self.is_first, entry, second)
        return jnp.concatenate(
            [jnp.where(self.is_first, mine, got), jnp.where(self.is_first, got, mine)], axis=2
        )


def shards(
    block_input,
    lengths,
    cache_keys,
    cache_values,
    w_query,
    w_key,
    w_value,
    w_attn_out,
    norm_gain,
    w_in,
    w_bc,
    w_dt,
    dt_bias,
    a_log,
    d_skip,
    gated_gain,
    w_out,
    ssm_init,
):
    requests, tok_block, _ = block_input.shape
    seq_count = lax.axis_size("seq")
    seq_index = lax.axis_index("seq")
    head_count = lax.axis_size("head")
    head_index = lax.axis_index("head")
    local_att = w_query.shape[1]
    local_heads = local_att // HEAD_DIM
    cache_block = cache_keys.shape[1]
    rows = w_query.shape[0]
    tokens = requests * tok_block
    flat_input = block_input.reshape(tokens, block_input.shape[2])

    order = ring_order(seq_count)
    half = seq_count // 2
    offsets = [0] + [sign * step for step in range(1, half) for sign in (1, -1)] + [half]
    places = jnp.asarray(
        [
            [order[(order.index(i) - offset) % seq_count] for offset in offsets]
            for i in range(seq_count)
        ],
        jnp.int32,
    )[seq_index]

    positions = (
        lengths[:, None] + seq_index * tok_block + jnp.arange(tok_block, dtype=jnp.int32)[None, :]
    ).reshape(tokens)
    half_dim = HEAD_DIM // 2
    frequency = jnp.exp(
        jnp.arange(half_dim, dtype=jnp.float32) * (-2.0 * math.log(10000.0) / HEAD_DIM)
    )
    angles = positions.astype(jnp.float32)[:, None] * frequency
    cosine = jnp.cos(angles)
    sine = jnp.sin(angles)
    cosine = jnp.concatenate([cosine, cosine], axis=1)
    sine = jnp.concatenate([-sine, sine], axis=1)

    clock = Clock()
    group = requests // GROUPS
    local_inner = w_in.shape[2]
    local_mheads = local_inner // MHEAD_DIM
    local_width = D // head_count
    made = {}

    def product(pieces, turned, base=(), kind=jnp.bfloat16):
        pieces = list(pieces)
        if pieces[-1][2].shape[0] < 128:
            (offset, row, upper), (_, _, lower) = pieces[-2:]
            pieces[-2:] = [(offset, row, jnp.concatenate([upper, lower], axis=0))]
        return project(
            places, offsets, rows, flat_input, pieces, cosine, sine, turned, base, kind
        )

    by_request = lambda value: value.reshape(requests, tok_block, local_att)

    def prepare():
        made["w_in"] = w_in.reshape(D, 2 * local_inner)
        first_state = ssm_init.reshape(requests, local_mheads, MHEAD_DIM, STATE)
        made["initial"] = jnp.transpose(first_state, (0, 3, 1, 2)).reshape(
            requests, STATE, local_inner
        )
        return (made["w_in"], made["initial"]), ()

    def enter():
        made["act"], made["maps"], size = enter_mixer(
            clock.hold(flat_input), norm_gain, w_bc, w_dt, dt_bias, made["w_in"]
        )
        size = size.reshape(requests, tok_block, local_mheads)
        log_decay = -size * jnp.exp(a_log)
        causal = jnp.arange(tok_block)[None, :] <= jnp.arange(tok_block)[:, None]
        decay = jnp.einsum(
            "tu,ruh->rth", causal.astype(jnp.float32), log_decay, precision=lax.Precision.HIGHEST
        )
        by_row = lambda value: jnp.transpose(value, (0, 2, 1)).reshape(
            requests, 1, local_mheads * tok_block
        )
        made["size"], made["decay"] = size, decay
        made["size_row"], made["decay_row"] = by_row(size), by_row(decay)
        return (made["act"], made["size_row"], made["decay_row"]), ()

    def inside():
        made["read"], made["local"], made["through"] = inside_block(
            requests,
            clock.hold(made["act"]),
            made["maps"],
            made["decay"],
            made["size"],
            made["decay_row"],
            made["size_row"],
            jnp.repeat(d_skip, MHEAD_DIM).reshape(1, local_inner),
        )
        return (made["read"], made["local"]), ()

    def start_relay():
        made["relay"] = relay = Relay(
            made["through"], clock.hold(made["local"]), made["initial"], seq_index, seq_count
        )
        return (), ((relay.pair_state,) if relay.paired else ())

    def hop():
        made["relay"].advance(clock)
        return (), (made["relay"].entry,)

    def end_relay():
        made["entry"] = made["relay"].result(clock)
        return (), (made["entry"],)

    def leave():
        gated, squares, chain = leave_mixer(
            clock.hold(made["entry"]),
            made["maps"],
            made["decay"],
            made["read"],
            made["act"],
            gated_gain.reshape(1, local_inner),
            made["local"],
            made["through"],
        )
        made["gated"] = gated
        made["squares"] = Exchange(
            squares[:, :1].reshape(1, tokens), "head", head_count, jnp.add
        ).result()
        made["chain"] = chain
        return (gated,), (made["squares"],)

    def leave_terms():
        made["terms"] = jnp.dot(
            clock.hold(made["gated"]), w_out, preferred_element_type=jnp.float32
        ) * lax.rsqrt(made["squares"].reshape(tokens, 1) / D_INNER + 1e-05)
        return (made["terms"],), ()

    def leave_chain():
        chain = clock.hold(made["chain"]).reshape(requests, STATE, local_mheads, MHEAD_DIM)
        made["chain"] = jnp.transpose(chain, (0, 2, 3, 1)).reshape(
            requests, 1, local_mheads, MHEAD_DIM * STATE
        )
        return (made["chain"],), ()

    query_ring, key_ring, value_ring = (Ring(w, order) for w in (w_query, w_key, w_value))
    slot_rings = []
    live = jnp.clip(lengths - seq_index * cache_block, 0, cache_block).astype(jnp.int32)
    first = (seq_index * tok_block).astype(jnp.int32).reshape(1)
    cached = []

    def make_queries():
        queries = by_request(product(query_ring.pieces, True))
        slot_rings.extend(
            Ring(queries[begin : begin + group], order) for begin in range(0, requests, group)
        )
        return (queries,), ()

    def make_keys():
        made["keys"] = by_request(product(key_ring.pieces, True))
        return (made["keys"],), ()

    def meet_cache(index):
        def work():
            ring = slot_rings[index]
            begin = index * group
            slots = [piece for _, _, piece in ring.pieces[:-2]]
            slots.append(jnp.concatenate([ring.pieces[-2][2], ring.pieces[-1][2]], axis=0))
            slots[0] = clock.hold(slots[0])
            cached.append(
                cache_part(
                    begin,
                    first,
                    places,
                    live[begin : begin + group],
                    slots,
                    cache_keys,
                    cache_values,
                    made["keys"],
                )
            )
            return tuple(cached[-1]), ()

        return work

    def join_peaks():
        peaks = jnp.concatenate([clock.hold(part[2]) for part in cached], axis=0)
        made["best"] = Exchange(peaks, "seq", seq_count, jnp.maximum)
        made["best"].step()
        return leave_chain()

    def make_values():
        made["best"].step()
        made["values"] = product(
            [(0, 0, clock.hold(value_ring.block))] + value_ring.pieces[1:-2],
            False,
            kind=jnp.float32,
        )
        return (made["values"],), ()

    def steps(rings, begin, end):
        return [ring for _ in range(begin, end) for ring in rings]

    def run(sends, works):
        for index in range(max(len(sends), len(works))):
            clock.turn(
                sends[index] if index < len(sends) else None,
                works[index] if index < len(works) else None,
            )

    both = steps([query_ring, key_ring], 0, half - 2) + [query_ring] * 2 + [key_ring] * 2
    works = [prepare, enter, inside, start_relay, hop, hop, hop]
    run(both, works + [None] * (len(both) - 1 - len(works)) + [make_queries])
    run(
        steps(slot_rings, 0, half),
        [end_relay, make_keys, leave, None, leave_terms],
    )
    run(
        steps([value_ring], 0, half),
        [meet_cache(0), meet_cache(1)] + [None] * (half - 4) + [join_peaks, make_values],
    )

    new_keys = made["keys"]
    best = made["best"].result()
    new_values = by_request(product(value_ring.pieces[-2:], False, base=(made["values"],)))

    own = lambda stat: lax.dynamic_slice_in_dim(stat, seq_index * tok_block, tok_block, 2)
    greatest_logit = jnp.transpose(own(best), (0, 2, 1)) * SCALE
    residual = lax.dynamic_slice_in_dim(
        flat_input, head_index * local_width, local_width, 1
    ).astype(jnp.float32)
    sums, ring_sums, mixed = [], [], []

    def finish(index):
        def work():
            joined, out, peaks, totals = cached[index]
            some_sums, *parts = finish_part(
                index * group,
                first,
                places,
                clock.hold(joined),
                new_keys,
                new_values,
                out,
                peaks,
                totals,
                best,
            )
            sums.append(some_sums)
            terms = {-offset: part for offset, part in zip(offsets, parts)}
            terms[half] = terms[-half]
            ring_sums.append(RingSum(terms, order))
            return (some_sums, *parts), ()

        return work

    def add_sums():
        if "sums" not in made:
            made["sums"] = Exchange(jnp.concatenate(sums, axis=0), "seq", seq_count, jnp.add)
        made["sums"].step()
        return (), ()

    run([], [finish(0)])
    run([ring_sums[0]], [finish(1)])
    run(steps(ring_sums[::-1], 0, half)[:-1], [add_sums, None, add_sums, None, add_sums])
    denominators = jnp.transpose(own(made["sums"].result()), (0, 2, 1))
    for index in range(GROUPS):
        begin = index * group
        denominator = denominators[begin : begin + group]
        numerator = ring_sums[index].total().reshape(group, tok_block, local_heads, HEAD_DIM)
        attended = (
            (numerator / denominator[..., None])
            .astype(jnp.bfloat16)
            .reshape(group * tok_block, local_att)
        )
        at = slice(begin * tok_block, (begin + group) * tok_block)
        attn_terms = jnp.dot(attended, w_attn_out, preferred_element_type=jnp.float32)
        summed = head_sum(attn_terms + made["terms"][at], head_count, head_index)
        mixed.append(
            (residual[at] + summed)
            .astype(jnp.bfloat16)
            .reshape(group, tok_block, local_width)
        )
    return (
        jnp.concatenate(mixed, axis=0),
        new_keys,
        new_values,
        made["chain"],
        greatest_logit,
    )


def solution(mesh):
    placed = (
        P(None, "seq", None),
        P(),
        P(None, "seq", "head"),
        P(None, "seq", "head"),
        P("seq", "head"),
        P("seq", "head"),
        P("seq", "head"),
        P("head", None),
        P(),
        P(None, None, "head"),
        P(),
        P(None, "head"),
        P("head"),
        P("head"),
        P("head"),
        P("head"),
        P("head", None),
        P(None, "head", None),
    )
    return jax.shard_map(
        shards,
        mesh=mesh,
        in_specs=placed,
        out_specs=(
            P(None, "seq", "head"),
            P(None, "seq", "head"),
            P(None, "seq", "head"),
            P(None, "seq", "head", None),
            P(None, "seq", "head"),
        ),
        check_vma=False,
    )
```

```python
import functools
import math

import jax
import jax.numpy as jnp
from jax import lax
from jax.experimental import pallas as pl
from jax.experimental.pallas import tpu as pltpu
from jax.sharding import PartitionSpec as P

D = 2048
HEAD_DIM = 128
MHEAD_DIM = 64
STATE = 64
D_INNER = 4096
SCALE = 1.0 / math.sqrt(HEAD_DIM)
EXP2_SCALE = SCALE * math.log2(math.e)
DEAD = -1e30
GROUPS = 2
VMEM_BYTES = 56 * 1024 * 1024


def ring_order(count):
    y_count = max(1, count // 4)
    z_count = count // y_count
    order = []
    for y in range(y_count):
        turn = range(z_count) if y % 2 == 0 else range(z_count - 1, -1, -1)
        order += [z * y_count + y for z in turn]
    return order


def ring_step(block, order, distance):
    count = len(order)
    route = [(order[i], order[(i + distance) % count]) for i in range(count)]
    return lax.ppermute(block, "seq", route)


class Ring:
    def __init__(self, block, order, first_row=0):
        self.order = order
        self.steps = len(order) // 2
        self.done = 0
        self.first_row = first_row
        self.block = self.ahead = self.back = block
        self.pieces = [(0, first_row, block)]

    def step(self, clock):
        self.done += 1
        half = self.block.shape[0] // 2
        last = self.done == self.steps
        ahead = self.ahead[:half] if last else self.ahead
        back = self.back[half:] if last else self.back
        ahead, back = clock.hold(ahead, back)
        self.ahead = ring_step(ahead, self.order, 1)
        self.back = ring_step(back, self.order, -1)
        at = self.first_row
        if last:
            self.pieces += [(self.steps, at, self.ahead), (self.steps, at + half, self.back)]
        else:
            self.pieces += [(self.done, at, self.ahead), (-self.done, at, self.back)]
        return [self.ahead, self.back]


class Clock:
    def __init__(self, mark):
        self.mark = mark
        self.late = ()

    def hold(self, *values):
        held = lax.optimization_barrier(tuple(values) + (self.mark,))[: len(values)]
        return held[0] if len(values) == 1 else held

    def turn(self, ring=None, work=None):
        moved = tuple(ring.step(self)) if ring is not None else ()
        done, deferred = work() if work is not None else ((), ())
        self.mark = lax.optimization_barrier((self.mark,) + self.late + tuple(done))[0]
        self.late = moved + tuple(deferred)


class Exchange:
    def __init__(self, value, axis, count, combine):
        self.value, self.axis, self.count, self.combine = value, axis, count, combine
        self.got = None
        self.bit = 1

    def join(self, clock):
        if self.got is not None:
            self.value = self.combine(*clock.hold(self.value, self.got))
            self.got = None

    def step(self, clock):
        self.join(clock)
        if self.bit < self.count:
            route = [(i, i ^ self.bit) for i in range(self.count)]
            self.got = lax.ppermute(self.value, self.axis, route)
            self.bit *= 2

    def result(self, clock):
        while self.bit < self.count:
            self.step(clock)
        self.join(clock)
        return self.value


class RingSum:
    def __init__(self, parts, order):
        self.parts, self.order = parts, order
        self.left = len(order) // 2
        self.half = parts[0].shape[0] // 2
        self.ahead = self.back = None

    def add(self, a, b):
        return (a.astype(jnp.float32) + b.astype(jnp.float32)).astype(jnp.bfloat16)

    def step(self, clock):
        half, left, far = self.half, self.left, len(self.order) // 2
        top, bottom = self.parts[left], self.parts[-left]
        if left == far:
            ahead, back = top[:half], bottom[half:]
        elif left == far - 1:
            ahead = jnp.concatenate([self.add(self.ahead, top[:half]), top[half:]], axis=0)
            back = jnp.concatenate([bottom[:half], self.add(self.back, bottom[half:])], axis=0)
        else:
            ahead, back = self.add(self.ahead, top), self.add(self.back, bottom)
        ahead, back = clock.hold(ahead, back)
        self.ahead = ring_step(ahead, self.order, 1)
        self.back = ring_step(back, self.order, -1)
        self.left -= 1
        return [self.ahead, self.back]

    def total(self):
        return sum(value.astype(jnp.float32) for value in (self.ahead, self.back, self.parts[0]))


def project_kernel(count, turned, places_ref, *refs):
    input_refs, weight_refs = refs[:count], refs[count : 2 * count]
    cosine_ref, sine_ref, *base_ref, out_ref = refs[2 * count :]
    total = base_ref[0][...] if base_ref else None
    for input_ref, weight_ref in zip(input_refs, weight_refs):
        term = jnp.dot(input_ref[...], weight_ref[...], preferred_element_type=jnp.float32)
        total = term if total is None else total + term
    if not turned:
        out_ref[...] = total.astype(out_ref.dtype)
        return
    cosine = cosine_ref[...]
    sine = sine_ref[...]
    for head in range(out_ref.shape[1] // HEAD_DIM):
        at = slice(head * HEAD_DIM, (head + 1) * HEAD_DIM)
        part = total[:, at]
        rolled = pltpu.roll(part, HEAD_DIM // 2, 1)
        out_ref[:, at] = (part * cosine + rolled * sine).astype(out_ref.dtype)


def project(places, offsets, rows, value, pieces, cosine, sine, turned, base=(), kind=jnp.bfloat16):
    tokens = value.shape[0]
    width = pieces[0][2].shape[1]
    block = min(width, 256)
    input_specs, weight_specs = [], []
    for offset, row, piece in pieces:
        depth = piece.shape[0]

        def place(j, places_ref, slot=offsets.index(offset), scale=rows // depth, at=row // depth):
            return (0, places_ref[slot] * scale + at)

        input_specs.append(pl.BlockSpec((tokens, depth), place))
        weight_specs.append(pl.BlockSpec((depth, block), lambda j, *_: (0, j)))
    angle = pl.BlockSpec((tokens, HEAD_DIM), lambda j, *_: (0, 0))
    return pl.pallas_call(
        functools.partial(project_kernel, len(pieces), turned),
        grid_spec=pltpu.PrefetchScalarGridSpec(
            num_scalar_prefetch=1,
            grid=(width // block,),
            in_specs=input_specs
            + weight_specs
            + [angle, angle]
            + [pl.BlockSpec((tokens, block), lambda j, *_: (0, j))] * len(base),
            out_specs=pl.BlockSpec((tokens, block), lambda j, *_: (0, j)),
        ),
        out_shape=jax.ShapeDtypeStruct((tokens, width), kind),
        compiler_params=pltpu.CompilerParams(vmem_limit_bytes=VMEM_BYTES),
        cost_estimate=pl.CostEstimate(
            flops=2 * tokens * sum(piece.shape[0] for _, _, piece in pieces) * width,
            bytes_accessed=2 * (tokens + width) * value.shape[1],
            transcendentals=0,
        ),
        name="project",
    )(places, *[value] * len(pieces), *[piece for _, _, piece in pieces], cosine, sine, *base)


def silu(value):
    return value / (1.0 + jnp.exp(-value))


def exact_dot(a, b):
    return jnp.dot(a, b, precision=lax.Precision.HIGHEST, preferred_element_type=jnp.float32)


def spread(heads, block):
    shape = (heads, heads * block)
    column = lax.broadcasted_iota(jnp.int32, shape, 1) // block
    return (column == lax.broadcasted_iota(jnp.int32, shape, 0)).astype(jnp.float32)


def enter_kernel(input_ref, gain_ref, bc_ref, dt_ref, bias_ref, weight_ref, act_ref, map_ref, size_ref, normed_ref):
    @pl.when(pl.program_id(0) == 0)
    def _():
        rows = input_ref.shape[0]
        chunk = min(rows, 64)
        for start in range(0, rows, chunk):
            at = slice(start, start + chunk)
            hidden = input_ref[at, :].astype(jnp.float32)
            scale = lax.rsqrt(jnp.mean(hidden * hidden, axis=-1, keepdims=True) + 1e-05)
            normed_ref[at, :] = (hidden * scale * gain_ref[...]).astype(jnp.bfloat16)
        normed = normed_ref[...]
        map_ref[...] = jnp.dot(normed, bc_ref[...], preferred_element_type=jnp.float32)
        size = jnp.dot(normed, dt_ref[...], preferred_element_type=jnp.float32) + bias_ref[...]
        size_ref[...] = jnp.maximum(size, 0.0) + jnp.log1p(jnp.exp(-jnp.abs(size)))

    act_ref[...] = silu(
        jnp.dot(normed_ref[...], weight_ref[...], preferred_element_type=jnp.float32)
    )


def enter_mixer(flat_input, norm_gain, w_bc, w_dt, dt_bias, weight):
    tokens = flat_input.shape[0]
    width = weight.shape[1]
    block = min(width, 512)
    heads = w_dt.shape[1]
    whole = lambda *shape: pl.BlockSpec(shape, lambda j: (0, 0))
    return pl.pallas_call(
        enter_kernel,
        grid=(width // block,),
        in_specs=[
            whole(tokens, D),
            whole(1, D),
            whole(D, 2 * STATE),
            whole(D, heads),
            whole(1, heads),
            pl.BlockSpec((D, block), lambda j: (0, j)),
        ],
        out_specs=[
            pl.BlockSpec((tokens, block), lambda j: (0, j)),
            whole(tokens, 2 * STATE),
            whole(tokens, heads),
        ],
        out_shape=[
            jax.ShapeDtypeStruct((tokens, width), jnp.float32),
            jax.ShapeDtypeStruct((tokens, 2 * STATE), jnp.float32),
            jax.ShapeDtypeStruct((tokens, heads), jnp.float32),
        ],
        scratch_shapes=[pltpu.VMEM((tokens, D), jnp.bfloat16)],
        compiler_params=pltpu.CompilerParams(vmem_limit_bytes=VMEM_BYTES),
        cost_estimate=pl.CostEstimate(
            flops=2 * tokens * D * width,
            bytes_accessed=2 * D * (width + tokens) + 4 * tokens * width,
            transcendentals=tokens * width,
        ),
        name="enter_mixer",
    )(flat_input, norm_gain.reshape(1, D), w_bc, w_dt, dt_bias.reshape(1, heads), weight)


def inside_kernel(inner_ref, map_ref, decay_ref, size_ref, decay_row_ref, size_row_ref, skip_ref, read_ref, local_ref, through_ref):
    tokens, heads = decay_ref.shape[1:]
    inner = inner_ref[...]
    input_map = map_ref[:, :STATE]
    output_map = map_ref[:, STATE:]
    decay = decay_ref[0]
    by_head = spread(heads, MHEAD_DIM)
    wide = (tokens, heads * tokens)
    contact = dot_nt(
        output_map.astype(jnp.bfloat16),
        jnp.concatenate([input_map.astype(jnp.bfloat16)] * heads, axis=0),
    )
    source = lax.rem(lax.broadcasted_iota(jnp.int32, wide, 1), tokens)
    causal = source <= lax.broadcasted_iota(jnp.int32, wide, 0)
    difference = exact_dot(decay, spread(heads, tokens)) - decay_row_ref[0]
    mixing = jnp.exp(jnp.where(causal, difference, DEAD)) * contact * size_row_ref[0]
    mixing = mixing.astype(jnp.bfloat16)
    inner_low = inner.astype(jnp.bfloat16)
    together = min(heads, 256 // MHEAD_DIM)
    shape = (together * tokens, together * MHEAD_DIM)
    own = (
        lax.broadcasted_iota(jnp.int32, shape, 0) // tokens
        == lax.broadcasted_iota(jnp.int32, shape, 1) // MHEAD_DIM
    )
    for begin in range(0, heads, together):
        at = slice(begin * MHEAD_DIM, (begin + together) * MHEAD_DIM)
        stacked = jnp.concatenate([inner_low[:, at]] * together, axis=0)
        stacked = jnp.where(own, stacked, jnp.zeros_like(stacked))
        read_ref[:, at] = (
            jnp.dot(
                mixing[:, begin * tokens : (begin + together) * tokens],
                stacked,
                preferred_element_type=jnp.float32,
            )
            + skip_ref[:, at] * inner[:, at]
        )
    last = decay[tokens - 1 :, :]
    tail = exact_dot(jnp.exp(last - decay) * size_ref[0], by_head)
    local_ref[0] = dot_tn(input_map.astype(jnp.bfloat16), (inner * tail).astype(jnp.bfloat16))
    through_ref[0] = exact_dot(jnp.exp(jnp.broadcast_to(last, (8, heads))), by_head)[:1]


def inside_block(requests, act, maps, decay, size, decay_row, size_row, skip):
    tokens, heads = decay.shape[1:]
    inner = act.shape[1] // 2
    one = lambda *shape: pl.BlockSpec((1,) + shape, lambda r: (r, 0, 0))
    return pl.pallas_call(
        inside_kernel,
        grid=(requests,),
        in_specs=[
            pl.BlockSpec((tokens, inner), lambda r: (r, 1)),
            pl.BlockSpec((tokens, 2 * STATE), lambda r: (r, 0)),
            one(tokens, heads),
            one(tokens, heads),
            one(1, heads * tokens),
            one(1, heads * tokens),
            pl.BlockSpec((1, inner), lambda r: (0, 0)),
        ],
        out_specs=[
            pl.BlockSpec((tokens, inner), lambda r: (r, 0)),
            one(STATE, inner),
            one(1, inner),
        ],
        out_shape=[
            jax.ShapeDtypeStruct((requests * tokens, inner), jnp.float32),
            jax.ShapeDtypeStruct((requests, STATE, inner), jnp.float32),
            jax.ShapeDtypeStruct((requests, 1, inner), jnp.float32),
        ],
        compiler_params=pltpu.CompilerParams(vmem_limit_bytes=VMEM_BYTES),
        cost_estimate=pl.CostEstimate(
            flops=12 * requests * tokens * tokens * inner,
            bytes_accessed=16 * requests * tokens * inner,
            transcendentals=requests * tokens * tokens * heads,
        ),
        name="inside_block",
    )(act, maps, decay, size, decay_row, size_row, skip)


def leave_kernel(entry_ref, map_ref, decay_ref, read_ref, gate_ref, gain_ref, local_ref, through_ref, gated_ref, square_ref, chain_ref):
    heads = decay_ref.shape[2]
    entry = entry_ref[0]
    grown = exact_dot(jnp.exp(decay_ref[0]), spread(heads, MHEAD_DIM))
    inter = jnp.dot(
        map_ref[:, STATE:].astype(jnp.bfloat16),
        entry.astype(jnp.bfloat16),
        preferred_element_type=jnp.float32,
    )
    mixed = (read_ref[...] + inter * grown) * gate_ref[...]
    squares = jnp.sum(mixed * mixed, axis=1, keepdims=True)
    square_ref[...] = jnp.broadcast_to(squares, square_ref.shape)
    gated_ref[...] = (mixed * gain_ref[...]).astype(jnp.bfloat16)
    chain_ref[0] = through_ref[0] * entry + local_ref[0]


def leave_mixer(entry, maps, decay, read, act, gain, local, through):
    requests, tokens, heads = decay.shape
    inner = read.shape[1]
    one = lambda *shape: pl.BlockSpec((1,) + shape, lambda r: (r, 0, 0))
    flat = lambda width: pl.BlockSpec((tokens, width), lambda r: (r, 0))
    return pl.pallas_call(
        leave_kernel,
        grid=(requests,),
        in_specs=[
            one(STATE, inner),
            flat(2 * STATE),
            one(tokens, heads),
            flat(inner),
            flat(inner),
            pl.BlockSpec((1, inner), lambda r: (0, 0)),
            one(STATE, inner),
            one(1, inner),
        ],
        out_specs=[flat(inner), flat(128), one(STATE, inner)],
        out_shape=[
            jax.ShapeDtypeStruct((requests * tokens, inner), jnp.bfloat16),
            jax.ShapeDtypeStruct((requests * tokens, 128), jnp.float32),
            jax.ShapeDtypeStruct((requests, STATE, inner), jnp.float32),
        ],
        compiler_params=pltpu.CompilerParams(vmem_limit_bytes=VMEM_BYTES),
        cost_estimate=pl.CostEstimate(
            flops=2 * requests * tokens * STATE * inner,
            bytes_accessed=24 * requests * tokens * inner,
            transcendentals=requests * tokens * heads,
        ),
        name="leave_mixer",
    )(entry, maps, decay, read, act, gain, local, through)


def dot_nt(a, b):
    return lax.dot_general(a, b, (((1,), (1,)), ((), ())), preferred_element_type=jnp.float32)


def dot_tn(a, b):
    return lax.dot_general(a, b, (((0,), (0,)), ((), ())), preferred_element_type=jnp.float32)


def group_scores(first, key, query):
    scores = dot_nt(key, query)
    shape = scores.shape
    live = first + lax.broadcasted_iota(jnp.int32, shape, 0) <= lax.broadcasted_iota(
        jnp.int32, shape, 1
    )
    return jnp.where(live, scores, DEAD)


def cache_kernel(slots, first_ref, place_ref, live_ref, *refs):
    query_refs = refs[:slots]
    key_ref, value_ref, group_ref, joined_ref, out_ref, peak_ref, total_ref = refs[slots:]
    tok_block = query_refs[0].shape[1]
    keys, width = key_ref.shape[1:]
    tokens = tok_block * slots
    for slot in range(slots):
        start = pl.multiple_of(place_ref[slot] * tok_block, tok_block)
        joined_ref[0, pl.ds(start, tok_block), :] = query_refs[slot][0]
    live = live_ref[pl.program_id(0)]
    bias = jnp.where(
        lax.broadcasted_iota(jnp.int32, (keys, 128), 0) < live, 0.0, DEAD
    ).astype(jnp.float32)
    bias = jnp.concatenate([bias] * (tokens // 128), axis=1)
    for head in range(width // HEAD_DIM):
        at = slice(head * HEAD_DIM, (head + 1) * HEAD_DIM)
        query = joined_ref[0, :, at]
        scores = dot_nt(key_ref[0, :, at], query) + bias
        peak = jnp.maximum(
            jnp.max(scores, axis=0, keepdims=True),
            jnp.max(
                group_scores(first_ref[0], group_ref[0, :, at], query), axis=0, keepdims=True
            ),
        )
        weights = jnp.exp2((scores - peak) * EXP2_SCALE)
        total_ref[0, head : head + 1, :] = jnp.sum(weights, axis=0, keepdims=True)
        peak_ref[0, head : head + 1, :] = peak
        out_ref[0, at, :] = dot_tn(value_ref[0, :, at], weights.astype(jnp.bfloat16)).astype(
            out_ref.dtype
        )


def cache_part(begin, first, places, live, query_slots, keys, values, new_keys):
    slots = len(query_slots)
    requests, tok_block, width = query_slots[0].shape
    tokens = tok_block * slots
    cache_block = keys.shape[1]
    heads = width // HEAD_DIM
    one = lambda rows, start: pl.BlockSpec((1, rows, width), lambda r, *_: (r + start, 0, 0))
    stat = pl.BlockSpec((1, heads, tokens), lambda r, *_: (r, 0, 0))
    return pl.pallas_call(
        functools.partial(cache_kernel, slots),
        grid_spec=pltpu.PrefetchScalarGridSpec(
            num_scalar_prefetch=3,
            grid=(requests,),
            in_specs=[one(tok_block, 0)] * slots
            + [one(cache_block, begin)] * 2
            + [one(tok_block, begin)],
            out_specs=[
                one(tokens, 0),
                pl.BlockSpec((1, width, tokens), lambda r, *_: (r, 0, 0)),
                stat,
                stat,
            ],
        ),
        out_shape=[
            jax.ShapeDtypeStruct((requests, tokens, width), jnp.bfloat16),
            jax.ShapeDtypeStruct((requests, width, tokens), jnp.bfloat16),
            jax.ShapeDtypeStruct((requests, heads, tokens), jnp.float32),
            jax.ShapeDtypeStruct((requests, heads, tokens), jnp.float32),
        ],
        compiler_params=pltpu.CompilerParams(vmem_limit_bytes=VMEM_BYTES),
        cost_estimate=pl.CostEstimate(
            flops=4 * requests * tokens * cache_block * width,
            bytes_accessed=2 * requests * width * (3 * tokens + 2 * cache_block),
            transcendentals=requests * tokens * cache_block * heads,
        ),
        name="cache_part",
    )(first, places, live, *query_slots, keys, values, new_keys)


def finish_kernel(slots, first_ref, place_ref, *refs):
    query_ref, key_ref, value_ref, cache_ref, peak_ref, total_ref, best_ref = refs[:7]
    sum_ref, *part_refs = refs[7:-1]
    joined_ref = refs[-1]
    tok_block = key_ref.shape[1]
    for head in range(query_ref.shape[2] // HEAD_DIM):
        at = slice(head * HEAD_DIM, (head + 1) * HEAD_DIM)
        row = slice(head, head + 1)
        scores = group_scores(first_ref[0], key_ref[0, :, at], query_ref[0, :, at])
        best = best_ref[0, row, :]
        weights = jnp.exp2((scores - best) * EXP2_SCALE)
        rescale = jnp.exp2((peak_ref[0, row, :] - best) * EXP2_SCALE)
        sum_ref[0, row, :] = total_ref[0, row, :] * rescale + jnp.sum(
            weights, axis=0, keepdims=True
        )
        joined = cache_ref[0, at, :].astype(jnp.float32) * rescale + dot_tn(
            value_ref[0, :, at], weights.astype(jnp.bfloat16)
        )
        joined_ref[:, at] = joined.astype(jnp.bfloat16).T
    for slot in range(slots):
        start = pl.multiple_of(place_ref[slot] * tok_block, tok_block)
        part_refs[slot][0] = joined_ref[pl.ds(start, tok_block), :]


def finish_part(begin, first, places, queries, new_keys, new_values, cached, peaks, totals, best):
    requests, tokens, width = queries.shape
    tok_block = new_keys.shape[1]
    slots = tokens // tok_block
    heads = width // HEAD_DIM
    one = lambda rows, start: pl.BlockSpec((1, rows, width), lambda r, *_: (r + start, 0, 0))
    stat = lambda start: pl.BlockSpec((1, heads, tokens), lambda r, *_: (r + start, 0, 0))
    return pl.pallas_call(
        functools.partial(finish_kernel, slots),
        grid_spec=pltpu.PrefetchScalarGridSpec(
            num_scalar_prefetch=2,
            grid=(requests,),
            in_specs=[
                one(tokens, 0),
                one(tok_block, begin),
                one(tok_block, begin),
                pl.BlockSpec((1, width, tokens), lambda r, *_: (r, 0, 0)),
                stat(0),
                stat(0),
                stat(begin),
            ],
            out_specs=[stat(0)] + [one(tok_block, 0)] * slots,
            scratch_shapes=[pltpu.VMEM((tokens, width), jnp.bfloat16)],
        ),
        out_shape=[jax.ShapeDtypeStruct((requests, heads, tokens), jnp.float32)]
        + [jax.ShapeDtypeStruct((requests, tok_block, width), jnp.bfloat16)] * slots,
        compiler_params=pltpu.CompilerParams(vmem_limit_bytes=VMEM_BYTES),
        cost_estimate=pl.CostEstimate(
            flops=4 * requests * tokens * tok_block * width,
            bytes_accessed=6 * requests * width * tokens,
            transcendentals=requests * tokens * tok_block * heads,
        ),
        name="finish_part",
    )(first, places, queries, new_keys, new_values, cached, peaks, totals, best)


def head_sum(terms, head_count, head_index):
    if head_count != 4:
        return lax.psum_scatter(
            terms.astype(jnp.bfloat16), "head", scatter_dimension=1, tiled=True
        ).astype(jnp.float32)
    width = terms.shape[1] // 4
    chunk = lambda index: lax.dynamic_slice_in_dim(terms, index * width, width, 1)
    core, column = head_index % 2, head_index // 2
    near, far = 2 * column, 2 * (1 - column)
    got = lax.ppermute(
        jnp.concatenate([chunk(near + 1 - core), chunk(far + 1 - core)], axis=1).astype(
            jnp.bfloat16
        ),
        "head",
        [(h, h ^ 1) for h in range(4)],
    ).astype(jnp.float32)
    keep = chunk(near + core) + got[:, :width]
    give = chunk(far + core) + got[:, width:]
    return keep + lax.ppermute(
        give.astype(jnp.bfloat16), "head", [(h, h ^ 2) for h in range(4)]
    ).astype(jnp.float32)


class Relay:
    def __init__(self, through, local, initial, seq_index, seq_count):
        self.factor, self.local = through, local
        self.paired = seq_count == 8
        self.hop = 0
        if not self.paired:
            self.hops = seq_count - 1
            self.entry = jnp.where(seq_index == 0, initial, 0.0)
            return
        self.hops = 3
        self.swap = [(i, i ^ 1) for i in range(8)]
        self.is_first = is_first = seq_index % 2 == 0
        half = local.shape[2] // 2
        side = lambda value: jnp.where(is_first, value[..., :half], value[..., half:])
        mine = side(local)
        got = self.exchange(jnp.where(is_first, local[..., half:], local[..., :half]))
        other_factor = side(lax.ppermute(through, "seq", self.swap))
        factor = side(through)
        self.first_state = jnp.where(is_first, mine, got)
        second_state = jnp.where(is_first, got, mine)
        self.first_factor = jnp.where(is_first, factor, other_factor)
        second_factor = jnp.where(is_first, other_factor, factor)
        self.pair_state = second_factor * self.first_state + second_state
        self.pair_factor = self.first_factor * second_factor
        self.entry = jnp.where(seq_index < 2, side(initial), 0.0)

    def exchange(self, value):
        return lax.ppermute(value.astype(jnp.bfloat16), "seq", self.swap).astype(jnp.float32)

    def advance(self, clock):
        if self.hop == self.hops:
            return
        factor, state = (
            (self.pair_factor, self.pair_state) if self.paired else (self.factor, self.local)
        )
        entry = clock.hold(self.entry)
        leaving = (factor * entry + state).astype(jnp.bfloat16)
        if self.paired:
            route = [(2 * self.hop + y, 2 * self.hop + 2 + y) for y in range(2)]
        else:
            route = [(self.hop, self.hop + 1)]
        self.hop += 1
        self.entry = entry + lax.ppermute(leaving, "seq", route).astype(jnp.float32)

    def result(self, clock):
        while self.hop < self.hops:
            self.advance(clock)
        entry = clock.hold(self.entry)
        if not self.paired:
            return entry
        second = self.first_factor * entry + self.first_state
        got = self.exchange(jnp.where(self.is_first, second, entry))
        mine = jnp.where(self.is_first, entry, second)
        return jnp.concatenate(
            [jnp.where(self.is_first, mine, got), jnp.where(self.is_first, got, mine)], axis=2
        )


def shards(
    block_input,
    lengths,
    cache_keys,
    cache_values,
    w_query,
    w_key,
    w_value,
    w_attn_out,
    norm_gain,
    w_in,
    w_bc,
    w_dt,
    dt_bias,
    a_log,
    d_skip,
    gated_gain,
    w_out,
    ssm_init,
):
    requests, tok_block, _ = block_input.shape
    seq_count = lax.axis_size("seq")
    seq_index = lax.axis_index("seq")
    head_count = lax.axis_size("head")
    head_index = lax.axis_index("head")
    local_att = w_query.shape[1]
    local_heads = local_att // HEAD_DIM
    cache_block = cache_keys.shape[1]
    rows = w_query.shape[0]
    tokens = requests * tok_block
    flat_input = block_input.reshape(tokens, block_input.shape[2])

    order = ring_order(seq_count)
    half = seq_count // 2
    offsets = [0] + [sign * step for step in range(1, half) for sign in (1, -1)] + [half]
    places = jnp.asarray(
        [
            [order[(order.index(i) - offset) % seq_count] for offset in offsets]
            for i in range(seq_count)
        ],
        jnp.int32,
    )[seq_index]

    positions = (
        lengths[:, None] + seq_index * tok_block + jnp.arange(tok_block, dtype=jnp.int32)[None, :]
    ).reshape(tokens)
    half_dim = HEAD_DIM // 2
    frequency = jnp.exp(
        jnp.arange(half_dim, dtype=jnp.float32) * (-2.0 * math.log(10000.0) / HEAD_DIM)
    )
    angles = positions.astype(jnp.float32)[:, None] * frequency
    cosine = jnp.cos(angles)
    sine = jnp.sin(angles)
    cosine = jnp.concatenate([cosine, cosine], axis=1)
    sine = jnp.concatenate([-sine, sine], axis=1)

    clock = Clock(jnp.zeros((1,), jnp.int32) + lengths[:1])
    group = requests // GROUPS
    local_inner = w_in.shape[2]
    local_mheads = local_inner // MHEAD_DIM
    local_width = D // head_count
    made = {}

    def product(pieces, turned, base=(), kind=jnp.bfloat16):
        pieces = list(pieces)
        if pieces[-1][2].shape[0] < 128:
            (offset, row, upper), (_, _, lower) = pieces[-2:]
            pieces[-2:] = [(offset, row, jnp.concatenate([upper, lower], axis=0))]
        return project(
            places, offsets, rows, flat_input, pieces, cosine, sine, turned, base, kind
        )

    by_request = lambda value: value.reshape(requests, tok_block, local_att)

    def prepare():
        made["w_in"] = w_in.reshape(D, 2 * local_inner)
        first_state = ssm_init.reshape(requests, local_mheads, MHEAD_DIM, STATE)
        made["initial"] = jnp.transpose(first_state, (0, 3, 1, 2)).reshape(
            requests, STATE, local_inner
        )
        return (made["w_in"], made["initial"]), ()

    def enter():
        made["act"], made["maps"], size = enter_mixer(
            clock.hold(flat_input), norm_gain, w_bc, w_dt, dt_bias, made["w_in"]
        )
        size = size.reshape(requests, tok_block, local_mheads)
        log_decay = -size * jnp.exp(a_log)
        causal = jnp.arange(tok_block)[None, :] <= jnp.arange(tok_block)[:, None]
        decay = jnp.einsum(
            "tu,ruh->rth", causal.astype(jnp.float32), log_decay, precision=lax.Precision.HIGHEST
        )
        by_row = lambda value: jnp.transpose(value, (0, 2, 1)).reshape(
            requests, 1, local_mheads * tok_block
        )
        made["size"], made["decay"] = size, decay
        made["size_row"], made["decay_row"] = by_row(size), by_row(decay)
        return (made["act"], made["size_row"], made["decay_row"]), ()

    def inside():
        made["read"], made["local"], made["through"] = inside_block(
            requests,
            clock.hold(made["act"]),
            made["maps"],
            made["decay"],
            made["size"],
            made["decay_row"],
            made["size_row"],
            jnp.repeat(d_skip, MHEAD_DIM).reshape(1, local_inner),
        )
        return (made["read"], made["local"]), ()

    def start_relay():
        made["relay"] = relay = Relay(
            made["through"], clock.hold(made["local"]), made["initial"], seq_index, seq_count
        )
        return (), ((relay.pair_state,) if relay.paired else ())

    def hop():
        made["relay"].advance(clock)
        return (), (made["relay"].entry,)

    def end_relay():
        made["entry"] = made["relay"].result(clock)
        return (), (made["entry"],)

    def leave():
        gated, squares, chain = leave_mixer(
            clock.hold(made["entry"]),
            made["maps"],
            made["decay"],
            made["read"],
            made["act"],
            gated_gain.reshape(1, local_inner),
            made["local"],
            made["through"],
        )
        made["gated"] = gated
        made["squares"] = Exchange(
            squares[:, :1].reshape(1, tokens), "head", head_count, jnp.add
        )
        made["squares"].step(clock)
        made["chain"] = chain
        return (gated,), ()

    def join_squares():
        made["squares"].step(clock)
        return (), ()

    def leave_terms():
        squares = made["squares"].result(clock).reshape(tokens, 1)
        made["terms"] = jnp.dot(
            clock.hold(made["gated"]), w_out, preferred_element_type=jnp.float32
        ) * lax.rsqrt(squares / D_INNER + 1e-05)
        return (made["terms"],), ()

    def leave_chain():
        chain = clock.hold(made["chain"]).reshape(requests, STATE, local_mheads, MHEAD_DIM)
        made["chain"] = jnp.transpose(chain, (0, 2, 3, 1)).reshape(
            requests, 1, local_mheads, MHEAD_DIM * STATE
        )
        return (made["chain"],), ()

    query_ring, key_ring, value_ring = (Ring(w, order) for w in (w_query, w_key, w_value))
    slot_rings = []
    live = jnp.clip(lengths - seq_index * cache_block, 0, cache_block).astype(jnp.int32)
    first = (seq_index * tok_block).astype(jnp.int32).reshape(1)
    cached = []

    def make_queries():
        queries = by_request(product(query_ring.pieces, True))
        slot_rings.extend(
            Ring(queries[begin : begin + group], order) for begin in range(0, requests, group)
        )
        return (queries,), ()

    def make_keys():
        made["keys"] = by_request(product(key_ring.pieces, True))
        return (made["keys"],), ()

    def meet_cache(index):
        def work():
            ring = slot_rings[index]
            begin = index * group
            slots = [piece for _, _, piece in ring.pieces[:-2]]
            slots.append(jnp.concatenate([ring.pieces[-2][2], ring.pieces[-1][2]], axis=0))
            slots[0] = clock.hold(slots[0])
            cached.append(
                cache_part(
                    begin,
                    first,
                    places,
                    live[begin : begin + group],
                    slots,
                    cache_keys,
                    cache_values,
                    made["keys"],
                )
            )
            return tuple(cached[-1]), ()

        return work

    def join_peaks():
        peaks = jnp.concatenate([clock.hold(part[2]) for part in cached], axis=0)
        made["best"] = Exchange(peaks, "seq", seq_count, jnp.maximum)
        made["best"].step(clock)
        return leave_chain()

    def make_values():
        made["best"].step(clock)
        made["values"] = product(
            [(0, 0, clock.hold(value_ring.block))] + value_ring.pieces[1:-2],
            False,
            kind=jnp.float32,
        )
        return (made["values"],), ()

    def steps(rings, begin, end):
        return [ring for _ in range(begin, end) for ring in rings]

    def run(sends, works):
        for index in range(max(len(sends), len(works))):
            clock.turn(
                sends[index] if index < len(sends) else None,
                works[index] if index < len(works) else None,
            )

    both = steps([query_ring, key_ring], 0, half - 2) + [query_ring] * 2 + [key_ring] * 2
    def make_queries_hop():
        done, _ = make_queries()
        return done, hop()[1]

    def make_keys_hop():
        deferred = hop()[1]
        return make_keys()[0], deferred

    works = [prepare, enter, inside, start_relay, None, hop]
    run(both, works + [None] * (len(both) - 1 - len(works)) + [make_queries_hop])
    run(
        steps(slot_rings, 0, half),
        [None, make_keys_hop, None, end_relay, None, leave, join_squares, leave_terms],
    )
    run(
        steps([value_ring], 0, half),
        [meet_cache(0), meet_cache(1)] + [None] * (half - 4) + [join_peaks, make_values],
    )

    new_keys = made["keys"]
    best = made["best"].result(clock)
    new_values = by_request(product(value_ring.pieces[-2:], False, base=(made["values"],)))

    own = lambda stat: lax.dynamic_slice_in_dim(stat, seq_index * tok_block, tok_block, 2)
    greatest_logit = jnp.transpose(own(best), (0, 2, 1)) * SCALE
    residual = lax.dynamic_slice_in_dim(
        flat_input, head_index * local_width, local_width, 1
    ).astype(jnp.float32)
    sums, ring_sums, mixed = [], [], []

    def finish(index):
        def work():
            joined, out, peaks, totals = cached[index]
            some_sums, *parts = finish_part(
                index * group,
                first,
                places,
                clock.hold(joined),
                new_keys,
                new_values,
                out,
                peaks,
                totals,
                best,
            )
            sums.append(some_sums)
            terms = {-offset: part for offset, part in zip(offsets, parts)}
            terms[half] = terms[-half]
            ring_sums.append(RingSum(terms, order))
            return (some_sums, *parts), ()

        return work

    def add_sums():
        if "sums" not in made:
            made["sums"] = Exchange(jnp.concatenate(sums, axis=0), "seq", seq_count, jnp.add)
        made["sums"].step(clock)
        return (), ()

    run([], [finish(0)])
    run([ring_sums[0]], [finish(1)])
    run(steps(ring_sums[::-1], 0, half)[:-1], [add_sums, None, add_sums, None, add_sums])
    denominators = jnp.transpose(own(made["sums"].result(clock)), (0, 2, 1))
    for index in range(GROUPS):
        begin = index * group
        denominator = denominators[begin : begin + group]
        numerator = ring_sums[index].total().reshape(group, tok_block, local_heads, HEAD_DIM)
        attended = (
            (numerator / denominator[..., None])
            .astype(jnp.bfloat16)
            .reshape(group * tok_block, local_att)
        )
        at = slice(begin * tok_block, (begin + group) * tok_block)
        attn_terms = jnp.dot(attended, w_attn_out, preferred_element_type=jnp.float32)
        summed = head_sum(attn_terms + made["terms"][at], head_count, head_index)
        mixed.append(
            (residual[at] + summed)
            .astype(jnp.bfloat16)
            .reshape(group, tok_block, local_width)
        )
    return (
        jnp.concatenate(mixed, axis=0),
        new_keys,
        new_values,
        made["chain"],
        greatest_logit,
    )


def solution(mesh):
    placed = (
        P(None, "seq", None),
        P(),
        P(None, "seq", "head"),
        P(None, "seq", "head"),
        P("seq", "head"),
        P("seq", "head"),
        P("seq", "head"),
        P("head", None),
        P(),
        P(None, None, "head"),
        P(),
        P(None, "head"),
        P("head"),
        P("head"),
        P("head"),
        P("head"),
        P("head", None),
        P(None, "head", None),
    )
    return jax.shard_map(
        shards,
        mesh=mesh,
        in_specs=placed,
        out_specs=(
            P(None, "seq", "head"),
            P(None, "seq", "head"),
            P(None, "seq", "head"),
            P(None, "seq", "head", None),
            P(None, "seq", "head"),
        ),
        check_vma=False,
    )
```

```python
import functools
import math

import jax
import jax.numpy as jnp
from jax import lax
from jax.experimental import pallas as pl
from jax.experimental.pallas import tpu as pltpu
from jax.sharding import PartitionSpec as P

D = 2048
HEAD_DIM = 128
MHEAD_DIM = 64
STATE = 64
D_INNER = 4096
SCALE = 1.0 / math.sqrt(HEAD_DIM)
EXP2_SCALE = SCALE * math.log2(math.e)
DEAD = -1e30
GROUPS = 2
VMEM_BYTES = 56 * 1024 * 1024
LIGHT = pl.CostEstimate(flops=0, bytes_accessed=0, transcendentals=0)


def ring_order(count):
    y_count = max(1, count // 4)
    z_count = count // y_count
    order = []
    for y in range(y_count):
        turn = range(z_count) if y % 2 == 0 else range(z_count - 1, -1, -1)
        order += [z * y_count + y for z in turn]
    return order


def ring_step(block, order, distance):
    count = len(order)
    route = [(order[i], order[(i + distance) % count]) for i in range(count)]
    return lax.ppermute(block, "seq", route)


class Ring:
    def __init__(self, block, order, first_row=0):
        self.order = order
        self.steps = len(order) // 2
        self.done = 0
        self.first_row = first_row
        self.block = self.ahead = self.back = block
        self.pieces = [(0, first_row, block)]

    def step(self, clock):
        self.done += 1
        half = self.block.shape[0] // 2
        last = self.done == self.steps
        ahead = self.ahead[:half] if last else self.ahead
        back = self.back[half:] if last else self.back
        ahead, back = clock.hold(ahead, back)
        self.ahead = ring_step(ahead, self.order, 1)
        self.back = ring_step(back, self.order, -1)
        at = self.first_row
        if last:
            self.pieces += [(self.steps, at, self.ahead), (self.steps, at + half, self.back)]
        else:
            self.pieces += [(self.done, at, self.ahead), (-self.done, at, self.back)]
        return [self.ahead, self.back]


class Clock:
    def __init__(self, mark):
        self.mark = mark
        self.late = ()

    def hold(self, *values):
        held = lax.optimization_barrier(tuple(values) + (self.mark,))[: len(values)]
        return held[0] if len(values) == 1 else held

    def turn(self, ring=None, work=None):
        moved = tuple(ring.step(self)) if ring is not None else ()
        done, deferred = work() if work is not None else ((), ())
        self.mark = lax.optimization_barrier((self.mark,) + self.late + tuple(done))[0]
        self.late = moved + tuple(deferred)


class Exchange:
    def __init__(self, value, axis, count, combine):
        self.value, self.axis, self.count, self.combine = value, axis, count, combine
        self.got = None
        self.bit = 1

    def join(self, clock):
        if self.got is not None:
            self.value = self.combine(*clock.hold(self.value, self.got))
            self.got = None

    def step(self, clock):
        self.join(clock)
        if self.bit < self.count:
            route = [(i, i ^ self.bit) for i in range(self.count)]
            self.got = lax.ppermute(self.value, self.axis, route)
            self.bit *= 2

    def result(self, clock):
        while self.bit < self.count:
            self.step(clock)
        self.join(clock)
        return self.value


class RingSum:
    def __init__(self, parts, order):
        self.parts, self.order = parts, order
        self.left = len(order) // 2
        self.half = parts[0].shape[0] // 2
        self.ahead = self.back = None

    def add(self, a, b):
        return (a.astype(jnp.float32) + b.astype(jnp.float32)).astype(jnp.bfloat16)

    def step(self, clock):
        half, left, far = self.half, self.left, len(self.order) // 2
        top, bottom = self.parts[left], self.parts[-left]
        if left == far:
            ahead, back = top[:half], bottom[half:]
        elif left == far - 1:
            ahead = jnp.concatenate([self.add(self.ahead, top[:half]), top[half:]], axis=0)
            back = jnp.concatenate([bottom[:half], self.add(self.back, bottom[half:])], axis=0)
        else:
            ahead, back = self.add(self.ahead, top), self.add(self.back, bottom)
        ahead, back = clock.hold(ahead, back)
        self.ahead = ring_step(ahead, self.order, 1)
        self.back = ring_step(back, self.order, -1)
        self.left -= 1
        return [self.ahead, self.back]

    def total(self):
        return sum(value.astype(jnp.float32) for value in (self.ahead, self.back, self.parts[0]))


def project_kernel(count, turned, places_ref, *refs):
    input_refs, weight_refs = refs[:count], refs[count : 2 * count]
    cosine_ref, sine_ref, *base_ref, out_ref = refs[2 * count :]
    total = base_ref[0][...] if base_ref else None
    for input_ref, weight_ref in zip(input_refs, weight_refs):
        term = jnp.dot(input_ref[...], weight_ref[...], preferred_element_type=jnp.float32)
        total = term if total is None else total + term
    if not turned:
        out_ref[...] = total.astype(out_ref.dtype)
        return
    cosine = cosine_ref[...]
    sine = sine_ref[...]
    for head in range(out_ref.shape[1] // HEAD_DIM):
        at = slice(head * HEAD_DIM, (head + 1) * HEAD_DIM)
        part = total[:, at]
        rolled = pltpu.roll(part, HEAD_DIM // 2, 1)
        out_ref[:, at] = (part * cosine + rolled * sine).astype(out_ref.dtype)


def project(places, offsets, rows, value, pieces, cosine, sine, turned, base=(), kind=jnp.bfloat16):
    tokens = value.shape[0]
    width = pieces[0][2].shape[1]
    block = min(width, 256)
    input_specs, weight_specs = [], []
    for offset, row, piece in pieces:
        depth = piece.shape[0]

        def place(j, places_ref, slot=offsets.index(offset), scale=rows // depth, at=row // depth):
            return (0, places_ref[slot] * scale + at)

        input_specs.append(pl.BlockSpec((tokens, depth), place))
        weight_specs.append(pl.BlockSpec((depth, block), lambda j, *_: (0, j)))
    angle = pl.BlockSpec((tokens, HEAD_DIM), lambda j, *_: (0, 0))
    return pl.pallas_call(
        functools.partial(project_kernel, len(pieces), turned),
        grid_spec=pltpu.PrefetchScalarGridSpec(
            num_scalar_prefetch=1,
            grid=(width // block,),
            in_specs=input_specs
            + weight_specs
            + [angle, angle]
            + [pl.BlockSpec((tokens, block), lambda j, *_: (0, j))] * len(base),
            out_specs=pl.BlockSpec((tokens, block), lambda j, *_: (0, j)),
        ),
        out_shape=jax.ShapeDtypeStruct((tokens, width), kind),
        compiler_params=pltpu.CompilerParams(vmem_limit_bytes=VMEM_BYTES),
        cost_estimate=LIGHT,
        name="project",
    )(places, *[value] * len(pieces), *[piece for _, _, piece in pieces], cosine, sine, *base)


def silu(value):
    return value / (1.0 + jnp.exp(-value))


def exact_dot(a, b):
    return jnp.dot(a, b, precision=lax.Precision.HIGHEST, preferred_element_type=jnp.float32)


def spread(heads, block):
    shape = (heads, heads * block)
    column = lax.broadcasted_iota(jnp.int32, shape, 1) // block
    return (column == lax.broadcasted_iota(jnp.int32, shape, 0)).astype(jnp.float32)


def enter_kernel(input_ref, gain_ref, bc_ref, dt_ref, bias_ref, weight_ref, act_ref, map_ref, size_ref, normed_ref):
    @pl.when(pl.program_id(0) == 0)
    def _():
        rows = input_ref.shape[0]
        chunk = min(rows, 64)
        for start in range(0, rows, chunk):
            at = slice(start, start + chunk)
            hidden = input_ref[at, :].astype(jnp.float32)
            scale = lax.rsqrt(jnp.mean(hidden * hidden, axis=-1, keepdims=True) + 1e-05)
            normed_ref[at, :] = (hidden * scale * gain_ref[...]).astype(jnp.bfloat16)
        normed = normed_ref[...]
        map_ref[...] = jnp.dot(normed, bc_ref[...], preferred_element_type=jnp.float32)
        size = jnp.dot(normed, dt_ref[...], preferred_element_type=jnp.float32) + bias_ref[...]
        size_ref[...] = jnp.maximum(size, 0.0) + jnp.log1p(jnp.exp(-jnp.abs(size)))

    act_ref[...] = silu(
        jnp.dot(normed_ref[...], weight_ref[...], preferred_element_type=jnp.float32)
    )


def enter_mixer(flat_input, norm_gain, w_bc, w_dt, dt_bias, weight):
    tokens = flat_input.shape[0]
    width = weight.shape[1]
    block = min(width, 512)
    heads = w_dt.shape[1]
    whole = lambda *shape: pl.BlockSpec(shape, lambda j: (0, 0))
    return pl.pallas_call(
        enter_kernel,
        grid=(width // block,),
        in_specs=[
            whole(tokens, D),
            whole(1, D),
            whole(D, 2 * STATE),
            whole(D, heads),
            whole(1, heads),
            pl.BlockSpec((D, block), lambda j: (0, j)),
        ],
        out_specs=[
            pl.BlockSpec((tokens, block), lambda j: (0, j)),
            whole(tokens, 2 * STATE),
            whole(tokens, heads),
        ],
        out_shape=[
            jax.ShapeDtypeStruct((tokens, width), jnp.float32),
            jax.ShapeDtypeStruct((tokens, 2 * STATE), jnp.float32),
            jax.ShapeDtypeStruct((tokens, heads), jnp.float32),
        ],
        scratch_shapes=[pltpu.VMEM((tokens, D), jnp.bfloat16)],
        compiler_params=pltpu.CompilerParams(vmem_limit_bytes=VMEM_BYTES),
        cost_estimate=LIGHT,
        name="enter_mixer",
    )(flat_input, norm_gain.reshape(1, D), w_bc, w_dt, dt_bias.reshape(1, heads), weight)


def inside_kernel(inner_ref, map_ref, decay_ref, size_ref, decay_row_ref, size_row_ref, skip_ref, read_ref, local_ref, through_ref):
    tokens, heads = decay_ref.shape[1:]
    inner = inner_ref[...]
    input_map = map_ref[:, :STATE]
    output_map = map_ref[:, STATE:]
    decay = decay_ref[0]
    by_head = spread(heads, MHEAD_DIM)
    wide = (tokens, heads * tokens)
    contact = dot_nt(
        output_map.astype(jnp.bfloat16),
        jnp.concatenate([input_map.astype(jnp.bfloat16)] * heads, axis=0),
    )
    source = lax.rem(lax.broadcasted_iota(jnp.int32, wide, 1), tokens)
    causal = source <= lax.broadcasted_iota(jnp.int32, wide, 0)
    difference = exact_dot(decay, spread(heads, tokens)) - decay_row_ref[0]
    mixing = jnp.exp(jnp.where(causal, difference, DEAD)) * contact * size_row_ref[0]
    mixing = mixing.astype(jnp.bfloat16)
    inner_low = inner.astype(jnp.bfloat16)
    together = min(heads, 256 // MHEAD_DIM)
    shape = (together * tokens, together * MHEAD_DIM)
    own = (
        lax.broadcasted_iota(jnp.int32, shape, 0) // tokens
        == lax.broadcasted_iota(jnp.int32, shape, 1) // MHEAD_DIM
    )
    for begin in range(0, heads, together):
        at = slice(begin * MHEAD_DIM, (begin + together) * MHEAD_DIM)
        stacked = jnp.concatenate([inner_low[:, at]] * together, axis=0)
        stacked = jnp.where(own, stacked, jnp.zeros_like(stacked))
        read_ref[:, at] = (
            jnp.dot(
                mixing[:, begin * tokens : (begin + together) * tokens],
                stacked,
                preferred_element_type=jnp.float32,
            )
            + skip_ref[:, at] * inner[:, at]
        )
    last = decay[tokens - 1 :, :]
    tail = exact_dot(jnp.exp(last - decay) * size_ref[0], by_head)
    local_ref[0] = dot_tn(input_map.astype(jnp.bfloat16), (inner * tail).astype(jnp.bfloat16))
    through_ref[0] = exact_dot(jnp.exp(jnp.broadcast_to(last, (8, heads))), by_head)[:1]


def inside_block(requests, act, maps, decay, size, decay_row, size_row, skip):
    tokens, heads = decay.shape[1:]
    inner = act.shape[1] // 2
    one = lambda *shape: pl.BlockSpec((1,) + shape, lambda r: (r, 0, 0))
    return pl.pallas_call(
        inside_kernel,
        grid=(requests,),
        in_specs=[
            pl.BlockSpec((tokens, inner), lambda r: (r, 1)),
            pl.BlockSpec((tokens, 2 * STATE), lambda r: (r, 0)),
            one(tokens, heads),
            one(tokens, heads),
            one(1, heads * tokens),
            one(1, heads * tokens),
            pl.BlockSpec((1, inner), lambda r: (0, 0)),
        ],
        out_specs=[
            pl.BlockSpec((tokens, inner), lambda r: (r, 0)),
            one(STATE, inner),
            one(1, inner),
        ],
        out_shape=[
            jax.ShapeDtypeStruct((requests * tokens, inner), jnp.float32),
            jax.ShapeDtypeStruct((requests, STATE, inner), jnp.float32),
            jax.ShapeDtypeStruct((requests, 1, inner), jnp.float32),
        ],
        compiler_params=pltpu.CompilerParams(vmem_limit_bytes=VMEM_BYTES),
        cost_estimate=LIGHT,
        name="inside_block",
    )(act, maps, decay, size, decay_row, size_row, skip)


def leave_kernel(entry_ref, map_ref, decay_ref, read_ref, gate_ref, gain_ref, local_ref, through_ref, gated_ref, square_ref, chain_ref):
    heads = decay_ref.shape[2]
    entry = entry_ref[0]
    grown = exact_dot(jnp.exp(decay_ref[0]), spread(heads, MHEAD_DIM))
    inter = jnp.dot(
        map_ref[:, STATE:].astype(jnp.bfloat16),
        entry.astype(jnp.bfloat16),
        preferred_element_type=jnp.float32,
    )
    mixed = (read_ref[...] + inter * grown) * gate_ref[...]
    squares = jnp.sum(mixed * mixed, axis=1, keepdims=True)
    square_ref[...] = jnp.broadcast_to(squares, square_ref.shape)
    gated_ref[...] = (mixed * gain_ref[...]).astype(jnp.bfloat16)
    chain_ref[0] = through_ref[0] * entry + local_ref[0]


def leave_mixer(entry, maps, decay, read, act, gain, local, through):
    requests, tokens, heads = decay.shape
    inner = read.shape[1]
    one = lambda *shape: pl.BlockSpec((1,) + shape, lambda r: (r, 0, 0))
    flat = lambda width: pl.BlockSpec((tokens, width), lambda r: (r, 0))
    return pl.pallas_call(
        leave_kernel,
        grid=(requests,),
        in_specs=[
            one(STATE, inner),
            flat(2 * STATE),
            one(tokens, heads),
            flat(inner),
            flat(inner),
            pl.BlockSpec((1, inner), lambda r: (0, 0)),
            one(STATE, inner),
            one(1, inner),
        ],
        out_specs=[flat(inner), flat(128), one(STATE, inner)],
        out_shape=[
            jax.ShapeDtypeStruct((requests * tokens, inner), jnp.bfloat16),
            jax.ShapeDtypeStruct((requests * tokens, 128), jnp.float32),
            jax.ShapeDtypeStruct((requests, STATE, inner), jnp.float32),
        ],
        compiler_params=pltpu.CompilerParams(vmem_limit_bytes=VMEM_BYTES),
        cost_estimate=LIGHT,
        name="leave_mixer",
    )(entry, maps, decay, read, act, gain, local, through)


def dot_nt(a, b):
    return lax.dot_general(a, b, (((1,), (1,)), ((), ())), preferred_element_type=jnp.float32)


def dot_tn(a, b):
    return lax.dot_general(a, b, (((0,), (0,)), ((), ())), preferred_element_type=jnp.float32)


def group_scores(first, key, query):
    scores = dot_nt(key, query)
    shape = scores.shape
    live = first + lax.broadcasted_iota(jnp.int32, shape, 0) <= lax.broadcasted_iota(
        jnp.int32, shape, 1
    )
    return jnp.where(live, scores, DEAD)


def cache_kernel(slots, first_ref, place_ref, live_ref, *refs):
    query_refs = refs[:slots]
    key_ref, value_ref, group_ref, joined_ref, out_ref, peak_ref, total_ref = refs[slots:]
    tok_block = query_refs[0].shape[1]
    keys, width = key_ref.shape[1:]
    tokens = tok_block * slots
    for slot in range(slots):
        start = pl.multiple_of(place_ref[slot] * tok_block, tok_block)
        joined_ref[0, pl.ds(start, tok_block), :] = query_refs[slot][0]
    live = live_ref[pl.program_id(0)]
    bias = jnp.where(
        lax.broadcasted_iota(jnp.int32, (keys, 128), 0) < live, 0.0, DEAD
    ).astype(jnp.float32)
    bias = jnp.concatenate([bias] * (tokens // 128), axis=1)
    for head in range(width // HEAD_DIM):
        at = slice(head * HEAD_DIM, (head + 1) * HEAD_DIM)
        query = joined_ref[0, :, at]
        scores = dot_nt(key_ref[0, :, at], query) + bias
        peak = jnp.maximum(
            jnp.max(scores, axis=0, keepdims=True),
            jnp.max(
                group_scores(first_ref[0], group_ref[0, :, at], query), axis=0, keepdims=True
            ),
        )
        weights = jnp.exp2((scores - peak) * EXP2_SCALE)
        total_ref[0, head : head + 1, :] = jnp.sum(weights, axis=0, keepdims=True)
        peak_ref[0, head : head + 1, :] = peak
        out_ref[0, at, :] = dot_tn(value_ref[0, :, at], weights.astype(jnp.bfloat16)).astype(
            out_ref.dtype
        )


def cache_part(begin, first, places, live, query_slots, keys, values, new_keys):
    slots = len(query_slots)
    requests, tok_block, width = query_slots[0].shape
    tokens = tok_block * slots
    cache_block = keys.shape[1]
    heads = width // HEAD_DIM
    one = lambda rows, start: pl.BlockSpec((1, rows, width), lambda r, *_: (r + start, 0, 0))
    stat = pl.BlockSpec((1, heads, tokens), lambda r, *_: (r, 0, 0))
    return pl.pallas_call(
        functools.partial(cache_kernel, slots),
        grid_spec=pltpu.PrefetchScalarGridSpec(
            num_scalar_prefetch=3,
            grid=(requests,),
            in_specs=[one(tok_block, 0)] * slots
            + [one(cache_block, begin)] * 2
            + [one(tok_block, begin)],
            out_specs=[
                one(tokens, 0),
                pl.BlockSpec((1, width, tokens), lambda r, *_: (r, 0, 0)),
                stat,
                stat,
            ],
        ),
        out_shape=[
            jax.ShapeDtypeStruct((requests, tokens, width), jnp.bfloat16),
            jax.ShapeDtypeStruct((requests, width, tokens), jnp.bfloat16),
            jax.ShapeDtypeStruct((requests, heads, tokens), jnp.float32),
            jax.ShapeDtypeStruct((requests, heads, tokens), jnp.float32),
        ],
        compiler_params=pltpu.CompilerParams(vmem_limit_bytes=VMEM_BYTES),
        cost_estimate=LIGHT,
        name="cache_part",
    )(first, places, live, *query_slots, keys, values, new_keys)


def finish_kernel(slots, first_ref, place_ref, *refs):
    query_ref, key_ref, value_ref, cache_ref, peak_ref, total_ref, best_ref = refs[:7]
    sum_ref, *part_refs = refs[7:-1]
    joined_ref = refs[-1]
    tok_block = key_ref.shape[1]
    for head in range(query_ref.shape[2] // HEAD_DIM):
        at = slice(head * HEAD_DIM, (head + 1) * HEAD_DIM)
        row = slice(head, head + 1)
        scores = group_scores(first_ref[0], key_ref[0, :, at], query_ref[0, :, at])
        best = best_ref[0, row, :]
        weights = jnp.exp2((scores - best) * EXP2_SCALE)
        rescale = jnp.exp2((peak_ref[0, row, :] - best) * EXP2_SCALE)
        sum_ref[0, row, :] = total_ref[0, row, :] * rescale + jnp.sum(
            weights, axis=0, keepdims=True
        )
        joined = cache_ref[0, at, :].astype(jnp.float32) * rescale + dot_tn(
            value_ref[0, :, at], weights.astype(jnp.bfloat16)
        )
        joined_ref[:, at] = joined.astype(jnp.bfloat16).T
    for slot in range(slots):
        start = pl.multiple_of(place_ref[slot] * tok_block, tok_block)
        part_refs[slot][0] = joined_ref[pl.ds(start, tok_block), :]


def finish_part(begin, first, places, queries, new_keys, new_values, cached, peaks, totals, best):
    requests, tokens, width = queries.shape
    tok_block = new_keys.shape[1]
    slots = tokens // tok_block
    heads = width // HEAD_DIM
    one = lambda rows, start: pl.BlockSpec((1, rows, width), lambda r, *_: (r + start, 0, 0))
    stat = lambda start: pl.BlockSpec((1, heads, tokens), lambda r, *_: (r + start, 0, 0))
    return pl.pallas_call(
        functools.partial(finish_kernel, slots),
        grid_spec=pltpu.PrefetchScalarGridSpec(
            num_scalar_prefetch=2,
            grid=(requests,),
            in_specs=[
                one(tokens, 0),
                one(tok_block, begin),
                one(tok_block, begin),
                pl.BlockSpec((1, width, tokens), lambda r, *_: (r, 0, 0)),
                stat(0),
                stat(0),
                stat(begin),
            ],
            out_specs=[stat(0)] + [one(tok_block, 0)] * slots,
            scratch_shapes=[pltpu.VMEM((tokens, width), jnp.bfloat16)],
        ),
        out_shape=[jax.ShapeDtypeStruct((requests, heads, tokens), jnp.float32)]
        + [jax.ShapeDtypeStruct((requests, tok_block, width), jnp.bfloat16)] * slots,
        compiler_params=pltpu.CompilerParams(vmem_limit_bytes=VMEM_BYTES),
        cost_estimate=LIGHT,
        name="finish_part",
    )(first, places, queries, new_keys, new_values, cached, peaks, totals, best)


def head_sum(terms, head_count, head_index):
    if head_count != 4:
        return lax.psum_scatter(
            terms.astype(jnp.bfloat16), "head", scatter_dimension=1, tiled=True
        ).astype(jnp.float32)
    width = terms.shape[1] // 4
    chunk = lambda index: lax.dynamic_slice_in_dim(terms, index * width, width, 1)
    core, column = head_index % 2, head_index // 2
    near, far = 2 * column, 2 * (1 - column)
    got = lax.ppermute(
        jnp.concatenate([chunk(near + 1 - core), chunk(far + 1 - core)], axis=1).astype(
            jnp.bfloat16
        ),
        "head",
        [(h, h ^ 1) for h in range(4)],
    ).astype(jnp.float32)
    keep = chunk(near + core) + got[:, :width]
    give = chunk(far + core) + got[:, width:]
    return keep + lax.ppermute(
        give.astype(jnp.bfloat16), "head", [(h, h ^ 2) for h in range(4)]
    ).astype(jnp.float32)


class Relay:
    def __init__(self, through, local, initial, seq_index, seq_count):
        self.factor, self.local = through, local
        self.paired = seq_count == 8
        self.hop = 0
        if not self.paired:
            self.hops = seq_count - 1
            self.entry = jnp.where(seq_index == 0, initial, 0.0)
            return
        self.hops = 3
        self.swap = [(i, i ^ 1) for i in range(8)]
        self.is_first = is_first = seq_index % 2 == 0
        half = local.shape[2] // 2
        side = lambda value: jnp.where(is_first, value[..., :half], value[..., half:])
        mine = side(local)
        got = self.exchange(jnp.where(is_first, local[..., half:], local[..., :half]))
        other_factor = side(lax.ppermute(through, "seq", self.swap))
        factor = side(through)
        self.first_state = jnp.where(is_first, mine, got)
        second_state = jnp.where(is_first, got, mine)
        self.first_factor = jnp.where(is_first, factor, other_factor)
        second_factor = jnp.where(is_first, other_factor, factor)
        self.pair_state = second_factor * self.first_state + second_state
        self.pair_factor = self.first_factor * second_factor
        self.entry = jnp.where(seq_index < 2, side(initial), 0.0)

    def exchange(self, value):
        return lax.ppermute(value.astype(jnp.bfloat16), "seq", self.swap).astype(jnp.float32)

    def advance(self, clock):
        if self.hop == self.hops:
            return
        factor, state = (
            (self.pair_factor, self.pair_state) if self.paired else (self.factor, self.local)
        )
        entry = clock.hold(self.entry)
        leaving = (factor * entry + state).astype(jnp.bfloat16)
        if self.paired:
            route = [(2 * self.hop + y, 2 * self.hop + 2 + y) for y in range(2)]
        else:
            route = [(self.hop, self.hop + 1)]
        self.hop += 1
        self.entry = entry + lax.ppermute(leaving, "seq", route).astype(jnp.float32)

    def result(self, clock):
        while self.hop < self.hops:
            self.advance(clock)
        entry = clock.hold(self.entry)
        if not self.paired:
            return entry
        second = self.first_factor * entry + self.first_state
        got = self.exchange(jnp.where(self.is_first, second, entry))
        mine = jnp.where(self.is_first, entry, second)
        return jnp.concatenate(
            [jnp.where(self.is_first, mine, got), jnp.where(self.is_first, got, mine)], axis=2
        )


def shards(
    block_input,
    lengths,
    cache_keys,
    cache_values,
    w_query,
    w_key,
    w_value,
    w_attn_out,
    norm_gain,
    w_in,
    w_bc,
    w_dt,
    dt_bias,
    a_log,
    d_skip,
    gated_gain,
    w_out,
    ssm_init,
):
    requests, tok_block, _ = block_input.shape
    seq_count = lax.axis_size("seq")
    seq_index = lax.axis_index("seq")
    head_count = lax.axis_size("head")
    head_index = lax.axis_index("head")
    local_att = w_query.shape[1]
    local_heads = local_att // HEAD_DIM
    cache_block = cache_keys.shape[1]
    rows = w_query.shape[0]
    tokens = requests * tok_block
    flat_input = block_input.reshape(tokens, block_input.shape[2])

    order = ring_order(seq_count)
    half = seq_count // 2
    offsets = [0] + [sign * step for step in range(1, half) for sign in (1, -1)] + [half]
    places = jnp.asarray(
        [
            [order[(order.index(i) - offset) % seq_count] for offset in offsets]
            for i in range(seq_count)
        ],
        jnp.int32,
    )[seq_index]

    positions = (
        lengths[:, None] + seq_index * tok_block + jnp.arange(tok_block, dtype=jnp.int32)[None, :]
    ).reshape(tokens)
    half_dim = HEAD_DIM // 2
    frequency = jnp.exp(
        jnp.arange(half_dim, dtype=jnp.float32) * (-2.0 * math.log(10000.0) / HEAD_DIM)
    )
    angles = positions.astype(jnp.float32)[:, None] * frequency
    cosine = jnp.cos(angles)
    sine = jnp.sin(angles)
    cosine = jnp.concatenate([cosine, cosine], axis=1)
    sine = jnp.concatenate([-sine, sine], axis=1)

    clock = Clock(jnp.zeros((1,), jnp.int32) + lengths[:1])
    group = requests // GROUPS
    local_inner = w_in.shape[2]
    local_mheads = local_inner // MHEAD_DIM
    local_width = D // head_count
    made = {}

    def product(pieces, turned, base=(), kind=jnp.bfloat16):
        pieces = list(pieces)
        if pieces[-1][2].shape[0] < 128:
            (offset, row, upper), (_, _, lower) = pieces[-2:]
            pieces[-2:] = [(offset, row, jnp.concatenate([upper, lower], axis=0))]
        return project(
            places, offsets, rows, flat_input, pieces, cosine, sine, turned, base, kind
        )

    by_request = lambda value: value.reshape(requests, tok_block, local_att)

    def prepare():
        made["w_in"] = w_in.reshape(D, 2 * local_inner)
        first_state = ssm_init.reshape(requests, local_mheads, MHEAD_DIM, STATE)
        made["initial"] = jnp.transpose(first_state, (0, 3, 1, 2)).reshape(
            requests, STATE, local_inner
        )
        return (made["w_in"], made["initial"]), ()

    def enter():
        made["act"], made["maps"], size = enter_mixer(
            clock.hold(flat_input), norm_gain, w_bc, w_dt, dt_bias, made["w_in"]
        )
        size = size.reshape(requests, tok_block, local_mheads)
        log_decay = -size * jnp.exp(a_log)
        causal = jnp.arange(tok_block)[None, :] <= jnp.arange(tok_block)[:, None]
        decay = jnp.einsum(
            "tu,ruh->rth", causal.astype(jnp.float32), log_decay, precision=lax.Precision.HIGHEST
        )
        by_row = lambda value: jnp.transpose(value, (0, 2, 1)).reshape(
            requests, 1, local_mheads * tok_block
        )
        made["size"], made["decay"] = size, decay
        made["size_row"], made["decay_row"] = by_row(size), by_row(decay)
        return (made["act"], made["size_row"], made["decay_row"]), ()

    def inside():
        made["read"], made["local"], made["through"] = inside_block(
            requests,
            clock.hold(made["act"]),
            made["maps"],
            made["decay"],
            made["size"],
            made["decay_row"],
            made["size_row"],
            jnp.repeat(d_skip, MHEAD_DIM).reshape(1, local_inner),
        )
        return (made["read"], made["local"]), ()

    def start_relay():
        made["relay"] = relay = Relay(
            made["through"], clock.hold(made["local"]), made["initial"], seq_index, seq_count
        )
        return (), ((relay.pair_state,) if relay.paired else ())

    def hop():
        made["relay"].advance(clock)
        return (), (made["relay"].entry,)

    def end_relay():
        made["entry"] = made["relay"].result(clock)
        return (), (made["entry"],)

    def leave():
        gated, squares, chain = leave_mixer(
            clock.hold(made["entry"]),
            made["maps"],
            made["decay"],
            made["read"],
            made["act"],
            gated_gain.reshape(1, local_inner),
            made["local"],
            made["through"],
        )
        made["gated"] = gated
        made["squares"] = Exchange(
            squares[:, :1].reshape(1, tokens), "head", head_count, jnp.add
        )
        made["squares"].step(clock)
        made["chain"] = chain
        return (gated,), ()

    def join_squares():
        made["squares"].step(clock)
        return (), ()

    def leave_terms():
        squares = made["squares"].result(clock).reshape(tokens, 1)
        made["terms"] = jnp.dot(
            clock.hold(made["gated"]), w_out, preferred_element_type=jnp.float32
        ) * lax.rsqrt(squares / D_INNER + 1e-05)
        return (made["terms"],), ()

    def chain_split():
        made["chain"] = clock.hold(made["chain"]).reshape(
            requests, STATE, local_mheads, MHEAD_DIM
        )
        return (made["chain"],), ()

    def chain_turn():
        made["chain"] = jnp.transpose(clock.hold(made["chain"]), (0, 2, 3, 1))
        return (made["chain"],), ()

    def chain_join():
        made["chain"] = clock.hold(made["chain"]).reshape(
            requests, 1, local_mheads, MHEAD_DIM * STATE
        )
        return (made["chain"],), ()

    query_ring, key_ring, value_ring = (Ring(w, order) for w in (w_query, w_key, w_value))
    slot_rings = []
    live = jnp.clip(lengths - seq_index * cache_block, 0, cache_block).astype(jnp.int32)
    first = (seq_index * tok_block).astype(jnp.int32).reshape(1)
    cached = []

    def make_queries():
        queries = by_request(product(query_ring.pieces, True))
        slot_rings.extend(
            Ring(queries[begin : begin + group], order) for begin in range(0, requests, group)
        )
        return (queries,), ()

    def make_keys():
        made["keys"] = by_request(product(key_ring.pieces, True))
        return (made["keys"],), ()

    def meet_cache(index):
        def work():
            ring = slot_rings[index]
            begin = index * group
            slots = [piece for _, _, piece in ring.pieces[:-2]]
            slots.append(jnp.concatenate([ring.pieces[-2][2], ring.pieces[-1][2]], axis=0))
            slots[0] = clock.hold(slots[0])
            cached.append(
                cache_part(
                    begin,
                    first,
                    places,
                    live[begin : begin + group],
                    slots,
                    cache_keys,
                    cache_values,
                    made["keys"],
                )
            )
            return tuple(cached[-1]), ()

        return work

    def join_peaks():
        peaks = jnp.concatenate([clock.hold(part[2]) for part in cached], axis=0)
        made["best"] = Exchange(peaks, "seq", seq_count, jnp.maximum)
        made["best"].step(clock)
        pieces = value_ring.pieces[1:-2]
        made["used"] = 1 + len(pieces)
        made["values"] = product(
            [(0, 0, clock.hold(value_ring.block))] + pieces, False, kind=jnp.float32
        )
        return (made["values"],), ()

    def join_more():
        made["best"].step(clock)
        return leave_terms()

    def steps(rings, begin, end):
        return [ring for _ in range(begin, end) for ring in rings]

    def run(sends, works):
        for index in range(max(len(sends), len(works))):
            clock.turn(
                sends[index] if index < len(sends) else None,
                works[index] if index < len(works) else None,
            )

    both = steps([query_ring, key_ring], 0, half - 2) + [query_ring] * 2 + [key_ring] * 2
    def make_queries_hop():
        done, _ = make_queries()
        return done, hop()[1]

    def make_keys_hop():
        deferred = hop()[1]
        return make_keys()[0], deferred

    works = [prepare, enter, inside, start_relay, None, hop]
    run(both, works + [None] * (len(both) - 1 - len(works)) + [make_queries_hop])
    run(
        steps(slot_rings, 0, half),
        [None, make_keys_hop, None, end_relay, None, leave, join_squares],
    )
    run(
        steps([value_ring], 0, half),
        [meet_cache(0), meet_cache(1)] + [None] * (half - 4) + [join_peaks, join_more],
    )

    new_keys = made["keys"]
    best = made["best"].result(clock)
    new_values = by_request(
        product(value_ring.pieces[made["used"] :], False, base=(made["values"],))
    )

    own = lambda stat: lax.dynamic_slice_in_dim(stat, seq_index * tok_block, tok_block, 2)
    greatest_logit = jnp.transpose(own(best), (0, 2, 1)) * SCALE
    residual = lax.dynamic_slice_in_dim(
        flat_input, head_index * local_width, local_width, 1
    ).astype(jnp.float32)
    sums, ring_sums, mixed = [], [], []

    def finish(index):
        def work():
            joined, out, peaks, totals = cached[index]
            some_sums, *parts = finish_part(
                index * group,
                first,
                places,
                clock.hold(joined),
                new_keys,
                new_values,
                out,
                peaks,
                totals,
                best,
            )
            sums.append(some_sums)
            terms = {-offset: part for offset, part in zip(offsets, parts)}
            terms[half] = terms[-half]
            ring_sums.append(RingSum(terms, order))
            return (some_sums, *parts), ()

        return work

    def add_sums():
        if "sums" not in made:
            made["sums"] = Exchange(jnp.concatenate(sums, axis=0), "seq", seq_count, jnp.add)
        made["sums"].step(clock)
        return (), ()

    run([], [finish(0)])
    run([ring_sums[0]], [finish(1)])
    run(
        steps(ring_sums[::-1], 0, half)[:-1],
        [add_sums, chain_split, add_sums, chain_turn, add_sums, chain_join],
    )
    denominators = jnp.transpose(own(made["sums"].result(clock)), (0, 2, 1))
    for index in range(GROUPS):
        begin = index * group
        denominator = denominators[begin : begin + group]
        numerator = ring_sums[index].total().reshape(group, tok_block, local_heads, HEAD_DIM)
        attended = (
            (numerator / denominator[..., None])
            .astype(jnp.bfloat16)
            .reshape(group * tok_block, local_att)
        )
        at = slice(begin * tok_block, (begin + group) * tok_block)
        attn_terms = jnp.dot(attended, w_attn_out, preferred_element_type=jnp.float32)
        summed = head_sum(attn_terms + made["terms"][at], head_count, head_index)
        mixed.append(
            (residual[at] + summed)
            .astype(jnp.bfloat16)
            .reshape(group, tok_block, local_width)
        )
    return (
        jnp.concatenate(mixed, axis=0),
        new_keys,
        new_values,
        made["chain"],
        greatest_logit,
    )


def solution(mesh):
    placed = (
        P(None, "seq", None),
        P(),
        P(None, "seq", "head"),
        P(None, "seq", "head"),
        P("seq", "head"),
        P("seq", "head"),
        P("seq", "head"),
        P("head", None),
        P(),
        P(None, None, "head"),
        P(),
        P(None, "head"),
        P("head"),
        P("head"),
        P("head"),
        P("head"),
        P("head", None),
        P(None, "head", None),
    )
    return jax.shard_map(
        shards,
        mesh=mesh,
        in_specs=placed,
        out_specs=(
            P(None, "seq", "head"),
            P(None, "seq", "head"),
            P(None, "seq", "head"),
            P(None, "seq", "head", None),
            P(None, "seq", "head"),
        ),
        check_vma=False,
    )
```

```python
import functools
import math

import jax
import jax.numpy as jnp
from jax import lax
from jax.experimental import pallas as pl
from jax.experimental.pallas import tpu as pltpu
from jax.sharding import PartitionSpec as P

D = 2048
HEAD_DIM = 128
MHEAD_DIM = 64
STATE = 64
D_INNER = 4096
SCALE = 1.0 / math.sqrt(HEAD_DIM)
EXP2_SCALE = SCALE * math.log2(math.e)
DEAD = -1e30
GROUPS = 2
VMEM_BYTES = 56 * 1024 * 1024
LIGHT = pl.CostEstimate(flops=0, bytes_accessed=0, transcendentals=0)


def ring_order(count):
    y_count = max(1, count // 4)
    z_count = count // y_count
    order = []
    for y in range(y_count):
        turn = range(z_count) if y % 2 == 0 else range(z_count - 1, -1, -1)
        order += [z * y_count + y for z in turn]
    return order


def ring_step(block, order, distance):
    count = len(order)
    route = [(order[i], order[(i + distance) % count]) for i in range(count)]
    return lax.ppermute(block, "seq", route)


class Ring:
    def __init__(self, block, order, first_row=0):
        self.order = order
        self.steps = len(order) // 2
        self.done = 0
        self.first_row = first_row
        self.block = self.ahead = self.back = block
        self.pieces = [(0, first_row, block)]

    def step(self, clock):
        self.done += 1
        half = self.block.shape[0] // 2
        last = self.done == self.steps
        ahead = self.ahead[:half] if last else self.ahead
        back = self.back[half:] if last else self.back
        ahead, back = clock.hold(ahead, back)
        self.ahead = ring_step(ahead, self.order, 1)
        self.back = ring_step(back, self.order, -1)
        at = self.first_row
        if last:
            self.pieces += [(self.steps, at, self.ahead), (self.steps, at + half, self.back)]
        else:
            self.pieces += [(self.done, at, self.ahead), (-self.done, at, self.back)]
        return [self.ahead, self.back]


class Clock:
    def __init__(self, mark):
        self.mark = mark
        self.late = ()

    def hold(self, *values):
        held = lax.optimization_barrier(tuple(values) + (self.mark,))[: len(values)]
        return held[0] if len(values) == 1 else held

    def turn(self, ring=None, work=None):
        moved = tuple(ring.step(self)) if ring is not None else ()
        done, deferred = work() if work is not None else ((), ())
        self.mark = lax.optimization_barrier((self.mark,) + self.late + tuple(done))[0]
        self.late = moved + tuple(deferred)


class Exchange:
    def __init__(self, value, axis, count, combine):
        self.value, self.axis, self.count, self.combine = value, axis, count, combine
        self.got = None
        self.bit = 1

    def join(self, clock):
        if self.got is not None:
            self.value = self.combine(*clock.hold(self.value, self.got))
            self.got = None

    def step(self, clock):
        self.join(clock)
        if self.bit < self.count:
            route = [(i, i ^ self.bit) for i in range(self.count)]
            self.got = lax.ppermute(self.value, self.axis, route)
            self.bit *= 2

    def result(self, clock):
        while self.bit < self.count:
            self.step(clock)
        self.join(clock)
        return self.value


class RingSum:
    def __init__(self, parts, order):
        self.parts, self.order = parts, order
        self.left = len(order) // 2
        self.half = parts[0].shape[0] // 2
        self.ahead = self.back = None

    def add(self, a, b):
        return (a.astype(jnp.float32) + b.astype(jnp.float32)).astype(jnp.bfloat16)

    def step(self, clock):
        half, left, far = self.half, self.left, len(self.order) // 2
        top, bottom = self.parts[left], self.parts[-left]
        if left == far:
            ahead, back = top[:half], bottom[half:]
        elif left == far - 1:
            ahead = jnp.concatenate([self.add(self.ahead, top[:half]), top[half:]], axis=0)
            back = jnp.concatenate([bottom[:half], self.add(self.back, bottom[half:])], axis=0)
        else:
            ahead, back = self.add(self.ahead, top), self.add(self.back, bottom)
        ahead, back = clock.hold(ahead, back)
        self.ahead = ring_step(ahead, self.order, 1)
        self.back = ring_step(back, self.order, -1)
        self.left -= 1
        return [self.ahead, self.back]


def project_kernel(count, turned, places_ref, *refs):
    input_refs, weight_refs = refs[:count], refs[count : 2 * count]
    cosine_ref, sine_ref, *base_ref, out_ref = refs[2 * count :]
    total = base_ref[0][...] if base_ref else None
    for input_ref, weight_ref in zip(input_refs, weight_refs):
        term = jnp.dot(input_ref[...], weight_ref[...], preferred_element_type=jnp.float32)
        total = term if total is None else total + term
    if not turned:
        out_ref[...] = total.astype(out_ref.dtype)
        return
    cosine = cosine_ref[...]
    sine = sine_ref[...]
    for head in range(out_ref.shape[1] // HEAD_DIM):
        at = slice(head * HEAD_DIM, (head + 1) * HEAD_DIM)
        part = total[:, at]
        rolled = pltpu.roll(part, HEAD_DIM // 2, 1)
        out_ref[:, at] = (part * cosine + rolled * sine).astype(out_ref.dtype)


def project(places, offsets, rows, value, pieces, cosine, sine, turned, base=(), kind=jnp.bfloat16):
    tokens = value.shape[0]
    width = pieces[0][2].shape[1]
    block = min(width, 256)
    input_specs, weight_specs = [], []
    for offset, row, piece in pieces:
        depth = piece.shape[0]

        def place(j, places_ref, slot=offsets.index(offset), scale=rows // depth, at=row // depth):
            return (0, places_ref[slot] * scale + at)

        input_specs.append(pl.BlockSpec((tokens, depth), place))
        weight_specs.append(pl.BlockSpec((depth, block), lambda j, *_: (0, j)))
    angle = pl.BlockSpec((tokens, HEAD_DIM), lambda j, *_: (0, 0))
    return pl.pallas_call(
        functools.partial(project_kernel, len(pieces), turned),
        grid_spec=pltpu.PrefetchScalarGridSpec(
            num_scalar_prefetch=1,
            grid=(width // block,),
            in_specs=input_specs
            + weight_specs
            + [angle, angle]
            + [pl.BlockSpec((tokens, block), lambda j, *_: (0, j))] * len(base),
            out_specs=pl.BlockSpec((tokens, block), lambda j, *_: (0, j)),
        ),
        out_shape=jax.ShapeDtypeStruct((tokens, width), kind),
        compiler_params=pltpu.CompilerParams(vmem_limit_bytes=VMEM_BYTES),
        cost_estimate=LIGHT,
        name="project",
    )(places, *[value] * len(pieces), *[piece for _, _, piece in pieces], cosine, sine, *base)


def silu(value):
    return value / (1.0 + jnp.exp(-value))


def exact_dot(a, b):
    return jnp.dot(a, b, precision=lax.Precision.HIGHEST, preferred_element_type=jnp.float32)


def spread(heads, block):
    shape = (heads, heads * block)
    column = lax.broadcasted_iota(jnp.int32, shape, 1) // block
    return (column == lax.broadcasted_iota(jnp.int32, shape, 0)).astype(jnp.float32)


def enter_kernel(input_ref, gain_ref, bc_ref, dt_ref, bias_ref, weight_ref, act_ref, map_ref, size_ref, normed_ref):
    @pl.when(pl.program_id(0) == 0)
    def _():
        rows = input_ref.shape[0]
        chunk = min(rows, 64)
        for start in range(0, rows, chunk):
            at = slice(start, start + chunk)
            hidden = input_ref[at, :].astype(jnp.float32)
            scale = lax.rsqrt(jnp.mean(hidden * hidden, axis=-1, keepdims=True) + 1e-05)
            normed_ref[at, :] = (hidden * scale * gain_ref[...]).astype(jnp.bfloat16)
        normed = normed_ref[...]
        map_ref[...] = jnp.dot(normed, bc_ref[...], preferred_element_type=jnp.float32)
        size = jnp.dot(normed, dt_ref[...], preferred_element_type=jnp.float32) + bias_ref[...]
        size_ref[...] = jnp.maximum(size, 0.0) + jnp.log1p(jnp.exp(-jnp.abs(size)))

    act_ref[...] = silu(
        jnp.dot(normed_ref[...], weight_ref[...], preferred_element_type=jnp.float32)
    )


def enter_mixer(flat_input, norm_gain, w_bc, w_dt, dt_bias, weight):
    tokens = flat_input.shape[0]
    width = weight.shape[1]
    block = min(width, 512)
    heads = w_dt.shape[1]
    whole = lambda *shape: pl.BlockSpec(shape, lambda j: (0, 0))
    return pl.pallas_call(
        enter_kernel,
        grid=(width // block,),
        in_specs=[
            whole(tokens, D),
            whole(1, D),
            whole(D, 2 * STATE),
            whole(D, heads),
            whole(1, heads),
            pl.BlockSpec((D, block), lambda j: (0, j)),
        ],
        out_specs=[
            pl.BlockSpec((tokens, block), lambda j: (0, j)),
            whole(tokens, 2 * STATE),
            whole(tokens, heads),
        ],
        out_shape=[
            jax.ShapeDtypeStruct((tokens, width), jnp.float32),
            jax.ShapeDtypeStruct((tokens, 2 * STATE), jnp.float32),
            jax.ShapeDtypeStruct((tokens, heads), jnp.float32),
        ],
        scratch_shapes=[pltpu.VMEM((tokens, D), jnp.bfloat16)],
        compiler_params=pltpu.CompilerParams(vmem_limit_bytes=VMEM_BYTES),
        cost_estimate=LIGHT,
        name="enter_mixer",
    )(flat_input, norm_gain.reshape(1, D), w_bc, w_dt, dt_bias.reshape(1, heads), weight)


def inside_kernel(inner_ref, map_ref, decay_ref, size_ref, decay_row_ref, size_row_ref, skip_ref, read_ref, local_ref, through_ref):
    tokens, heads = decay_ref.shape[1:]
    inner = inner_ref[...]
    input_map = map_ref[:, :STATE]
    output_map = map_ref[:, STATE:]
    decay = decay_ref[0]
    by_head = spread(heads, MHEAD_DIM)
    wide = (tokens, heads * tokens)
    contact = dot_nt(
        output_map.astype(jnp.bfloat16),
        jnp.concatenate([input_map.astype(jnp.bfloat16)] * heads, axis=0),
    )
    source = lax.rem(lax.broadcasted_iota(jnp.int32, wide, 1), tokens)
    causal = source <= lax.broadcasted_iota(jnp.int32, wide, 0)
    difference = exact_dot(decay, spread(heads, tokens)) - decay_row_ref[0]
    mixing = jnp.exp(jnp.where(causal, difference, DEAD)) * contact * size_row_ref[0]
    mixing = mixing.astype(jnp.bfloat16)
    inner_low = inner.astype(jnp.bfloat16)
    together = min(heads, 256 // MHEAD_DIM)
    shape = (together * tokens, together * MHEAD_DIM)
    own = (
        lax.broadcasted_iota(jnp.int32, shape, 0) // tokens
        == lax.broadcasted_iota(jnp.int32, shape, 1) // MHEAD_DIM
    )
    for begin in range(0, heads, together):
        at = slice(begin * MHEAD_DIM, (begin + together) * MHEAD_DIM)
        stacked = jnp.concatenate([inner_low[:, at]] * together, axis=0)
        stacked = jnp.where(own, stacked, jnp.zeros_like(stacked))
        read_ref[:, at] = (
            jnp.dot(
                mixing[:, begin * tokens : (begin + together) * tokens],
                stacked,
                preferred_element_type=jnp.float32,
            )
            + skip_ref[:, at] * inner[:, at]
        )
    last = decay[tokens - 1 :, :]
    tail = exact_dot(jnp.exp(last - decay) * size_ref[0], by_head)
    local_ref[0] = dot_tn(input_map.astype(jnp.bfloat16), (inner * tail).astype(jnp.bfloat16))
    through_ref[0] = exact_dot(jnp.exp(jnp.broadcast_to(last, (8, heads))), by_head)[:1]


def inside_block(requests, act, maps, decay, size, decay_row, size_row, skip):
    tokens, heads = decay.shape[1:]
    inner = act.shape[1] // 2
    one = lambda *shape: pl.BlockSpec((1,) + shape, lambda r: (r, 0, 0))
    return pl.pallas_call(
        inside_kernel,
        grid=(requests,),
        in_specs=[
            pl.BlockSpec((tokens, inner), lambda r: (r, 1)),
            pl.BlockSpec((tokens, 2 * STATE), lambda r: (r, 0)),
            one(tokens, heads),
            one(tokens, heads),
            one(1, heads * tokens),
            one(1, heads * tokens),
            pl.BlockSpec((1, inner), lambda r: (0, 0)),
        ],
        out_specs=[
            pl.BlockSpec((tokens, inner), lambda r: (r, 0)),
            one(STATE, inner),
            one(1, inner),
        ],
        out_shape=[
            jax.ShapeDtypeStruct((requests * tokens, inner), jnp.float32),
            jax.ShapeDtypeStruct((requests, STATE, inner), jnp.float32),
            jax.ShapeDtypeStruct((requests, 1, inner), jnp.float32),
        ],
        compiler_params=pltpu.CompilerParams(vmem_limit_bytes=VMEM_BYTES),
        cost_estimate=LIGHT,
        name="inside_block",
    )(act, maps, decay, size, decay_row, size_row, skip)


def leave_kernel(entry_ref, map_ref, decay_ref, read_ref, gate_ref, gain_ref, local_ref, through_ref, gated_ref, square_ref, chain_ref):
    heads = decay_ref.shape[2]
    entry = entry_ref[0]
    grown = exact_dot(jnp.exp(decay_ref[0]), spread(heads, MHEAD_DIM))
    inter = jnp.dot(
        map_ref[:, STATE:].astype(jnp.bfloat16),
        entry.astype(jnp.bfloat16),
        preferred_element_type=jnp.float32,
    )
    mixed = (read_ref[...] + inter * grown) * gate_ref[...]
    squares = jnp.sum(mixed * mixed, axis=1, keepdims=True)
    square_ref[...] = jnp.broadcast_to(squares, square_ref.shape)
    gated_ref[...] = (mixed * gain_ref[...]).astype(jnp.bfloat16)
    chain_ref[0] = through_ref[0] * entry + local_ref[0]


def leave_mixer(entry, maps, decay, read, act, gain, local, through):
    requests, tokens, heads = decay.shape
    inner = read.shape[1]
    one = lambda *shape: pl.BlockSpec((1,) + shape, lambda r: (r, 0, 0))
    flat = lambda width: pl.BlockSpec((tokens, width), lambda r: (r, 0))
    return pl.pallas_call(
        leave_kernel,
        grid=(requests,),
        in_specs=[
            one(STATE, inner),
            flat(2 * STATE),
            one(tokens, heads),
            flat(inner),
            flat(inner),
            pl.BlockSpec((1, inner), lambda r: (0, 0)),
            one(STATE, inner),
            one(1, inner),
        ],
        out_specs=[flat(inner), flat(128), one(STATE, inner)],
        out_shape=[
            jax.ShapeDtypeStruct((requests * tokens, inner), jnp.bfloat16),
            jax.ShapeDtypeStruct((requests * tokens, 128), jnp.float32),
            jax.ShapeDtypeStruct((requests, STATE, inner), jnp.float32),
        ],
        compiler_params=pltpu.CompilerParams(vmem_limit_bytes=VMEM_BYTES),
        cost_estimate=LIGHT,
        name="leave_mixer",
    )(entry, maps, decay, read, act, gain, local, through)


def dot_nt(a, b):
    return lax.dot_general(a, b, (((1,), (1,)), ((), ())), preferred_element_type=jnp.float32)


def dot_tn(a, b):
    return lax.dot_general(a, b, (((0,), (0,)), ((), ())), preferred_element_type=jnp.float32)


def group_scores(first, key, query):
    scores = dot_nt(key, query)
    shape = scores.shape
    live = first + lax.broadcasted_iota(jnp.int32, shape, 0) <= lax.broadcasted_iota(
        jnp.int32, shape, 1
    )
    return jnp.where(live, scores, DEAD)


def cache_kernel(slots, first_ref, place_ref, live_ref, *refs):
    query_refs = refs[:slots]
    key_ref, value_ref, group_ref, joined_ref, out_ref, peak_ref, total_ref = refs[slots:]
    tok_block = query_refs[0].shape[1]
    keys, width = key_ref.shape[1:]
    tokens = tok_block * slots
    for slot in range(slots):
        start = pl.multiple_of(place_ref[slot] * tok_block, tok_block)
        joined_ref[0, pl.ds(start, tok_block), :] = query_refs[slot][0]
    live = live_ref[pl.program_id(0)]
    bias = jnp.where(
        lax.broadcasted_iota(jnp.int32, (keys, 128), 0) < live, 0.0, DEAD
    ).astype(jnp.float32)
    bias = jnp.concatenate([bias] * (tokens // 128), axis=1)
    for head in range(width // HEAD_DIM):
        at = slice(head * HEAD_DIM, (head + 1) * HEAD_DIM)
        query = joined_ref[0, :, at]
        scores = dot_nt(key_ref[0, :, at], query) + bias
        peak = jnp.maximum(
            jnp.max(scores, axis=0, keepdims=True),
            jnp.max(
                group_scores(first_ref[0], group_ref[0, :, at], query), axis=0, keepdims=True
            ),
        )
        weights = jnp.exp2((scores - peak) * EXP2_SCALE)
        total_ref[0, head : head + 1, :] = jnp.sum(weights, axis=0, keepdims=True)
        peak_ref[0, head : head + 1, :] = peak
        out_ref[0, at, :] = dot_tn(value_ref[0, :, at], weights.astype(jnp.bfloat16)).astype(
            out_ref.dtype
        )


def cache_part(begin, first, places, live, query_slots, keys, values, new_keys):
    slots = len(query_slots)
    requests, tok_block, width = query_slots[0].shape
    tokens = tok_block * slots
    cache_block = keys.shape[1]
    heads = width // HEAD_DIM
    one = lambda rows, start: pl.BlockSpec((1, rows, width), lambda r, *_: (r + start, 0, 0))
    stat = pl.BlockSpec((1, heads, tokens), lambda r, *_: (r, 0, 0))
    return pl.pallas_call(
        functools.partial(cache_kernel, slots),
        grid_spec=pltpu.PrefetchScalarGridSpec(
            num_scalar_prefetch=3,
            grid=(requests,),
            in_specs=[one(tok_block, 0)] * slots
            + [one(cache_block, begin)] * 2
            + [one(tok_block, begin)],
            out_specs=[
                one(tokens, 0),
                pl.BlockSpec((1, width, tokens), lambda r, *_: (r, 0, 0)),
                stat,
                stat,
            ],
        ),
        out_shape=[
            jax.ShapeDtypeStruct((requests, tokens, width), jnp.bfloat16),
            jax.ShapeDtypeStruct((requests, width, tokens), jnp.bfloat16),
            jax.ShapeDtypeStruct((requests, heads, tokens), jnp.float32),
            jax.ShapeDtypeStruct((requests, heads, tokens), jnp.float32),
        ],
        compiler_params=pltpu.CompilerParams(vmem_limit_bytes=VMEM_BYTES),
        cost_estimate=LIGHT,
        name="cache_part",
    )(first, places, live, *query_slots, keys, values, new_keys)


def finish_kernel(slots, filled, first_ref, place_ref, *refs):
    query_ref, key_ref, value_ref, cache_ref, peak_ref, total_ref, best_ref = refs[:7]
    sum_ref, *part_refs = refs[7 + filled : -1]
    joined_ref = refs[-1]
    tok_block = key_ref.shape[1]
    for head in range(query_ref.shape[2] // HEAD_DIM):
        at = slice(head * HEAD_DIM, (head + 1) * HEAD_DIM)
        row = slice(head, head + 1)
        scores = group_scores(first_ref[0], key_ref[0, :, at], query_ref[0, :, at])
        best = best_ref[0, row, :]
        weights = jnp.exp2((scores - best) * EXP2_SCALE)
        rescale = jnp.exp2((peak_ref[0, row, :] - best) * EXP2_SCALE)
        sum_ref[0, row, :] = total_ref[0, row, :] * rescale + jnp.sum(
            weights, axis=0, keepdims=True
        )
        joined = cache_ref[0, at, :].astype(jnp.float32) * rescale + dot_tn(
            value_ref[0, :, at], weights.astype(jnp.bfloat16)
        )
        joined_ref[:, at] = joined.astype(jnp.bfloat16).T
    for slot in range(slots):
        start = pl.multiple_of(place_ref[slot] * tok_block, tok_block)
        part_refs[slot][0] = joined_ref[pl.ds(start, tok_block), :]


def finish_part(begin, at, count, first, places, queries, new_keys, new_values, cached, peaks, totals, best, filled=()):
    requests, tokens, width = queries.shape
    tok_block = new_keys.shape[1]
    slots = tokens // tok_block
    heads = width // HEAD_DIM
    one = lambda rows, start: pl.BlockSpec((1, rows, width), lambda r, *_: (r + start, 0, 0))
    stat = lambda start: pl.BlockSpec((1, heads, tokens), lambda r, *_: (r + start, 0, 0))
    inputs = (queries, new_keys, new_values, cached, peaks, totals, best)
    return pl.pallas_call(
        functools.partial(finish_kernel, slots, len(filled)),
        grid_spec=pltpu.PrefetchScalarGridSpec(
            num_scalar_prefetch=2,
            grid=(count,),
            in_specs=[
                one(tokens, at),
                one(tok_block, begin + at),
                one(tok_block, begin + at),
                pl.BlockSpec((1, width, tokens), lambda r, *_: (r + at, 0, 0)),
                stat(at),
                stat(at),
                stat(begin + at),
            ]
            + [pl.BlockSpec(memory_space=pl.ANY)] * len(filled),
            out_specs=[stat(at)] + [one(tok_block, at)] * slots,
            scratch_shapes=[pltpu.VMEM((tokens, width), jnp.bfloat16)],
        ),
        out_shape=[jax.ShapeDtypeStruct((requests, heads, tokens), jnp.float32)]
        + [jax.ShapeDtypeStruct((requests, tok_block, width), jnp.bfloat16)] * slots,
        input_output_aliases={2 + len(inputs) + i: i for i in range(len(filled))},
        compiler_params=pltpu.CompilerParams(vmem_limit_bytes=VMEM_BYTES),
        cost_estimate=pl.CostEstimate(
            flops=4 * count * tokens * tok_block * width,
            bytes_accessed=6 * count * width * tokens,
            transcendentals=count * tokens * tok_block * heads,
        ),
        name="finish_part",
    )(first, places, *inputs, *filled)


def leave_attention_kernel(order_ref, *refs):
    ahead_ref, back_ref, own_ref, sums_ref, weight_ref, terms_ref, give_ref, keep_ref, attended_ref = refs
    step = pl.program_id(0)

    @pl.when(step == 0)
    def _():
        for head in range(attended_ref.shape[1] // HEAD_DIM):
            at = slice(head * HEAD_DIM, (head + 1) * HEAD_DIM)
            total = ahead_ref[:, at].astype(jnp.float32) + back_ref[:, at].astype(jnp.float32)
            total = total + own_ref[:, at].astype(jnp.float32)
            attended_ref[:, at] = (total / sums_ref[:, head : head + 1]).astype(jnp.bfloat16)

    terms = terms_ref[...] + jnp.dot(
        attended_ref[...], weight_ref[...], preferred_element_type=jnp.float32
    )

    @pl.when(step < 2)
    def _():
        give_ref[...] = terms.astype(jnp.bfloat16)

    @pl.when(step >= 2)
    def _():
        keep_ref[...] = terms


def leave_attention(order, index, ahead, back, own, sums, weight, terms):
    rows, width = ahead.shape
    heads = sums.shape[1]
    block = weight.shape[1] // 4
    whole = lambda *shape: pl.BlockSpec(shape, lambda j, *_: (0, 0))
    return pl.pallas_call(
        leave_attention_kernel,
        grid_spec=pltpu.PrefetchScalarGridSpec(
            num_scalar_prefetch=1,
            grid=(4,),
            in_specs=[
                whole(rows, width),
                whole(rows, width),
                whole(rows, width),
                whole(rows, heads),
                pl.BlockSpec((width, block), lambda j, order_ref: (0, order_ref[j])),
                pl.BlockSpec((rows, block), lambda j, order_ref: (index, order_ref[j])),
            ],
            out_specs=[
                pl.BlockSpec((rows, block), lambda j, *_: (0, jnp.minimum(j, 1))),
                pl.BlockSpec((rows, block), lambda j, *_: (0, jnp.maximum(j - 2, 0))),
            ],
            scratch_shapes=[pltpu.VMEM((rows, width), jnp.bfloat16)],
        ),
        out_shape=[
            jax.ShapeDtypeStruct((rows, 2 * block), jnp.bfloat16),
            jax.ShapeDtypeStruct((rows, 2 * block), jnp.float32),
        ],
        compiler_params=pltpu.CompilerParams(vmem_limit_bytes=VMEM_BYTES),
        cost_estimate=LIGHT,
        name="leave_attention",
    )(order, ahead, back, own, sums, weight, terms)


def head_sum(give, keep):
    width = keep.shape[1] // 2
    got = lax.ppermute(give, "head", [(h, h ^ 1) for h in range(4)]).astype(jnp.float32)
    leaving = (keep[:, width:] + got[:, width:]).astype(jnp.bfloat16)
    last = lax.ppermute(leaving, "head", [(h, h ^ 2) for h in range(4)]).astype(jnp.float32)
    return keep[:, :width] + got[:, :width] + last


class Relay:
    def __init__(self, through, local, initial, seq_index, seq_count):
        self.factor, self.local = through, local
        self.paired = seq_count == 8
        self.hop = 0
        if not self.paired:
            self.hops = seq_count - 1
            self.entry = jnp.where(seq_index == 0, initial, 0.0)
            return
        self.hops = 3
        self.swap = [(i, i ^ 1) for i in range(8)]
        self.is_first = is_first = seq_index % 2 == 0
        half = local.shape[2] // 2
        side = lambda value: jnp.where(is_first, value[..., :half], value[..., half:])
        mine = side(local)
        got = self.exchange(jnp.where(is_first, local[..., half:], local[..., :half]))
        other_factor = side(lax.ppermute(through, "seq", self.swap))
        factor = side(through)
        self.first_state = jnp.where(is_first, mine, got)
        second_state = jnp.where(is_first, got, mine)
        self.first_factor = jnp.where(is_first, factor, other_factor)
        second_factor = jnp.where(is_first, other_factor, factor)
        self.pair_state = second_factor * self.first_state + second_state
        self.pair_factor = self.first_factor * second_factor
        self.entry = jnp.where(seq_index < 2, side(initial), 0.0)

    def exchange(self, value):
        return lax.ppermute(value.astype(jnp.bfloat16), "seq", self.swap).astype(jnp.float32)

    def advance(self, clock):
        if self.hop == self.hops:
            return
        factor, state = (
            (self.pair_factor, self.pair_state) if self.paired else (self.factor, self.local)
        )
        entry = clock.hold(self.entry)
        leaving = (factor * entry + state).astype(jnp.bfloat16)
        if self.paired:
            route = [(2 * self.hop + y, 2 * self.hop + 2 + y) for y in range(2)]
        else:
            route = [(self.hop, self.hop + 1)]
        self.hop += 1
        self.entry = entry + lax.ppermute(leaving, "seq", route).astype(jnp.float32)

    def result(self, clock):
        while self.hop < self.hops:
            self.advance(clock)
        entry = clock.hold(self.entry)
        if not self.paired:
            return entry
        second = self.first_factor * entry + self.first_state
        got = self.exchange(jnp.where(self.is_first, second, entry))
        mine = jnp.where(self.is_first, entry, second)
        return jnp.concatenate(
            [jnp.where(self.is_first, mine, got), jnp.where(self.is_first, got, mine)], axis=2
        )


def shards(
    block_input,
    lengths,
    cache_keys,
    cache_values,
    w_query,
    w_key,
    w_value,
    w_attn_out,
    norm_gain,
    w_in,
    w_bc,
    w_dt,
    dt_bias,
    a_log,
    d_skip,
    gated_gain,
    w_out,
    ssm_init,
):
    requests, tok_block, _ = block_input.shape
    seq_count = lax.axis_size("seq")
    seq_index = lax.axis_index("seq")
    head_count = lax.axis_size("head")
    head_index = lax.axis_index("head")
    local_att = w_query.shape[1]
    local_heads = local_att // HEAD_DIM
    cache_block = cache_keys.shape[1]
    rows = w_query.shape[0]
    tokens = requests * tok_block
    flat_input = block_input.reshape(tokens, block_input.shape[2])

    order = ring_order(seq_count)
    half = seq_count // 2
    offsets = [0] + [sign * step for step in range(1, half) for sign in (1, -1)] + [half]
    places = jnp.asarray(
        [
            [order[(order.index(i) - offset) % seq_count] for offset in offsets]
            for i in range(seq_count)
        ],
        jnp.int32,
    )[seq_index]

    positions = (
        lengths[:, None] + seq_index * tok_block + jnp.arange(tok_block, dtype=jnp.int32)[None, :]
    ).reshape(tokens)
    half_dim = HEAD_DIM // 2
    frequency = jnp.exp(
        jnp.arange(half_dim, dtype=jnp.float32) * (-2.0 * math.log(10000.0) / HEAD_DIM)
    )
    angles = positions.astype(jnp.float32)[:, None] * frequency
    cosine = jnp.cos(angles)
    sine = jnp.sin(angles)
    cosine = jnp.concatenate([cosine, cosine], axis=1)
    sine = jnp.concatenate([-sine, sine], axis=1)

    clock = Clock(jnp.zeros((1,), jnp.int32) + lengths[:1])
    group = requests // GROUPS
    local_inner = w_in.shape[2]
    local_mheads = local_inner // MHEAD_DIM
    local_width = D // head_count
    made = {}

    def product(pieces, turned, base=(), kind=jnp.bfloat16):
        pieces = list(pieces)
        if pieces[-1][2].shape[0] < 128:
            (offset, row, upper), (_, _, lower) = pieces[-2:]
            pieces[-2:] = [(offset, row, jnp.concatenate([upper, lower], axis=0))]
        return project(
            places, offsets, rows, flat_input, pieces, cosine, sine, turned, base, kind
        )

    by_request = lambda value: value.reshape(requests, tok_block, local_att)

    def prepare():
        made["w_in"] = w_in.reshape(D, 2 * local_inner)
        first_state = ssm_init.reshape(requests, local_mheads, MHEAD_DIM, STATE)
        made["initial"] = jnp.transpose(first_state, (0, 3, 1, 2)).reshape(
            requests, STATE, local_inner
        )
        return (made["w_in"], made["initial"]), ()

    def enter():
        made["act"], made["maps"], size = enter_mixer(
            clock.hold(flat_input), norm_gain, w_bc, w_dt, dt_bias, made["w_in"]
        )
        size = size.reshape(requests, tok_block, local_mheads)
        log_decay = -size * jnp.exp(a_log)
        causal = jnp.arange(tok_block)[None, :] <= jnp.arange(tok_block)[:, None]
        decay = jnp.einsum(
            "tu,ruh->rth", causal.astype(jnp.float32), log_decay, precision=lax.Precision.HIGHEST
        )
        by_row = lambda value: jnp.transpose(value, (0, 2, 1)).reshape(
            requests, 1, local_mheads * tok_block
        )
        made["size"], made["decay"] = size, decay
        made["size_row"], made["decay_row"] = by_row(size), by_row(decay)
        return (made["act"], made["size_row"], made["decay_row"]), ()

    def inside():
        made["read"], made["local"], made["through"] = inside_block(
            requests,
            clock.hold(made["act"]),
            made["maps"],
            made["decay"],
            made["size"],
            made["decay_row"],
            made["size_row"],
            jnp.repeat(d_skip, MHEAD_DIM).reshape(1, local_inner),
        )
        return (made["read"], made["local"]), ()

    def start_relay():
        made["relay"] = relay = Relay(
            made["through"], clock.hold(made["local"]), made["initial"], seq_index, seq_count
        )
        return (), ((relay.pair_state,) if relay.paired else ())

    def hop():
        made["relay"].advance(clock)
        return (), (made["relay"].entry,)

    def end_relay():
        made["entry"] = made["relay"].result(clock)
        return (), (made["entry"],)

    def leave():
        gated, squares, chain = leave_mixer(
            clock.hold(made["entry"]),
            made["maps"],
            made["decay"],
            made["read"],
            made["act"],
            gated_gain.reshape(1, local_inner),
            made["local"],
            made["through"],
        )
        made["gated"] = gated
        made["squares"] = Exchange(
            squares[:, :1].reshape(1, tokens), "head", head_count, jnp.add
        )
        made["squares"].step(clock)
        made["chain"] = chain
        return (gated,), ()

    def join_squares():
        made["squares"].step(clock)
        return (), ()

    def leave_terms():
        squares = made["squares"].result(clock).reshape(tokens, 1)
        made["terms"] = jnp.dot(
            clock.hold(made["gated"]), w_out, preferred_element_type=jnp.float32
        ) * lax.rsqrt(squares / D_INNER + 1e-05)
        return (made["terms"],), ()

    def chain_split():
        made["chain"] = clock.hold(made["chain"]).reshape(
            requests, STATE, local_mheads, MHEAD_DIM
        )
        return (made["chain"],), ()

    def chain_turn():
        made["chain"] = jnp.transpose(clock.hold(made["chain"]), (0, 2, 3, 1))
        return (made["chain"],), ()

    def chain_join():
        made["chain"] = clock.hold(made["chain"]).reshape(
            requests, 1, local_mheads, MHEAD_DIM * STATE
        )
        return (made["chain"],), ()

    query_ring, key_ring, value_ring = (Ring(w, order) for w in (w_query, w_key, w_value))
    slot_rings = []
    live = jnp.clip(lengths - seq_index * cache_block, 0, cache_block).astype(jnp.int32)
    first = (seq_index * tok_block).astype(jnp.int32).reshape(1)
    cached = []

    def make_queries():
        queries = by_request(product(query_ring.pieces, True))
        slot_rings.extend(
            Ring(queries[begin : begin + group], order) for begin in range(0, requests, group)
        )
        return (queries,), ()

    def make_keys():
        made["keys"] = by_request(product(key_ring.pieces, True))
        return (made["keys"],), ()

    def meet_cache(index):
        def work():
            ring = slot_rings[index]
            begin = index * group
            slots = [piece for _, _, piece in ring.pieces[:-2]]
            slots.append(jnp.concatenate([ring.pieces[-2][2], ring.pieces[-1][2]], axis=0))
            slots[0] = clock.hold(slots[0])
            cached.append(
                cache_part(
                    begin,
                    first,
                    places,
                    live[begin : begin + group],
                    slots,
                    cache_keys,
                    cache_values,
                    made["keys"],
                )
            )
            return tuple(cached[-1]), ()

        return work

    def join_peaks():
        peaks = jnp.concatenate([clock.hold(part[2]) for part in cached], axis=0)
        made["best"] = Exchange(peaks, "seq", seq_count, jnp.maximum)
        made["best"].step(clock)
        pieces = value_ring.pieces[1:-2]
        made["used"] = 1 + len(pieces)
        made["values"] = product(
            [(0, 0, clock.hold(value_ring.block))] + pieces, False, kind=jnp.float32
        )
        return (made["values"],) + leave_terms()[0], ()

    def join_more():
        made["best"].step(clock)
        return (), ()

    def steps(rings, begin, end):
        return [ring for _ in range(begin, end) for ring in rings]

    def run(sends, works):
        for index in range(max(len(sends), len(works))):
            clock.turn(
                sends[index] if index < len(sends) else None,
                works[index] if index < len(works) else None,
            )

    both = steps([query_ring, key_ring], 0, half - 2) + [query_ring] * 2 + [key_ring] * 2
    def make_queries_hop():
        done, _ = make_queries()
        return done, hop()[1]

    def make_keys_hop():
        deferred = hop()[1]
        return make_keys()[0], deferred

    works = [prepare, enter, inside, start_relay, None, hop]
    run(both, works + [None] * (len(both) - 1 - len(works)) + [make_queries_hop])
    run(
        steps(slot_rings, 0, half),
        [None, make_keys_hop, None, end_relay, None, leave, join_squares],
    )
    run(
        steps([value_ring], 0, half),
        [meet_cache(0), meet_cache(1)] + [None] * (half - 4) + [join_peaks, join_more],
    )

    new_keys = made["keys"]
    best = made["best"].result(clock)
    new_values = by_request(
        product(value_ring.pieces[made["used"] :], False, base=(made["values"],))
    )

    own = lambda stat: lax.dynamic_slice_in_dim(stat, seq_index * tok_block, tok_block, 2)
    greatest_logit = jnp.transpose(own(best), (0, 2, 1)) * SCALE
    residual = lax.dynamic_slice_in_dim(
        flat_input, head_index * local_width, local_width, 1
    ).astype(jnp.float32)
    mixed = []

    filled = {}

    def finish(index, at, count):
        def work():
            joined, out, peaks, totals = cached[index]
            filled[index] = finish_part(
                index * group,
                at,
                count,
                first,
                places,
                clock.hold(joined),
                new_keys,
                new_values,
                out,
                peaks,
                totals,
                best,
                filled.get(index, ()),
            )
            return tuple(filled[index]), ()

        return work

    def ring_sum(index):
        terms = {-offset: part for offset, part in zip(offsets, filled[index][1:])}
        terms[half] = terms[-half]
        return RingSum(terms, order)

    def add_sums():
        if "sums" not in made:
            sums = jnp.concatenate([filled[index][0] for index in range(GROUPS)], axis=0)
            made["sums"] = Exchange(sums, "seq", seq_count, jnp.add)
        made["sums"].step(clock)
        return (), ()

    def together(*works):
        def work():
            done = [work() for work in works]
            return sum((d for d, _ in done), ()), sum((d for _, d in done), ())

        return work

    run([], [finish(0, 0, group)])
    sum_rings = [ring_sum(0)]
    run(sum_rings, [finish(1, 0, group // 2)])
    clock.mark = clock.hold(clock.mark, sum_rings[0].ahead)[0]
    run([], [finish(1, group // 2, group - group // 2)])
    sum_rings.append(ring_sum(1))
    run(
        steps(sum_rings[::-1], 0, half)[:-1],
        [
            together(add_sums, chain_split),
            chain_turn,
            together(add_sums, chain_join),
            None,
            add_sums,
        ],
    )
    denominators = jnp.transpose(own(made["sums"].result(clock)), (0, 2, 1)).reshape(
        tokens, local_heads
    )
    if head_count == 4:
        core, column = head_index % 2, head_index // 2
        near, far = 2 * column, 2 * (1 - column)
        blocks = jnp.stack([near + 1 - core, far + 1 - core, near + core, far + core])
    else:
        blocks = jnp.arange(4)
    group_rows = group * tok_block
    for index in range(GROUPS):
        at = slice(index * group_rows, (index + 1) * group_rows)
        ring = sum_rings[index]
        give, keep = leave_attention(
            blocks.astype(jnp.int32),
            index,
            *(
                value.reshape(group_rows, local_att)
                for value in (ring.ahead, ring.back, ring.parts[0])
            ),
            denominators[at],
            w_attn_out,
            made["terms"],
        )
        if head_count == 4:
            summed = head_sum(give, keep)
        else:
            summed = lax.psum_scatter(
                jnp.concatenate([give, keep.astype(jnp.bfloat16)], axis=1),
                "head",
                scatter_dimension=1,
                tiled=True,
            ).astype(jnp.float32)
        mixed.append(
            (residual[at] + summed)
            .astype(jnp.bfloat16)
            .reshape(group, tok_block, local_width)
        )
    return (
        jnp.concatenate(mixed, axis=0),
        new_keys,
        new_values,
        made["chain"],
        greatest_logit,
    )


def solution(mesh):
    placed = (
        P(None, "seq", None),
        P(),
        P(None, "seq", "head"),
        P(None, "seq", "head"),
        P("seq", "head"),
        P("seq", "head"),
        P("seq", "head"),
        P("head", None),
        P(),
        P(None, None, "head"),
        P(),
        P(None, "head"),
        P("head"),
        P("head"),
        P("head"),
        P("head"),
        P("head", None),
        P(None, "head", None),
    )
    return jax.shard_map(
        shards,
        mesh=mesh,
        in_specs=placed,
        out_specs=(
            P(None, "seq", "head"),
            P(None, "seq", "head"),
            P(None, "seq", "head"),
            P(None, "seq", "head", None),
            P(None, "seq", "head"),
        ),
        check_vma=False,
    )
```

```python
import functools
import math

import jax
import jax.numpy as jnp
from jax import lax
from jax.experimental import pallas as pl
from jax.experimental.pallas import tpu as pltpu
from jax.sharding import PartitionSpec as P

D = 2048
HEAD_DIM = 128
MHEAD_DIM = 64
STATE = 64
D_INNER = 4096
SCALE = 1.0 / math.sqrt(HEAD_DIM)
EXP2_SCALE = SCALE * math.log2(math.e)
DEAD = -1e30
GROUPS = 2
VMEM_BYTES = 56 * 1024 * 1024
LIGHT = pl.CostEstimate(flops=0, bytes_accessed=0, transcendentals=0)


def ring_order(count):
    y_count = max(1, count // 4)
    z_count = count // y_count
    order = []
    for y in range(y_count):
        turn = range(z_count) if y % 2 == 0 else range(z_count - 1, -1, -1)
        order += [z * y_count + y for z in turn]
    return order


def ring_step(block, order, distance):
    count = len(order)
    route = [(order[i], order[(i + distance) % count]) for i in range(count)]
    return lax.ppermute(block, "seq", route)


class Ring:
    def __init__(self, block, order, first_row=0):
        self.order = order
        self.steps = len(order) // 2
        self.done = 0
        self.first_row = first_row
        self.block = self.ahead = self.back = block
        self.pieces = [(0, first_row, block)]

    def step(self, clock):
        self.done += 1
        half = self.block.shape[0] // 2
        last = self.done == self.steps
        ahead = self.ahead[:half] if last else self.ahead
        back = self.back[half:] if last else self.back
        ahead, back = clock.hold(ahead, back)
        self.ahead = ring_step(ahead, self.order, 1)
        self.back = ring_step(back, self.order, -1)
        at = self.first_row
        if last:
            self.pieces += [(self.steps, at, self.ahead), (self.steps, at + half, self.back)]
        else:
            self.pieces += [(self.done, at, self.ahead), (-self.done, at, self.back)]
        return [self.ahead, self.back]


class Clock:
    def __init__(self, mark):
        self.mark = mark
        self.late = ()

    def hold(self, *values):
        held = lax.optimization_barrier(tuple(values) + (self.mark,))[: len(values)]
        return held[0] if len(values) == 1 else held

    def turn(self, ring=None, work=None):
        moved = tuple(ring.step(self)) if ring is not None else ()
        done, deferred = work() if work is not None else ((), ())
        self.mark = lax.optimization_barrier((self.mark,) + self.late + tuple(done))[0]
        self.late = moved + tuple(deferred)


class Exchange:
    def __init__(self, value, axis, count, combine):
        self.value, self.axis, self.count, self.combine = value, axis, count, combine
        self.got = None
        self.bit = 1

    def join(self, clock):
        if self.got is not None:
            self.value = self.combine(*clock.hold(self.value, self.got))
            self.got = None

    def step(self, clock):
        self.join(clock)
        if self.bit < self.count:
            route = [(i, i ^ self.bit) for i in range(self.count)]
            self.got = lax.ppermute(self.value, self.axis, route)
            self.bit *= 2

    def result(self, clock):
        while self.bit < self.count:
            self.step(clock)
        self.join(clock)
        return self.value


class RingSum:
    def __init__(self, parts, order):
        self.parts, self.order = parts, order
        self.left = len(order) // 2
        self.half = parts[0].shape[0] // 2
        self.ahead = self.back = None

    def add(self, a, b):
        return (a.astype(jnp.float32) + b.astype(jnp.float32)).astype(jnp.bfloat16)

    def step(self, clock):
        half, left, far = self.half, self.left, len(self.order) // 2
        top, bottom = self.parts[left], self.parts[-left]
        if left == far:
            ahead, back = top[:half], bottom[half:]
        elif left == far - 1:
            ahead = jnp.concatenate([self.add(self.ahead, top[:half]), top[half:]], axis=0)
            back = jnp.concatenate([bottom[:half], self.add(self.back, bottom[half:])], axis=0)
        else:
            ahead, back = self.add(self.ahead, top), self.add(self.back, bottom)
        ahead, back = clock.hold(ahead, back)
        self.ahead = ring_step(ahead, self.order, 1)
        self.back = ring_step(back, self.order, -1)
        self.left -= 1
        return [self.ahead, self.back]

    def total(self):
        return sum(value.astype(jnp.float32) for value in (self.ahead, self.back, self.parts[0]))


def project_kernel(count, turned, places_ref, *refs):
    input_refs, weight_refs = refs[:count], refs[count : 2 * count]
    cosine_ref, sine_ref, *base_ref, out_ref = refs[2 * count :]
    total = base_ref[0][...] if base_ref else None
    for input_ref, weight_ref in zip(input_refs, weight_refs):
        term = jnp.dot(input_ref[...], weight_ref[...], preferred_element_type=jnp.float32)
        total = term if total is None else total + term
    if not turned:
        out_ref[...] = total.astype(out_ref.dtype)
        return
    cosine = cosine_ref[...]
    sine = sine_ref[...]
    for head in range(out_ref.shape[1] // HEAD_DIM):
        at = slice(head * HEAD_DIM, (head + 1) * HEAD_DIM)
        part = total[:, at]
        rolled = pltpu.roll(part, HEAD_DIM // 2, 1)
        out_ref[:, at] = (part * cosine + rolled * sine).astype(out_ref.dtype)


def project(places, offsets, rows, value, pieces, cosine, sine, turned, base=(), kind=jnp.bfloat16):
    tokens = value.shape[0]
    width = pieces[0][2].shape[1]
    block = min(width, 256)
    input_specs, weight_specs = [], []
    for offset, row, piece in pieces:
        depth = piece.shape[0]

        def place(j, places_ref, slot=offsets.index(offset), scale=rows // depth, at=row // depth):
            return (0, places_ref[slot] * scale + at)

        input_specs.append(pl.BlockSpec((tokens, depth), place))
        weight_specs.append(pl.BlockSpec((depth, block), lambda j, *_: (0, j)))
    angle = pl.BlockSpec((tokens, HEAD_DIM), lambda j, *_: (0, 0))
    return pl.pallas_call(
        functools.partial(project_kernel, len(pieces), turned),
        grid_spec=pltpu.PrefetchScalarGridSpec(
            num_scalar_prefetch=1,
            grid=(width // block,),
            in_specs=input_specs
            + weight_specs
            + [angle, angle]
            + [pl.BlockSpec((tokens, block), lambda j, *_: (0, j))] * len(base),
            out_specs=pl.BlockSpec((tokens, block), lambda j, *_: (0, j)),
        ),
        out_shape=jax.ShapeDtypeStruct((tokens, width), kind),
        compiler_params=pltpu.CompilerParams(vmem_limit_bytes=VMEM_BYTES),
        cost_estimate=LIGHT,
        name="project",
    )(places, *[value] * len(pieces), *[piece for _, _, piece in pieces], cosine, sine, *base)


def silu(value):
    return value / (1.0 + jnp.exp(-value))


def exact_dot(a, b):
    return jnp.dot(a, b, precision=lax.Precision.HIGHEST, preferred_element_type=jnp.float32)


def spread(heads, block):
    shape = (heads, heads * block)
    column = lax.broadcasted_iota(jnp.int32, shape, 1) // block
    return (column == lax.broadcasted_iota(jnp.int32, shape, 0)).astype(jnp.float32)


def enter_kernel(input_ref, gain_ref, bc_ref, dt_ref, bias_ref, weight_ref, act_ref, map_ref, size_ref, normed_ref):
    @pl.when(pl.program_id(0) == 0)
    def _():
        rows = input_ref.shape[0]
        chunk = min(rows, 64)
        for start in range(0, rows, chunk):
            at = slice(start, start + chunk)
            hidden = input_ref[at, :].astype(jnp.float32)
            scale = lax.rsqrt(jnp.mean(hidden * hidden, axis=-1, keepdims=True) + 1e-05)
            normed_ref[at, :] = (hidden * scale * gain_ref[...]).astype(jnp.bfloat16)
        normed = normed_ref[...]
        map_ref[...] = jnp.dot(normed, bc_ref[...], preferred_element_type=jnp.float32)
        size = jnp.dot(normed, dt_ref[...], preferred_element_type=jnp.float32) + bias_ref[...]
        size_ref[...] = jnp.maximum(size, 0.0) + jnp.log1p(jnp.exp(-jnp.abs(size)))

    act_ref[...] = silu(
        jnp.dot(normed_ref[...], weight_ref[...], preferred_element_type=jnp.float32)
    )


def enter_mixer(flat_input, norm_gain, w_bc, w_dt, dt_bias, weight):
    tokens = flat_input.shape[0]
    width = weight.shape[1]
    block = min(width, 512)
    heads = w_dt.shape[1]
    whole = lambda *shape: pl.BlockSpec(shape, lambda j: (0, 0))
    return pl.pallas_call(
        enter_kernel,
        grid=(width // block,),
        in_specs=[
            whole(tokens, D),
            whole(1, D),
            whole(D, 2 * STATE),
            whole(D, heads),
            whole(1, heads),
            pl.BlockSpec((D, block), lambda j: (0, j)),
        ],
        out_specs=[
            pl.BlockSpec((tokens, block), lambda j: (0, j)),
            whole(tokens, 2 * STATE),
            whole(tokens, heads),
        ],
        out_shape=[
            jax.ShapeDtypeStruct((tokens, width), jnp.float32),
            jax.ShapeDtypeStruct((tokens, 2 * STATE), jnp.float32),
            jax.ShapeDtypeStruct((tokens, heads), jnp.float32),
        ],
        scratch_shapes=[pltpu.VMEM((tokens, D), jnp.bfloat16)],
        compiler_params=pltpu.CompilerParams(vmem_limit_bytes=VMEM_BYTES),
        cost_estimate=LIGHT,
        name="enter_mixer",
    )(flat_input, norm_gain.reshape(1, D), w_bc, w_dt, dt_bias.reshape(1, heads), weight)


def inside_kernel(inner_ref, map_ref, decay_ref, size_ref, decay_row_ref, size_row_ref, skip_ref, read_ref, local_ref, through_ref):
    tokens, heads = decay_ref.shape[1:]
    inner = inner_ref[...]
    input_map = map_ref[:, :STATE]
    output_map = map_ref[:, STATE:]
    decay = decay_ref[0]
    by_head = spread(heads, MHEAD_DIM)
    wide = (tokens, heads * tokens)
    contact = dot_nt(
        output_map.astype(jnp.bfloat16),
        jnp.concatenate([input_map.astype(jnp.bfloat16)] * heads, axis=0),
    )
    source = lax.rem(lax.broadcasted_iota(jnp.int32, wide, 1), tokens)
    causal = source <= lax.broadcasted_iota(jnp.int32, wide, 0)
    difference = exact_dot(decay, spread(heads, tokens)) - decay_row_ref[0]
    mixing = jnp.exp(jnp.where(causal, difference, DEAD)) * contact * size_row_ref[0]
    mixing = mixing.astype(jnp.bfloat16)
    inner_low = inner.astype(jnp.bfloat16)
    together = min(heads, 256 // MHEAD_DIM)
    shape = (together * tokens, together * MHEAD_DIM)
    own = (
        lax.broadcasted_iota(jnp.int32, shape, 0) // tokens
        == lax.broadcasted_iota(jnp.int32, shape, 1) // MHEAD_DIM
    )
    for begin in range(0, heads, together):
        at = slice(begin * MHEAD_DIM, (begin + together) * MHEAD_DIM)
        stacked = jnp.concatenate([inner_low[:, at]] * together, axis=0)
        stacked = jnp.where(own, stacked, jnp.zeros_like(stacked))
        read_ref[:, at] = (
            jnp.dot(
                mixing[:, begin * tokens : (begin + together) * tokens],
                stacked,
                preferred_element_type=jnp.float32,
            )
            + skip_ref[:, at] * inner[:, at]
        )
    last = decay[tokens - 1 :, :]
    tail = exact_dot(jnp.exp(last - decay) * size_ref[0], by_head)
    local_ref[0] = dot_tn(input_map.astype(jnp.bfloat16), (inner * tail).astype(jnp.bfloat16))
    through_ref[0] = exact_dot(jnp.exp(jnp.broadcast_to(last, (8, heads))), by_head)[:1]


def inside_block(requests, act, maps, decay, size, decay_row, size_row, skip):
    tokens, heads = decay.shape[1:]
    inner = act.shape[1] // 2
    one = lambda *shape: pl.BlockSpec((1,) + shape, lambda r: (r, 0, 0))
    return pl.pallas_call(
        inside_kernel,
        grid=(requests,),
        in_specs=[
            pl.BlockSpec((tokens, inner), lambda r: (r, 1)),
            pl.BlockSpec((tokens, 2 * STATE), lambda r: (r, 0)),
            one(tokens, heads),
            one(tokens, heads),
            one(1, heads * tokens),
            one(1, heads * tokens),
            pl.BlockSpec((1, inner), lambda r: (0, 0)),
        ],
        out_specs=[
            pl.BlockSpec((tokens, inner), lambda r: (r, 0)),
            one(STATE, inner),
            one(1, inner),
        ],
        out_shape=[
            jax.ShapeDtypeStruct((requests * tokens, inner), jnp.float32),
            jax.ShapeDtypeStruct((requests, STATE, inner), jnp.float32),
            jax.ShapeDtypeStruct((requests, 1, inner), jnp.float32),
        ],
        compiler_params=pltpu.CompilerParams(vmem_limit_bytes=VMEM_BYTES),
        cost_estimate=LIGHT,
        name="inside_block",
    )(act, maps, decay, size, decay_row, size_row, skip)


def leave_kernel(entry_ref, map_ref, decay_ref, read_ref, gate_ref, gain_ref, local_ref, through_ref, gated_ref, square_ref, chain_ref):
    heads = decay_ref.shape[2]
    entry = entry_ref[0]
    grown = exact_dot(jnp.exp(decay_ref[0]), spread(heads, MHEAD_DIM))
    inter = jnp.dot(
        map_ref[:, STATE:].astype(jnp.bfloat16),
        entry.astype(jnp.bfloat16),
        preferred_element_type=jnp.float32,
    )
    mixed = (read_ref[...] + inter * grown) * gate_ref[...]
    squares = jnp.sum(mixed * mixed, axis=1, keepdims=True)
    square_ref[...] = jnp.broadcast_to(squares, square_ref.shape)
    gated_ref[...] = (mixed * gain_ref[...]).astype(jnp.bfloat16)
    chain_ref[0] = through_ref[0] * entry + local_ref[0]


def leave_mixer(entry, maps, decay, read, act, gain, local, through):
    requests, tokens, heads = decay.shape
    inner = read.shape[1]
    one = lambda *shape: pl.BlockSpec((1,) + shape, lambda r: (r, 0, 0))
    flat = lambda width: pl.BlockSpec((tokens, width), lambda r: (r, 0))
    return pl.pallas_call(
        leave_kernel,
        grid=(requests,),
        in_specs=[
            one(STATE, inner),
            flat(2 * STATE),
            one(tokens, heads),
            flat(inner),
            flat(inner),
            pl.BlockSpec((1, inner), lambda r: (0, 0)),
            one(STATE, inner),
            one(1, inner),
        ],
        out_specs=[flat(inner), flat(128), one(STATE, inner)],
        out_shape=[
            jax.ShapeDtypeStruct((requests * tokens, inner), jnp.bfloat16),
            jax.ShapeDtypeStruct((requests * tokens, 128), jnp.float32),
            jax.ShapeDtypeStruct((requests, STATE, inner), jnp.float32),
        ],
        compiler_params=pltpu.CompilerParams(vmem_limit_bytes=VMEM_BYTES),
        cost_estimate=LIGHT,
        name="leave_mixer",
    )(entry, maps, decay, read, act, gain, local, through)


def dot_nt(a, b):
    return lax.dot_general(a, b, (((1,), (1,)), ((), ())), preferred_element_type=jnp.float32)


def dot_tn(a, b):
    return lax.dot_general(a, b, (((0,), (0,)), ((), ())), preferred_element_type=jnp.float32)


def group_scores(first, key, query):
    scores = dot_nt(key, query)
    shape = scores.shape
    live = first + lax.broadcasted_iota(jnp.int32, shape, 0) <= lax.broadcasted_iota(
        jnp.int32, shape, 1
    )
    return jnp.where(live, scores, DEAD)


def cache_kernel(slots, first_ref, place_ref, live_ref, *refs):
    query_refs = refs[:slots]
    key_ref, value_ref, group_ref, joined_ref, out_ref, peak_ref, total_ref = refs[slots:]
    tok_block = query_refs[0].shape[1]
    keys, width = key_ref.shape[1:]
    tokens = tok_block * slots
    for slot in range(slots):
        start = pl.multiple_of(place_ref[slot] * tok_block, tok_block)
        joined_ref[0, pl.ds(start, tok_block), :] = query_refs[slot][0]
    live = live_ref[pl.program_id(0)]
    bias = jnp.where(
        lax.broadcasted_iota(jnp.int32, (keys, 128), 0) < live, 0.0, DEAD
    ).astype(jnp.float32)
    bias = jnp.concatenate([bias] * (tokens // 128), axis=1)
    for head in range(width // HEAD_DIM):
        at = slice(head * HEAD_DIM, (head + 1) * HEAD_DIM)
        query = joined_ref[0, :, at]
        scores = dot_nt(key_ref[0, :, at], query) + bias
        peak = jnp.maximum(
            jnp.max(scores, axis=0, keepdims=True),
            jnp.max(
                group_scores(first_ref[0], group_ref[0, :, at], query), axis=0, keepdims=True
            ),
        )
        weights = jnp.exp2((scores - peak) * EXP2_SCALE)
        total_ref[0, head : head + 1, :] = jnp.sum(weights, axis=0, keepdims=True)
        peak_ref[0, head : head + 1, :] = peak
        out_ref[0, at, :] = dot_tn(value_ref[0, :, at], weights.astype(jnp.bfloat16)).astype(
            out_ref.dtype
        )


def cache_part(begin, first, places, live, query_slots, keys, values, new_keys):
    slots = len(query_slots)
    requests, tok_block, width = query_slots[0].shape
    tokens = tok_block * slots
    cache_block = keys.shape[1]
    heads = width // HEAD_DIM
    one = lambda rows, start: pl.BlockSpec((1, rows, width), lambda r, *_: (r + start, 0, 0))
    stat = pl.BlockSpec((1, heads, tokens), lambda r, *_: (r, 0, 0))
    return pl.pallas_call(
        functools.partial(cache_kernel, slots),
        grid_spec=pltpu.PrefetchScalarGridSpec(
            num_scalar_prefetch=3,
            grid=(requests,),
            in_specs=[one(tok_block, 0)] * slots
            + [one(cache_block, begin)] * 2
            + [one(tok_block, begin)],
            out_specs=[
                one(tokens, 0),
                pl.BlockSpec((1, width, tokens), lambda r, *_: (r, 0, 0)),
                stat,
                stat,
            ],
        ),
        out_shape=[
            jax.ShapeDtypeStruct((requests, tokens, width), jnp.bfloat16),
            jax.ShapeDtypeStruct((requests, width, tokens), jnp.bfloat16),
            jax.ShapeDtypeStruct((requests, heads, tokens), jnp.float32),
            jax.ShapeDtypeStruct((requests, heads, tokens), jnp.float32),
        ],
        compiler_params=pltpu.CompilerParams(vmem_limit_bytes=VMEM_BYTES),
        cost_estimate=LIGHT,
        name="cache_part",
    )(first, places, live, *query_slots, keys, values, new_keys)


def finish_kernel(slots, filled, first_ref, place_ref, *refs):
    query_ref, key_ref, value_ref, cache_ref, peak_ref, total_ref, best_ref = refs[:7]
    sum_ref, *part_refs = refs[7 + filled : -1]
    joined_ref = refs[-1]
    tok_block = key_ref.shape[1]
    for head in range(query_ref.shape[2] // HEAD_DIM):
        at = slice(head * HEAD_DIM, (head + 1) * HEAD_DIM)
        row = slice(head, head + 1)
        scores = group_scores(first_ref[0], key_ref[0, :, at], query_ref[0, :, at])
        best = best_ref[0, row, :]
        weights = jnp.exp2((scores - best) * EXP2_SCALE)
        rescale = jnp.exp2((peak_ref[0, row, :] - best) * EXP2_SCALE)
        sum_ref[0, row, :] = total_ref[0, row, :] * rescale + jnp.sum(
            weights, axis=0, keepdims=True
        )
        joined = cache_ref[0, at, :].astype(jnp.float32) * rescale + dot_tn(
            value_ref[0, :, at], weights.astype(jnp.bfloat16)
        )
        joined_ref[:, at] = joined.astype(jnp.bfloat16).T
    for slot in range(slots):
        start = pl.multiple_of(place_ref[slot] * tok_block, tok_block)
        part_refs[slot][0] = joined_ref[pl.ds(start, tok_block), :]


def finish_part(begin, at, count, first, places, queries, new_keys, new_values, cached, peaks, totals, best, filled=()):
    requests, tokens, width = queries.shape
    tok_block = new_keys.shape[1]
    slots = tokens // tok_block
    heads = width // HEAD_DIM
    one = lambda rows, start: pl.BlockSpec((1, rows, width), lambda r, *_: (r + start, 0, 0))
    stat = lambda start: pl.BlockSpec((1, heads, tokens), lambda r, *_: (r + start, 0, 0))
    inputs = (queries, new_keys, new_values, cached, peaks, totals, best)
    return pl.pallas_call(
        functools.partial(finish_kernel, slots, len(filled)),
        grid_spec=pltpu.PrefetchScalarGridSpec(
            num_scalar_prefetch=2,
            grid=(count,),
            in_specs=[
                one(tokens, at),
                one(tok_block, begin + at),
                one(tok_block, begin + at),
                pl.BlockSpec((1, width, tokens), lambda r, *_: (r + at, 0, 0)),
                stat(at),
                stat(at),
                stat(begin + at),
            ]
            + [pl.BlockSpec(memory_space=pl.ANY)] * len(filled),
            out_specs=[stat(at)] + [one(tok_block, at)] * slots,
            scratch_shapes=[pltpu.VMEM((tokens, width), jnp.bfloat16)],
        ),
        out_shape=[jax.ShapeDtypeStruct((requests, heads, tokens), jnp.float32)]
        + [jax.ShapeDtypeStruct((requests, tok_block, width), jnp.bfloat16)] * slots,
        input_output_aliases={2 + len(inputs) + i: i for i in range(len(filled))},
        compiler_params=pltpu.CompilerParams(vmem_limit_bytes=VMEM_BYTES),
        cost_estimate=pl.CostEstimate(
            flops=4 * count * tokens * tok_block * width,
            bytes_accessed=6 * count * width * tokens,
            transcendentals=count * tokens * tok_block * heads,
        ),
        name="finish_part",
    )(first, places, *inputs, *filled)


def head_sum(terms, head_count, head_index):
    if head_count != 4:
        return lax.psum_scatter(
            terms.astype(jnp.bfloat16), "head", scatter_dimension=1, tiled=True
        ).astype(jnp.float32)
    width = terms.shape[1] // 4
    chunk = lambda index: lax.dynamic_slice_in_dim(terms, index * width, width, 1)
    core, column = head_index % 2, head_index // 2
    near, far = 2 * column, 2 * (1 - column)
    got = lax.ppermute(
        jnp.concatenate([chunk(near + 1 - core), chunk(far + 1 - core)], axis=1).astype(
            jnp.bfloat16
        ),
        "head",
        [(h, h ^ 1) for h in range(4)],
    ).astype(jnp.float32)
    keep = chunk(near + core) + got[:, :width]
    give = chunk(far + core) + got[:, width:]
    return keep + lax.ppermute(
        give.astype(jnp.bfloat16), "head", [(h, h ^ 2) for h in range(4)]
    ).astype(jnp.float32)


class Relay:
    def __init__(self, through, local, initial, seq_index, seq_count):
        self.factor, self.local = through, local
        self.paired = seq_count == 8
        self.hop = 0
        if not self.paired:
            self.hops = seq_count - 1
            self.entry = jnp.where(seq_index == 0, initial, 0.0)
            return
        self.hops = 3
        self.swap = [(i, i ^ 1) for i in range(8)]
        self.is_first = is_first = seq_index % 2 == 0
        half = local.shape[2] // 2
        side = lambda value: jnp.where(is_first, value[..., :half], value[..., half:])
        mine = side(local)
        got = self.exchange(jnp.where(is_first, local[..., half:], local[..., :half]))
        other_factor = side(lax.ppermute(through, "seq", self.swap))
        factor = side(through)
        self.first_state = jnp.where(is_first, mine, got)
        second_state = jnp.where(is_first, got, mine)
        self.first_factor = jnp.where(is_first, factor, other_factor)
        second_factor = jnp.where(is_first, other_factor, factor)
        self.pair_state = second_factor * self.first_state + second_state
        self.pair_factor = self.first_factor * second_factor
        self.entry = jnp.where(seq_index < 2, side(initial), 0.0)

    def exchange(self, value):
        return lax.ppermute(value.astype(jnp.bfloat16), "seq", self.swap).astype(jnp.float32)

    def advance(self, clock):
        if self.hop == self.hops:
            return
        factor, state = (
            (self.pair_factor, self.pair_state) if self.paired else (self.factor, self.local)
        )
        entry = clock.hold(self.entry)
        leaving = (factor * entry + state).astype(jnp.bfloat16)
        if self.paired:
            route = [(2 * self.hop + y, 2 * self.hop + 2 + y) for y in range(2)]
        else:
            route = [(self.hop, self.hop + 1)]
        self.hop += 1
        self.entry = entry + lax.ppermute(leaving, "seq", route).astype(jnp.float32)

    def result(self, clock):
        while self.hop < self.hops:
            self.advance(clock)
        entry = clock.hold(self.entry)
        if not self.paired:
            return entry
        second = self.first_factor * entry + self.first_state
        got = self.exchange(jnp.where(self.is_first, second, entry))
        mine = jnp.where(self.is_first, entry, second)
        return jnp.concatenate(
            [jnp.where(self.is_first, mine, got), jnp.where(self.is_first, got, mine)], axis=2
        )


def shards(
    block_input,
    lengths,
    cache_keys,
    cache_values,
    w_query,
    w_key,
    w_value,
    w_attn_out,
    norm_gain,
    w_in,
    w_bc,
    w_dt,
    dt_bias,
    a_log,
    d_skip,
    gated_gain,
    w_out,
    ssm_init,
):
    requests, tok_block, _ = block_input.shape
    seq_count = lax.axis_size("seq")
    seq_index = lax.axis_index("seq")
    head_count = lax.axis_size("head")
    head_index = lax.axis_index("head")
    local_att = w_query.shape[1]
    local_heads = local_att // HEAD_DIM
    cache_block = cache_keys.shape[1]
    rows = w_query.shape[0]
    tokens = requests * tok_block
    flat_input = block_input.reshape(tokens, block_input.shape[2])

    order = ring_order(seq_count)
    half = seq_count // 2
    offsets = [0] + [sign * step for step in range(1, half) for sign in (1, -1)] + [half]
    places = jnp.asarray(
        [
            [order[(order.index(i) - offset) % seq_count] for offset in offsets]
            for i in range(seq_count)
        ],
        jnp.int32,
    )[seq_index]

    positions = (
        lengths[:, None] + seq_index * tok_block + jnp.arange(tok_block, dtype=jnp.int32)[None, :]
    ).reshape(tokens)
    half_dim = HEAD_DIM // 2
    frequency = jnp.exp(
        jnp.arange(half_dim, dtype=jnp.float32) * (-2.0 * math.log(10000.0) / HEAD_DIM)
    )
    angles = positions.astype(jnp.float32)[:, None] * frequency
    cosine = jnp.cos(angles)
    sine = jnp.sin(angles)
    cosine = jnp.concatenate([cosine, cosine], axis=1)
    sine = jnp.concatenate([-sine, sine], axis=1)

    clock = Clock(jnp.zeros((1,), jnp.int32) + lengths[:1])
    group = requests // GROUPS
    local_inner = w_in.shape[2]
    local_mheads = local_inner // MHEAD_DIM
    local_width = D // head_count
    made = {}

    def product(pieces, turned, base=(), kind=jnp.bfloat16):
        pieces = list(pieces)
        if pieces[-1][2].shape[0] < 128:
            (offset, row, upper), (_, _, lower) = pieces[-2:]
            pieces[-2:] = [(offset, row, jnp.concatenate([upper, lower], axis=0))]
        return project(
            places, offsets, rows, flat_input, pieces, cosine, sine, turned, base, kind
        )

    by_request = lambda value: value.reshape(requests, tok_block, local_att)

    def prepare():
        made["w_in"] = w_in.reshape(D, 2 * local_inner)
        first_state = ssm_init.reshape(requests, local_mheads, MHEAD_DIM, STATE)
        made["initial"] = jnp.transpose(first_state, (0, 3, 1, 2)).reshape(
            requests, STATE, local_inner
        )
        return (made["w_in"], made["initial"]), ()

    def enter():
        made["act"], made["maps"], size = enter_mixer(
            clock.hold(flat_input), norm_gain, w_bc, w_dt, dt_bias, made["w_in"]
        )
        size = size.reshape(requests, tok_block, local_mheads)
        log_decay = -size * jnp.exp(a_log)
        causal = jnp.arange(tok_block)[None, :] <= jnp.arange(tok_block)[:, None]
        decay = jnp.einsum(
            "tu,ruh->rth", causal.astype(jnp.float32), log_decay, precision=lax.Precision.HIGHEST
        )
        by_row = lambda value: jnp.transpose(value, (0, 2, 1)).reshape(
            requests, 1, local_mheads * tok_block
        )
        made["size"], made["decay"] = size, decay
        made["size_row"], made["decay_row"] = by_row(size), by_row(decay)
        return (made["act"], made["size_row"], made["decay_row"]), ()

    def inside():
        made["read"], made["local"], made["through"] = inside_block(
            requests,
            clock.hold(made["act"]),
            made["maps"],
            made["decay"],
            made["size"],
            made["decay_row"],
            made["size_row"],
            jnp.repeat(d_skip, MHEAD_DIM).reshape(1, local_inner),
        )
        return (made["read"], made["local"]), ()

    def start_relay():
        made["relay"] = relay = Relay(
            made["through"], clock.hold(made["local"]), made["initial"], seq_index, seq_count
        )
        return (), ((relay.pair_state,) if relay.paired else ())

    def hop():
        made["relay"].advance(clock)
        return (), (made["relay"].entry,)

    def end_relay():
        made["entry"] = made["relay"].result(clock)
        return (), (made["entry"],)

    def leave():
        gated, squares, chain = leave_mixer(
            clock.hold(made["entry"]),
            made["maps"],
            made["decay"],
            made["read"],
            made["act"],
            gated_gain.reshape(1, local_inner),
            made["local"],
            made["through"],
        )
        made["gated"] = gated
        made["squares"] = Exchange(
            squares[:, :1].reshape(1, tokens), "head", head_count, jnp.add
        )
        made["squares"].step(clock)
        made["chain"] = chain
        return (gated,), ()

    def join_squares():
        made["squares"].step(clock)
        return (), ()

    def leave_terms():
        squares = made["squares"].result(clock).reshape(tokens, 1)
        made["terms"] = jnp.dot(
            clock.hold(made["gated"]), w_out, preferred_element_type=jnp.float32
        ) * lax.rsqrt(squares / D_INNER + 1e-05)
        return (made["terms"],), ()

    def chain_split():
        made["chain"] = clock.hold(made["chain"]).reshape(
            requests, STATE, local_mheads, MHEAD_DIM
        )
        return (made["chain"],), ()

    def chain_turn():
        made["chain"] = jnp.transpose(clock.hold(made["chain"]), (0, 2, 3, 1))
        return (made["chain"],), ()

    def chain_join():
        made["chain"] = clock.hold(made["chain"]).reshape(
            requests, 1, local_mheads, MHEAD_DIM * STATE
        )
        return (made["chain"],), ()

    query_ring, key_ring, value_ring = (Ring(w, order) for w in (w_query, w_key, w_value))
    slot_rings = []
    live = jnp.clip(lengths - seq_index * cache_block, 0, cache_block).astype(jnp.int32)
    first = (seq_index * tok_block).astype(jnp.int32).reshape(1)
    cached = []

    def make_queries():
        queries = by_request(product(query_ring.pieces, True))
        slot_rings.extend(
            Ring(queries[begin : begin + group], order) for begin in range(0, requests, group)
        )
        return (queries,), ()

    def make_keys():
        made["keys"] = by_request(product(key_ring.pieces, True))
        return (made["keys"],), ()

    def meet_cache(index):
        def work():
            ring = slot_rings[index]
            begin = index * group
            slots = [piece for _, _, piece in ring.pieces[:-2]]
            slots.append(jnp.concatenate([ring.pieces[-2][2], ring.pieces[-1][2]], axis=0))
            slots[0] = clock.hold(slots[0])
            cached.append(
                cache_part(
                    begin,
                    first,
                    places,
                    live[begin : begin + group],
                    slots,
                    cache_keys,
                    cache_values,
                    made["keys"],
                )
            )
            return tuple(cached[-1]), ()

        return work

    def join_peaks():
        peaks = jnp.concatenate([clock.hold(part[2]) for part in cached], axis=0)
        made["best"] = Exchange(peaks, "seq", seq_count, jnp.maximum)
        made["best"].step(clock)
        pieces = value_ring.pieces[1:-2]
        made["used"] = 1 + len(pieces)
        made["values"] = product(
            [(0, 0, clock.hold(value_ring.block))] + pieces, False, kind=jnp.float32
        )
        return (made["values"],) + leave_terms()[0], ()

    def join_more():
        made["best"].step(clock)
        chain_split()
        chain_turn()
        return chain_join()

    def steps(rings, begin, end):
        return [ring for _ in range(begin, end) for ring in rings]

    def run(sends, works):
        for index in range(max(len(sends), len(works))):
            clock.turn(
                sends[index] if index < len(sends) else None,
                works[index] if index < len(works) else None,
            )

    both = steps([query_ring, key_ring], 0, half - 2) + [query_ring] * 2 + [key_ring] * 2
    def make_queries_hop():
        done, _ = make_queries()
        return done, hop()[1]

    def make_keys_hop():
        deferred = hop()[1]
        return make_keys()[0], deferred

    works = [prepare, enter, inside, start_relay, None, hop]
    run(both, works + [None] * (len(both) - 1 - len(works)) + [make_queries_hop])
    run(
        steps(slot_rings, 0, half),
        [None, make_keys_hop, None, end_relay, None, leave, join_squares],
    )
    run(
        steps([value_ring], 0, half),
        [meet_cache(0), meet_cache(1)] + [None] * (half - 4) + [join_peaks, join_more],
    )

    new_keys = made["keys"]
    best = made["best"].result(clock)
    new_values = by_request(
        product(value_ring.pieces[made["used"] :], False, base=(made["values"],))
    )

    own = lambda stat: lax.dynamic_slice_in_dim(stat, seq_index * tok_block, tok_block, 2)
    greatest_logit = jnp.transpose(own(best), (0, 2, 1)) * SCALE
    residual = lax.dynamic_slice_in_dim(
        flat_input, head_index * local_width, local_width, 1
    ).astype(jnp.float32)
    mixed = []

    filled = {}

    def finish(index, at, count):
        def work():
            joined, out, peaks, totals = cached[index]
            filled[index] = finish_part(
                index * group,
                at,
                count,
                first,
                places,
                clock.hold(joined),
                new_keys,
                new_values,
                out,
                peaks,
                totals,
                best,
                filled.get(index, ()),
            )
            return tuple(filled[index]), ()

        return work

    def ring_sum(index):
        terms = {-offset: part for offset, part in zip(offsets, filled[index][1:])}
        terms[half] = terms[-half]
        return RingSum(terms, order)

    def add_sums():
        if "sums" not in made:
            sums = jnp.concatenate([filled[index][0] for index in range(GROUPS)], axis=0)
            made["sums"] = Exchange(sums, "seq", seq_count, jnp.add)
        made["sums"].step(clock)
        return (), ()

    run([], [finish(0, 0, group)])
    sum_rings = [ring_sum(0)]
    run(sum_rings, [finish(1, 0, group // 2)])
    clock.mark = clock.hold(clock.mark, sum_rings[0].ahead)[0]
    run(sum_rings, [finish(1, group // 2, group - group // 2)])
    sum_rings.append(ring_sum(1))
    turns = steps(sum_rings[::-1], 0, half)
    run(turns[: 2 * half - 3], [add_sums, None, add_sums, None, add_sums])
    denominators = jnp.transpose(own(made["sums"].result(clock)), (0, 2, 1))
    last = sum_rings[1]
    while last.left > 0:
        run([last], [])

    for index in range(GROUPS):
        begin = index * group
        denominator = denominators[begin : begin + group]
        numerator = sum_rings[index].total().reshape(group, tok_block, local_heads, HEAD_DIM)
        attended = (
            (numerator / denominator[..., None])
            .astype(jnp.bfloat16)
            .reshape(group * tok_block, local_att)
        )
        at = slice(begin * tok_block, (begin + group) * tok_block)
        attn_terms = jnp.dot(attended, w_attn_out, preferred_element_type=jnp.float32)
        summed = head_sum(attn_terms + made["terms"][at], head_count, head_index)
        mixed.append(
            (residual[at] + summed)
            .astype(jnp.bfloat16)
            .reshape(group, tok_block, local_width)
        )
    return (
        jnp.concatenate(mixed, axis=0),
        new_keys,
        new_values,
        made["chain"],
        greatest_logit,
    )


def solution(mesh):
    placed = (
        P(None, "seq", None),
        P(),
        P(None, "seq", "head"),
        P(None, "seq", "head"),
        P("seq", "head"),
        P("seq", "head"),
        P("seq", "head"),
        P("head", None),
        P(),
        P(None, None, "head"),
        P(),
        P(None, "head"),
        P("head"),
        P("head"),
        P("head"),
        P("head"),
        P("head", None),
        P(None, "head", None),
    )
    return jax.shard_map(
        shards,
        mesh=mesh,
        in_specs=placed,
        out_specs=(
            P(None, "seq", "head"),
            P(None, "seq", "head"),
            P(None, "seq", "head"),
            P(None, "seq", "head", None),
            P(None, "seq", "head"),
        ),
        check_vma=False,
    )
```

```python
import functools
import math

import jax
import jax.numpy as jnp
from jax import lax
from jax.experimental import pallas as pl
from jax.experimental.pallas import tpu as pltpu
from jax.sharding import PartitionSpec as P

D = 2048
HEAD_DIM = 128
MHEAD_DIM = 64
STATE = 64
D_INNER = 4096
SCALE = 1.0 / math.sqrt(HEAD_DIM)
EXP2_SCALE = SCALE * math.log2(math.e)
DEAD = -1e30
GROUPS = 2
VMEM_BYTES = 56 * 1024 * 1024


def ring_order(count):
    y_count = max(1, count // 4)
    z_count = count // y_count
    order = []
    for y in range(y_count):
        turn = range(z_count) if y % 2 == 0 else range(z_count - 1, -1, -1)
        order += [z * y_count + y for z in turn]
    return order


def ring_step(block, order, distance):
    count = len(order)
    route = [(order[i], order[(i + distance) % count]) for i in range(count)]
    return lax.ppermute(block, "seq", route)


class Ring:
    def __init__(self, block, order, first_row=0):
        self.order = order
        self.steps = len(order) // 2
        self.done = 0
        self.first_row = first_row
        self.block = self.ahead = self.back = block
        self.pieces = [(0, first_row, block)]

    def step(self, clock):
        self.done += 1
        half = self.block.shape[0] // 2
        last = self.done == self.steps
        ahead = self.ahead[:half] if last else self.ahead
        back = self.back[half:] if last else self.back
        ahead, back = clock.hold(ahead, back)
        self.ahead = ring_step(ahead, self.order, 1)
        self.back = ring_step(back, self.order, -1)
        at = self.first_row
        if last:
            self.pieces += [(self.steps, at, self.ahead), (self.steps, at + half, self.back)]
        else:
            self.pieces += [(self.done, at, self.ahead), (-self.done, at, self.back)]
        return [self.ahead, self.back]


class Clock:
    def __init__(self, mark):
        self.mark = mark
        self.late = ()

    def hold(self, *values):
        held = lax.optimization_barrier(tuple(values) + (self.mark,))[: len(values)]
        return held[0] if len(values) == 1 else held

    def turn(self, ring=None, work=None):
        moved = tuple(ring.step(self)) if ring is not None else ()
        done, deferred = work() if work is not None else ((), ())
        self.mark = lax.optimization_barrier((self.mark,) + self.late + tuple(done))[0]
        self.late = moved + tuple(deferred)


class Exchange:
    def __init__(self, value, axis, count, combine):
        self.value, self.axis, self.count, self.combine = value, axis, count, combine
        self.got = None
        self.bit = 1

    def join(self, clock):
        if self.got is not None:
            self.value = self.combine(*clock.hold(self.value, self.got))
            self.got = None

    def step(self, clock):
        self.join(clock)
        if self.bit < self.count:
            route = [(i, i ^ self.bit) for i in range(self.count)]
            self.got = lax.ppermute(self.value, self.axis, route)
            self.bit *= 2

    def result(self, clock):
        while self.bit < self.count:
            self.step(clock)
        self.join(clock)
        return self.value


class RingSum:
    def __init__(self, parts, order):
        self.parts, self.order = parts, order
        self.left = len(order) // 2
        self.half = parts[0].shape[0] // 2
        self.ahead = self.back = None

    def add(self, a, b):
        return (a.astype(jnp.float32) + b.astype(jnp.float32)).astype(jnp.bfloat16)

    def step(self, clock):
        half, left, far = self.half, self.left, len(self.order) // 2
        top, bottom = self.parts[left], self.parts[-left]
        if left == far:
            ahead, back = top[:half], bottom[half:]
        elif left == far - 1:
            ahead = jnp.concatenate([self.add(self.ahead, top[:half]), top[half:]], axis=0)
            back = jnp.concatenate([bottom[:half], self.add(self.back, bottom[half:])], axis=0)
        else:
            ahead, back = self.add(self.ahead, top), self.add(self.back, bottom)
        ahead, back = clock.hold(ahead, back)
        self.ahead = ring_step(ahead, self.order, 1)
        self.back = ring_step(back, self.order, -1)
        self.left -= 1
        return [self.ahead, self.back]

    def total(self):
        return sum(value.astype(jnp.float32) for value in (self.ahead, self.back, self.parts[0]))


def project_kernel(count, turned, places_ref, *refs):
    input_refs, weight_refs = refs[:count], refs[count : 2 * count]
    cosine_ref, sine_ref, *base_ref, out_ref = refs[2 * count :]
    total = base_ref[0][...] if base_ref else None
    for input_ref, weight_ref in zip(input_refs, weight_refs):
        term = jnp.dot(input_ref[...], weight_ref[...], preferred_element_type=jnp.float32)
        total = term if total is None else total + term
    if not turned:
        out_ref[...] = total.astype(out_ref.dtype)
        return
    cosine = cosine_ref[...]
    sine = sine_ref[...]
    for head in range(out_ref.shape[1] // HEAD_DIM):
        at = slice(head * HEAD_DIM, (head + 1) * HEAD_DIM)
        part = total[:, at]
        rolled = pltpu.roll(part, HEAD_DIM // 2, 1)
        out_ref[:, at] = (part * cosine + rolled * sine).astype(out_ref.dtype)


def project(places, offsets, rows, value, pieces, cosine, sine, turned, base=(), kind=jnp.bfloat16):
    tokens = value.shape[0]
    width = pieces[0][2].shape[1]
    block = min(width, 256)
    input_specs, weight_specs = [], []
    for offset, row, piece in pieces:
        depth = piece.shape[0]

        def place(j, places_ref, slot=offsets.index(offset), scale=rows // depth, at=row // depth):
            return (0, places_ref[slot] * scale + at)

        input_specs.append(pl.BlockSpec((tokens, depth), place))
        weight_specs.append(pl.BlockSpec((depth, block), lambda j, *_: (0, j)))
    angle = pl.BlockSpec((tokens, HEAD_DIM), lambda j, *_: (0, 0))
    return pl.pallas_call(
        functools.partial(project_kernel, len(pieces), turned),
        grid_spec=pltpu.PrefetchScalarGridSpec(
            num_scalar_prefetch=1,
            grid=(width // block,),
            in_specs=input_specs
            + weight_specs
            + [angle, angle]
            + [pl.BlockSpec((tokens, block), lambda j, *_: (0, j))] * len(base),
            out_specs=pl.BlockSpec((tokens, block), lambda j, *_: (0, j)),
        ),
        out_shape=jax.ShapeDtypeStruct((tokens, width), kind),
        compiler_params=pltpu.CompilerParams(vmem_limit_bytes=VMEM_BYTES),
        cost_estimate=pl.CostEstimate(
            flops=2 * tokens * sum(piece.shape[0] for _, _, piece in pieces) * width,
            bytes_accessed=2 * (tokens + width) * value.shape[1],
            transcendentals=0,
        ),
        name="project",
    )(places, *[value] * len(pieces), *[piece for _, _, piece in pieces], cosine, sine, *base)


def silu(value):
    return value / (1.0 + jnp.exp(-value))


def exact_dot(a, b):
    return jnp.dot(a, b, precision=lax.Precision.HIGHEST, preferred_element_type=jnp.float32)


def spread(heads, block):
    shape = (heads, heads * block)
    column = lax.broadcasted_iota(jnp.int32, shape, 1) // block
    return (column == lax.broadcasted_iota(jnp.int32, shape, 0)).astype(jnp.float32)


def enter_kernel(input_ref, gain_ref, bc_ref, dt_ref, bias_ref, weight_ref, act_ref, map_ref, size_ref, normed_ref):
    @pl.when(pl.program_id(0) == 0)
    def _():
        rows = input_ref.shape[0]
        chunk = min(rows, 64)
        for start in range(0, rows, chunk):
            at = slice(start, start + chunk)
            hidden = input_ref[at, :].astype(jnp.float32)
            scale = lax.rsqrt(jnp.mean(hidden * hidden, axis=-1, keepdims=True) + 1e-05)
            normed_ref[at, :] = (hidden * scale * gain_ref[...]).astype(jnp.bfloat16)
        normed = normed_ref[...]
        map_ref[...] = jnp.dot(normed, bc_ref[...], preferred_element_type=jnp.float32)
        size = jnp.dot(normed, dt_ref[...], preferred_element_type=jnp.float32) + bias_ref[...]
        size_ref[...] = jnp.maximum(size, 0.0) + jnp.log1p(jnp.exp(-jnp.abs(size)))

    act_ref[...] = silu(
        jnp.dot(normed_ref[...], weight_ref[...], preferred_element_type=jnp.float32)
    )


def enter_mixer(flat_input, norm_gain, w_bc, w_dt, dt_bias, weight):
    tokens = flat_input.shape[0]
    width = weight.shape[1]
    block = min(width, 512)
    heads = w_dt.shape[1]
    whole = lambda *shape: pl.BlockSpec(shape, lambda j: (0, 0))
    return pl.pallas_call(
        enter_kernel,
        grid=(width // block,),
        in_specs=[
            whole(tokens, D),
            whole(1, D),
            whole(D, 2 * STATE),
            whole(D, heads),
            whole(1, heads),
            pl.BlockSpec((D, block), lambda j: (0, j)),
        ],
        out_specs=[
            pl.BlockSpec((tokens, block), lambda j: (0, j)),
            whole(tokens, 2 * STATE),
            whole(tokens, heads),
        ],
        out_shape=[
            jax.ShapeDtypeStruct((tokens, width), jnp.float32),
            jax.ShapeDtypeStruct((tokens, 2 * STATE), jnp.float32),
            jax.ShapeDtypeStruct((tokens, heads), jnp.float32),
        ],
        scratch_shapes=[pltpu.VMEM((tokens, D), jnp.bfloat16)],
        compiler_params=pltpu.CompilerParams(vmem_limit_bytes=VMEM_BYTES),
        cost_estimate=pl.CostEstimate(
            flops=2 * tokens * D * width,
            bytes_accessed=2 * D * (width + tokens) + 4 * tokens * width,
            transcendentals=tokens * width,
        ),
        name="enter_mixer",
    )(flat_input, norm_gain.reshape(1, D), w_bc, w_dt, dt_bias.reshape(1, heads), weight)


def inside_kernel(inner_ref, map_ref, decay_ref, size_ref, decay_row_ref, size_row_ref, skip_ref, read_ref, local_ref, through_ref):
    tokens, heads = decay_ref.shape[1:]
    inner = inner_ref[...]
    input_map = map_ref[:, :STATE]
    output_map = map_ref[:, STATE:]
    decay = decay_ref[0]
    by_head = spread(heads, MHEAD_DIM)
    wide = (tokens, heads * tokens)
    contact = dot_nt(
        output_map.astype(jnp.bfloat16),
        jnp.concatenate([input_map.astype(jnp.bfloat16)] * heads, axis=0),
    )
    source = lax.rem(lax.broadcasted_iota(jnp.int32, wide, 1), tokens)
    causal = source <= lax.broadcasted_iota(jnp.int32, wide, 0)
    difference = exact_dot(decay, spread(heads, tokens)) - decay_row_ref[0]
    mixing = jnp.exp(jnp.where(causal, difference, DEAD)) * contact * size_row_ref[0]
    mixing = mixing.astype(jnp.bfloat16)
    inner_low = inner.astype(jnp.bfloat16)
    together = min(heads, 256 // MHEAD_DIM)
    shape = (together * tokens, together * MHEAD_DIM)
    own = (
        lax.broadcasted_iota(jnp.int32, shape, 0) // tokens
        == lax.broadcasted_iota(jnp.int32, shape, 1) // MHEAD_DIM
    )
    for begin in range(0, heads, together):
        at = slice(begin * MHEAD_DIM, (begin + together) * MHEAD_DIM)
        stacked = jnp.concatenate([inner_low[:, at]] * together, axis=0)
        stacked = jnp.where(own, stacked, jnp.zeros_like(stacked))
        read_ref[:, at] = (
            jnp.dot(
                mixing[:, begin * tokens : (begin + together) * tokens],
                stacked,
                preferred_element_type=jnp.float32,
            )
            + skip_ref[:, at] * inner[:, at]
        )
    last = decay[tokens - 1 :, :]
    tail = exact_dot(jnp.exp(last - decay) * size_ref[0], by_head)
    local_ref[0] = dot_tn(input_map.astype(jnp.bfloat16), (inner * tail).astype(jnp.bfloat16))
    through_ref[0] = exact_dot(jnp.exp(jnp.broadcast_to(last, (8, heads))), by_head)[:1]


def inside_block(requests, act, maps, decay, size, decay_row, size_row, skip):
    tokens, heads = decay.shape[1:]
    inner = act.shape[1] // 2
    one = lambda *shape: pl.BlockSpec((1,) + shape, lambda r: (r, 0, 0))
    return pl.pallas_call(
        inside_kernel,
        grid=(requests,),
        in_specs=[
            pl.BlockSpec((tokens, inner), lambda r: (r, 1)),
            pl.BlockSpec((tokens, 2 * STATE), lambda r: (r, 0)),
            one(tokens, heads),
            one(tokens, heads),
            one(1, heads * tokens),
            one(1, heads * tokens),
            pl.BlockSpec((1, inner), lambda r: (0, 0)),
        ],
        out_specs=[
            pl.BlockSpec((tokens, inner), lambda r: (r, 0)),
            one(STATE, inner),
            one(1, inner),
        ],
        out_shape=[
            jax.ShapeDtypeStruct((requests * tokens, inner), jnp.float32),
            jax.ShapeDtypeStruct((requests, STATE, inner), jnp.float32),
            jax.ShapeDtypeStruct((requests, 1, inner), jnp.float32),
        ],
        compiler_params=pltpu.CompilerParams(vmem_limit_bytes=VMEM_BYTES),
        cost_estimate=pl.CostEstimate(
            flops=12 * requests * tokens * tokens * inner,
            bytes_accessed=16 * requests * tokens * inner,
            transcendentals=requests * tokens * tokens * heads,
        ),
        name="inside_block",
    )(act, maps, decay, size, decay_row, size_row, skip)


def leave_kernel(entry_ref, map_ref, decay_ref, read_ref, gate_ref, gain_ref, local_ref, through_ref, gated_ref, square_ref, chain_ref):
    heads = decay_ref.shape[2]
    entry = entry_ref[0]
    grown = exact_dot(jnp.exp(decay_ref[0]), spread(heads, MHEAD_DIM))
    inter = jnp.dot(
        map_ref[:, STATE:].astype(jnp.bfloat16),
        entry.astype(jnp.bfloat16),
        preferred_element_type=jnp.float32,
    )
    mixed = (read_ref[...] + inter * grown) * gate_ref[...]
    squares = jnp.sum(mixed * mixed, axis=1, keepdims=True)
    square_ref[...] = jnp.broadcast_to(squares, square_ref.shape)
    gated_ref[...] = (mixed * gain_ref[...]).astype(jnp.bfloat16)
    chain_ref[0] = (through_ref[0] * entry + local_ref[0]).T


def leave_mixer(entry, maps, decay, read, act, gain, local, through):
    requests, tokens, heads = decay.shape
    inner = read.shape[1]
    one = lambda *shape: pl.BlockSpec((1,) + shape, lambda r: (r, 0, 0))
    flat = lambda width: pl.BlockSpec((tokens, width), lambda r: (r, 0))
    return pl.pallas_call(
        leave_kernel,
        grid=(requests,),
        in_specs=[
            one(STATE, inner),
            flat(2 * STATE),
            one(tokens, heads),
            flat(inner),
            flat(inner),
            pl.BlockSpec((1, inner), lambda r: (0, 0)),
            one(STATE, inner),
            one(1, inner),
        ],
        out_specs=[flat(inner), flat(128), one(inner, STATE)],
        out_shape=[
            jax.ShapeDtypeStruct((requests * tokens, inner), jnp.bfloat16),
            jax.ShapeDtypeStruct((requests * tokens, 128), jnp.float32),
            jax.ShapeDtypeStruct((requests, inner, STATE), jnp.float32),
        ],
        compiler_params=pltpu.CompilerParams(vmem_limit_bytes=VMEM_BYTES),
        cost_estimate=pl.CostEstimate(
            flops=2 * requests * tokens * STATE * inner,
            bytes_accessed=24 * requests * tokens * inner,
            transcendentals=requests * tokens * heads,
        ),
        name="leave_mixer",
    )(entry, maps, decay, read, act, gain, local, through)


def dot_nt(a, b):
    return lax.dot_general(a, b, (((1,), (1,)), ((), ())), preferred_element_type=jnp.float32)


def dot_tn(a, b):
    return lax.dot_general(a, b, (((0,), (0,)), ((), ())), preferred_element_type=jnp.float32)


def group_scores(first, key, query):
    scores = dot_nt(key, query)
    shape = scores.shape
    live = first + lax.broadcasted_iota(jnp.int32, shape, 0) <= lax.broadcasted_iota(
        jnp.int32, shape, 1
    )
    return jnp.where(live, scores, DEAD)


def cache_kernel(slots, first_ref, place_ref, live_ref, *refs):
    query_refs = refs[:slots]
    key_ref, value_ref, group_ref, joined_ref, out_ref, peak_ref, total_ref = refs[slots:]
    tok_block = query_refs[0].shape[1]
    keys, width = key_ref.shape[1:]
    tokens = tok_block * slots
    for slot in range(slots):
        start = pl.multiple_of(place_ref[slot] * tok_block, tok_block)
        joined_ref[0, pl.ds(start, tok_block), :] = query_refs[slot][0]
    live = live_ref[pl.program_id(0)]
    bias = jnp.where(
        lax.broadcasted_iota(jnp.int32, (keys, 128), 0) < live, 0.0, DEAD
    ).astype(jnp.float32)
    bias = jnp.concatenate([bias] * (tokens // 128), axis=1)
    for head in range(width // HEAD_DIM):
        at = slice(head * HEAD_DIM, (head + 1) * HEAD_DIM)
        query = joined_ref[0, :, at]
        scores = dot_nt(key_ref[0, :, at], query) + bias
        peak = jnp.maximum(
            jnp.max(scores, axis=0, keepdims=True),
            jnp.max(
                group_scores(first_ref[0], group_ref[0, :, at], query), axis=0, keepdims=True
            ),
        )
        weights = jnp.exp2((scores - peak) * EXP2_SCALE)
        total_ref[0, head : head + 1, :] = jnp.sum(weights, axis=0, keepdims=True)
        peak_ref[0, head : head + 1, :] = peak
        out_ref[0, at, :] = dot_tn(value_ref[0, :, at], weights.astype(jnp.bfloat16)).astype(
            out_ref.dtype
        )


def cache_part(begin, first, places, live, query_slots, keys, values, new_keys):
    slots = len(query_slots)
    requests, tok_block, width = query_slots[0].shape
    tokens = tok_block * slots
    cache_block = keys.shape[1]
    heads = width // HEAD_DIM
    one = lambda rows, start: pl.BlockSpec((1, rows, width), lambda r, *_: (r + start, 0, 0))
    stat = pl.BlockSpec((1, heads, tokens), lambda r, *_: (r, 0, 0))
    return pl.pallas_call(
        functools.partial(cache_kernel, slots),
        grid_spec=pltpu.PrefetchScalarGridSpec(
            num_scalar_prefetch=3,
            grid=(requests,),
            in_specs=[one(tok_block, 0)] * slots
            + [one(cache_block, begin)] * 2
            + [one(tok_block, begin)],
            out_specs=[
                one(tokens, 0),
                pl.BlockSpec((1, width, tokens), lambda r, *_: (r, 0, 0)),
                stat,
                stat,
            ],
        ),
        out_shape=[
            jax.ShapeDtypeStruct((requests, tokens, width), jnp.bfloat16),
            jax.ShapeDtypeStruct((requests, width, tokens), jnp.bfloat16),
            jax.ShapeDtypeStruct((requests, heads, tokens), jnp.float32),
            jax.ShapeDtypeStruct((requests, heads, tokens), jnp.float32),
        ],
        compiler_params=pltpu.CompilerParams(vmem_limit_bytes=VMEM_BYTES),
        cost_estimate=pl.CostEstimate(
            flops=4 * requests * tokens * cache_block * width,
            bytes_accessed=2 * requests * width * (3 * tokens + 2 * cache_block),
            transcendentals=requests * tokens * cache_block * heads,
        ),
        name="cache_part",
    )(first, places, live, *query_slots, keys, values, new_keys)


def finish_kernel(slots, first_ref, place_ref, *refs):
    query_ref, key_ref, value_ref, cache_ref, peak_ref, total_ref, best_ref = refs[:7]
    sum_ref, *part_refs = refs[7:-1]
    joined_ref = refs[-1]
    tok_block = key_ref.shape[1]
    for head in range(query_ref.shape[2] // HEAD_DIM):
        at = slice(head * HEAD_DIM, (head + 1) * HEAD_DIM)
        row = slice(head, head + 1)
        scores = group_scores(first_ref[0], key_ref[0, :, at], query_ref[0, :, at])
        best = best_ref[0, row, :]
        weights = jnp.exp2((scores - best) * EXP2_SCALE)
        rescale = jnp.exp2((peak_ref[0, row, :] - best) * EXP2_SCALE)
        sum_ref[0, row, :] = total_ref[0, row, :] * rescale + jnp.sum(
            weights, axis=0, keepdims=True
        )
        joined = cache_ref[0, at, :].astype(jnp.float32) * rescale + dot_tn(
            value_ref[0, :, at], weights.astype(jnp.bfloat16)
        )
        joined_ref[:, at] = joined.astype(jnp.bfloat16).T
    for slot in range(slots):
        start = pl.multiple_of(place_ref[slot] * tok_block, tok_block)
        part_refs[slot][0] = joined_ref[pl.ds(start, tok_block), :]


def finish_part(begin, first, places, queries, new_keys, new_values, cached, peaks, totals, best):
    requests, tokens, width = queries.shape
    tok_block = new_keys.shape[1]
    slots = tokens // tok_block
    heads = width // HEAD_DIM
    one = lambda rows, start: pl.BlockSpec((1, rows, width), lambda r, *_: (r + start, 0, 0))
    stat = lambda start: pl.BlockSpec((1, heads, tokens), lambda r, *_: (r + start, 0, 0))
    return pl.pallas_call(
        functools.partial(finish_kernel, slots),
        grid_spec=pltpu.PrefetchScalarGridSpec(
            num_scalar_prefetch=2,
            grid=(requests,),
            in_specs=[
                one(tokens, 0),
                one(tok_block, begin),
                one(tok_block, begin),
                pl.BlockSpec((1, width, tokens), lambda r, *_: (r, 0, 0)),
                stat(0),
                stat(0),
                stat(begin),
            ],
            out_specs=[stat(0)] + [one(tok_block, 0)] * slots,
            scratch_shapes=[pltpu.VMEM((tokens, width), jnp.bfloat16)],
        ),
        out_shape=[jax.ShapeDtypeStruct((requests, heads, tokens), jnp.float32)]
        + [jax.ShapeDtypeStruct((requests, tok_block, width), jnp.bfloat16)] * slots,
        compiler_params=pltpu.CompilerParams(vmem_limit_bytes=VMEM_BYTES),
        cost_estimate=pl.CostEstimate(
            flops=4 * requests * tokens * tok_block * width,
            bytes_accessed=6 * requests * width * tokens,
            transcendentals=requests * tokens * tok_block * heads,
        ),
        name="finish_part",
    )(first, places, queries, new_keys, new_values, cached, peaks, totals, best)


def head_sum(terms, head_count, head_index):
    if head_count != 4:
        return lax.psum_scatter(
            terms.astype(jnp.bfloat16), "head", scatter_dimension=1, tiled=True
        ).astype(jnp.float32)
    width = terms.shape[1] // 4
    chunk = lambda index: lax.dynamic_slice_in_dim(terms, index * width, width, 1)
    core, column = head_index % 2, head_index // 2
    near, far = 2 * column, 2 * (1 - column)
    got = lax.ppermute(
        jnp.concatenate([chunk(near + 1 - core), chunk(far + 1 - core)], axis=1).astype(
            jnp.bfloat16
        ),
        "head",
        [(h, h ^ 1) for h in range(4)],
    ).astype(jnp.float32)
    keep = chunk(near + core) + got[:, :width]
    give = chunk(far + core) + got[:, width:]
    return keep + lax.ppermute(
        give.astype(jnp.bfloat16), "head", [(h, h ^ 2) for h in range(4)]
    ).astype(jnp.float32)


class Relay:
    def __init__(self, through, local, initial, seq_index, seq_count):
        self.factor, self.local = through, local
        self.paired = seq_count == 8
        self.hop = 0
        if not self.paired:
            self.hops = seq_count - 1
            self.entry = jnp.where(seq_index == 0, initial, 0.0)
            return
        self.hops = 3
        self.swap = [(i, i ^ 1) for i in range(8)]
        self.is_first = is_first = seq_index % 2 == 0
        half = local.shape[2] // 2
        side = lambda value: jnp.where(is_first, value[..., :half], value[..., half:])
        mine = side(local)
        got = self.exchange(jnp.where(is_first, local[..., half:], local[..., :half]))
        other_factor = side(lax.ppermute(through, "seq", self.swap))
        factor = side(through)
        self.first_state = jnp.where(is_first, mine, got)
        second_state = jnp.where(is_first, got, mine)
        self.first_factor = jnp.where(is_first, factor, other_factor)
        second_factor = jnp.where(is_first, other_factor, factor)
        self.pair_state = second_factor * self.first_state + second_state
        self.pair_factor = self.first_factor * second_factor
        self.entry = jnp.where(seq_index < 2, side(initial), 0.0)

    def exchange(self, value):
        return lax.ppermute(value.astype(jnp.bfloat16), "seq", self.swap).astype(jnp.float32)

    def advance(self, clock):
        if self.hop == self.hops:
            return
        factor, state = (
            (self.pair_factor, self.pair_state) if self.paired else (self.factor, self.local)
        )
        entry = clock.hold(self.entry)
        leaving = (factor * entry + state).astype(jnp.bfloat16)
        if self.paired:
            route = [(2 * self.hop + y, 2 * self.hop + 2 + y) for y in range(2)]
        else:
            route = [(self.hop, self.hop + 1)]
        self.hop += 1
        self.entry = entry + lax.ppermute(leaving, "seq", route).astype(jnp.float32)

    def result(self, clock):
        while self.hop < self.hops:
            self.advance(clock)
        entry = clock.hold(self.entry)
        if not self.paired:
            return entry
        second = self.first_factor * entry + self.first_state
        got = self.exchange(jnp.where(self.is_first, second, entry))
        mine = jnp.where(self.is_first, entry, second)
        return jnp.concatenate(
            [jnp.where(self.is_first, mine, got), jnp.where(self.is_first, got, mine)], axis=2
        )


def shards(
    block_input,
    lengths,
    cache_keys,
    cache_values,
    w_query,
    w_key,
    w_value,
    w_attn_out,
    norm_gain,
    w_in,
    w_bc,
    w_dt,
    dt_bias,
    a_log,
    d_skip,
    gated_gain,
    w_out,
    ssm_init,
):
    requests, tok_block, _ = block_input.shape
    seq_count = lax.axis_size("seq")
    seq_index = lax.axis_index("seq")
    head_count = lax.axis_size("head")
    head_index = lax.axis_index("head")
    local_att = w_query.shape[1]
    local_heads = local_att // HEAD_DIM
    cache_block = cache_keys.shape[1]
    rows = w_query.shape[0]
    tokens = requests * tok_block
    flat_input = block_input.reshape(tokens, block_input.shape[2])

    order = ring_order(seq_count)
    half = seq_count // 2
    offsets = [0] + [sign * step for step in range(1, half) for sign in (1, -1)] + [half]
    places = jnp.asarray(
        [
            [order[(order.index(i) - offset) % seq_count] for offset in offsets]
            for i in range(seq_count)
        ],
        jnp.int32,
    )[seq_index]

    positions = (
        lengths[:, None] + seq_index * tok_block + jnp.arange(tok_block, dtype=jnp.int32)[None, :]
    ).reshape(tokens)
    half_dim = HEAD_DIM // 2
    frequency = jnp.exp(
        jnp.arange(half_dim, dtype=jnp.float32) * (-2.0 * math.log(10000.0) / HEAD_DIM)
    )
    angles = positions.astype(jnp.float32)[:, None] * frequency
    cosine = jnp.cos(angles)
    sine = jnp.sin(angles)
    cosine = jnp.concatenate([cosine, cosine], axis=1)
    sine = jnp.concatenate([-sine, sine], axis=1)

    clock = Clock(jnp.zeros((1,), jnp.int32) + lengths[:1])
    group = requests // GROUPS
    local_inner = w_in.shape[2]
    local_mheads = local_inner // MHEAD_DIM
    local_width = D // head_count
    made = {}

    def product(pieces, turned, base=(), kind=jnp.bfloat16):
        pieces = list(pieces)
        if pieces[-1][2].shape[0] < 128:
            (offset, row, upper), (_, _, lower) = pieces[-2:]
            pieces[-2:] = [(offset, row, jnp.concatenate([upper, lower], axis=0))]
        return project(
            places, offsets, rows, flat_input, pieces, cosine, sine, turned, base, kind
        )

    by_request = lambda value: value.reshape(requests, tok_block, local_att)

    def prepare():
        made["w_in"] = w_in.reshape(D, 2 * local_inner)
        first_state = ssm_init.reshape(requests, local_mheads, MHEAD_DIM, STATE)
        made["initial"] = jnp.transpose(first_state, (0, 3, 1, 2)).reshape(
            requests, STATE, local_inner
        )
        return (made["w_in"], made["initial"]), ()

    def enter():
        made["act"], made["maps"], size = enter_mixer(
            clock.hold(flat_input), norm_gain, w_bc, w_dt, dt_bias, made["w_in"]
        )
        size = size.reshape(requests, tok_block, local_mheads)
        log_decay = -size * jnp.exp(a_log)
        causal = jnp.arange(tok_block)[None, :] <= jnp.arange(tok_block)[:, None]
        decay = jnp.einsum(
            "tu,ruh->rth", causal.astype(jnp.float32), log_decay, precision=lax.Precision.HIGHEST
        )
        by_row = lambda value: jnp.transpose(value, (0, 2, 1)).reshape(
            requests, 1, local_mheads * tok_block
        )
        made["size"], made["decay"] = size, decay
        made["size_row"], made["decay_row"] = by_row(size), by_row(decay)
        return (made["act"], made["size_row"], made["decay_row"]), ()

    def inside():
        made["read"], made["local"], made["through"] = inside_block(
            requests,
            clock.hold(made["act"]),
            made["maps"],
            made["decay"],
            made["size"],
            made["decay_row"],
            made["size_row"],
            jnp.repeat(d_skip, MHEAD_DIM).reshape(1, local_inner),
        )
        return (made["read"], made["local"]), ()

    def start_relay():
        made["relay"] = relay = Relay(
            made["through"], clock.hold(made["local"]), made["initial"], seq_index, seq_count
        )
        return (), ((relay.pair_state,) if relay.paired else ())

    def hop():
        made["relay"].advance(clock)
        return (), (made["relay"].entry,)

    def end_relay():
        made["entry"] = made["relay"].result(clock)
        return (), (made["entry"],)

    def leave():
        gated, squares, chain = leave_mixer(
            clock.hold(made["entry"]),
            made["maps"],
            made["decay"],
            made["read"],
            made["act"],
            gated_gain.reshape(1, local_inner),
            made["local"],
            made["through"],
        )
        made["gated"] = gated
        made["squares"] = Exchange(
            squares[:, :1].reshape(1, tokens), "head", head_count, jnp.add
        )
        made["squares"].step(clock)
        made["chain"] = chain
        return (gated,), ()

    def join_squares():
        made["squares"].step(clock)
        return (), ()

    def leave_terms():
        squares = made["squares"].result(clock).reshape(tokens, 1)
        made["terms"] = jnp.dot(
            clock.hold(made["gated"]), w_out, preferred_element_type=jnp.float32
        ) * lax.rsqrt(squares / D_INNER + 1e-05)
        return (made["terms"],), ()

    def leave_chain():
        made["chain"] = (
            clock.hold(made["chain"])
            .reshape(requests, local_mheads, MHEAD_DIM, STATE)
            .reshape(requests, 1, local_mheads, MHEAD_DIM * STATE)
        )
        return (made["chain"],), ()

    query_ring, key_ring, value_ring = (Ring(w, order) for w in (w_query, w_key, w_value))
    slot_rings = []
    live = jnp.clip(lengths - seq_index * cache_block, 0, cache_block).astype(jnp.int32)
    first = (seq_index * tok_block).astype(jnp.int32).reshape(1)
    cached = []

    def make_queries():
        queries = by_request(product(query_ring.pieces, True))
        slot_rings.extend(
            Ring(queries[begin : begin + group], order) for begin in range(0, requests, group)
        )
        return (queries,), ()

    def make_keys():
        made["keys"] = by_request(product(key_ring.pieces, True))
        return (made["keys"],), ()

    def meet_cache(index):
        def work():
            ring = slot_rings[index]
            begin = index * group
            slots = [piece for _, _, piece in ring.pieces[:-2]]
            slots.append(jnp.concatenate([ring.pieces[-2][2], ring.pieces[-1][2]], axis=0))
            slots[0] = clock.hold(slots[0])
            cached.append(
                cache_part(
                    begin,
                    first,
                    places,
                    live[begin : begin + group],
                    slots,
                    cache_keys,
                    cache_values,
                    made["keys"],
                )
            )
            return tuple(cached[-1]), ()

        return work

    def join_peaks():
        peaks = jnp.concatenate([clock.hold(part[2]) for part in cached], axis=0)
        made["best"] = Exchange(peaks, "seq", seq_count, jnp.maximum)
        made["best"].step(clock)
        pieces = value_ring.pieces[1:-2]
        made["used"] = 1 + len(pieces)
        made["values"] = product(
            [(0, 0, clock.hold(value_ring.block))] + pieces, False, kind=jnp.float32
        )
        return (made["values"],) + leave_terms()[0], ()

    def join_more():
        made["best"].step(clock)
        return leave_chain()

    def steps(rings, begin, end):
        return [ring for _ in range(begin, end) for ring in rings]

    def run(sends, works):
        for index in range(max(len(sends), len(works))):
            clock.turn(
                sends[index] if index < len(sends) else None,
                works[index] if index < len(works) else None,
            )

    both = steps([query_ring, key_ring], 0, half - 2) + [query_ring] * 2 + [key_ring] * 2
    def make_queries_hop():
        done, _ = make_queries()
        return done, hop()[1]

    def make_keys_hop():
        deferred = hop()[1]
        return make_keys()[0], deferred

    works = [prepare, enter, inside, start_relay, None, hop]
    run(both, works + [None] * (len(both) - 1 - len(works)) + [make_queries_hop])
    run(
        steps(slot_rings, 0, half),
        [None, make_keys_hop, None, end_relay, None, leave, join_squares],
    )
    run(
        steps([value_ring], 0, half),
        [meet_cache(0), meet_cache(1)] + [None] * (half - 4) + [join_peaks, join_more],
    )

    new_keys = made["keys"]
    best = made["best"].result(clock)
    new_values = by_request(
        product(value_ring.pieces[made["used"] :], False, base=(made["values"],))
    )

    own = lambda stat: lax.dynamic_slice_in_dim(stat, seq_index * tok_block, tok_block, 2)
    greatest_logit = jnp.transpose(own(best), (0, 2, 1)) * SCALE
    residual = lax.dynamic_slice_in_dim(
        flat_input, head_index * local_width, local_width, 1
    ).astype(jnp.float32)
    sums, ring_sums, mixed = [], [], []

    def finish(index):
        def work():
            joined, out, peaks, totals = cached[index]
            some_sums, *parts = finish_part(
                index * group,
                first,
                places,
                clock.hold(joined),
                new_keys,
                new_values,
                out,
                peaks,
                totals,
                best,
            )
            sums.append(some_sums)
            terms = {-offset: part for offset, part in zip(offsets, parts)}
            terms[half] = terms[-half]
            ring_sums.append(RingSum(terms, order))
            return (some_sums, *parts), ()

        return work

    def add_sums():
        if "sums" not in made:
            made["sums"] = Exchange(jnp.concatenate(sums, axis=0), "seq", seq_count, jnp.add)
        made["sums"].step(clock)
        return (), ()

    run([], [finish(0)])
    run([ring_sums[0]], [finish(1)])
    run(steps(ring_sums[::-1], 0, half)[:-1], [add_sums, None, add_sums, None, add_sums])
    denominators = jnp.transpose(own(made["sums"].result(clock)), (0, 2, 1))
    for index in range(GROUPS):
        begin = index * group
        denominator = denominators[begin : begin + group]
        numerator = ring_sums[index].total().reshape(group, tok_block, local_heads, HEAD_DIM)
        attended = (
            (numerator / denominator[..., None])
            .astype(jnp.bfloat16)
            .reshape(group * tok_block, local_att)
        )
        at = slice(begin * tok_block, (begin + group) * tok_block)
        attn_terms = jnp.dot(attended, w_attn_out, preferred_element_type=jnp.float32)
        summed = head_sum(attn_terms + made["terms"][at], head_count, head_index)
        mixed.append(
            (residual[at] + summed)
            .astype(jnp.bfloat16)
            .reshape(group, tok_block, local_width)
        )
    return (
        jnp.concatenate(mixed, axis=0),
        new_keys,
        new_values,
        made["chain"],
        greatest_logit,
    )


def solution(mesh):
    placed = (
        P(None, "seq", None),
        P(),
        P(None, "seq", "head"),
        P(None, "seq", "head"),
        P("seq", "head"),
        P("seq", "head"),
        P("seq", "head"),
        P("head", None),
        P(),
        P(None, None, "head"),
        P(),
        P(None, "head"),
        P("head"),
        P("head"),
        P("head"),
        P("head"),
        P("head", None),
        P(None, "head", None),
    )
    return jax.shard_map(
        shards,
        mesh=mesh,
        in_specs=placed,
        out_specs=(
            P(None, "seq", "head"),
            P(None, "seq", "head"),
            P(None, "seq", "head"),
            P(None, "seq", "head", None),
            P(None, "seq", "head"),
        ),
        check_vma=False,
    )
```

```python
import functools
import math

import jax
import jax.numpy as jnp
from jax import lax
from jax.experimental import pallas as pl
from jax.experimental.pallas import tpu as pltpu
from jax.sharding import PartitionSpec as P

D = 2048
HEAD_DIM = 128
MHEAD_DIM = 64
STATE = 64
D_INNER = 4096
SCALE = 1.0 / math.sqrt(HEAD_DIM)
EXP2_SCALE = SCALE * math.log2(math.e)
DEAD = -1e30
GROUPS = 2
VMEM_BYTES = 56 * 1024 * 1024


def ring_order(count):
    y_count = max(1, count // 4)
    z_count = count // y_count
    order = []
    for y in range(y_count):
        turn = range(z_count) if y % 2 == 0 else range(z_count - 1, -1, -1)
        order += [z * y_count + y for z in turn]
    return order


def ring_step(block, order, distance):
    count = len(order)
    route = [(order[i], order[(i + distance) % count]) for i in range(count)]
    return lax.ppermute(block, "seq", route)


class Ring:
    def __init__(self, block, order, first_row=0):
        self.order = order
        self.steps = len(order) // 2
        self.done = 0
        self.first_row = first_row
        self.block = self.ahead = self.back = block
        self.pieces = [(0, first_row, block)]

    def step(self, clock):
        self.done += 1
        half = self.block.shape[0] // 2
        last = self.done == self.steps
        ahead = self.ahead[:half] if last else self.ahead
        back = self.back[half:] if last else self.back
        ahead, back = clock.hold(ahead, back)
        self.ahead = ring_step(ahead, self.order, 1)
        self.back = ring_step(back, self.order, -1)
        at = self.first_row
        if last:
            self.pieces += [(self.steps, at, self.ahead), (self.steps, at + half, self.back)]
        else:
            self.pieces += [(self.done, at, self.ahead), (-self.done, at, self.back)]
        return [self.ahead, self.back]


class Clock:
    def __init__(self, mark):
        self.mark = mark
        self.late = ()

    def hold(self, *values):
        held = lax.optimization_barrier(tuple(values) + (self.mark,))[: len(values)]
        return held[0] if len(values) == 1 else held

    def turn(self, ring=None, work=None):
        moved = tuple(ring.step(self)) if ring is not None else ()
        done, deferred = work() if work is not None else ((), ())
        self.mark = lax.optimization_barrier((self.mark,) + self.late + tuple(done))[0]
        self.late = moved + tuple(deferred)


class Exchange:
    def __init__(self, value, axis, count, combine):
        self.value, self.axis, self.count, self.combine = value, axis, count, combine
        self.got = None
        self.bit = 1

    def join(self, clock):
        if self.got is not None:
            self.value = self.combine(*clock.hold(self.value, self.got))
            self.got = None

    def step(self, clock):
        self.join(clock)
        if self.bit < self.count:
            route = [(i, i ^ self.bit) for i in range(self.count)]
            self.got = lax.ppermute(self.value, self.axis, route)
            self.bit *= 2

    def result(self, clock):
        while self.bit < self.count:
            self.step(clock)
        self.join(clock)
        return self.value


class RingSum:
    def __init__(self, parts, order):
        self.parts, self.order = parts, order
        self.left = len(order) // 2
        self.half = parts[0].shape[0] // 2
        self.ahead = self.back = None

    def add(self, a, b):
        return (a.astype(jnp.float32) + b.astype(jnp.float32)).astype(jnp.bfloat16)

    def step(self, clock):
        half, left, far = self.half, self.left, len(self.order) // 2
        top, bottom = self.parts[left], self.parts[-left]
        if left == far:
            ahead, back = top[:half], bottom[half:]
        elif left == far - 1:
            ahead = jnp.concatenate([self.add(self.ahead, top[:half]), top[half:]], axis=0)
            back = jnp.concatenate([bottom[:half], self.add(self.back, bottom[half:])], axis=0)
        else:
            ahead, back = self.add(self.ahead, top), self.add(self.back, bottom)
        ahead, back = clock.hold(ahead, back)
        self.ahead = ring_step(ahead, self.order, 1)
        self.back = ring_step(back, self.order, -1)
        self.left -= 1
        return [self.ahead, self.back]

    def total(self):
        return sum(value.astype(jnp.float32) for value in (self.ahead, self.back, self.parts[0]))


def project_kernel(count, turned, places_ref, *refs):
    input_refs, weight_refs = refs[:count], refs[count : 2 * count]
    cosine_ref, sine_ref, *base_ref, out_ref = refs[2 * count :]
    total = base_ref[0][...] if base_ref else None
    for input_ref, weight_ref in zip(input_refs, weight_refs):
        term = jnp.dot(input_ref[...], weight_ref[...], preferred_element_type=jnp.float32)
        total = term if total is None else total + term
    if not turned:
        out_ref[...] = total.astype(out_ref.dtype)
        return
    cosine = cosine_ref[...]
    sine = sine_ref[...]
    for head in range(out_ref.shape[1] // HEAD_DIM):
        at = slice(head * HEAD_DIM, (head + 1) * HEAD_DIM)
        part = total[:, at]
        rolled = pltpu.roll(part, HEAD_DIM // 2, 1)
        out_ref[:, at] = (part * cosine + rolled * sine).astype(out_ref.dtype)


def project(places, offsets, rows, value, pieces, cosine, sine, turned, base=(), kind=jnp.bfloat16):
    tokens = value.shape[0]
    width = pieces[0][2].shape[1]
    block = min(width, 256)
    input_specs, weight_specs = [], []
    for offset, row, piece in pieces:
        depth = piece.shape[0]

        def place(j, places_ref, slot=offsets.index(offset), scale=rows // depth, at=row // depth):
            return (0, places_ref[slot] * scale + at)

        input_specs.append(pl.BlockSpec((tokens, depth), place))
        weight_specs.append(pl.BlockSpec((depth, block), lambda j, *_: (0, j)))
    angle = pl.BlockSpec((tokens, HEAD_DIM), lambda j, *_: (0, 0))
    return pl.pallas_call(
        functools.partial(project_kernel, len(pieces), turned),
        grid_spec=pltpu.PrefetchScalarGridSpec(
            num_scalar_prefetch=1,
            grid=(width // block,),
            in_specs=input_specs
            + weight_specs
            + [angle, angle]
            + [pl.BlockSpec((tokens, block), lambda j, *_: (0, j))] * len(base),
            out_specs=pl.BlockSpec((tokens, block), lambda j, *_: (0, j)),
        ),
        out_shape=jax.ShapeDtypeStruct((tokens, width), kind),
        compiler_params=pltpu.CompilerParams(vmem_limit_bytes=VMEM_BYTES),
        cost_estimate=pl.CostEstimate(
            flops=2 * tokens * sum(piece.shape[0] for _, _, piece in pieces) * width,
            bytes_accessed=2 * (tokens + width) * value.shape[1],
            transcendentals=0,
        ),
        name="project",
    )(places, *[value] * len(pieces), *[piece for _, _, piece in pieces], cosine, sine, *base)


def silu(value):
    return value / (1.0 + jnp.exp(-value))


def exact_dot(a, b):
    return jnp.dot(a, b, precision=lax.Precision.HIGHEST, preferred_element_type=jnp.float32)


def spread(heads, block):
    shape = (heads, heads * block)
    column = lax.broadcasted_iota(jnp.int32, shape, 1) // block
    return (column == lax.broadcasted_iota(jnp.int32, shape, 0)).astype(jnp.float32)


def enter_kernel(input_ref, gain_ref, bc_ref, dt_ref, bias_ref, weight_ref, act_ref, map_ref, size_ref, normed_ref):
    @pl.when(pl.program_id(0) == 0)
    def _():
        rows = input_ref.shape[0]
        chunk = min(rows, 64)
        for start in range(0, rows, chunk):
            at = slice(start, start + chunk)
            hidden = input_ref[at, :].astype(jnp.float32)
            scale = lax.rsqrt(jnp.mean(hidden * hidden, axis=-1, keepdims=True) + 1e-05)
            normed_ref[at, :] = (hidden * scale * gain_ref[...]).astype(jnp.bfloat16)
        normed = normed_ref[...]
        map_ref[...] = jnp.dot(normed, bc_ref[...], preferred_element_type=jnp.float32)
        size = jnp.dot(normed, dt_ref[...], preferred_element_type=jnp.float32) + bias_ref[...]
        size_ref[...] = jnp.maximum(size, 0.0) + jnp.log1p(jnp.exp(-jnp.abs(size)))

    act_ref[...] = silu(
        jnp.dot(normed_ref[...], weight_ref[...], preferred_element_type=jnp.float32)
    )


def enter_mixer(flat_input, norm_gain, w_bc, w_dt, dt_bias, weight):
    tokens = flat_input.shape[0]
    width = weight.shape[1]
    block = min(width, 512)
    heads = w_dt.shape[1]
    whole = lambda *shape: pl.BlockSpec(shape, lambda j: (0, 0))
    return pl.pallas_call(
        enter_kernel,
        grid=(width // block,),
        in_specs=[
            whole(tokens, D),
            whole(1, D),
            whole(D, 2 * STATE),
            whole(D, heads),
            whole(1, heads),
            pl.BlockSpec((D, block), lambda j: (0, j)),
        ],
        out_specs=[
            pl.BlockSpec((tokens, block), lambda j: (0, j)),
            whole(tokens, 2 * STATE),
            whole(tokens, heads),
        ],
        out_shape=[
            jax.ShapeDtypeStruct((tokens, width), jnp.float32),
            jax.ShapeDtypeStruct((tokens, 2 * STATE), jnp.float32),
            jax.ShapeDtypeStruct((tokens, heads), jnp.float32),
        ],
        scratch_shapes=[pltpu.VMEM((tokens, D), jnp.bfloat16)],
        compiler_params=pltpu.CompilerParams(vmem_limit_bytes=VMEM_BYTES),
        cost_estimate=pl.CostEstimate(
            flops=2 * tokens * D * width,
            bytes_accessed=2 * D * (width + tokens) + 4 * tokens * width,
            transcendentals=tokens * width,
        ),
        name="enter_mixer",
    )(flat_input, norm_gain.reshape(1, D), w_bc, w_dt, dt_bias.reshape(1, heads), weight)


def inside_kernel(inner_ref, map_ref, decay_ref, size_ref, decay_row_ref, size_row_ref, skip_ref, read_ref, local_ref, through_ref):
    tokens, heads = decay_ref.shape[1:]
    inner = inner_ref[...]
    input_map = map_ref[:, :STATE]
    output_map = map_ref[:, STATE:]
    decay = decay_ref[0]
    by_head = spread(heads, MHEAD_DIM)
    wide = (tokens, heads * tokens)
    contact = dot_nt(
        output_map.astype(jnp.bfloat16),
        jnp.concatenate([input_map.astype(jnp.bfloat16)] * heads, axis=0),
    )
    source = lax.rem(lax.broadcasted_iota(jnp.int32, wide, 1), tokens)
    causal = source <= lax.broadcasted_iota(jnp.int32, wide, 0)
    difference = exact_dot(decay, spread(heads, tokens)) - decay_row_ref[0]
    mixing = jnp.exp(jnp.where(causal, difference, DEAD)) * contact * size_row_ref[0]
    mixing = mixing.astype(jnp.bfloat16)
    inner_low = inner.astype(jnp.bfloat16)
    together = min(heads, 256 // MHEAD_DIM)
    shape = (together * tokens, together * MHEAD_DIM)
    own = (
        lax.broadcasted_iota(jnp.int32, shape, 0) // tokens
        == lax.broadcasted_iota(jnp.int32, shape, 1) // MHEAD_DIM
    )
    for begin in range(0, heads, together):
        at = slice(begin * MHEAD_DIM, (begin + together) * MHEAD_DIM)
        stacked = jnp.concatenate([inner_low[:, at]] * together, axis=0)
        stacked = jnp.where(own, stacked, jnp.zeros_like(stacked))
        read_ref[:, at] = (
            jnp.dot(
                mixing[:, begin * tokens : (begin + together) * tokens],
                stacked,
                preferred_element_type=jnp.float32,
            )
            + skip_ref[:, at] * inner[:, at]
        )
    last = decay[tokens - 1 :, :]
    tail = exact_dot(jnp.exp(last - decay) * size_ref[0], by_head)
    local_ref[0] = dot_tn(input_map.astype(jnp.bfloat16), (inner * tail).astype(jnp.bfloat16))
    through_ref[0] = exact_dot(jnp.exp(jnp.broadcast_to(last, (8, heads))), by_head)[:1]


def inside_block(requests, act, maps, decay, size, decay_row, size_row, skip):
    tokens, heads = decay.shape[1:]
    inner = act.shape[1] // 2
    one = lambda *shape: pl.BlockSpec((1,) + shape, lambda r: (r, 0, 0))
    return pl.pallas_call(
        inside_kernel,
        grid=(requests,),
        in_specs=[
            pl.BlockSpec((tokens, inner), lambda r: (r, 1)),
            pl.BlockSpec((tokens, 2 * STATE), lambda r: (r, 0)),
            one(tokens, heads),
            one(tokens, heads),
            one(1, heads * tokens),
            one(1, heads * tokens),
            pl.BlockSpec((1, inner), lambda r: (0, 0)),
        ],
        out_specs=[
            pl.BlockSpec((tokens, inner), lambda r: (r, 0)),
            one(STATE, inner),
            one(1, inner),
        ],
        out_shape=[
            jax.ShapeDtypeStruct((requests * tokens, inner), jnp.float32),
            jax.ShapeDtypeStruct((requests, STATE, inner), jnp.float32),
            jax.ShapeDtypeStruct((requests, 1, inner), jnp.float32),
        ],
        compiler_params=pltpu.CompilerParams(vmem_limit_bytes=VMEM_BYTES),
        cost_estimate=pl.CostEstimate(
            flops=12 * requests * tokens * tokens * inner,
            bytes_accessed=16 * requests * tokens * inner,
            transcendentals=requests * tokens * tokens * heads,
        ),
        name="inside_block",
    )(act, maps, decay, size, decay_row, size_row, skip)


def leave_kernel(entry_ref, map_ref, decay_ref, read_ref, gate_ref, gain_ref, local_ref, through_ref, gated_ref, square_ref, chain_ref):
    heads = decay_ref.shape[2]
    entry = entry_ref[0]
    grown = exact_dot(jnp.exp(decay_ref[0]), spread(heads, MHEAD_DIM))
    inter = jnp.dot(
        map_ref[:, STATE:].astype(jnp.bfloat16),
        entry.astype(jnp.bfloat16),
        preferred_element_type=jnp.float32,
    )
    mixed = (read_ref[...] + inter * grown) * gate_ref[...]
    squares = jnp.sum(mixed * mixed, axis=1, keepdims=True)
    square_ref[...] = jnp.broadcast_to(squares, square_ref.shape)
    gated_ref[...] = (mixed * gain_ref[...]).astype(jnp.bfloat16)
    chain_ref[0] = through_ref[0] * entry + local_ref[0]


def leave_mixer(entry, maps, decay, read, act, gain, local, through):
    requests, tokens, heads = decay.shape
    inner = read.shape[1]
    one = lambda *shape: pl.BlockSpec((1,) + shape, lambda r: (r, 0, 0))
    flat = lambda width: pl.BlockSpec((tokens, width), lambda r: (r, 0))
    return pl.pallas_call(
        leave_kernel,
        grid=(requests,),
        in_specs=[
            one(STATE, inner),
            flat(2 * STATE),
            one(tokens, heads),
            flat(inner),
            flat(inner),
            pl.BlockSpec((1, inner), lambda r: (0, 0)),
            one(STATE, inner),
            one(1, inner),
        ],
        out_specs=[flat(inner), flat(128), one(STATE, inner)],
        out_shape=[
            jax.ShapeDtypeStruct((requests * tokens, inner), jnp.bfloat16),
            jax.ShapeDtypeStruct((requests * tokens, 128), jnp.float32),
            jax.ShapeDtypeStruct((requests, STATE, inner), jnp.float32),
        ],
        compiler_params=pltpu.CompilerParams(vmem_limit_bytes=VMEM_BYTES),
        cost_estimate=pl.CostEstimate(
            flops=2 * requests * tokens * STATE * inner,
            bytes_accessed=24 * requests * tokens * inner,
            transcendentals=requests * tokens * heads,
        ),
        name="leave_mixer",
    )(entry, maps, decay, read, act, gain, local, through)


def dot_nt(a, b):
    return lax.dot_general(a, b, (((1,), (1,)), ((), ())), preferred_element_type=jnp.float32)


def dot_tn(a, b):
    return lax.dot_general(a, b, (((0,), (0,)), ((), ())), preferred_element_type=jnp.float32)


def group_scores(first, key, query):
    scores = dot_nt(key, query)
    shape = scores.shape
    live = first + lax.broadcasted_iota(jnp.int32, shape, 0) <= lax.broadcasted_iota(
        jnp.int32, shape, 1
    )
    return jnp.where(live, scores, DEAD)


def cache_kernel(slots, first_ref, place_ref, live_ref, *refs):
    query_refs = refs[:slots]
    key_ref, value_ref, group_ref, joined_ref, out_ref, peak_ref, total_ref = refs[slots:]
    tok_block = query_refs[0].shape[1]
    keys, width = key_ref.shape[1:]
    tokens = tok_block * slots
    for slot in range(slots):
        start = pl.multiple_of(place_ref[slot] * tok_block, tok_block)
        joined_ref[0, pl.ds(start, tok_block), :] = query_refs[slot][0]
    live = live_ref[pl.program_id(0)]
    bias = jnp.where(
        lax.broadcasted_iota(jnp.int32, (keys, 128), 0) < live, 0.0, DEAD
    ).astype(jnp.float32)
    bias = jnp.concatenate([bias] * (tokens // 128), axis=1)
    for head in range(width // HEAD_DIM):
        at = slice(head * HEAD_DIM, (head + 1) * HEAD_DIM)
        query = joined_ref[0, :, at]
        scores = dot_nt(key_ref[0, :, at], query) + bias
        peak = jnp.maximum(
            jnp.max(scores, axis=0, keepdims=True),
            jnp.max(
                group_scores(first_ref[0], group_ref[0, :, at], query), axis=0, keepdims=True
            ),
        )
        weights = jnp.exp2((scores - peak) * EXP2_SCALE)
        total_ref[0, head : head + 1, :] = jnp.sum(weights, axis=0, keepdims=True)
        peak_ref[0, head : head + 1, :] = peak
        out_ref[0, at, :] = dot_tn(value_ref[0, :, at], weights.astype(jnp.bfloat16)).astype(
            out_ref.dtype
        )


def cache_part(begin, first, places, live, query_slots, keys, values, new_keys):
    slots = len(query_slots)
    requests, tok_block, width = query_slots[0].shape
    tokens = tok_block * slots
    cache_block = keys.shape[1]
    heads = width // HEAD_DIM
    one = lambda rows, start: pl.BlockSpec((1, rows, width), lambda r, *_: (r + start, 0, 0))
    stat = pl.BlockSpec((1, heads, tokens), lambda r, *_: (r, 0, 0))
    return pl.pallas_call(
        functools.partial(cache_kernel, slots),
        grid_spec=pltpu.PrefetchScalarGridSpec(
            num_scalar_prefetch=3,
            grid=(requests,),
            in_specs=[one(tok_block, 0)] * slots
            + [one(cache_block, begin)] * 2
            + [one(tok_block, begin)],
            out_specs=[
                one(tokens, 0),
                pl.BlockSpec((1, width, tokens), lambda r, *_: (r, 0, 0)),
                stat,
                stat,
            ],
        ),
        out_shape=[
            jax.ShapeDtypeStruct((requests, tokens, width), jnp.bfloat16),
            jax.ShapeDtypeStruct((requests, width, tokens), jnp.bfloat16),
            jax.ShapeDtypeStruct((requests, heads, tokens), jnp.float32),
            jax.ShapeDtypeStruct((requests, heads, tokens), jnp.float32),
        ],
        compiler_params=pltpu.CompilerParams(vmem_limit_bytes=VMEM_BYTES),
        cost_estimate=pl.CostEstimate(
            flops=4 * requests * tokens * cache_block * width,
            bytes_accessed=2 * requests * width * (3 * tokens + 2 * cache_block),
            transcendentals=requests * tokens * cache_block * heads,
        ),
        name="cache_part",
    )(first, places, live, *query_slots, keys, values, new_keys)


def finish_kernel(slots, first_ref, place_ref, *refs):
    query_ref, key_ref, value_ref, cache_ref, peak_ref, total_ref, best_ref = refs[:7]
    sum_ref, *part_refs = refs[7:-1]
    joined_ref = refs[-1]
    tok_block = key_ref.shape[1]
    for head in range(query_ref.shape[2] // HEAD_DIM):
        at = slice(head * HEAD_DIM, (head + 1) * HEAD_DIM)
        row = slice(head, head + 1)
        scores = group_scores(first_ref[0], key_ref[0, :, at], query_ref[0, :, at])
        best = best_ref[0, row, :]
        weights = jnp.exp2((scores - best) * EXP2_SCALE)
        rescale = jnp.exp2((peak_ref[0, row, :] - best) * EXP2_SCALE)
        sum_ref[0, row, :] = total_ref[0, row, :] * rescale + jnp.sum(
            weights, axis=0, keepdims=True
        )
        joined = cache_ref[0, at, :].astype(jnp.float32) * rescale + dot_tn(
            value_ref[0, :, at], weights.astype(jnp.bfloat16)
        )
        joined_ref[:, at] = joined.astype(jnp.bfloat16).T
    for slot in range(slots):
        start = pl.multiple_of(place_ref[slot] * tok_block, tok_block)
        part_refs[slot][0] = joined_ref[pl.ds(start, tok_block), :]


def finish_part(begin, first, places, queries, new_keys, new_values, cached, peaks, totals, best):
    requests, tokens, width = queries.shape
    tok_block = new_keys.shape[1]
    slots = tokens // tok_block
    heads = width // HEAD_DIM
    one = lambda rows, start: pl.BlockSpec((1, rows, width), lambda r, *_: (r + start, 0, 0))
    stat = lambda start: pl.BlockSpec((1, heads, tokens), lambda r, *_: (r + start, 0, 0))
    return pl.pallas_call(
        functools.partial(finish_kernel, slots),
        grid_spec=pltpu.PrefetchScalarGridSpec(
            num_scalar_prefetch=2,
            grid=(requests,),
            in_specs=[
                one(tokens, 0),
                one(tok_block, begin),
                one(tok_block, begin),
                pl.BlockSpec((1, width, tokens), lambda r, *_: (r, 0, 0)),
                stat(0),
                stat(0),
                stat(begin),
            ],
            out_specs=[stat(0)] + [one(tok_block, 0)] * slots,
            scratch_shapes=[pltpu.VMEM((tokens, width), jnp.bfloat16)],
        ),
        out_shape=[jax.ShapeDtypeStruct((requests, heads, tokens), jnp.float32)]
        + [jax.ShapeDtypeStruct((requests, tok_block, width), jnp.bfloat16)] * slots,
        compiler_params=pltpu.CompilerParams(vmem_limit_bytes=VMEM_BYTES),
        cost_estimate=pl.CostEstimate(
            flops=4 * requests * tokens * tok_block * width,
            bytes_accessed=6 * requests * width * tokens,
            transcendentals=requests * tokens * tok_block * heads,
        ),
        name="finish_part",
    )(first, places, queries, new_keys, new_values, cached, peaks, totals, best)


def head_sum(terms, head_count, head_index):
    if head_count != 4:
        return lax.psum_scatter(
            terms.astype(jnp.bfloat16), "head", scatter_dimension=1, tiled=True
        ).astype(jnp.float32)
    width = terms.shape[1] // 4
    chunk = lambda index: lax.dynamic_slice_in_dim(terms, index * width, width, 1)
    core, column = head_index % 2, head_index // 2
    near, far = 2 * column, 2 * (1 - column)
    got = lax.ppermute(
        jnp.concatenate([chunk(near + 1 - core), chunk(far + 1 - core)], axis=1).astype(
            jnp.bfloat16
        ),
        "head",
        [(h, h ^ 1) for h in range(4)],
    ).astype(jnp.float32)
    keep = chunk(near + core) + got[:, :width]
    give = chunk(far + core) + got[:, width:]
    return keep + lax.ppermute(
        give.astype(jnp.bfloat16), "head", [(h, h ^ 2) for h in range(4)]
    ).astype(jnp.float32)


class Relay:
    def __init__(self, through, local, initial, seq_index, seq_count):
        self.factor, self.local = through, local
        self.paired = seq_count == 8
        self.hop = 0
        if not self.paired:
            self.hops = seq_count - 1
            self.entry = jnp.where(seq_index == 0, initial, 0.0)
            return
        self.hops = 3
        self.swap = [(i, i ^ 1) for i in range(8)]
        self.is_first = is_first = seq_index % 2 == 0
        half = local.shape[2] // 2
        side = lambda value: jnp.where(is_first, value[..., :half], value[..., half:])
        mine = side(local)
        got = self.exchange(jnp.where(is_first, local[..., half:], local[..., :half]))
        other_factor = side(lax.ppermute(through, "seq", self.swap))
        factor = side(through)
        self.first_state = jnp.where(is_first, mine, got)
        second_state = jnp.where(is_first, got, mine)
        self.first_factor = jnp.where(is_first, factor, other_factor)
        second_factor = jnp.where(is_first, other_factor, factor)
        self.pair_state = second_factor * self.first_state + second_state
        self.pair_factor = self.first_factor * second_factor
        self.entry = jnp.where(seq_index < 2, side(initial), 0.0)

    def exchange(self, value):
        return lax.ppermute(value.astype(jnp.bfloat16), "seq", self.swap).astype(jnp.float32)

    def advance(self, clock):
        if self.hop == self.hops:
            return
        factor, state = (
            (self.pair_factor, self.pair_state) if self.paired else (self.factor, self.local)
        )
        entry = clock.hold(self.entry)
        leaving = (factor * entry + state).astype(jnp.bfloat16)
        if self.paired:
            route = [(2 * self.hop + y, 2 * self.hop + 2 + y) for y in range(2)]
        else:
            route = [(self.hop, self.hop + 1)]
        self.hop += 1
        self.entry = entry + lax.ppermute(leaving, "seq", route).astype(jnp.float32)

    def result(self, clock):
        while self.hop < self.hops:
            self.advance(clock)
        entry = clock.hold(self.entry)
        if not self.paired:
            return entry
        second = self.first_factor * entry + self.first_state
        got = self.exchange(jnp.where(self.is_first, second, entry))
        mine = jnp.where(self.is_first, entry, second)
        return jnp.concatenate(
            [jnp.where(self.is_first, mine, got), jnp.where(self.is_first, got, mine)], axis=2
        )


def shards(
    block_input,
    lengths,
    cache_keys,
    cache_values,
    w_query,
    w_key,
    w_value,
    w_attn_out,
    norm_gain,
    w_in,
    w_bc,
    w_dt,
    dt_bias,
    a_log,
    d_skip,
    gated_gain,
    w_out,
    ssm_init,
):
    requests, tok_block, _ = block_input.shape
    seq_count = lax.axis_size("seq")
    seq_index = lax.axis_index("seq")
    head_count = lax.axis_size("head")
    head_index = lax.axis_index("head")
    local_att = w_query.shape[1]
    local_heads = local_att // HEAD_DIM
    cache_block = cache_keys.shape[1]
    rows = w_query.shape[0]
    tokens = requests * tok_block
    flat_input = block_input.reshape(tokens, block_input.shape[2])

    order = ring_order(seq_count)
    half = seq_count // 2
    offsets = [0] + [sign * step for step in range(1, half) for sign in (1, -1)] + [half]
    places = jnp.asarray(
        [
            [order[(order.index(i) - offset) % seq_count] for offset in offsets]
            for i in range(seq_count)
        ],
        jnp.int32,
    )[seq_index]

    positions = (
        lengths[:, None] + seq_index * tok_block + jnp.arange(tok_block, dtype=jnp.int32)[None, :]
    ).reshape(tokens)
    half_dim = HEAD_DIM // 2
    frequency = jnp.exp(
        jnp.arange(half_dim, dtype=jnp.float32) * (-2.0 * math.log(10000.0) / HEAD_DIM)
    )
    angles = positions.astype(jnp.float32)[:, None] * frequency
    cosine = jnp.cos(angles)
    sine = jnp.sin(angles)
    cosine = jnp.concatenate([cosine, cosine], axis=1)
    sine = jnp.concatenate([-sine, sine], axis=1)

    clock = Clock(jnp.zeros((1,), jnp.int32) + lengths[:1])
    group = requests // GROUPS
    local_inner = w_in.shape[2]
    local_mheads = local_inner // MHEAD_DIM
    local_width = D // head_count
    made = {}

    def product(pieces, turned, base=(), kind=jnp.bfloat16):
        pieces = list(pieces)
        if pieces[-1][2].shape[0] < 128:
            (offset, row, upper), (_, _, lower) = pieces[-2:]
            pieces[-2:] = [(offset, row, jnp.concatenate([upper, lower], axis=0))]
        return project(
            places, offsets, rows, flat_input, pieces, cosine, sine, turned, base, kind
        )

    by_request = lambda value: value.reshape(requests, tok_block, local_att)

    def order_weight():
        made["w_in"] = w_in.reshape(D, 2 * local_inner)
        return (made["w_in"],), ()

    def enter():
        made["act"], made["maps"], size = enter_mixer(
            clock.hold(flat_input), norm_gain, w_bc, w_dt, dt_bias, made["w_in"]
        )
        size = size.reshape(requests, tok_block, local_mheads)
        log_decay = -size * jnp.exp(a_log)
        causal = jnp.arange(tok_block)[None, :] <= jnp.arange(tok_block)[:, None]
        decay = jnp.einsum(
            "tu,ruh->rth", causal.astype(jnp.float32), log_decay, precision=lax.Precision.HIGHEST
        )
        by_row = lambda value: jnp.transpose(value, (0, 2, 1)).reshape(
            requests, 1, local_mheads * tok_block
        )
        made["size"], made["decay"] = size, decay
        made["size_row"], made["decay_row"] = by_row(size), by_row(decay)
        return (made["act"], made["size_row"], made["decay_row"]), ()

    def inside():
        made["read"], made["local"], made["through"] = inside_block(
            requests,
            clock.hold(made["act"]),
            made["maps"],
            made["decay"],
            made["size"],
            made["decay_row"],
            made["size_row"],
            jnp.repeat(d_skip, MHEAD_DIM).reshape(1, local_inner),
        )
        return (made["read"], made["local"]), ()

    def start_relay():
        first_state = clock.hold(ssm_init).reshape(requests, local_mheads, MHEAD_DIM, STATE)
        initial = jnp.transpose(first_state, (0, 3, 1, 2)).reshape(requests, STATE, local_inner)
        made["relay"] = relay = Relay(
            made["through"], clock.hold(made["local"]), initial, seq_index, seq_count
        )
        return (initial,), ((relay.pair_state,) if relay.paired else ())

    def hop():
        made["relay"].advance(clock)
        return (), (made["relay"].entry,)

    def end_relay():
        made["entry"] = made["relay"].result(clock)
        return (), (made["entry"],)

    def leave():
        gated, squares, chain = leave_mixer(
            clock.hold(made["entry"]),
            made["maps"],
            made["decay"],
            made["read"],
            made["act"],
            gated_gain.reshape(1, local_inner),
            made["local"],
            made["through"],
        )
        made["gated"] = gated
        made["squares"] = Exchange(
            squares[:, :1].reshape(1, tokens), "head", head_count, jnp.add
        )
        made["squares"].step(clock)
        made["chain"] = chain
        return (gated,), ()

    def join_squares():
        made["squares"].step(clock)
        return (), ()

    def leave_terms():
        squares = made["squares"].result(clock).reshape(tokens, 1)
        made["terms"] = jnp.dot(
            clock.hold(made["gated"]), w_out, preferred_element_type=jnp.float32
        ) * lax.rsqrt(squares / D_INNER + 1e-05)
        return (made["terms"],), ()

    def leave_chain():
        chain = clock.hold(made["chain"]).reshape(requests, STATE, local_mheads, MHEAD_DIM)
        made["chain"] = jnp.transpose(chain, (0, 2, 3, 1)).reshape(
            requests, 1, local_mheads, MHEAD_DIM * STATE
        )
        return (made["chain"],), ()

    query_ring, key_ring, value_ring = (Ring(w, order) for w in (w_query, w_key, w_value))
    slot_rings = []
    live = jnp.clip(lengths - seq_index * cache_block, 0, cache_block).astype(jnp.int32)
    first = (seq_index * tok_block).astype(jnp.int32).reshape(1)
    cached = []

    def make_queries():
        queries = by_request(product(query_ring.pieces, True))
        slot_rings.extend(
            Ring(queries[begin : begin + group], order) for begin in range(0, requests, group)
        )
        return (queries,), ()

    def make_keys():
        made["keys"] = by_request(product(key_ring.pieces, True))
        return (made["keys"],), ()

    def meet_cache(index):
        def work():
            ring = slot_rings[index]
            begin = index * group
            slots = [piece for _, _, piece in ring.pieces[:-2]]
            slots.append(jnp.concatenate([ring.pieces[-2][2], ring.pieces[-1][2]], axis=0))
            slots[0] = clock.hold(slots[0])
            cached.append(
                cache_part(
                    begin,
                    first,
                    places,
                    live[begin : begin + group],
                    slots,
                    cache_keys,
                    cache_values,
                    made["keys"],
                )
            )
            return tuple(cached[-1]), ()

        return work

    def join_peaks():
        peaks = jnp.concatenate([clock.hold(part[2]) for part in cached], axis=0)
        made["best"] = Exchange(peaks, "seq", seq_count, jnp.maximum)
        made["best"].step(clock)
        return leave_chain()

    def make_values():
        made["best"].step(clock)
        made["values"] = product(
            [(0, 0, clock.hold(value_ring.block))] + value_ring.pieces[1:-2],
            False,
            kind=jnp.float32,
        )
        return (made["values"],), ()

    def steps(rings, begin, end):
        return [ring for _ in range(begin, end) for ring in rings]

    def run(sends, works):
        for index in range(max(len(sends), len(works))):
            clock.turn(
                sends[index] if index < len(sends) else None,
                works[index] if index < len(works) else None,
            )

    both = steps([query_ring, key_ring], 0, half - 2) + [query_ring] * 2 + [key_ring] * 2
    works = [order_weight, enter, inside, start_relay, hop, None, hop]
    run(both, works + [None] * (len(both) - 1 - len(works)) + [make_queries])
    run(
        steps(slot_rings, 0, half),
        [hop, make_keys, end_relay, None, leave, join_squares, leave_terms],
    )
    run(
        steps([value_ring], 0, half),
        [meet_cache(0), meet_cache(1)] + [None] * (half - 4) + [join_peaks, make_values],
    )

    new_keys = made["keys"]
    best = made["best"].result(clock)
    new_values = by_request(product(value_ring.pieces[-2:], False, base=(made["values"],)))

    own = lambda stat: lax.dynamic_slice_in_dim(stat, seq_index * tok_block, tok_block, 2)
    greatest_logit = jnp.transpose(own(best), (0, 2, 1)) * SCALE
    residual = lax.dynamic_slice_in_dim(
        flat_input, head_index * local_width, local_width, 1
    ).astype(jnp.float32)
    sums, ring_sums, mixed = [], [], []

    def finish(index):
        def work():
            joined, out, peaks, totals = cached[index]
            some_sums, *parts = finish_part(
                index * group,
                first,
                places,
                clock.hold(joined),
                new_keys,
                new_values,
                out,
                peaks,
                totals,
                best,
            )
            sums.append(some_sums)
            terms = {-offset: part for offset, part in zip(offsets, parts)}
            terms[half] = terms[-half]
            ring_sums.append(RingSum(terms, order))
            return (some_sums, *parts), ()

        return work

    def add_sums():
        if "sums" not in made:
            made["sums"] = Exchange(jnp.concatenate(sums, axis=0), "seq", seq_count, jnp.add)
        made["sums"].step(clock)
        return (), ()

    run([], [finish(0)])
    run([ring_sums[0]], [finish(1)])
    run(steps(ring_sums[::-1], 0, half)[:-1], [add_sums, None, add_sums, None, add_sums])
    denominators = jnp.transpose(own(made["sums"].result(clock)), (0, 2, 1))
    for index in range(GROUPS):
        begin = index * group
        denominator = denominators[begin : begin + group]
        numerator = ring_sums[index].total().reshape(group, tok_block, local_heads, HEAD_DIM)
        attended = (
            (numerator / denominator[..., None])
            .astype(jnp.bfloat16)
            .reshape(group * tok_block, local_att)
        )
        at = slice(begin * tok_block, (begin + group) * tok_block)
        attn_terms = jnp.dot(attended, w_attn_out, preferred_element_type=jnp.float32)
        summed = head_sum(attn_terms + made["terms"][at], head_count, head_index)
        mixed.append(
            (residual[at] + summed)
            .astype(jnp.bfloat16)
            .reshape(group, tok_block, local_width)
        )
    return (
        jnp.concatenate(mixed, axis=0),
        new_keys,
        new_values,
        made["chain"],
        greatest_logit,
    )


def solution(mesh):
    placed = (
        P(None, "seq", None),
        P(),
        P(None, "seq", "head"),
        P(None, "seq", "head"),
        P("seq", "head"),
        P("seq", "head"),
        P("seq", "head"),
        P("head", None),
        P(),
        P(None, None, "head"),
        P(),
        P(None, "head"),
        P("head"),
        P("head"),
        P("head"),
        P("head"),
        P("head", None),
        P(None, "head", None),
    )
    return jax.shard_map(
        shards,
        mesh=mesh,
        in_specs=placed,
        out_specs=(
            P(None, "seq", "head"),
            P(None, "seq", "head"),
            P(None, "seq", "head"),
            P(None, "seq", "head", None),
            P(None, "seq", "head"),
        ),
        check_vma=False,
    )
```

```python
import functools
import math

import jax
import jax.numpy as jnp
from jax import lax
from jax.experimental import pallas as pl
from jax.experimental.pallas import tpu as pltpu
from jax.sharding import PartitionSpec as P

D = 2048
HEAD_DIM = 128
MHEAD_DIM = 64
STATE = 64
D_INNER = 4096
SCALE = 1.0 / math.sqrt(HEAD_DIM)
EXP2_SCALE = SCALE * math.log2(math.e)
DEAD = -1e30
GROUPS = 2
VMEM_BYTES = 56 * 1024 * 1024
LIGHT = pl.CostEstimate(flops=0, bytes_accessed=0, transcendentals=0)


def ring_order(count):
    y_count = max(1, count // 4)
    z_count = count // y_count
    order = []
    for y in range(y_count):
        turn = range(z_count) if y % 2 == 0 else range(z_count - 1, -1, -1)
        order += [z * y_count + y for z in turn]
    return order


def ring_step(block, order, distance):
    count = len(order)
    route = [(order[i], order[(i + distance) % count]) for i in range(count)]
    return lax.ppermute(block, "seq", route)


class Ring:
    def __init__(self, block, order, first_row=0):
        self.order = order
        self.steps = len(order) // 2
        self.done = 0
        self.first_row = first_row
        self.block = self.ahead = self.back = block
        self.pieces = [(0, first_row, block)]

    def step(self, clock):
        self.done += 1
        half = self.block.shape[0] // 2
        last = self.done == self.steps
        ahead = self.ahead[:half] if last else self.ahead
        back = self.back[half:] if last else self.back
        ahead, back = clock.hold(ahead, back)
        self.ahead = ring_step(ahead, self.order, 1)
        self.back = ring_step(back, self.order, -1)
        at = self.first_row
        if last:
            self.pieces += [(self.steps, at, self.ahead), (self.steps, at + half, self.back)]
        else:
            self.pieces += [(self.done, at, self.ahead), (-self.done, at, self.back)]
        return [self.ahead, self.back]


class Clock:
    def __init__(self, mark):
        self.mark = mark
        self.late = ()

    def hold(self, *values):
        held = lax.optimization_barrier(tuple(values) + (self.mark,))[: len(values)]
        return held[0] if len(values) == 1 else held

    def turn(self, ring=None, work=None):
        moved = tuple(ring.step(self)) if ring is not None else ()
        done, deferred = work() if work is not None else ((), ())
        self.mark = lax.optimization_barrier((self.mark,) + self.late + tuple(done))[0]
        self.late = moved + tuple(deferred)


class Exchange:
    def __init__(self, value, axis, count, combine):
        self.value, self.axis, self.count, self.combine = value, axis, count, combine
        self.got = None
        self.bit = 1

    def join(self, clock):
        if self.got is not None:
            self.value = self.combine(*clock.hold(self.value, self.got))
            self.got = None

    def step(self, clock):
        self.join(clock)
        if self.bit < self.count:
            route = [(i, i ^ self.bit) for i in range(self.count)]
            self.got = lax.ppermute(self.value, self.axis, route)
            self.bit *= 2

    def result(self, clock):
        while self.bit < self.count:
            self.step(clock)
        self.join(clock)
        return self.value


class RingSum:
    def __init__(self, parts, order):
        self.parts, self.order = parts, order
        self.left = len(order) // 2
        self.half = parts[0].shape[0] // 2
        self.ahead = self.back = None

    def add(self, a, b):
        return (a.astype(jnp.float32) + b.astype(jnp.float32)).astype(jnp.bfloat16)

    def step(self, clock):
        half, left, far = self.half, self.left, len(self.order) // 2
        top, bottom = self.parts[left], self.parts[-left]
        if left == far:
            ahead, back = top[:half], bottom[half:]
        elif left == far - 1:
            ahead = jnp.concatenate([self.add(self.ahead, top[:half]), top[half:]], axis=0)
            back = jnp.concatenate([bottom[:half], self.add(self.back, bottom[half:])], axis=0)
        else:
            ahead, back = self.add(self.ahead, top), self.add(self.back, bottom)
        ahead, back = clock.hold(ahead, back)
        self.ahead = ring_step(ahead, self.order, 1)
        self.back = ring_step(back, self.order, -1)
        self.left -= 1
        return [self.ahead, self.back]

    def total(self):
        return sum(value.astype(jnp.float32) for value in (self.ahead, self.back, self.parts[0]))


def project_kernel(count, turned, places_ref, *refs):
    input_refs, weight_refs = refs[:count], refs[count : 2 * count]
    cosine_ref, sine_ref, *base_ref, out_ref = refs[2 * count :]
    total = base_ref[0][...] if base_ref else None
    for input_ref, weight_ref in zip(input_refs, weight_refs):
        term = jnp.dot(input_ref[...], weight_ref[...], preferred_element_type=jnp.float32)
        total = term if total is None else total + term
    if not turned:
        out_ref[...] = total.astype(out_ref.dtype)
        return
    cosine = cosine_ref[...]
    sine = sine_ref[...]
    for head in range(out_ref.shape[1] // HEAD_DIM):
        at = slice(head * HEAD_DIM, (head + 1) * HEAD_DIM)
        part = total[:, at]
        rolled = pltpu.roll(part, HEAD_DIM // 2, 1)
        out_ref[:, at] = (part * cosine + rolled * sine).astype(out_ref.dtype)


def project(places, offsets, rows, value, pieces, cosine, sine, turned, base=(), kind=jnp.bfloat16):
    tokens = value.shape[0]
    width = pieces[0][2].shape[1]
    block = min(width, 256)
    input_specs, weight_specs = [], []
    for offset, row, piece in pieces:
        depth = piece.shape[0]

        def place(j, places_ref, slot=offsets.index(offset), scale=rows // depth, at=row // depth):
            return (0, places_ref[slot] * scale + at)

        input_specs.append(pl.BlockSpec((tokens, depth), place))
        weight_specs.append(pl.BlockSpec((depth, block), lambda j, *_: (0, j)))
    angle = pl.BlockSpec((tokens, HEAD_DIM), lambda j, *_: (0, 0))
    return pl.pallas_call(
        functools.partial(project_kernel, len(pieces), turned),
        grid_spec=pltpu.PrefetchScalarGridSpec(
            num_scalar_prefetch=1,
            grid=(width // block,),
            in_specs=input_specs
            + weight_specs
            + [angle, angle]
            + [pl.BlockSpec((tokens, block), lambda j, *_: (0, j))] * len(base),
            out_specs=pl.BlockSpec((tokens, block), lambda j, *_: (0, j)),
        ),
        out_shape=jax.ShapeDtypeStruct((tokens, width), kind),
        compiler_params=pltpu.CompilerParams(vmem_limit_bytes=VMEM_BYTES),
        cost_estimate=LIGHT,
        name="project",
    )(places, *[value] * len(pieces), *[piece for _, _, piece in pieces], cosine, sine, *base)


def silu(value):
    return value / (1.0 + jnp.exp(-value))


def exact_dot(a, b):
    return jnp.dot(a, b, precision=lax.Precision.HIGHEST, preferred_element_type=jnp.float32)


def spread(heads, block):
    shape = (heads, heads * block)
    column = lax.broadcasted_iota(jnp.int32, shape, 1) // block
    return (column == lax.broadcasted_iota(jnp.int32, shape, 0)).astype(jnp.float32)


def enter_kernel(input_ref, gain_ref, bc_ref, dt_ref, bias_ref, weight_ref, act_ref, map_ref, size_ref, normed_ref):
    @pl.when(pl.program_id(0) == 0)
    def _():
        rows = input_ref.shape[0]
        chunk = min(rows, 64)
        for start in range(0, rows, chunk):
            at = slice(start, start + chunk)
            hidden = input_ref[at, :].astype(jnp.float32)
            scale = lax.rsqrt(jnp.mean(hidden * hidden, axis=-1, keepdims=True) + 1e-05)
            normed_ref[at, :] = (hidden * scale * gain_ref[...]).astype(jnp.bfloat16)
        normed = normed_ref[...]
        map_ref[...] = jnp.dot(normed, bc_ref[...], preferred_element_type=jnp.float32)
        size = jnp.dot(normed, dt_ref[...], preferred_element_type=jnp.float32) + bias_ref[...]
        size_ref[...] = jnp.maximum(size, 0.0) + jnp.log1p(jnp.exp(-jnp.abs(size)))

    act_ref[...] = silu(
        jnp.dot(normed_ref[...], weight_ref[...], preferred_element_type=jnp.float32)
    )


def enter_mixer(flat_input, norm_gain, w_bc, w_dt, dt_bias, weight):
    tokens = flat_input.shape[0]
    width = weight.shape[1]
    block = min(width, 512)
    heads = w_dt.shape[1]
    whole = lambda *shape: pl.BlockSpec(shape, lambda j: (0, 0))
    return pl.pallas_call(
        enter_kernel,
        grid=(width // block,),
        in_specs=[
            whole(tokens, D),
            whole(1, D),
            whole(D, 2 * STATE),
            whole(D, heads),
            whole(1, heads),
            pl.BlockSpec((D, block), lambda j: (0, j)),
        ],
        out_specs=[
            pl.BlockSpec((tokens, block), lambda j: (0, j)),
            whole(tokens, 2 * STATE),
            whole(tokens, heads),
        ],
        out_shape=[
            jax.ShapeDtypeStruct((tokens, width), jnp.float32),
            jax.ShapeDtypeStruct((tokens, 2 * STATE), jnp.float32),
            jax.ShapeDtypeStruct((tokens, heads), jnp.float32),
        ],
        scratch_shapes=[pltpu.VMEM((tokens, D), jnp.bfloat16)],
        compiler_params=pltpu.CompilerParams(vmem_limit_bytes=VMEM_BYTES),
        cost_estimate=LIGHT,
        name="enter_mixer",
    )(flat_input, norm_gain.reshape(1, D), w_bc, w_dt, dt_bias.reshape(1, heads), weight)


def inside_kernel(inner_ref, map_ref, decay_ref, size_ref, decay_row_ref, size_row_ref, skip_ref, read_ref, local_ref, through_ref):
    tokens, heads = decay_ref.shape[1:]
    inner = inner_ref[...]
    input_map = map_ref[:, :STATE]
    output_map = map_ref[:, STATE:]
    decay = decay_ref[0]
    by_head = spread(heads, MHEAD_DIM)
    wide = (tokens, heads * tokens)
    contact = dot_nt(
        output_map.astype(jnp.bfloat16),
        jnp.concatenate([input_map.astype(jnp.bfloat16)] * heads, axis=0),
    )
    source = lax.rem(lax.broadcasted_iota(jnp.int32, wide, 1), tokens)
    causal = source <= lax.broadcasted_iota(jnp.int32, wide, 0)
    difference = exact_dot(decay, spread(heads, tokens)) - decay_row_ref[0]
    mixing = jnp.exp(jnp.where(causal, difference, DEAD)) * contact * size_row_ref[0]
    mixing = mixing.astype(jnp.bfloat16)
    inner_low = inner.astype(jnp.bfloat16)
    together = min(heads, 256 // MHEAD_DIM)
    shape = (together * tokens, together * MHEAD_DIM)
    own = (
        lax.broadcasted_iota(jnp.int32, shape, 0) // tokens
        == lax.broadcasted_iota(jnp.int32, shape, 1) // MHEAD_DIM
    )
    for begin in range(0, heads, together):
        at = slice(begin * MHEAD_DIM, (begin + together) * MHEAD_DIM)
        stacked = jnp.concatenate([inner_low[:, at]] * together, axis=0)
        stacked = jnp.where(own, stacked, jnp.zeros_like(stacked))
        read_ref[:, at] = (
            jnp.dot(
                mixing[:, begin * tokens : (begin + together) * tokens],
                stacked,
                preferred_element_type=jnp.float32,
            )
            + skip_ref[:, at] * inner[:, at]
        )
    last = decay[tokens - 1 :, :]
    tail = exact_dot(jnp.exp(last - decay) * size_ref[0], by_head)
    local_ref[0] = dot_tn(input_map.astype(jnp.bfloat16), (inner * tail).astype(jnp.bfloat16))
    through_ref[0] = exact_dot(jnp.exp(jnp.broadcast_to(last, (8, heads))), by_head)[:1]


def inside_block(requests, act, maps, decay, size, decay_row, size_row, skip):
    tokens, heads = decay.shape[1:]
    inner = act.shape[1] // 2
    one = lambda *shape: pl.BlockSpec((1,) + shape, lambda r: (r, 0, 0))
    return pl.pallas_call(
        inside_kernel,
        grid=(requests,),
        in_specs=[
            pl.BlockSpec((tokens, inner), lambda r: (r, 1)),
            pl.BlockSpec((tokens, 2 * STATE), lambda r: (r, 0)),
            one(tokens, heads),
            one(tokens, heads),
            one(1, heads * tokens),
            one(1, heads * tokens),
            pl.BlockSpec((1, inner), lambda r: (0, 0)),
        ],
        out_specs=[
            pl.BlockSpec((tokens, inner), lambda r: (r, 0)),
            one(STATE, inner),
            one(1, inner),
        ],
        out_shape=[
            jax.ShapeDtypeStruct((requests * tokens, inner), jnp.float32),
            jax.ShapeDtypeStruct((requests, STATE, inner), jnp.float32),
            jax.ShapeDtypeStruct((requests, 1, inner), jnp.float32),
        ],
        compiler_params=pltpu.CompilerParams(vmem_limit_bytes=VMEM_BYTES),
        cost_estimate=LIGHT,
        name="inside_block",
    )(act, maps, decay, size, decay_row, size_row, skip)


def leave_kernel(entry_ref, map_ref, decay_ref, read_ref, gate_ref, gain_ref, local_ref, through_ref, gated_ref, square_ref, chain_ref):
    heads = decay_ref.shape[2]
    entry = entry_ref[0]
    grown = exact_dot(jnp.exp(decay_ref[0]), spread(heads, MHEAD_DIM))
    inter = jnp.dot(
        map_ref[:, STATE:].astype(jnp.bfloat16),
        entry.astype(jnp.bfloat16),
        preferred_element_type=jnp.float32,
    )
    mixed = (read_ref[...] + inter * grown) * gate_ref[...]
    squares = jnp.sum(mixed * mixed, axis=1, keepdims=True)
    square_ref[...] = jnp.broadcast_to(squares, square_ref.shape)
    gated_ref[...] = (mixed * gain_ref[...]).astype(jnp.bfloat16)
    chain_ref[0] = (through_ref[0] * entry + local_ref[0]).T


def leave_mixer(entry, maps, decay, read, act, gain, local, through):
    requests, tokens, heads = decay.shape
    inner = read.shape[1]
    one = lambda *shape: pl.BlockSpec((1,) + shape, lambda r: (r, 0, 0))
    flat = lambda width: pl.BlockSpec((tokens, width), lambda r: (r, 0))
    return pl.pallas_call(
        leave_kernel,
        grid=(requests,),
        in_specs=[
            one(STATE, inner),
            flat(2 * STATE),
            one(tokens, heads),
            flat(inner),
            flat(inner),
            pl.BlockSpec((1, inner), lambda r: (0, 0)),
            one(STATE, inner),
            one(1, inner),
        ],
        out_specs=[flat(inner), flat(128), one(inner, STATE)],
        out_shape=[
            jax.ShapeDtypeStruct((requests * tokens, inner), jnp.bfloat16),
            jax.ShapeDtypeStruct((requests * tokens, 128), jnp.float32),
            jax.ShapeDtypeStruct((requests, inner, STATE), jnp.float32),
        ],
        compiler_params=pltpu.CompilerParams(vmem_limit_bytes=VMEM_BYTES),
        cost_estimate=LIGHT,
        name="leave_mixer",
    )(entry, maps, decay, read, act, gain, local, through)


def dot_nt(a, b):
    return lax.dot_general(a, b, (((1,), (1,)), ((), ())), preferred_element_type=jnp.float32)


def dot_tn(a, b):
    return lax.dot_general(a, b, (((0,), (0,)), ((), ())), preferred_element_type=jnp.float32)


def group_scores(first, key, query):
    scores = dot_nt(key, query)
    shape = scores.shape
    live = first + lax.broadcasted_iota(jnp.int32, shape, 0) <= lax.broadcasted_iota(
        jnp.int32, shape, 1
    )
    return jnp.where(live, scores, DEAD)


def cache_kernel(slots, first_ref, place_ref, live_ref, *refs):
    query_refs = refs[:slots]
    key_ref, value_ref, group_ref, joined_ref, out_ref, peak_ref, total_ref = refs[slots:]
    tok_block = query_refs[0].shape[1]
    keys, width = key_ref.shape[1:]
    tokens = tok_block * slots
    for slot in range(slots):
        start = pl.multiple_of(place_ref[slot] * tok_block, tok_block)
        joined_ref[0, pl.ds(start, tok_block), :] = query_refs[slot][0]
    live = live_ref[pl.program_id(0)]
    bias = jnp.where(
        lax.broadcasted_iota(jnp.int32, (keys, 128), 0) < live, 0.0, DEAD
    ).astype(jnp.float32)
    bias = jnp.concatenate([bias] * (tokens // 128), axis=1)
    for head in range(width // HEAD_DIM):
        at = slice(head * HEAD_DIM, (head + 1) * HEAD_DIM)
        query = joined_ref[0, :, at]
        scores = dot_nt(key_ref[0, :, at], query) + bias
        peak = jnp.maximum(
            jnp.max(scores, axis=0, keepdims=True),
            jnp.max(
                group_scores(first_ref[0], group_ref[0, :, at], query), axis=0, keepdims=True
            ),
        )
        weights = jnp.exp2((scores - peak) * EXP2_SCALE)
        total_ref[0, head : head + 1, :] = jnp.sum(weights, axis=0, keepdims=True)
        peak_ref[0, head : head + 1, :] = peak
        out_ref[0, at, :] = dot_tn(value_ref[0, :, at], weights.astype(jnp.bfloat16)).astype(
            out_ref.dtype
        )


def cache_part(begin, first, places, live, query_slots, keys, values, new_keys):
    slots = len(query_slots)
    requests, tok_block, width = query_slots[0].shape
    tokens = tok_block * slots
    cache_block = keys.shape[1]
    heads = width // HEAD_DIM
    one = lambda rows, start: pl.BlockSpec((1, rows, width), lambda r, *_: (r + start, 0, 0))
    stat = pl.BlockSpec((1, heads, tokens), lambda r, *_: (r, 0, 0))
    return pl.pallas_call(
        functools.partial(cache_kernel, slots),
        grid_spec=pltpu.PrefetchScalarGridSpec(
            num_scalar_prefetch=3,
            grid=(requests,),
            in_specs=[one(tok_block, 0)] * slots
            + [one(cache_block, begin)] * 2
            + [one(tok_block, begin)],
            out_specs=[
                one(tokens, 0),
                pl.BlockSpec((1, width, tokens), lambda r, *_: (r, 0, 0)),
                stat,
                stat,
            ],
        ),
        out_shape=[
            jax.ShapeDtypeStruct((requests, tokens, width), jnp.bfloat16),
            jax.ShapeDtypeStruct((requests, width, tokens), jnp.bfloat16),
            jax.ShapeDtypeStruct((requests, heads, tokens), jnp.float32),
            jax.ShapeDtypeStruct((requests, heads, tokens), jnp.float32),
        ],
        compiler_params=pltpu.CompilerParams(vmem_limit_bytes=VMEM_BYTES),
        cost_estimate=LIGHT,
        name="cache_part",
    )(first, places, live, *query_slots, keys, values, new_keys)


def finish_kernel(slots, first_ref, place_ref, *refs):
    query_ref, key_ref, value_ref, cache_ref, peak_ref, total_ref, best_ref = refs[:7]
    sum_ref, *part_refs = refs[7:-1]
    joined_ref = refs[-1]
    tok_block = key_ref.shape[1]
    for head in range(query_ref.shape[2] // HEAD_DIM):
        at = slice(head * HEAD_DIM, (head + 1) * HEAD_DIM)
        row = slice(head, head + 1)
        scores = group_scores(first_ref[0], key_ref[0, :, at], query_ref[0, :, at])
        best = best_ref[0, row, :]
        weights = jnp.exp2((scores - best) * EXP2_SCALE)
        rescale = jnp.exp2((peak_ref[0, row, :] - best) * EXP2_SCALE)
        sum_ref[0, row, :] = total_ref[0, row, :] * rescale + jnp.sum(
            weights, axis=0, keepdims=True
        )
        joined = cache_ref[0, at, :].astype(jnp.float32) * rescale + dot_tn(
            value_ref[0, :, at], weights.astype(jnp.bfloat16)
        )
        joined_ref[:, at] = joined.astype(jnp.bfloat16).T
    for slot in range(slots):
        start = pl.multiple_of(place_ref[slot] * tok_block, tok_block)
        part_refs[slot][0] = joined_ref[pl.ds(start, tok_block), :]


def finish_part(begin, first, places, queries, new_keys, new_values, cached, peaks, totals, best):
    requests, tokens, width = queries.shape
    tok_block = new_keys.shape[1]
    slots = tokens // tok_block
    heads = width // HEAD_DIM
    one = lambda rows, start: pl.BlockSpec((1, rows, width), lambda r, *_: (r + start, 0, 0))
    stat = lambda start: pl.BlockSpec((1, heads, tokens), lambda r, *_: (r + start, 0, 0))
    return pl.pallas_call(
        functools.partial(finish_kernel, slots),
        grid_spec=pltpu.PrefetchScalarGridSpec(
            num_scalar_prefetch=2,
            grid=(requests,),
            in_specs=[
                one(tokens, 0),
                one(tok_block, begin),
                one(tok_block, begin),
                pl.BlockSpec((1, width, tokens), lambda r, *_: (r, 0, 0)),
                stat(0),
                stat(0),
                stat(begin),
            ],
            out_specs=[stat(0)] + [one(tok_block, 0)] * slots,
            scratch_shapes=[pltpu.VMEM((tokens, width), jnp.bfloat16)],
        ),
        out_shape=[jax.ShapeDtypeStruct((requests, heads, tokens), jnp.float32)]
        + [jax.ShapeDtypeStruct((requests, tok_block, width), jnp.bfloat16)] * slots,
        compiler_params=pltpu.CompilerParams(vmem_limit_bytes=VMEM_BYTES),
        cost_estimate=LIGHT,
        name="finish_part",
    )(first, places, queries, new_keys, new_values, cached, peaks, totals, best)


def head_sum(terms, head_count, head_index):
    if head_count != 4:
        return lax.psum_scatter(
            terms.astype(jnp.bfloat16), "head", scatter_dimension=1, tiled=True
        ).astype(jnp.float32)
    width = terms.shape[1] // 4
    chunk = lambda index: lax.dynamic_slice_in_dim(terms, index * width, width, 1)
    core, column = head_index % 2, head_index // 2
    near, far = 2 * column, 2 * (1 - column)
    got = lax.ppermute(
        jnp.concatenate([chunk(near + 1 - core), chunk(far + 1 - core)], axis=1).astype(
            jnp.bfloat16
        ),
        "head",
        [(h, h ^ 1) for h in range(4)],
    ).astype(jnp.float32)
    keep = chunk(near + core) + got[:, :width]
    give = chunk(far + core) + got[:, width:]
    return keep + lax.ppermute(
        give.astype(jnp.bfloat16), "head", [(h, h ^ 2) for h in range(4)]
    ).astype(jnp.float32)


class Relay:
    def __init__(self, through, local, initial, seq_index, seq_count):
        self.factor, self.local = through, local
        self.paired = seq_count == 8
        self.hop = 0
        if not self.paired:
            self.hops = seq_count - 1
            self.entry = jnp.where(seq_index == 0, initial, 0.0)
            return
        self.hops = 3
        self.swap = [(i, i ^ 1) for i in range(8)]
        self.is_first = is_first = seq_index % 2 == 0
        half = local.shape[2] // 2
        side = lambda value: jnp.where(is_first, value[..., :half], value[..., half:])
        mine = side(local)
        got = self.exchange(jnp.where(is_first, local[..., half:], local[..., :half]))
        other_factor = side(lax.ppermute(through, "seq", self.swap))
        factor = side(through)
        self.first_state = jnp.where(is_first, mine, got)
        second_state = jnp.where(is_first, got, mine)
        self.first_factor = jnp.where(is_first, factor, other_factor)
        second_factor = jnp.where(is_first, other_factor, factor)
        self.pair_state = second_factor * self.first_state + second_state
        self.pair_factor = self.first_factor * second_factor
        self.entry = jnp.where(seq_index < 2, side(initial), 0.0)

    def exchange(self, value):
        return lax.ppermute(value.astype(jnp.bfloat16), "seq", self.swap).astype(jnp.float32)

    def advance(self, clock):
        if self.hop == self.hops:
            return
        factor, state = (
            (self.pair_factor, self.pair_state) if self.paired else (self.factor, self.local)
        )
        entry = clock.hold(self.entry)
        leaving = (factor * entry + state).astype(jnp.bfloat16)
        if self.paired:
            route = [(2 * self.hop + y, 2 * self.hop + 2 + y) for y in range(2)]
        else:
            route = [(self.hop, self.hop + 1)]
        self.hop += 1
        self.entry = entry + lax.ppermute(leaving, "seq", route).astype(jnp.float32)

    def result(self, clock):
        while self.hop < self.hops:
            self.advance(clock)
        entry = clock.hold(self.entry)
        if not self.paired:
            return entry
        second = self.first_factor * entry + self.first_state
        got = self.exchange(jnp.where(self.is_first, second, entry))
        mine = jnp.where(self.is_first, entry, second)
        return jnp.concatenate(
            [jnp.where(self.is_first, mine, got), jnp.where(self.is_first, got, mine)], axis=2
        )


def shards(
    block_input,
    lengths,
    cache_keys,
    cache_values,
    w_query,
    w_key,
    w_value,
    w_attn_out,
    norm_gain,
    w_in,
    w_bc,
    w_dt,
    dt_bias,
    a_log,
    d_skip,
    gated_gain,
    w_out,
    ssm_init,
):
    requests, tok_block, _ = block_input.shape
    seq_count = lax.axis_size("seq")
    seq_index = lax.axis_index("seq")
    head_count = lax.axis_size("head")
    head_index = lax.axis_index("head")
    local_att = w_query.shape[1]
    local_heads = local_att // HEAD_DIM
    cache_block = cache_keys.shape[1]
    rows = w_query.shape[0]
    tokens = requests * tok_block
    flat_input = block_input.reshape(tokens, block_input.shape[2])

    order = ring_order(seq_count)
    half = seq_count // 2
    offsets = [0] + [sign * step for step in range(1, half) for sign in (1, -1)] + [half]
    places = jnp.asarray(
        [
            [order[(order.index(i) - offset) % seq_count] for offset in offsets]
            for i in range(seq_count)
        ],
        jnp.int32,
    )[seq_index]

    positions = (
        lengths[:, None] + seq_index * tok_block + jnp.arange(tok_block, dtype=jnp.int32)[None, :]
    ).reshape(tokens)
    half_dim = HEAD_DIM // 2
    frequency = jnp.exp(
        jnp.arange(half_dim, dtype=jnp.float32) * (-2.0 * math.log(10000.0) / HEAD_DIM)
    )
    angles = positions.astype(jnp.float32)[:, None] * frequency
    cosine = jnp.cos(angles)
    sine = jnp.sin(angles)
    cosine = jnp.concatenate([cosine, cosine], axis=1)
    sine = jnp.concatenate([-sine, sine], axis=1)

    clock = Clock(jnp.zeros((1,), jnp.int32) + lengths[:1])
    group = requests // GROUPS
    local_inner = w_in.shape[2]
    local_mheads = local_inner // MHEAD_DIM
    local_width = D // head_count
    made = {}

    def product(pieces, turned, base=(), kind=jnp.bfloat16):
        pieces = list(pieces)
        if pieces[-1][2].shape[0] < 128:
            (offset, row, upper), (_, _, lower) = pieces[-2:]
            pieces[-2:] = [(offset, row, jnp.concatenate([upper, lower], axis=0))]
        return project(
            places, offsets, rows, flat_input, pieces, cosine, sine, turned, base, kind
        )

    by_request = lambda value: value.reshape(requests, tok_block, local_att)

    def prepare():
        made["w_in"] = w_in.reshape(D, 2 * local_inner)
        first_state = ssm_init.reshape(requests, local_mheads, MHEAD_DIM, STATE)
        made["initial"] = jnp.transpose(first_state, (0, 3, 1, 2)).reshape(
            requests, STATE, local_inner
        )
        return (made["w_in"], made["initial"]), ()

    def enter():
        made["act"], made["maps"], size = enter_mixer(
            clock.hold(flat_input), norm_gain, w_bc, w_dt, dt_bias, made["w_in"]
        )
        size = size.reshape(requests, tok_block, local_mheads)
        log_decay = -size * jnp.exp(a_log)
        causal = jnp.arange(tok_block)[None, :] <= jnp.arange(tok_block)[:, None]
        decay = jnp.einsum(
            "tu,ruh->rth", causal.astype(jnp.float32), log_decay, precision=lax.Precision.HIGHEST
        )
        by_row = lambda value: jnp.transpose(value, (0, 2, 1)).reshape(
            requests, 1, local_mheads * tok_block
        )
        made["size"], made["decay"] = size, decay
        made["size_row"], made["decay_row"] = by_row(size), by_row(decay)
        return (made["act"], made["size_row"], made["decay_row"]), ()

    def inside():
        made["read"], made["local"], made["through"] = inside_block(
            requests,
            clock.hold(made["act"]),
            made["maps"],
            made["decay"],
            made["size"],
            made["decay_row"],
            made["size_row"],
            jnp.repeat(d_skip, MHEAD_DIM).reshape(1, local_inner),
        )
        return (made["read"], made["local"]), ()

    def start_relay():
        made["relay"] = relay = Relay(
            made["through"], clock.hold(made["local"]), made["initial"], seq_index, seq_count
        )
        return (), ((relay.pair_state,) if relay.paired else ())

    def hop():
        made["relay"].advance(clock)
        return (), (made["relay"].entry,)

    def end_relay():
        made["entry"] = made["relay"].result(clock)
        return (), (made["entry"],)

    def leave():
        gated, squares, chain = leave_mixer(
            clock.hold(made["entry"]),
            made["maps"],
            made["decay"],
            made["read"],
            made["act"],
            gated_gain.reshape(1, local_inner),
            made["local"],
            made["through"],
        )
        made["gated"] = gated
        made["squares"] = Exchange(
            squares[:, :1].reshape(1, tokens), "head", head_count, jnp.add
        )
        made["squares"].step(clock)
        made["chain"] = chain
        return (gated,), ()

    def join_squares():
        made["squares"].step(clock)
        return (), ()

    def leave_terms():
        squares = made["squares"].result(clock).reshape(tokens, 1)
        made["terms"] = jnp.dot(
            clock.hold(made["gated"]), w_out, preferred_element_type=jnp.float32
        ) * lax.rsqrt(squares / D_INNER + 1e-05)
        return (made["terms"],), ()

    query_ring, key_ring, value_ring = (Ring(w, order) for w in (w_query, w_key, w_value))
    slot_rings = []
    live = jnp.clip(lengths - seq_index * cache_block, 0, cache_block).astype(jnp.int32)
    first = (seq_index * tok_block).astype(jnp.int32).reshape(1)
    cached = []

    def make_queries():
        queries = by_request(product(query_ring.pieces, True))
        slot_rings.extend(
            Ring(queries[begin : begin + group], order) for begin in range(0, requests, group)
        )
        return (queries,), ()

    def make_keys():
        made["keys"] = by_request(product(key_ring.pieces, True))
        return (made["keys"],), ()

    def meet_cache(index):
        def work():
            ring = slot_rings[index]
            begin = index * group
            slots = [piece for _, _, piece in ring.pieces[:-2]]
            slots.append(jnp.concatenate([ring.pieces[-2][2], ring.pieces[-1][2]], axis=0))
            slots[0] = clock.hold(slots[0])
            cached.append(
                cache_part(
                    begin,
                    first,
                    places,
                    live[begin : begin + group],
                    slots,
                    cache_keys,
                    cache_values,
                    made["keys"],
                )
            )
            return tuple(cached[-1]), ()

        return work

    def join_peaks():
        peaks = jnp.concatenate([clock.hold(part[2]) for part in cached], axis=0)
        made["best"] = Exchange(peaks, "seq", seq_count, jnp.maximum)
        made["best"].step(clock)
        pieces = value_ring.pieces[1:-2]
        made["used"] = 1 + len(pieces)
        made["values"] = product(
            [(0, 0, clock.hold(value_ring.block))] + pieces, False, kind=jnp.float32
        )
        return (made["values"],), ()

    def join_more():
        made["best"].step(clock)
        return leave_terms()

    def steps(rings, begin, end):
        return [ring for _ in range(begin, end) for ring in rings]

    def run(sends, works):
        for index in range(max(len(sends), len(works))):
            clock.turn(
                sends[index] if index < len(sends) else None,
                works[index] if index < len(works) else None,
            )

    both = steps([query_ring, key_ring], 0, half - 2) + [query_ring] * 2 + [key_ring] * 2
    def make_queries_hop():
        done, _ = make_queries()
        return done, hop()[1]

    def make_keys_hop():
        deferred = hop()[1]
        return make_keys()[0], deferred

    works = [prepare, enter, inside, start_relay, None, hop]
    run(both, works + [None] * (len(both) - 1 - len(works)) + [make_queries_hop])
    run(
        steps(slot_rings, 0, half),
        [None, make_keys_hop, None, end_relay, None, leave, join_squares],
    )
    run(
        steps([value_ring], 0, half),
        [meet_cache(0), meet_cache(1)] + [None] * (half - 4) + [join_peaks, join_more],
    )

    new_keys = made["keys"]
    best = made["best"].result(clock)
    new_values = by_request(
        product(value_ring.pieces[made["used"] :], False, base=(made["values"],))
    )

    own = lambda stat: lax.dynamic_slice_in_dim(stat, seq_index * tok_block, tok_block, 2)
    greatest_logit = jnp.transpose(own(best), (0, 2, 1)) * SCALE
    residual = lax.dynamic_slice_in_dim(
        flat_input, head_index * local_width, local_width, 1
    ).astype(jnp.float32)
    sums, ring_sums, mixed = [], [], []

    def finish(index):
        def work():
            joined, out, peaks, totals = cached[index]
            some_sums, *parts = finish_part(
                index * group,
                first,
                places,
                clock.hold(joined),
                new_keys,
                new_values,
                out,
                peaks,
                totals,
                best,
            )
            sums.append(some_sums)
            terms = {-offset: part for offset, part in zip(offsets, parts)}
            terms[half] = terms[-half]
            ring_sums.append(RingSum(terms, order))
            return (some_sums, *parts), ()

        return work

    def add_sums():
        if "sums" not in made:
            made["sums"] = Exchange(jnp.concatenate(sums, axis=0), "seq", seq_count, jnp.add)
        made["sums"].step(clock)
        return (), ()

    run([], [finish(0)])
    run([ring_sums[0]], [finish(1)])
    run(
        steps(ring_sums[::-1], 0, half)[:-1],
        [add_sums, None, add_sums, None, add_sums],
    )
    denominators = jnp.transpose(own(made["sums"].result(clock)), (0, 2, 1))
    for index in range(GROUPS):
        begin = index * group
        denominator = denominators[begin : begin + group]
        numerator = ring_sums[index].total().reshape(group, tok_block, local_heads, HEAD_DIM)
        attended = (
            (numerator / denominator[..., None])
            .astype(jnp.bfloat16)
            .reshape(group * tok_block, local_att)
        )
        at = slice(begin * tok_block, (begin + group) * tok_block)
        attn_terms = jnp.dot(attended, w_attn_out, preferred_element_type=jnp.float32)
        summed = head_sum(attn_terms + made["terms"][at], head_count, head_index)
        mixed.append(
            (residual[at] + summed)
            .astype(jnp.bfloat16)
            .reshape(group, tok_block, local_width)
        )
    return (
        jnp.concatenate(mixed, axis=0),
        new_keys,
        new_values,
        made["chain"].reshape(requests, 1, local_mheads, MHEAD_DIM * STATE),
        greatest_logit,
    )


def solution(mesh):
    placed = (
        P(None, "seq", None),
        P(),
        P(None, "seq", "head"),
        P(None, "seq", "head"),
        P("seq", "head"),
        P("seq", "head"),
        P("seq", "head"),
        P("head", None),
        P(),
        P(None, None, "head"),
        P(),
        P(None, "head"),
        P("head"),
        P("head"),
        P("head"),
        P("head"),
        P("head", None),
        P(None, "head", None),
    )
    return jax.shard_map(
        shards,
        mesh=mesh,
        in_specs=placed,
        out_specs=(
            P(None, "seq", "head"),
            P(None, "seq", "head"),
            P(None, "seq", "head"),
            P(None, "seq", "head", None),
            P(None, "seq", "head"),
        ),
        check_vma=False,
    )
```

```python
import functools
import math

import jax
import jax.numpy as jnp
from jax import lax
from jax.experimental import pallas as pl
from jax.experimental.pallas import tpu as pltpu
from jax.sharding import PartitionSpec as P

D = 2048
HEAD_DIM = 128
MHEAD_DIM = 64
STATE = 64
D_INNER = 4096
SCALE = 1.0 / math.sqrt(HEAD_DIM)
EXP2_SCALE = SCALE * math.log2(math.e)
DEAD = -1e30
GROUPS = 2
VMEM_BYTES = 56 * 1024 * 1024


def ring_order(count):
    y_count = max(1, count // 4)
    z_count = count // y_count
    order = []
    for y in range(y_count):
        turn = range(z_count) if y % 2 == 0 else range(z_count - 1, -1, -1)
        order += [z * y_count + y for z in turn]
    return order


def ring_step(block, order, distance):
    count = len(order)
    route = [(order[i], order[(i + distance) % count]) for i in range(count)]
    return lax.ppermute(block, "seq", route)


class Ring:
    def __init__(self, block, order, first_row=0):
        self.order = order
        self.steps = len(order) // 2
        self.done = 0
        self.first_row = first_row
        self.block = self.ahead = self.back = block
        self.pieces = [(0, first_row, block)]

    def step(self, clock):
        self.done += 1
        half = self.block.shape[0] // 2
        last = self.done == self.steps
        ahead = self.ahead[:half] if last else self.ahead
        back = self.back[half:] if last else self.back
        ahead, back = clock.hold(ahead, back)
        self.ahead = ring_step(ahead, self.order, 1)
        self.back = ring_step(back, self.order, -1)
        at = self.first_row
        if last:
            self.pieces += [(self.steps, at, self.ahead), (self.steps, at + half, self.back)]
        else:
            self.pieces += [(self.done, at, self.ahead), (-self.done, at, self.back)]
        return [self.ahead, self.back]


class Clock:
    def __init__(self, mark):
        self.mark = mark
        self.late = ()

    def hold(self, *values):
        held = lax.optimization_barrier(tuple(values) + (self.mark,))[: len(values)]
        return held[0] if len(values) == 1 else held

    def turn(self, ring=None, work=None):
        moved = tuple(ring.step(self)) if ring is not None else ()
        done, deferred = work() if work is not None else ((), ())
        self.mark = lax.optimization_barrier((self.mark,) + self.late + tuple(done))[0]
        self.late = moved + tuple(deferred)


class Exchange:
    def __init__(self, value, axis, count, combine):
        self.value, self.axis, self.count, self.combine = value, axis, count, combine
        self.got = None
        self.bit = 1

    def join(self, clock):
        if self.got is not None:
            self.value = self.combine(*clock.hold(self.value, self.got))
            self.got = None

    def step(self, clock):
        self.join(clock)
        if self.bit < self.count:
            route = [(i, i ^ self.bit) for i in range(self.count)]
            self.got = lax.ppermute(self.value, self.axis, route)
            self.bit *= 2

    def result(self, clock):
        while self.bit < self.count:
            self.step(clock)
        self.join(clock)
        return self.value


class RingSum:
    def __init__(self, parts, order):
        self.parts, self.order = parts, order
        self.left = len(order) // 2
        self.half = parts[0].shape[0] // 2
        self.ahead = self.back = None

    def add(self, a, b):
        return (a.astype(jnp.float32) + b.astype(jnp.float32)).astype(jnp.bfloat16)

    def step(self, clock):
        half, left, far = self.half, self.left, len(self.order) // 2
        top, bottom = self.parts[left], self.parts[-left]
        if left == far:
            ahead, back = top[:half], bottom[half:]
        elif left == far - 1:
            ahead = jnp.concatenate([self.add(self.ahead, top[:half]), top[half:]], axis=0)
            back = jnp.concatenate([bottom[:half], self.add(self.back, bottom[half:])], axis=0)
        else:
            ahead, back = self.add(self.ahead, top), self.add(self.back, bottom)
        ahead, back = clock.hold(ahead, back)
        self.ahead = ring_step(ahead, self.order, 1)
        self.back = ring_step(back, self.order, -1)
        self.left -= 1
        return [self.ahead, self.back]

    def total(self):
        return sum(value.astype(jnp.float32) for value in (self.ahead, self.back, self.parts[0]))


def project_kernel(count, turned, places_ref, *refs):
    input_refs, weight_refs = refs[:count], refs[count : 2 * count]
    cosine_ref, sine_ref, *base_ref, out_ref = refs[2 * count :]
    total = base_ref[0][...] if base_ref else None
    for input_ref, weight_ref in zip(input_refs, weight_refs):
        term = jnp.dot(input_ref[...], weight_ref[...], preferred_element_type=jnp.float32)
        total = term if total is None else total + term
    if not turned:
        out_ref[...] = total.astype(out_ref.dtype)
        return
    cosine = cosine_ref[...]
    sine = sine_ref[...]
    for head in range(out_ref.shape[1] // HEAD_DIM):
        at = slice(head * HEAD_DIM, (head + 1) * HEAD_DIM)
        part = total[:, at]
        rolled = pltpu.roll(part, HEAD_DIM // 2, 1)
        out_ref[:, at] = (part * cosine + rolled * sine).astype(out_ref.dtype)


def project(places, offsets, rows, value, pieces, cosine, sine, turned, base=(), kind=jnp.bfloat16):
    tokens = value.shape[0]
    width = pieces[0][2].shape[1]
    block = min(width, 256)
    input_specs, weight_specs = [], []
    for offset, row, piece in pieces:
        depth = piece.shape[0]

        def place(j, places_ref, slot=offsets.index(offset), scale=rows // depth, at=row // depth):
            return (0, places_ref[slot] * scale + at)

        input_specs.append(pl.BlockSpec((tokens, depth), place))
        weight_specs.append(pl.BlockSpec((depth, block), lambda j, *_: (0, j)))
    angle = pl.BlockSpec((tokens, HEAD_DIM), lambda j, *_: (0, 0))
    return pl.pallas_call(
        functools.partial(project_kernel, len(pieces), turned),
        grid_spec=pltpu.PrefetchScalarGridSpec(
            num_scalar_prefetch=1,
            grid=(width // block,),
            in_specs=input_specs
            + weight_specs
            + [angle, angle]
            + [pl.BlockSpec((tokens, block), lambda j, *_: (0, j))] * len(base),
            out_specs=pl.BlockSpec((tokens, block), lambda j, *_: (0, j)),
        ),
        out_shape=jax.ShapeDtypeStruct((tokens, width), kind),
        compiler_params=pltpu.CompilerParams(vmem_limit_bytes=VMEM_BYTES),
        cost_estimate=pl.CostEstimate(
            flops=2 * tokens * sum(piece.shape[0] for _, _, piece in pieces) * width,
            bytes_accessed=2 * (tokens + width) * value.shape[1],
            transcendentals=0,
        ),
        name="project",
    )(places, *[value] * len(pieces), *[piece for _, _, piece in pieces], cosine, sine, *base)


def silu(value):
    return value / (1.0 + jnp.exp(-value))


def exact_dot(a, b):
    return jnp.dot(a, b, precision=lax.Precision.HIGHEST, preferred_element_type=jnp.float32)


def spread(heads, block):
    shape = (heads, heads * block)
    column = lax.broadcasted_iota(jnp.int32, shape, 1) // block
    return (column == lax.broadcasted_iota(jnp.int32, shape, 0)).astype(jnp.float32)


def enter_kernel(input_ref, gain_ref, bc_ref, dt_ref, bias_ref, weight_ref, act_ref, map_ref, size_ref, normed_ref):
    @pl.when(pl.program_id(0) == 0)
    def _():
        rows = input_ref.shape[0]
        chunk = min(rows, 64)
        for start in range(0, rows, chunk):
            at = slice(start, start + chunk)
            hidden = input_ref[at, :].astype(jnp.float32)
            scale = lax.rsqrt(jnp.mean(hidden * hidden, axis=-1, keepdims=True) + 1e-05)
            normed_ref[at, :] = (hidden * scale * gain_ref[...]).astype(jnp.bfloat16)
        normed = normed_ref[...]
        map_ref[...] = jnp.dot(normed, bc_ref[...], preferred_element_type=jnp.float32)
        size = jnp.dot(normed, dt_ref[...], preferred_element_type=jnp.float32) + bias_ref[...]
        size_ref[...] = jnp.maximum(size, 0.0) + jnp.log1p(jnp.exp(-jnp.abs(size)))

    act_ref[...] = silu(
        jnp.dot(normed_ref[...], weight_ref[...], preferred_element_type=jnp.float32)
    )


def enter_mixer(flat_input, norm_gain, w_bc, w_dt, dt_bias, weight):
    tokens = flat_input.shape[0]
    width = weight.shape[1]
    block = min(width, 512)
    heads = w_dt.shape[1]
    whole = lambda *shape: pl.BlockSpec(shape, lambda j: (0, 0))
    return pl.pallas_call(
        enter_kernel,
        grid=(width // block,),
        in_specs=[
            whole(tokens, D),
            whole(1, D),
            whole(D, 2 * STATE),
            whole(D, heads),
            whole(1, heads),
            pl.BlockSpec((D, block), lambda j: (0, j)),
        ],
        out_specs=[
            pl.BlockSpec((tokens, block), lambda j: (0, j)),
            whole(tokens, 2 * STATE),
            whole(tokens, heads),
        ],
        out_shape=[
            jax.ShapeDtypeStruct((tokens, width), jnp.float32),
            jax.ShapeDtypeStruct((tokens, 2 * STATE), jnp.float32),
            jax.ShapeDtypeStruct((tokens, heads), jnp.float32),
        ],
        scratch_shapes=[pltpu.VMEM((tokens, D), jnp.bfloat16)],
        compiler_params=pltpu.CompilerParams(vmem_limit_bytes=VMEM_BYTES),
        cost_estimate=pl.CostEstimate(
            flops=2 * tokens * D * width,
            bytes_accessed=2 * D * (width + tokens) + 4 * tokens * width,
            transcendentals=tokens * width,
        ),
        name="enter_mixer",
    )(flat_input, norm_gain.reshape(1, D), w_bc, w_dt, dt_bias.reshape(1, heads), weight)


def inside_kernel(inner_ref, map_ref, decay_ref, size_ref, decay_row_ref, size_row_ref, skip_ref, read_ref, local_ref, through_ref):
    tokens, heads = decay_ref.shape[1:]
    inner = inner_ref[...]
    input_map = map_ref[:, :STATE]
    output_map = map_ref[:, STATE:]
    decay = decay_ref[0]
    by_head = spread(heads, MHEAD_DIM)
    wide = (tokens, heads * tokens)
    contact = dot_nt(
        output_map.astype(jnp.bfloat16),
        jnp.concatenate([input_map.astype(jnp.bfloat16)] * heads, axis=0),
    )
    source = lax.rem(lax.broadcasted_iota(jnp.int32, wide, 1), tokens)
    causal = source <= lax.broadcasted_iota(jnp.int32, wide, 0)
    difference = exact_dot(decay, spread(heads, tokens)) - decay_row_ref[0]
    mixing = jnp.exp(jnp.where(causal, difference, DEAD)) * contact * size_row_ref[0]
    mixing = mixing.astype(jnp.bfloat16)
    inner_low = inner.astype(jnp.bfloat16)
    together = min(heads, 256 // MHEAD_DIM)
    shape = (together * tokens, together * MHEAD_DIM)
    own = (
        lax.broadcasted_iota(jnp.int32, shape, 0) // tokens
        == lax.broadcasted_iota(jnp.int32, shape, 1) // MHEAD_DIM
    )
    for begin in range(0, heads, together):
        at = slice(begin * MHEAD_DIM, (begin + together) * MHEAD_DIM)
        stacked = jnp.concatenate([inner_low[:, at]] * together, axis=0)
        stacked = jnp.where(own, stacked, jnp.zeros_like(stacked))
        read_ref[:, at] = (
            jnp.dot(
                mixing[:, begin * tokens : (begin + together) * tokens],
                stacked,
                preferred_element_type=jnp.float32,
            )
            + skip_ref[:, at] * inner[:, at]
        )
    last = decay[tokens - 1 :, :]
    tail = exact_dot(jnp.exp(last - decay) * size_ref[0], by_head)
    local_ref[0] = dot_tn(input_map.astype(jnp.bfloat16), (inner * tail).astype(jnp.bfloat16))
    through_ref[0] = exact_dot(jnp.exp(jnp.broadcast_to(last, (8, heads))), by_head)[:1]


def inside_block(requests, act, maps, decay, size, decay_row, size_row, skip):
    tokens, heads = decay.shape[1:]
    inner = act.shape[1] // 2
    one = lambda *shape: pl.BlockSpec((1,) + shape, lambda r: (r, 0, 0))
    return pl.pallas_call(
        inside_kernel,
        grid=(requests,),
        in_specs=[
            pl.BlockSpec((tokens, inner), lambda r: (r, 1)),
            pl.BlockSpec((tokens, 2 * STATE), lambda r: (r, 0)),
            one(tokens, heads),
            one(tokens, heads),
            one(1, heads * tokens),
            one(1, heads * tokens),
            pl.BlockSpec((1, inner), lambda r: (0, 0)),
        ],
        out_specs=[
            pl.BlockSpec((tokens, inner), lambda r: (r, 0)),
            one(STATE, inner),
            one(1, inner),
        ],
        out_shape=[
            jax.ShapeDtypeStruct((requests * tokens, inner), jnp.float32),
            jax.ShapeDtypeStruct((requests, STATE, inner), jnp.float32),
            jax.ShapeDtypeStruct((requests, 1, inner), jnp.float32),
        ],
        compiler_params=pltpu.CompilerParams(vmem_limit_bytes=VMEM_BYTES),
        cost_estimate=pl.CostEstimate(
            flops=12 * requests * tokens * tokens * inner,
            bytes_accessed=16 * requests * tokens * inner,
            transcendentals=requests * tokens * tokens * heads,
        ),
        name="inside_block",
    )(act, maps, decay, size, decay_row, size_row, skip)


def leave_kernel(entry_ref, map_ref, decay_ref, read_ref, gate_ref, gain_ref, local_ref, through_ref, gated_ref, square_ref, chain_ref):
    heads = decay_ref.shape[2]
    entry = entry_ref[0]
    grown = exact_dot(jnp.exp(decay_ref[0]), spread(heads, MHEAD_DIM))
    inter = jnp.dot(
        map_ref[:, STATE:].astype(jnp.bfloat16),
        entry.astype(jnp.bfloat16),
        preferred_element_type=jnp.float32,
    )
    mixed = (read_ref[...] + inter * grown) * gate_ref[...]
    squares = jnp.sum(mixed * mixed, axis=1, keepdims=True)
    square_ref[...] = jnp.broadcast_to(squares, square_ref.shape)
    gated_ref[...] = (mixed * gain_ref[...]).astype(jnp.bfloat16)
    chain_ref[0] = through_ref[0] * entry + local_ref[0]


def leave_mixer(entry, maps, decay, read, act, gain, local, through):
    requests, tokens, heads = decay.shape
    inner = read.shape[1]
    one = lambda *shape: pl.BlockSpec((1,) + shape, lambda r: (r, 0, 0))
    flat = lambda width: pl.BlockSpec((tokens, width), lambda r: (r, 0))
    return pl.pallas_call(
        leave_kernel,
        grid=(requests,),
        in_specs=[
            one(STATE, inner),
            flat(2 * STATE),
            one(tokens, heads),
            flat(inner),
            flat(inner),
            pl.BlockSpec((1, inner), lambda r: (0, 0)),
            one(STATE, inner),
            one(1, inner),
        ],
        out_specs=[flat(inner), flat(128), one(STATE, inner)],
        out_shape=[
            jax.ShapeDtypeStruct((requests * tokens, inner), jnp.bfloat16),
            jax.ShapeDtypeStruct((requests * tokens, 128), jnp.float32),
            jax.ShapeDtypeStruct((requests, STATE, inner), jnp.float32),
        ],
        compiler_params=pltpu.CompilerParams(vmem_limit_bytes=VMEM_BYTES),
        cost_estimate=pl.CostEstimate(
            flops=2 * requests * tokens * STATE * inner,
            bytes_accessed=24 * requests * tokens * inner,
            transcendentals=requests * tokens * heads,
        ),
        name="leave_mixer",
    )(entry, maps, decay, read, act, gain, local, through)


def dot_nt(a, b):
    return lax.dot_general(a, b, (((1,), (1,)), ((), ())), preferred_element_type=jnp.float32)


def dot_tn(a, b):
    return lax.dot_general(a, b, (((0,), (0,)), ((), ())), preferred_element_type=jnp.float32)


def group_scores(first, key, query):
    scores = dot_nt(key, query)
    shape = scores.shape
    live = first + lax.broadcasted_iota(jnp.int32, shape, 0) <= lax.broadcasted_iota(
        jnp.int32, shape, 1
    )
    return jnp.where(live, scores, DEAD)


def cache_kernel(slots, first_ref, place_ref, live_ref, *refs):
    query_refs = refs[:slots]
    key_ref, value_ref, group_ref, joined_ref, out_ref, peak_ref, total_ref = refs[slots:]
    tok_block = query_refs[0].shape[1]
    keys, width = key_ref.shape[1:]
    tokens = tok_block * slots
    for slot in range(slots):
        start = pl.multiple_of(place_ref[slot] * tok_block, tok_block)
        joined_ref[0, pl.ds(start, tok_block), :] = query_refs[slot][0]
    live = live_ref[pl.program_id(0)]
    bias = jnp.where(
        lax.broadcasted_iota(jnp.int32, (keys, 128), 0) < live, 0.0, DEAD
    ).astype(jnp.float32)
    bias = jnp.concatenate([bias] * (tokens // 128), axis=1)
    for head in range(width // HEAD_DIM):
        at = slice(head * HEAD_DIM, (head + 1) * HEAD_DIM)
        query = joined_ref[0, :, at]
        scores = dot_nt(key_ref[0, :, at], query) + bias
        peak = jnp.maximum(
            jnp.max(scores, axis=0, keepdims=True),
            jnp.max(
                group_scores(first_ref[0], group_ref[0, :, at], query), axis=0, keepdims=True
            ),
        )
        weights = jnp.exp2((scores - peak) * EXP2_SCALE)
        total_ref[0, head : head + 1, :] = jnp.sum(weights, axis=0, keepdims=True)
        peak_ref[0, head : head + 1, :] = peak
        out_ref[0, at, :] = dot_tn(value_ref[0, :, at], weights.astype(jnp.bfloat16)).astype(
            out_ref.dtype
        )


def cache_part(begin, first, places, live, query_slots, keys, values, new_keys):
    slots = len(query_slots)
    requests, tok_block, width = query_slots[0].shape
    tokens = tok_block * slots
    cache_block = keys.shape[1]
    heads = width // HEAD_DIM
    one = lambda rows, start: pl.BlockSpec((1, rows, width), lambda r, *_: (r + start, 0, 0))
    stat = pl.BlockSpec((1, heads, tokens), lambda r, *_: (r, 0, 0))
    return pl.pallas_call(
        functools.partial(cache_kernel, slots),
        grid_spec=pltpu.PrefetchScalarGridSpec(
            num_scalar_prefetch=3,
            grid=(requests,),
            in_specs=[one(tok_block, 0)] * slots
            + [one(cache_block, begin)] * 2
            + [one(tok_block, begin)],
            out_specs=[
                one(tokens, 0),
                pl.BlockSpec((1, width, tokens), lambda r, *_: (r, 0, 0)),
                stat,
                stat,
            ],
        ),
        out_shape=[
            jax.ShapeDtypeStruct((requests, tokens, width), jnp.bfloat16),
            jax.ShapeDtypeStruct((requests, width, tokens), jnp.bfloat16),
            jax.ShapeDtypeStruct((requests, heads, tokens), jnp.float32),
            jax.ShapeDtypeStruct((requests, heads, tokens), jnp.float32),
        ],
        compiler_params=pltpu.CompilerParams(vmem_limit_bytes=VMEM_BYTES),
        cost_estimate=pl.CostEstimate(
            flops=4 * requests * tokens * cache_block * width,
            bytes_accessed=2 * requests * width * (3 * tokens + 2 * cache_block),
            transcendentals=requests * tokens * cache_block * heads,
        ),
        name="cache_part",
    )(first, places, live, *query_slots, keys, values, new_keys)


def finish_kernel(slots, first_ref, place_ref, *refs):
    query_ref, key_ref, value_ref, cache_ref, peak_ref, total_ref, best_ref = refs[:7]
    sum_ref, *part_refs = refs[7:-1]
    joined_ref = refs[-1]
    tok_block = key_ref.shape[1]
    for head in range(query_ref.shape[2] // HEAD_DIM):
        at = slice(head * HEAD_DIM, (head + 1) * HEAD_DIM)
        row = slice(head, head + 1)
        scores = group_scores(first_ref[0], key_ref[0, :, at], query_ref[0, :, at])
        best = best_ref[0, row, :]
        weights = jnp.exp2((scores - best) * EXP2_SCALE)
        rescale = jnp.exp2((peak_ref[0, row, :] - best) * EXP2_SCALE)
        sum_ref[0, row, :] = total_ref[0, row, :] * rescale + jnp.sum(
            weights, axis=0, keepdims=True
        )
        joined = cache_ref[0, at, :].astype(jnp.float32) * rescale + dot_tn(
            value_ref[0, :, at], weights.astype(jnp.bfloat16)
        )
        joined_ref[:, at] = joined.astype(jnp.bfloat16).T
    for slot in range(slots):
        start = pl.multiple_of(place_ref[slot] * tok_block, tok_block)
        part_refs[slot][0] = joined_ref[pl.ds(start, tok_block), :]


def finish_part(begin, first, places, queries, new_keys, new_values, cached, peaks, totals, best):
    requests, tokens, width = queries.shape
    tok_block = new_keys.shape[1]
    slots = tokens // tok_block
    heads = width // HEAD_DIM
    one = lambda rows, start: pl.BlockSpec((1, rows, width), lambda r, *_: (r + start, 0, 0))
    stat = lambda start: pl.BlockSpec((1, heads, tokens), lambda r, *_: (r + start, 0, 0))
    return pl.pallas_call(
        functools.partial(finish_kernel, slots),
        grid_spec=pltpu.PrefetchScalarGridSpec(
            num_scalar_prefetch=2,
            grid=(requests,),
            in_specs=[
                one(tokens, 0),
                one(tok_block, begin),
                one(tok_block, begin),
                pl.BlockSpec((1, width, tokens), lambda r, *_: (r, 0, 0)),
                stat(0),
                stat(0),
                stat(begin),
            ],
            out_specs=[stat(0)] + [one(tok_block, 0)] * slots,
            scratch_shapes=[pltpu.VMEM((tokens, width), jnp.bfloat16)],
        ),
        out_shape=[jax.ShapeDtypeStruct((requests, heads, tokens), jnp.float32)]
        + [jax.ShapeDtypeStruct((requests, tok_block, width), jnp.bfloat16)] * slots,
        compiler_params=pltpu.CompilerParams(vmem_limit_bytes=VMEM_BYTES),
        cost_estimate=pl.CostEstimate(
            flops=4 * requests * tokens * tok_block * width,
            bytes_accessed=6 * requests * width * tokens,
            transcendentals=requests * tokens * tok_block * heads,
        ),
        name="finish_part",
    )(first, places, queries, new_keys, new_values, cached, peaks, totals, best)


def head_sum(terms, head_count, head_index):
    if head_count != 4:
        return lax.psum_scatter(
            terms.astype(jnp.bfloat16), "head", scatter_dimension=1, tiled=True
        ).astype(jnp.float32)
    width = terms.shape[1] // 4
    chunk = lambda index: lax.dynamic_slice_in_dim(terms, index * width, width, 1)
    core, column = head_index % 2, head_index // 2
    near, far = 2 * column, 2 * (1 - column)
    got = lax.ppermute(
        jnp.concatenate([chunk(near + 1 - core), chunk(far + 1 - core)], axis=1).astype(
            jnp.bfloat16
        ),
        "head",
        [(h, h ^ 1) for h in range(4)],
    ).astype(jnp.float32)
    keep = chunk(near + core) + got[:, :width]
    give = chunk(far + core) + got[:, width:]
    return keep + lax.ppermute(
        give.astype(jnp.bfloat16), "head", [(h, h ^ 2) for h in range(4)]
    ).astype(jnp.float32)


class Relay:
    def __init__(self, through, local, initial, seq_index, seq_count):
        self.factor, self.local = through, local
        self.paired = seq_count == 8
        self.hop = 0
        if not self.paired:
            self.hops = seq_count - 1
            self.entry = jnp.where(seq_index == 0, initial, 0.0)
            return
        self.hops = 3
        self.swap = [(i, i ^ 1) for i in range(8)]
        self.is_first = is_first = seq_index % 2 == 0
        half = local.shape[2] // 2
        side = lambda value: jnp.where(is_first, value[..., :half], value[..., half:])
        mine = side(local)
        got = self.exchange(jnp.where(is_first, local[..., half:], local[..., :half]))
        other_factor = side(lax.ppermute(through, "seq", self.swap))
        factor = side(through)
        self.first_state = jnp.where(is_first, mine, got)
        second_state = jnp.where(is_first, got, mine)
        self.first_factor = jnp.where(is_first, factor, other_factor)
        second_factor = jnp.where(is_first, other_factor, factor)
        self.pair_state = second_factor * self.first_state + second_state
        self.pair_factor = self.first_factor * second_factor
        self.entry = jnp.where(seq_index < 2, side(initial), 0.0)

    def exchange(self, value):
        return lax.ppermute(value.astype(jnp.bfloat16), "seq", self.swap).astype(jnp.float32)

    def advance(self, clock):
        if self.hop == self.hops:
            return
        factor, state = (
            (self.pair_factor, self.pair_state) if self.paired else (self.factor, self.local)
        )
        entry = clock.hold(self.entry)
        leaving = (factor * entry + state).astype(jnp.bfloat16)
        if self.paired:
            route = [(2 * self.hop + y, 2 * self.hop + 2 + y) for y in range(2)]
        else:
            route = [(self.hop, self.hop + 1)]
        self.hop += 1
        self.entry = entry + lax.ppermute(leaving, "seq", route).astype(jnp.float32)

    def result(self, clock):
        while self.hop < self.hops:
            self.advance(clock)
        entry = clock.hold(self.entry)
        if not self.paired:
            return entry
        second = self.first_factor * entry + self.first_state
        got = self.exchange(jnp.where(self.is_first, second, entry))
        mine = jnp.where(self.is_first, entry, second)
        return jnp.concatenate(
            [jnp.where(self.is_first, mine, got), jnp.where(self.is_first, got, mine)], axis=2
        )


def shards(
    block_input,
    lengths,
    cache_keys,
    cache_values,
    w_query,
    w_key,
    w_value,
    w_attn_out,
    norm_gain,
    w_in,
    w_bc,
    w_dt,
    dt_bias,
    a_log,
    d_skip,
    gated_gain,
    w_out,
    ssm_init,
):
    requests, tok_block, _ = block_input.shape
    seq_count = lax.axis_size("seq")
    seq_index = lax.axis_index("seq")
    head_count = lax.axis_size("head")
    head_index = lax.axis_index("head")
    local_att = w_query.shape[1]
    local_heads = local_att // HEAD_DIM
    cache_block = cache_keys.shape[1]
    rows = w_query.shape[0]
    tokens = requests * tok_block
    flat_input = block_input.reshape(tokens, block_input.shape[2])

    order = ring_order(seq_count)
    half = seq_count // 2
    offsets = [0] + [sign * step for step in range(1, half) for sign in (1, -1)] + [half]
    places = jnp.asarray(
        [
            [order[(order.index(i) - offset) % seq_count] for offset in offsets]
            for i in range(seq_count)
        ],
        jnp.int32,
    )[seq_index]

    positions = (
        lengths[:, None] + seq_index * tok_block + jnp.arange(tok_block, dtype=jnp.int32)[None, :]
    ).reshape(tokens)
    half_dim = HEAD_DIM // 2
    frequency = jnp.exp(
        jnp.arange(half_dim, dtype=jnp.float32) * (-2.0 * math.log(10000.0) / HEAD_DIM)
    )
    angles = positions.astype(jnp.float32)[:, None] * frequency
    cosine = jnp.cos(angles)
    sine = jnp.sin(angles)
    cosine = jnp.concatenate([cosine, cosine], axis=1)
    sine = jnp.concatenate([-sine, sine], axis=1)

    clock = Clock(jnp.zeros((1,), jnp.int32) + lengths[:1])
    group = requests // GROUPS
    local_inner = w_in.shape[2]
    local_mheads = local_inner // MHEAD_DIM
    local_width = D // head_count
    made = {}

    def product(pieces, turned, base=(), kind=jnp.bfloat16):
        pieces = list(pieces)
        if pieces[-1][2].shape[0] < 128:
            (offset, row, upper), (_, _, lower) = pieces[-2:]
            pieces[-2:] = [(offset, row, jnp.concatenate([upper, lower], axis=0))]
        return project(
            places, offsets, rows, flat_input, pieces, cosine, sine, turned, base, kind
        )

    by_request = lambda value: value.reshape(requests, tok_block, local_att)

    def prepare():
        made["w_in"] = w_in.reshape(D, 2 * local_inner)
        first_state = ssm_init.reshape(requests, local_mheads, MHEAD_DIM, STATE)
        made["initial"] = jnp.transpose(first_state, (0, 3, 1, 2)).reshape(
            requests, STATE, local_inner
        )
        return (made["w_in"], made["initial"]), ()

    def enter():
        made["act"], made["maps"], size = enter_mixer(
            clock.hold(flat_input), norm_gain, w_bc, w_dt, dt_bias, made["w_in"]
        )
        size = size.reshape(requests, tok_block, local_mheads)
        log_decay = -size * jnp.exp(a_log)
        causal = jnp.arange(tok_block)[None, :] <= jnp.arange(tok_block)[:, None]
        decay = jnp.einsum(
            "tu,ruh->rth", causal.astype(jnp.float32), log_decay, precision=lax.Precision.HIGHEST
        )
        by_row = lambda value: jnp.transpose(value, (0, 2, 1)).reshape(
            requests, 1, local_mheads * tok_block
        )
        made["size"], made["decay"] = size, decay
        made["size_row"], made["decay_row"] = by_row(size), by_row(decay)
        return (made["act"], made["size_row"], made["decay_row"]), ()

    def inside():
        made["read"], made["local"], made["through"] = inside_block(
            requests,
            clock.hold(made["act"]),
            made["maps"],
            made["decay"],
            made["size"],
            made["decay_row"],
            made["size_row"],
            jnp.repeat(d_skip, MHEAD_DIM).reshape(1, local_inner),
        )
        return (made["read"], made["local"]), ()

    def start_relay():
        made["relay"] = relay = Relay(
            made["through"], clock.hold(made["local"]), made["initial"], seq_index, seq_count
        )
        return (), ((relay.pair_state,) if relay.paired else ())

    def hop():
        made["relay"].advance(clock)
        return (), (made["relay"].entry,)

    def end_relay():
        made["entry"] = made["relay"].result(clock)
        return (), (made["entry"],)

    def leave():
        gated, squares, chain = leave_mixer(
            clock.hold(made["entry"]),
            made["maps"],
            made["decay"],
            made["read"],
            made["act"],
            gated_gain.reshape(1, local_inner),
            made["local"],
            made["through"],
        )
        made["gated"] = gated
        made["squares"] = Exchange(
            squares[:, :1].reshape(1, tokens), "head", head_count, jnp.add
        )
        made["squares"].step(clock)
        made["chain"] = chain
        return (gated,), ()

    def join_squares():
        made["squares"].step(clock)
        return (), ()

    def leave_terms():
        squares = made["squares"].result(clock).reshape(tokens, 1)
        made["terms"] = jnp.dot(
            clock.hold(made["gated"]), w_out, preferred_element_type=jnp.float32
        ) * lax.rsqrt(squares / D_INNER + 1e-05)
        return (made["terms"],), ()

    def leave_chain():
        chain = clock.hold(made["chain"]).reshape(requests, STATE, local_mheads, MHEAD_DIM)
        made["chain"] = jnp.transpose(chain, (0, 2, 3, 1)).reshape(
            requests, 1, local_mheads, MHEAD_DIM * STATE
        )
        return (made["chain"],), ()

    query_ring, key_ring, value_ring = (Ring(w, order) for w in (w_query, w_key, w_value))
    slot_rings = []
    live = jnp.clip(lengths - seq_index * cache_block, 0, cache_block).astype(jnp.int32)
    first = (seq_index * tok_block).astype(jnp.int32).reshape(1)
    cached = []

    def make_queries():
        queries = by_request(product(query_ring.pieces, True))
        slot_rings.extend(
            Ring(queries[begin : begin + group], order) for begin in range(0, requests, group)
        )
        return (queries,), ()

    def make_keys():
        made["keys"] = by_request(product(key_ring.pieces, True))
        return (made["keys"],), ()

    def meet_cache(index):
        def work():
            ring = slot_rings[index]
            begin = index * group
            slots = [piece for _, _, piece in ring.pieces[:-2]]
            slots.append(jnp.concatenate([ring.pieces[-2][2], ring.pieces[-1][2]], axis=0))
            slots[0] = clock.hold(slots[0])
            cached.append(
                cache_part(
                    begin,
                    first,
                    places,
                    live[begin : begin + group],
                    slots,
                    cache_keys,
                    cache_values,
                    made["keys"],
                )
            )
            return tuple(cached[-1]), ()

        return work

    def join_peaks():
        peaks = jnp.concatenate([clock.hold(part[2]) for part in cached], axis=0)
        made["best"] = Exchange(peaks, "seq", seq_count, jnp.maximum)
        made["best"].step(clock)
        pieces = value_ring.pieces[1:-2]
        made["used"] = 1 + len(pieces)
        made["values"] = product(
            [(0, 0, clock.hold(value_ring.block))] + pieces, False, kind=jnp.float32
        )
        return (made["values"],) + leave_chain()[0], ()

    def join_more():
        made["best"].step(clock)
        return leave_terms()

    def steps(rings, begin, end):
        return [ring for _ in range(begin, end) for ring in rings]

    def run(sends, works):
        for index in range(max(len(sends), len(works))):
            clock.turn(
                sends[index] if index < len(sends) else None,
                works[index] if index < len(works) else None,
            )

    both = steps([query_ring, key_ring], 0, half - 2) + [query_ring] * 2 + [key_ring] * 2
    def make_queries_hop():
        done, _ = make_queries()
        return done, hop()[1]

    def make_keys_hop():
        deferred = hop()[1]
        return make_keys()[0], deferred

    works = [prepare, enter, inside, start_relay, None, hop]
    run(both, works + [None] * (len(both) - 1 - len(works)) + [make_queries_hop])
    run(
        steps(slot_rings, 0, half),
        [None, make_keys_hop, None, end_relay, None, leave, join_squares],
    )
    run(
        steps([value_ring], 0, half),
        [meet_cache(0), meet_cache(1)] + [None] * (half - 4) + [join_peaks, join_more],
    )

    new_keys = made["keys"]
    best = made["best"].result(clock)
    new_values = by_request(
        product(value_ring.pieces[made["used"] :], False, base=(made["values"],))
    )

    own = lambda stat: lax.dynamic_slice_in_dim(stat, seq_index * tok_block, tok_block, 2)
    greatest_logit = jnp.transpose(own(best), (0, 2, 1)) * SCALE
    residual = lax.dynamic_slice_in_dim(
        flat_input, head_index * local_width, local_width, 1
    ).astype(jnp.float32)
    sums, ring_sums, mixed = [], [], []

    def finish(index):
        def work():
            joined, out, peaks, totals = cached[index]
            some_sums, *parts = finish_part(
                index * group,
                first,
                places,
                clock.hold(joined),
                new_keys,
                new_values,
                out,
                peaks,
                totals,
                best,
            )
            sums.append(some_sums)
            terms = {-offset: part for offset, part in zip(offsets, parts)}
            terms[half] = terms[-half]
            ring_sums.append(RingSum(terms, order))
            return (some_sums, *parts), ()

        return work

    def add_sums():
        if "sums" not in made:
            made["sums"] = Exchange(jnp.concatenate(sums, axis=0), "seq", seq_count, jnp.add)
        made["sums"].step(clock)
        return (), ()

    run([], [finish(0)])
    run([ring_sums[0]], [finish(1)])
    run(steps(ring_sums[::-1], 0, half)[:-1], [add_sums, None, add_sums, None, add_sums])
    denominators = jnp.transpose(own(made["sums"].result(clock)), (0, 2, 1))
    for index in range(GROUPS):
        begin = index * group
        denominator = denominators[begin : begin + group]
        numerator = ring_sums[index].total().reshape(group, tok_block, local_heads, HEAD_DIM)
        attended = (
            (numerator / denominator[..., None])
            .astype(jnp.bfloat16)
            .reshape(group * tok_block, local_att)
        )
        at = slice(begin * tok_block, (begin + group) * tok_block)
        attn_terms = jnp.dot(attended, w_attn_out, preferred_element_type=jnp.float32)
        summed = head_sum(attn_terms + made["terms"][at], head_count, head_index)
        mixed.append(
            (residual[at] + summed)
            .astype(jnp.bfloat16)
            .reshape(group, tok_block, local_width)
        )
    return (
        jnp.concatenate(mixed, axis=0),
        new_keys,
        new_values,
        made["chain"],
        greatest_logit,
    )


def solution(mesh):
    placed = (
        P(None, "seq", None),
        P(),
        P(None, "seq", "head"),
        P(None, "seq", "head"),
        P("seq", "head"),
        P("seq", "head"),
        P("seq", "head"),
        P("head", None),
        P(),
        P(None, None, "head"),
        P(),
        P(None, "head"),
        P("head"),
        P("head"),
        P("head"),
        P("head"),
        P("head", None),
        P(None, "head", None),
    )
    return jax.shard_map(
        shards,
        mesh=mesh,
        in_specs=placed,
        out_specs=(
            P(None, "seq", "head"),
            P(None, "seq", "head"),
            P(None, "seq", "head"),
            P(None, "seq", "head", None),
            P(None, "seq", "head"),
        ),
        check_vma=False,
    )
```
